32 devices in a mesh: groups: 2 (over y), ctx: 4 (over z), dom: 2 (over x), tp: 2 (over core).
Axes of the slice: x: 2, y: 2, z: 4, core: 2. Of those that a mesh axis runs over, the one named last changes fastest.
Arguments:
- queries: bfloat16 [8, 32, 8, 8, 128], P('groups', 'dom', 'tp'), parts along dimension 0, may hold values from -8 to 8
- prompt_cache: bfloat16 [4, 8192, 8, 128], P('groups', 'ctx', 'tp'), parts along dimension 0, may hold values from -8 to 8
- suffix_cache: bfloat16 [4, 32, 16, 8, 128], P('groups', 'dom', 'ctx', 'tp'), parts along dimension 0, may hold values from -8 to 8
- new_kv: bfloat16 [8, 2, 32, 8, 128], P('groups', None, 'dom', 'tp'), parts along dimension 0, may hold values from -8 to 8
- ancestors: int32 [8, 32], P('groups'), parts along dimension 0, may hold values from 0 to 31, as said below
- lengths: int32 [64], P('groups'), parts along dimension 0, may hold values from 1 to 12, as said below
Outputs:
- attended: bfloat16 [8, 32, 8, 8, 128], P('groups', 'dom', 'tp'), parts along dimension 0
The draws below stay inside these ranges and needn't reach their ends.
There are 2 independent parts, one for each index of `groups`. The reference program is written for one: setup_inputs(seed, part) draws one part's arguments, and reference() takes and returns one part's arrays. A program takes and returns all parts, laid end to end along the dimension named above; each array names one. Nothing has to cross between parts.
Inputs may be any that keep to these rules, and one draw needn't show every extreme that they name: `ancestors`: particle p is owned by owner p // 16. In every step, of the 16 offspring of one owner at most 16 have their ancestor among the particles of any one owner, and each owner has exactly 16 from some one owner. `lengths`: the largest length is reached in every draw.
All inputs are finite; a program needn't handle non-finite values.
Results may differ from the reference program's by a relative error of at most 0.005.
Values may be sent and summed in bfloat16 or wider, within the bound.
No kernel may reach another device: no remote copies, remote signals or barrier semaphores. Data moves between devices by JAX's collectives and lax.ppermute only.
A program may use at most 128 MiB of HBM per device.

```python
import math
import jax
import jax.numpy as jnp
from jax import lax

KVH = 8
GROUP = 8
HD = 128
PART_DEV = 16
STEPS = 4
OWNERS = 2
PARTICLES = 32
PROMPT = 8192
SUF = 16
CAP = 16


def shared_dirs(key):
    base_key = jax.random.fold_in(key, 977)
    along_key = jax.random.fold_in(base_key, 0)
    suffix_dir = (jax.random.randint(along_key, (KVH, HD), 0, 2) * 2 - 1).astype(jnp.float32)
    return suffix_dir


def suffix_shift():
    mass_ratio = max(math.log(PROMPT / SUF), 1.0)
    return math.sqrt(mass_ratio / (math.sqrt(HD) + 2.0))


def drawn_noise(noise_key, full_shape):
    return jnp.clip(jax.random.normal(noise_key, full_shape, jnp.float32), -6.0, 6.0)


def draw_queries(key, part):
    suffix_dir = shared_dirs(key)
    shift_size = suffix_shift()
    noise_key = jax.random.fold_in(jax.random.fold_in(key, 1), 0)
    full_shape = (STEPS, PARTICLES, KVH, GROUP, HD)
    direction = suffix_dir[None, None, :, None, :]
    values = 2.0 * drawn_noise(noise_key, full_shape) + shift_size * direction
    return jnp.clip(values, -8.0, 8.0).astype(jnp.bfloat16)


def draw_prompt_cache(key, part):
    noise_key = jax.random.fold_in(jax.random.fold_in(key, 2), 0)
    full_shape = (2, PROMPT, KVH, HD)
    values = drawn_noise(noise_key, full_shape)
    return jnp.clip(values, -8.0, 8.0).astype(jnp.bfloat16)


def draw_suffix_cache(key, part):
    suffix_dir = shared_dirs(key)
    shift_size = suffix_shift()
    noise_key = jax.random.fold_in(jax.random.fold_in(key, 3), 0)
    full_shape = (2, PARTICLES, SUF, KVH, HD)
    noise_part = drawn_noise(noise_key, full_shape)
    key_rows = noise_part[0] + shift_size * suffix_dir[None, None]
    values = jnp.stack([key_rows, noise_part[1]])
    return jnp.clip(values, -8.0, 8.0).astype(jnp.bfloat16)


def draw_new_kv(key, part):
    suffix_dir = shared_dirs(key)
    shift_size = suffix_shift()
    noise_key = jax.random.fold_in(jax.random.fold_in(key, 4), 0)
    full_shape = (STEPS, 2, PARTICLES, KVH, HD)
    noise_part = drawn_noise(noise_key, full_shape)
    key_rows = noise_part[:, 0] + shift_size * suffix_dir[None, None]
    values = jnp.stack([key_rows, noise_part[:, 1]], axis=1)
    return jnp.clip(values, -8.0, 8.0).astype(jnp.bfloat16)


def draw_lengths(key, part):
    value_key, pick_key = jax.random.split(jax.random.fold_in(key, 5))
    values = jax.random.randint(value_key, (PARTICLES,), 1, SUF - STEPS + 1)
    chosen = jax.random.randint(pick_key, (), 0, PARTICLES)
    return jnp.where(jnp.arange(PARTICLES) == chosen, SUF - STEPS, values).astype(jnp.int32)


def draw_ancestors(key, part):

    def one_owner(owner_key):
        first_key, other_key, order_key, local_key = jax.random.split(owner_key, 4)
        first_source = jax.random.randint(first_key, (), 0, OWNERS)
        others = (first_source + 1 + jnp.arange((OWNERS - 1) * CAP) // CAP) % OWNERS
        others = jax.random.permutation(other_key, others)[:PART_DEV - CAP]
        sources = jnp.concatenate([jnp.full((CAP,), first_source, jnp.int32), others.astype(jnp.int32)])
        sources = jax.random.permutation(order_key, sources)
        local_index = jax.random.randint(local_key, (PART_DEV,), 0, PART_DEV)
        return (sources * PART_DEV + local_index).astype(jnp.int32)

    def one_step(step_key):
        return jax.vmap(one_owner)(jax.random.split(step_key, OWNERS)).reshape(PARTICLES)
    return jax.vmap(one_step)(jax.random.split(jax.random.fold_in(key, 6), STEPS))


def setup_inputs(seed: int = 0, part: int = 0) -> dict:
    arg_keys = jax.random.split(jax.random.key(seed), 7)
    part_splits = jax.random.split(jax.random.fold_in(arg_keys[6], part), 7)
    return {
        "queries": draw_queries(jax.random.fold_in(jax.random.fold_in(arg_keys[6], part), 71), part),
        "prompt_cache": draw_prompt_cache(jax.random.fold_in(jax.random.fold_in(arg_keys[6], part), 71), part),
        "suffix_cache": draw_suffix_cache(jax.random.fold_in(jax.random.fold_in(arg_keys[6], part), 71), part),
        "new_kv": draw_new_kv(jax.random.fold_in(jax.random.fold_in(arg_keys[6], part), 71), part),
        "ancestors": draw_ancestors(jax.random.fold_in(jax.random.fold_in(arg_keys[6], part), 71), part),
        "lengths": draw_lengths(jax.random.fold_in(jax.random.fold_in(arg_keys[6], part), 71), part),
    }


def attend(query_block, prompt_cache, suffix_rows, visible, score_scale):
    operands = (jnp.moveaxis(query_block, 1, 0), jnp.moveaxis(prompt_cache[0], 1, 0), jnp.moveaxis(prompt_cache[1], 1, 0), jnp.moveaxis(suffix_rows[0], 2, 0), jnp.moveaxis(suffix_rows[1], 2, 0))

    def one_head(pieces):
        query_head, prompt_keys, prompt_values, suffix_keys, suffix_values = pieces
        query_wide = query_head.astype(jnp.float32)
        prompt_scores = jnp.einsum('pgd,td->pgt', query_wide, prompt_keys.astype(jnp.float32)) * score_scale
        suffix_scores = jnp.einsum('pgd,psd->pgs', query_wide, suffix_keys.astype(jnp.float32)) * score_scale
        suffix_scores = jnp.where(visible[:, None, :], suffix_scores, -jnp.inf)
        peak_score = jnp.maximum(lax.optimization_barrier(jnp.max(prompt_scores, axis=-1)), lax.optimization_barrier(jnp.max(suffix_scores, axis=-1)))
        prompt_exp = jnp.exp(prompt_scores - peak_score[..., None])
        suffix_exp = jnp.exp(suffix_scores - peak_score[..., None])
        totals = lax.optimization_barrier(jnp.sum(prompt_exp, axis=-1)) + lax.optimization_barrier(jnp.sum(suffix_exp, axis=-1))
        prompt_weights = lax.optimization_barrier(prompt_exp.astype(jnp.bfloat16)).astype(jnp.float32)
        suffix_weights = lax.optimization_barrier(suffix_exp.astype(jnp.bfloat16)).astype(jnp.float32)
        numerator = jnp.einsum('pgt,td->pgd', prompt_weights, prompt_values.astype(jnp.float32))
        numerator = numerator + jnp.einsum('pgs,psd->pgd', suffix_weights, suffix_values.astype(jnp.float32))
        return (numerator / totals[..., None]).astype(jnp.bfloat16)
    per_head = lax.map(one_head, operands)
    return jnp.moveaxis(per_head, 0, 1)

def reference(queries, prompt_cache, suffix_cache, new_kv, ancestors, lengths):
    score_scale = 1.0 / math.sqrt(HD)
    suffix_rows = suffix_cache
    lengths_now = lengths
    positions = jnp.arange(SUF).astype(jnp.int32)
    results = []
    for step_index in range(STEPS):
        parents = ancestors[step_index]
        suffix_rows = jnp.take(suffix_rows, parents, axis=1)
        lengths_now = jnp.take(lengths_now, parents)
        new_slot = positions[None, :] == lengths_now[:, None]
        suffix_rows = jnp.where(new_slot[None, :, :, None, None], new_kv[step_index][:, :, None], suffix_rows)
        visible = positions[None, :] <= lengths_now[:, None]
        results.append(attend(queries[step_index], prompt_cache, suffix_rows, visible, score_scale))
        lengths_now = lengths_now + 1
    return jnp.stack(results)
```

```python
import functools
import math

import jax
import jax.numpy as jnp
from jax import lax
from jax.experimental import pallas as pl
from jax.experimental.pallas import tpu as pltpu
from jax.sharding import PartitionSpec as P

LANES = 128
HIDDEN = -1e30
NN = (((1,), (0,)), ((), ()))
NT = (((1,), (1,)), ((), ()))


def round_up(value, multiple):
    return -(-value // multiple) * multiple


def dot(a, b, dims):
    return lax.dot_general(a, b, dims, preferred_element_type=jnp.float32)


def eye_mask(rows):
    shape = (rows, LANES)
    return lax.broadcasted_iota(jnp.int32, shape, 0) == lax.broadcasted_iota(jnp.int32, shape, 1)


def column_to_lanes(column):
    rows = column.shape[0]
    block = min(rows, LANES)
    mask = eye_mask(block)
    return jnp.concatenate(
        [
            jnp.sum(jnp.where(mask, column[at : at + block], 0.0), axis=0, keepdims=True)
            for at in range(0, rows, block)
        ],
        axis=0,
    )


def lanes_to_column(lanes, rows):
    block = min(rows, LANES)
    mask = eye_mask(block)
    return jnp.concatenate(
        [
            jnp.sum(jnp.where(mask, lanes[i : i + 1], 0.0), axis=1, keepdims=True)
            for i in range(lanes.shape[0])
        ],
        axis=0,
    )


def tail_rows(rows):
    return round_up(3 * -(-rows // LANES), 16)


def pack_tail(column):
    lanes = column_to_lanes(column)
    high = lanes.astype(jnp.bfloat16).astype(jnp.float32)
    middle = (lanes - high).astype(jnp.bfloat16).astype(jnp.float32)
    low = lanes - high - middle
    parts = jnp.concatenate([high, middle, low], axis=0)
    spare = tail_rows(column.shape[0]) - parts.shape[0]
    return jnp.concatenate([parts, jnp.zeros((spare, LANES), jnp.float32)], axis=0).astype(
        jnp.bfloat16
    )


def unpack_tail(tail, rows):
    tail = tail.astype(jnp.float32)
    blocks = -(-rows // LANES)
    lanes = tail[:blocks] + tail[blocks : 2 * blocks] + tail[2 * blocks : 3 * blocks]
    return lanes_to_column(lanes, rows)


def split_heads_kernel(heads, rows_ref, out_ref, wide):
    wide[...] = rows_ref[0].astype(jnp.float32)
    steps = out_ref.shape[2]
    for head in range(heads):
        out_ref[0, head] = wide[pl.ds(head, steps, stride=heads), :].astype(out_ref.dtype)


def split_heads(rows, heads):
    total = rows.shape[1] // heads
    block = math.gcd(total, 512)
    size = rows.shape[2]
    return pl.pallas_call(
        functools.partial(split_heads_kernel, heads),
        grid=(2, total // block),
        in_specs=[pl.BlockSpec((1, block * heads, size), lambda kind, at: (kind, at, 0))],
        out_specs=pl.BlockSpec((1, heads, block, size), lambda kind, at: (kind, 0, at, 0)),
        out_shape=jax.ShapeDtypeStruct((2, heads, total, size), rows.dtype),
        scratch_shapes=[pltpu.VMEM((block * heads, size), jnp.float32)],
        compiler_params=pltpu.CompilerParams(vmem_limit_bytes=16 << 20),
        cost_estimate=pl.CostEstimate(
            flops=0, bytes_accessed=4 * rows.size, transcendentals=0
        ),
    )(rows)


def suffix_kernel(
    heads, per_owner, suffix_dev, tokens_dev, *refs
):
    *row_refs, ancestors_ref, lengths_ref, keys_ref, bias_ref, wide = refs
    owners = len(row_refs)
    particles = owners * per_owner
    steps = ancestors_ref.shape[0]
    slots = suffix_dev + tokens_dev
    columns = owners * per_owner * slots
    padded = keys_ref.shape[2]
    my_owner = lax.axis_index("dom")
    my_shard = lax.axis_index("ctx")
    each = per_owner * slots
    for kind in range(2):
        for at, ref in enumerate(row_refs):
            wide[pl.ds(at * each * heads, each * heads), :] = ref[kind].astype(jnp.float32)
        for head in range(heads):
            pieces = [wide[pl.ds(head, columns, stride=heads), :]]
            if padded > columns:
                pieces.append(jnp.zeros((padded - columns, LANES), jnp.float32))
            keys_ref[kind, head] = jnp.concatenate(pieces, axis=0).astype(keys_ref.dtype)

    def iota(shape, axis):
        return lax.broadcasted_iota(jnp.int32, shape, axis)

    square = (particles, particles)
    same = iota(square, 0) == iota(square, 1)

    def as_column(row):
        return jnp.sum(jnp.where(same, row, 0), axis=1, keepdims=True)

    unit = same.astype(jnp.float32)
    state = jnp.concatenate([unit, jnp.zeros((particles, tokens_dev * particles), jnp.float32)], axis=1)
    pick = (iota((per_owner, particles), 1) == iota((per_owner, particles), 0) + my_owner * per_owner)
    pick = pick.astype(jnp.bfloat16)
    mine = []
    for step in range(steps):
        parent = as_column(ancestors_ref[step : step + 1, :])
        move = (parent == iota(square, 1)).astype(jnp.bfloat16)
        state = dot(move, state.astype(jnp.bfloat16), NN)
        blocks = [state[:, :particles]]
        for token in range(tokens_dev):
            written = my_shard * tokens_dev + token
            old = state[:, (1 + token) * particles : (2 + token) * particles]
            blocks.append(jnp.where(written == step, unit, old))
        state = jnp.concatenate(blocks, axis=1)
        mine.append(dot(pick, state.astype(jnp.bfloat16), NN))
    mine = jnp.concatenate(mine, axis=0).astype(jnp.bfloat16)
    lengths = as_column(lengths_ref[...])
    column = iota((particles, padded), 1)
    source = column // each
    owner = lax.rem(my_owner + owners - source, owners)
    inner = column - source * each
    particle = owner * per_owner + inner // slots
    slot = lax.rem(inner, slots)
    here = (iota((particles, padded), 0) == particle) & (column < columns)
    position = my_shard * suffix_dev + slot
    seen = [here & (slot < suffix_dev) & (position < lengths)]
    seen += [here & (slot == suffix_dev + token) for token in range(tokens_dev)]
    table = jnp.concatenate([s.astype(jnp.bfloat16) for s in seen], axis=0)
    bias_ref[...] = jnp.where(dot(mine, table, NN) > 0.5, 0.0, HIDDEN)


def suffix_part(row_list, ancestors, lengths, heads, suffix_dev, tokens_dev):
    per_owner = row_list[0].shape[1] // (heads * (suffix_dev + tokens_dev))
    columns = len(row_list) * row_list[0].shape[1] // heads
    padded = round_up(columns, LANES)
    size = row_list[0].shape[2]
    steps = ancestors.shape[0]
    return pl.pallas_call(
        functools.partial(suffix_kernel, heads, per_owner, suffix_dev, tokens_dev),
        out_shape=(
            jax.ShapeDtypeStruct((2, heads, padded, size), jnp.bfloat16),
            jax.ShapeDtypeStruct((steps * per_owner, padded), jnp.float32),
        ),
        scratch_shapes=[pltpu.VMEM((columns * heads, size), jnp.float32)],
        compiler_params=pltpu.CompilerParams(vmem_limit_bytes=24 << 20),
        cost_estimate=pl.CostEstimate(flops=0, bytes_accessed=1 << 20, transcendentals=0),
    )(*row_list, ancestors, lengths.reshape(1, -1))


def attend_kernel(scale, q_ref, k_ref, v_ref, kx_ref, vx_ref, bias_ref, send_ref, keep_ref, sums_ref):
    steps, per_owner, _, group, size = q_ref.shape
    half = steps * per_owner // 2
    rows = half * group
    columns = bias_ref.shape[1]
    bit = lax.rem(lax.axis_index("ctx"), 2)
    factor = scale * math.log2(math.e)

    def one_half(which):
        q = q_ref[pl.ds(which * (steps // 2), steps // 2)].reshape(rows, size)
        bias = bias_ref[pl.ds(pl.multiple_of(which * half, half), half), :]
        bias = jnp.broadcast_to(bias[:, None, :], (half, group, columns)).reshape(rows, columns)
        scores = dot(q, k_ref[0, 0], NT)
        extra = dot(q, kx_ref[0, 0], NT) + bias
        peak = jnp.maximum(
            jnp.max(scores, axis=1, keepdims=True), jnp.max(extra, axis=1, keepdims=True)
        )
        offset = peak * factor
        weight = jnp.exp2(scores * factor - offset).astype(jnp.bfloat16)
        weight_extra = jnp.exp2(extra * factor - offset).astype(jnp.bfloat16)

        def with_ones(values):
            return jnp.concatenate([values, jnp.ones_like(values)], axis=1)

        total = dot(weight, with_ones(v_ref[0, 0]), NN) + dot(
            weight_extra, with_ones(vx_ref[0, 0]), NN
        )
        sums = total[:, size:]
        return total[:, :size] / sums, offset + jnp.log2(sums[:, :1])

    out, log_sum = one_half(1 - bit)
    send_ref[0, :rows] = out.astype(jnp.bfloat16)
    send_ref[0, rows:] = pack_tail(log_sum)
    out, log_sum = one_half(bit)
    keep_ref[0] = out
    sums_ref[0] = jnp.broadcast_to(log_sum, sums_ref.shape[1:])


def attend(queries, prompt, extra, bias, head, count, scale):
    steps, per_owner, _, group, size = queries.shape
    total = prompt.shape[2]
    padded = extra.shape[2]
    rows = steps * per_owner * group // 2
    message = rows + tail_rows(rows)

    def kind_spec(length, kind):
        return pl.BlockSpec((1, 1, length, size), lambda i: (kind, head + i, 0, 0))

    return pl.pallas_call(
        functools.partial(attend_kernel, scale),
        grid=(count,),
        in_specs=[
            pl.BlockSpec((steps, per_owner, 1, group, size), lambda i: (0, 0, head + i, 0, 0)),
            kind_spec(total, 0),
            kind_spec(total, 1),
            kind_spec(padded, 0),
            kind_spec(padded, 1),
            pl.BlockSpec(bias.shape, lambda i: (0, 0)),
        ],
        out_specs=[
            pl.BlockSpec((1, message, size), lambda i: (i, 0, 0)),
            pl.BlockSpec((1, rows, size), lambda i: (i, 0, 0)),
            pl.BlockSpec((1, rows, LANES), lambda i: (i, 0, 0)),
        ],
        out_shape=(
            jax.ShapeDtypeStruct((count, message, size), jnp.bfloat16),
            jax.ShapeDtypeStruct((count, rows, size), jnp.float32),
            jax.ShapeDtypeStruct((count, rows, LANES), jnp.float32),
        ),
        compiler_params=pltpu.CompilerParams(vmem_limit_bytes=40 << 20),
        cost_estimate=pl.CostEstimate(
            flops=count * 8 * rows * (total + padded) * size,
            bytes_accessed=count * 4 * total * size,
            transcendentals=count * 2 * rows * (total + padded),
        ),
    )(queries, prompt, prompt, extra, extra, bias)


def merge(out_a, sum_a, out_b, sum_b):
    top = jnp.maximum(sum_a, sum_b)
    weight_a = jnp.exp2(sum_a - top)
    weight_b = jnp.exp2(sum_b - top)
    total = weight_a + weight_b
    return (out_a * weight_a + out_b * weight_b) / total, top + jnp.log2(total)


def merge_kernel(level, last, keep_ref, sums_ref, got_ref, *outs):
    rows = keep_ref.shape[1]
    for i in range(keep_ref.shape[0]):
        got_sum = unpack_tail(got_ref[i, rows:], rows)
        out, log_sum = merge(
            keep_ref[i], sums_ref[i][:, :1], got_ref[i, :rows].astype(jnp.float32), got_sum
        )
        if last:
            outs[0][i, :rows] = out.astype(jnp.bfloat16)
            outs[0][i, rows:] = pack_tail(log_sum)
        else:
            half = rows // 2
            bit = lax.rem(lax.axis_index("ctx") >> level, 2) == 1
            send, keep, wide = outs

            def choose(first, value):
                return jnp.where(first, value[:half], value[half:])

            send[i, :half] = choose(bit, out).astype(jnp.bfloat16)
            send[i, half:] = pack_tail(choose(bit, log_sum))
            keep[i] = choose(~bit, out)
            wide[i] = jnp.broadcast_to(choose(~bit, log_sum), (half, LANES))


def merge_parts(keep, sums, got, level, last):
    count, rows, size = keep.shape
    part = rows if last else rows // 2
    shapes = [jax.ShapeDtypeStruct((count, part + tail_rows(part), size), jnp.bfloat16)]
    if not last:
        shapes.append(jax.ShapeDtypeStruct((count, part, size), jnp.float32))
        shapes.append(jax.ShapeDtypeStruct((count, part, LANES), jnp.float32))
    return pl.pallas_call(
        functools.partial(merge_kernel, level, last),
        out_shape=tuple(shapes),
        compiler_params=pltpu.CompilerParams(vmem_limit_bytes=16 << 20),
        cost_estimate=pl.CostEstimate(
            flops=8 * keep.size, bytes_accessed=8 * keep.size, transcendentals=0
        ),
    )(keep, sums, got)


def finish_kernel(mine_ref, got_ref, out_ref):
    rows = out_ref.shape[1]
    for i in range(mine_ref.shape[0]):
        out, _ = merge(
            mine_ref[i, :rows].astype(jnp.float32),
            unpack_tail(mine_ref[i, rows:], rows),
            got_ref[i, :rows].astype(jnp.float32),
            unpack_tail(got_ref[i, rows:], rows),
        )
        out_ref[i] = out.astype(jnp.bfloat16)


def finish(mine, got, rows):
    count, _, size = mine.shape
    return pl.pallas_call(
        finish_kernel,
        out_shape=jax.ShapeDtypeStruct((count, rows, size), jnp.bfloat16),
        compiler_params=pltpu.CompilerParams(vmem_limit_bytes=16 << 20),
        cost_estimate=pl.CostEstimate(
            flops=8 * mine.size, bytes_accessed=6 * mine.size, transcendentals=0
        ),
    )(mine, got)


def place_kernel(chunks, *refs):
    *halves, out_ref = refs
    both, _, group, size = (out_ref.shape[0] * out_ref.shape[1],) + out_ref.shape[2:]
    steps, per_owner = out_ref.shape[:2]
    half = steps // 2
    bit = lax.rem(lax.axis_index("ctx"), 2)
    head = 0
    for chunk in range(chunks):
        own, other = halves[2 * chunk : 2 * chunk + 2]
        for i in range(own.shape[0]):
            shape = (half, per_owner, group, size)
            out_ref[pl.ds(bit * half, half), :, head] = own[i].reshape(shape)
            out_ref[pl.ds((1 - bit) * half, half), :, head] = other[i].reshape(shape)
            head += 1


def place(pairs, shape):
    flat = [half for pair in pairs for half in pair]
    return pl.pallas_call(
        functools.partial(place_kernel, len(pairs)),
        out_shape=jax.ShapeDtypeStruct(shape, jnp.bfloat16),
        compiler_params=pltpu.CompilerParams(vmem_limit_bytes=16 << 20),
        cost_estimate=pl.CostEstimate(flops=0, bytes_accessed=1 << 20, transcendentals=0),
    )(*flat)


def on_device(shards, owners, chunks, queries, prompt_cache, suffix_cache, new_kv, ancestors, lengths):
    steps, per_owner, heads, group, size = queries.shape
    suffix_dev = suffix_cache.shape[2]
    my_shard = lax.axis_index("ctx")
    scale = 1.0 / math.sqrt(size)
    levels = shards.bit_length() - 1

    def swap(value, bit):
        return lax.ppermute(value, "ctx", [(i, i ^ (1 << bit)) for i in range(shards)])

    tokens_dev = -(-steps // shards)
    first = jnp.minimum(my_shard * tokens_dev, steps - tokens_dev)
    tokens = lax.dynamic_slice_in_dim(new_kv, first, tokens_dev, axis=0)
    rows = jnp.concatenate([suffix_cache, jnp.moveaxis(tokens, 0, 2)], axis=2)
    rows = rows.reshape(2, -1, size)
    row_list = [rows] + [
        lax.ppermute(rows, "dom", [(i, (i + hop) % owners) for i in range(owners)])
        for hop in range(1, owners)
    ]
    prompt = split_heads(prompt_cache.reshape(2, -1, size), heads)
    extra, bias = suffix_part(row_list, ancestors, lengths, heads, suffix_dev, tokens_dev)

    each = heads // chunks
    pairs = []
    for chunk in range(chunks):
        send, keep, sums = attend(queries, prompt, extra, bias, chunk * each, each, scale)
        for level in range(1, levels):
            got = swap(send, level - 1)
            outs = merge_parts(keep, sums, got, level, level == levels - 1)
            if level == levels - 1:
                (send,) = outs
            else:
                send, keep, sums = outs
        part = steps * per_owner * group >> (levels - 1)
        done = finish(send, swap(send, levels - 1), part)
        for level in range(levels - 2, 0, -1):
            other = swap(done, level)
            flip = (my_shard >> level) % 2 == 1
            done = jnp.where(
                flip,
                jnp.concatenate([other, done], axis=1),
                jnp.concatenate([done, other], axis=1),
            )
        pairs.append((done, swap(done, 0)))
    return place(pairs, queries.shape)


def solution(mesh):
    return jax.shard_map(
        functools.partial(on_device, mesh.shape["ctx"], mesh.shape["dom"], 4),
        mesh=mesh,
        in_specs=(
            P("groups", "dom", "tp", None, None),
            P("groups", "ctx", "tp", None),
            P("groups", "dom", "ctx", "tp", None),
            P("groups", None, "dom", "tp", None),
            P("groups", None),
            P("groups"),
        ),
        out_specs=P("groups", "dom", "tp", None, None),
        check_vma=False,
    )
```

```python
import functools
import math

import jax
import jax.numpy as jnp
from jax import lax
from jax.experimental import pallas as pl
from jax.experimental.pallas import tpu as pltpu
from jax.sharding import PartitionSpec as P

LANES = 128
HIDDEN = -1e30
NN = (((1,), (0,)), ((), ()))
NT = (((1,), (1,)), ((), ()))
SMALL = pl.CostEstimate(flops=0, bytes_accessed=4096, transcendentals=0)


def round_up(value, multiple):
    return -(-value // multiple) * multiple


def dot(a, b, dims):
    return lax.dot_general(a, b, dims, preferred_element_type=jnp.float32)


def eye_mask(rows):
    shape = (rows, LANES)
    return lax.broadcasted_iota(jnp.int32, shape, 0) == lax.broadcasted_iota(jnp.int32, shape, 1)


def column_to_lanes(column):
    rows = column.shape[0]
    block = min(rows, LANES)
    mask = eye_mask(block)
    return jnp.concatenate(
        [
            jnp.sum(jnp.where(mask, column[at : at + block], 0.0), axis=0, keepdims=True)
            for at in range(0, rows, block)
        ],
        axis=0,
    )


def lanes_to_column(lanes, rows):
    block = min(rows, LANES)
    mask = eye_mask(block)
    return jnp.concatenate(
        [
            jnp.sum(jnp.where(mask, lanes[i : i + 1], 0.0), axis=1, keepdims=True)
            for i in range(lanes.shape[0])
        ],
        axis=0,
    )


def tail_rows(rows):
    return round_up(3 * -(-rows // LANES), 16)


def pack_tail(column):
    lanes = column_to_lanes(column)
    high = lanes.astype(jnp.bfloat16).astype(jnp.float32)
    middle = (lanes - high).astype(jnp.bfloat16).astype(jnp.float32)
    low = lanes - high - middle
    parts = jnp.concatenate([high, middle, low], axis=0)
    spare = tail_rows(column.shape[0]) - parts.shape[0]
    return jnp.concatenate([parts, jnp.zeros((spare, LANES), jnp.float32)], axis=0).astype(
        jnp.bfloat16
    )


def unpack_tail(tail, rows):
    tail = tail.astype(jnp.float32)
    blocks = -(-rows // LANES)
    lanes = tail[:blocks] + tail[blocks : 2 * blocks] + tail[2 * blocks : 3 * blocks]
    return lanes_to_column(lanes, rows)


def message_kernel(suffix_ref, new_ref, out_ref, sems):
    rows, each = suffix_ref.shape[1], new_ref.shape[2]
    count = (out_ref.shape[1] - rows) // each
    first = jnp.minimum(lax.axis_index("ctx") * count, new_ref.shape[0] - count)
    copies = [pltpu.make_async_copy(suffix_ref, out_ref.at[:, pl.ds(0, rows)], sems.at[0])]
    for token in range(count):
        there = out_ref.at[:, pl.ds(rows + token * each, each)]
        copies.append(pltpu.make_async_copy(new_ref.at[first + token], there, sems.at[1 + token]))
    for copy in copies:
        copy.start()
    for copy in copies:
        copy.wait()


def build_message(suffix, new, tokens_dev):
    shape = (2, suffix.shape[1] + tokens_dev * new.shape[2], suffix.shape[2])
    return pl.pallas_call(
        message_kernel,
        in_specs=[pl.BlockSpec(memory_space=pltpu.HBM)] * 2,
        out_shape=jax.ShapeDtypeStruct(shape, suffix.dtype),
        scratch_shapes=[pltpu.SemaphoreType.DMA((1 + tokens_dev,))],
        compiler_params=pltpu.CompilerParams(vmem_limit_bytes=16 << 20),
        cost_estimate=SMALL,
    )(in_hbm(suffix), in_hbm(new))


def in_hbm(array):
    return pltpu.with_memory_space_constraint(array, pltpu.HBM)


def split_heads_kernel(heads, block, rows_ref, out_ref, here, wide, sems):
    total = out_ref.shape[2]
    places = [(kind, at) for kind in range(2) for at in range(0, total, block)]
    copies = [
        pltpu.make_async_copy(
            rows_ref.at[kind, pl.ds(at * heads, block * heads)],
            here.at[kind, pl.ds(at * heads, block * heads)],
            sems.at[i],
        )
        for i, (kind, at) in enumerate(places)
    ]
    for copy in copies:
        copy.start()
    for i, (kind, at) in enumerate(places):
        copies[i].wait()
        wide[i % 2] = here[kind, at * heads : (at + block) * heads].astype(jnp.float32)
        for head in range(heads):
            out_ref[kind, head, at : at + block] = wide[
                i % 2, pl.ds(head, block, stride=heads), :
            ].astype(out_ref.dtype)


def split_heads(rows, heads):
    total = rows.shape[1] // heads
    block = math.gcd(total, 512)
    size = rows.shape[2]
    return pl.pallas_call(
        functools.partial(split_heads_kernel, heads, block),
        in_specs=[pl.BlockSpec(memory_space=pltpu.HBM)],
        out_shape=jax.ShapeDtypeStruct((2, heads, total, size), rows.dtype),
        scratch_shapes=[
            pltpu.VMEM(rows.shape, rows.dtype),
            pltpu.VMEM((2, block * heads, size), jnp.float32),
            pltpu.SemaphoreType.DMA((2 * total // block,)),
        ],
        compiler_params=pltpu.CompilerParams(vmem_limit_bytes=24 << 20),
        cost_estimate=SMALL,
    )(in_hbm(rows))


def iota(shape, axis):
    return lax.broadcasted_iota(jnp.int32, shape, axis)


def lineage_bias(ancestors_ref, lengths_ref, owners, per_owner, suffix_dev, tokens_dev, padded):
    particles = owners * per_owner
    steps = ancestors_ref.shape[0]
    suffix_columns = per_owner * suffix_dev
    each = suffix_columns + per_owner * tokens_dev
    my_owner = lax.axis_index("dom")
    my_shard = lax.axis_index("ctx")
    square = (particles, particles)
    same = iota(square, 0) == iota(square, 1)

    def as_column(row):
        return jnp.sum(jnp.where(same, row, 0), axis=1, keepdims=True)

    unit = same.astype(jnp.float32)
    nothing = jnp.zeros((particles, tokens_dev * particles), jnp.float32)
    state = jnp.concatenate([unit, nothing], axis=1)
    pick = iota((per_owner, particles), 1) == iota((per_owner, particles), 0) + my_owner * per_owner
    pick = pick.astype(jnp.bfloat16)
    mine = []
    for step in range(steps):
        parent = as_column(ancestors_ref[step : step + 1, :])
        move = (parent == iota(square, 1)).astype(jnp.bfloat16)
        state = dot(move, state.astype(jnp.bfloat16), NN)
        blocks = [state[:, :particles]]
        for token in range(tokens_dev):
            written = my_shard * tokens_dev + token
            old = state[:, (1 + token) * particles : (2 + token) * particles]
            blocks.append(jnp.where(written == step, unit, old))
        state = jnp.concatenate(blocks, axis=1)
        mine.append(dot(pick, state.astype(jnp.bfloat16), NN))
    mine = jnp.concatenate(mine, axis=0).astype(jnp.bfloat16)
    lengths = as_column(lengths_ref[...])
    shape = (particles, padded)
    column = iota(shape, 1)
    source = column // each
    owner = lax.rem(my_owner + owners - source, owners)
    inner = column - source * each
    after = inner - suffix_columns
    in_suffix = after < 0
    local = jnp.where(in_suffix, inner // suffix_dev, lax.rem(jnp.maximum(after, 0), per_owner))
    here = (iota(shape, 0) == owner * per_owner + local) & (column < owners * each)
    position = my_shard * suffix_dev + lax.rem(inner, suffix_dev)
    seen = [here & in_suffix & (position < lengths)]
    for token in range(tokens_dev):
        seen.append(here & (after >= token * per_owner) & (after < (token + 1) * per_owner))
    table = jnp.concatenate([s.astype(jnp.bfloat16) for s in seen], axis=0)
    return jnp.where(dot(mine, table, NN) > 0.5, 0.0, HIDDEN)


def attend_kernel(scale, owners, suffix_dev, tokens_dev, heads, head, *refs):
    q_ref, k_ref, v_ref = refs[:3]
    row_refs = refs[3 : 3 + owners]
    ancestors_ref, lengths_ref, _, send_ref, keep_ref, sums_ref, wide, bias_ref = refs[3 + owners :]
    steps, per_owner, _, group, size = q_ref.shape
    total = k_ref.shape[2]
    columns = wide.shape[1] // heads
    padded = bias_ref.shape[1]
    factor = scale * math.log2(math.e)

    bias_ref[...] = lineage_bias(
        ancestors_ref, lengths_ref, owners, per_owner, suffix_dev, tokens_dev, padded
    )
    extra = []
    for kind in range(2):
        for at, ref in enumerate(row_refs):
            wide[kind, at * ref.shape[1] : (at + 1) * ref.shape[1]] = ref[kind].astype(jnp.float32)
        pieces = [wide[kind, pl.ds(head, columns, stride=heads), :]]
        if padded > columns:
            pieces.append(jnp.zeros((padded - columns, size), jnp.float32))
        extra.append(jnp.concatenate(pieces, axis=0).astype(jnp.bfloat16))
    extra_keys, extra_values = extra

    def with_ones(values):
        return jnp.concatenate([values, jnp.ones_like(values)], axis=1)

    def rows_of(first, count):
        rows = count * per_owner * group
        q = q_ref[pl.ds(first, count)].reshape(rows, size)
        at = pl.multiple_of(first * per_owner, per_owner)
        bias = bias_ref[pl.ds(at, count * per_owner), :]
        bias = jnp.broadcast_to(bias[:, None, :], (count * per_owner, group, padded))
        return q, dot(q, extra_keys, NT) + bias.reshape(rows, padded)

    block = math.gcd(total, 512)
    count = max(steps // 2, 1)
    worst = jnp.zeros((1, size), jnp.float32)
    for first in range(0, steps, count):
        rows = count * per_owner * group
        q, suffix_scores = rows_of(first, count)
        scores = dot(q, k_ref[0, 0, :block], NT)
        peak = jnp.maximum(
            jnp.max(scores, axis=1, keepdims=True), jnp.max(suffix_scores, axis=1, keepdims=True)
        )
        offset = peak * factor
        weight = jnp.exp2(suffix_scores * factor - offset).astype(jnp.bfloat16)
        together = dot(weight, with_ones(extra_values), NN)
        for at in range(0, total, block):
            if at:
                scores = dot(q, k_ref[0, 0, at : at + block], NT)
            weight = jnp.exp2(scores * factor - offset).astype(jnp.bfloat16)
            together = together + dot(weight, with_ones(v_ref[0, 0, at : at + block]), NN)
        sums = together[:, size:]
        here = slice(first * per_owner * group, first * per_owner * group + rows)
        keep_ref[here] = together[:, :size] / sums
        sums_ref[here] = offset + jnp.log2(sums)
        worst = jnp.maximum(worst, jnp.max(sums, axis=0, keepdims=True))

    @pl.when(jnp.logical_not(jnp.max(worst) < 2.0**100))
    def _():
        @pl.loop(0, steps)
        def _(step):
            rows = per_owner * group
            q, suffix_scores = rows_of(step, 1)
            scores = dot(q, k_ref[0, 0], NT)
            peak = jnp.maximum(
                jnp.max(scores, axis=1, keepdims=True),
                jnp.max(suffix_scores, axis=1, keepdims=True),
            )
            offset = peak * factor
            weight = jnp.exp2(scores * factor - offset).astype(jnp.bfloat16)
            together = dot(weight, with_ones(v_ref[0, 0]), NN)
            weight = jnp.exp2(suffix_scores * factor - offset).astype(jnp.bfloat16)
            together = together + dot(weight, with_ones(extra_values), NN)
            sums = together[:, size:]
            at = pl.multiple_of(step * rows, rows)
            keep_ref[pl.ds(at, rows), :] = together[:, :size] / sums
            sums_ref[pl.ds(at, rows), :] = offset + jnp.log2(sums)

    rows = keep_ref.shape[0]
    send_ref[:rows] = keep_ref[...].astype(jnp.bfloat16)
    send_ref[rows:] = pack_tail(sums_ref[:, :1])


def attend(queries, prompt, row_list, ancestors, lengths, head, scale, suffix_dev, tokens_dev, after):
    steps, per_owner, heads, group, size = queries.shape
    total = prompt.shape[2]
    owners = len(row_list)
    wide_rows = owners * row_list[0].shape[1]
    padded = round_up(wide_rows // heads, LANES)
    rows = steps * per_owner * group
    message = rows + tail_rows(rows)

    def whole(array):
        return pl.BlockSpec(array.shape, lambda i: (0,) * array.ndim)

    lengths = lengths.reshape(1, -1)
    return pl.pallas_call(
        functools.partial(attend_kernel, scale, owners, suffix_dev, tokens_dev, heads, head),
        grid=(1,),
        in_specs=[
            pl.BlockSpec((steps, per_owner, 1, group, size), lambda i: (0, 0, head, 0, 0)),
            pl.BlockSpec((1, 1, total, size), lambda i: (0, head, 0, 0)),
            pl.BlockSpec((1, 1, total, size), lambda i: (1, head, 0, 0)),
            *[whole(r) for r in row_list],
            whole(ancestors),
            whole(lengths),
            pl.BlockSpec(memory_space=pl.ANY),
        ],
        out_specs=[
            pl.BlockSpec((message, size), lambda i: (0, 0)),
            pl.BlockSpec((rows, size), lambda i: (0, 0)),
            pl.BlockSpec((rows, LANES), lambda i: (0, 0)),
        ],
        out_shape=(
            jax.ShapeDtypeStruct((message, size), jnp.bfloat16),
            jax.ShapeDtypeStruct((rows, size), jnp.float32),
            jax.ShapeDtypeStruct((rows, LANES), jnp.float32),
        ),
        scratch_shapes=[
            pltpu.VMEM((2, wide_rows, size), jnp.float32),
            pltpu.VMEM((steps * per_owner, padded), jnp.float32),
        ],
        compiler_params=pltpu.CompilerParams(vmem_limit_bytes=32 << 20),
        cost_estimate=SMALL,
    )(queries, prompt, prompt, *row_list, ancestors, lengths, after)


def merge(out_a, sum_a, out_b, sum_b):
    top = jnp.maximum(sum_a, sum_b)
    weight_a = jnp.exp2(sum_a - top)
    weight_b = jnp.exp2(sum_b - top)
    total = weight_a + weight_b
    return (out_a * weight_a + out_b * weight_b) / total, top + jnp.log2(total)


def merge_kernel(keep_ref, sums_ref, got_ref, _, out_ref):
    rows = keep_ref.shape[0]
    out, log_sum = merge(
        keep_ref[...],
        sums_ref[:, :1],
        got_ref[:rows].astype(jnp.float32),
        unpack_tail(got_ref[rows:], rows),
    )
    out_ref[:rows] = out.astype(jnp.bfloat16)
    out_ref[rows:] = pack_tail(log_sum)


def finish_kernel(mine_ref, got_ref, _, out_ref):
    rows = out_ref.shape[0]
    out, _ = merge(
        mine_ref[:rows].astype(jnp.float32),
        unpack_tail(mine_ref[rows:], rows),
        got_ref[:rows].astype(jnp.float32),
        unpack_tail(got_ref[rows:], rows),
    )
    out_ref[...] = out.astype(jnp.bfloat16)


def small_call(kernel, shape, args, after):
    return pl.pallas_call(
        kernel,
        in_specs=[pl.BlockSpec(memory_space=pltpu.VMEM)] * len(args)
        + [pl.BlockSpec(memory_space=pl.ANY)],
        out_shape=jax.ShapeDtypeStruct(shape, jnp.bfloat16),
        compiler_params=pltpu.CompilerParams(vmem_limit_bytes=16 << 20),
        cost_estimate=SMALL,
    )(*args, after)


def place_kernel(shards, *refs):
    *parts, out_ref = refs
    steps, per_owner, heads, group, size = out_ref.shape
    shard = lax.axis_index("ctx")
    at_end = (shard == 0) | (shard == shards - 1)

    def take(which):
        for head in range(heads):
            out_ref[:, :, head] = parts[2 * head + which][...].reshape(
                steps, per_owner, group, size
            )

    if shards <= 2:
        take(0)
        return

    @pl.when(at_end)
    def _():
        take(1)

    @pl.when(jnp.logical_not(at_end))
    def _():
        take(0)


def place(pairs, shape, shards):
    flat = [part for pair in pairs for part in pair]
    return pl.pallas_call(
        functools.partial(place_kernel, shards),
        out_shape=jax.ShapeDtypeStruct(shape, jnp.bfloat16),
        compiler_params=pltpu.CompilerParams(vmem_limit_bytes=16 << 20),
        cost_estimate=SMALL,
    )(*flat)


def on_device(shards, owners, queries, prompt_cache, suffix_cache, new_kv, ancestors, lengths):
    steps, per_owner, heads, group, size = queries.shape
    suffix_dev = suffix_cache.shape[2]
    scale = 1.0 / math.sqrt(size)
    tokens_dev = -(-steps // shards)
    rows = steps * per_owner * group
    message = (rows + tail_rows(rows), size)
    middle = shards // 2
    shard = lax.axis_index("ctx")

    mine = build_message(
        suffix_cache.reshape(2, -1, size), new_kv.reshape(steps, 2, -1, size), tokens_dev
    )
    row_list = [mine] + [
        lax.ppermute(mine, "dom", [(i, (i + hop) % owners) for i in range(owners)])
        for hop in range(1, owners)
    ]
    prompt = split_heads(prompt_cache.reshape(2, -1, size), heads)

    inward = [[(j, j + 1), (shards - 1 - j, shards - 2 - j)] for j in range(middle - 1)]
    outward = [[(b, a) for a, b in hop] for hop in reversed(inward)]
    stages = [[] for _ in range(heads)]
    parts = [None] * heads
    state = {}
    last = [lengths]

    def run_attend(head):
        send, keep, sums = attend(
            queries, prompt, row_list, ancestors, lengths, head, scale, suffix_dev, tokens_dev, last[0]
        )
        last[0] = send
        state[head] = send, keep, sums
        stages[head] = ["merge"] * len(inward) + ["finish"]
        parts[head] = send_on(head, send)

    def send_on(head, value):
        hops = len(inward) - stages[head].count("merge")
        if hops < len(inward):
            return lax.ppermute(value, "ctx", inward[hops])
        return lax.ppermute(value, "ctx", [(middle - 1, middle), (middle, middle - 1)])

    def advance(head):
        stage = stages[head].pop(0)
        send, keep, sums = state[head]
        if stage == "merge":
            send = small_call(merge_kernel, message, (keep, sums, parts[head]), last[0])
            last[0] = send
            state[head] = send, keep, sums
            parts[head] = send_on(head, send)
        else:
            done = small_call(finish_kernel, (rows, size), (send, parts[head]), last[0])
            last[0] = done
            got = done
            for at, hop in enumerate(outward):
                got = lax.ppermute(done, "ctx", hop)
                if at < len(outward) - 1:
                    done = jnp.where(sum(shard == b for _, b in hop) > 0, got, done)
            parts[head] = done, got

    order = schedule(heads, len(inward))
    for what, head in order:
        (run_attend if what == "attend" else advance)(head)
    return place(parts, queries.shape, shards)


def schedule(heads, merges):
    order = [("attend", head) for head in range(min(heads, 3))]
    order.append(("next", 0))
    order += [("attend", head) for head in range(3, heads)]
    left = {head: merges + 1 for head in range(heads)}
    left[0] -= 1
    turn = 1
    while any(left.values()):
        ready = [h for h in range(heads) if left[h]]
        head = min(ready, key=lambda h: (h + 2 * (merges + 1 - left[h]), -h))
        order.append(("next", head))
        left[head] -= 1
    return order


def solution(mesh):
    return jax.shard_map(
        functools.partial(on_device, mesh.shape["ctx"], mesh.shape["dom"]),
        mesh=mesh,
        in_specs=(
            P("groups", "dom", "tp", None, None),
            P("groups", "ctx", "tp", None),
            P("groups", "dom", "ctx", "tp", None),
            P("groups", None, "dom", "tp", None),
            P("groups", None),
            P("groups"),
        ),
        out_specs=P("groups", "dom", "tp", None, None),
        check_vma=False,
    )
```

```python
import functools
import math

import jax
import jax.numpy as jnp
from jax import lax
from jax.experimental import pallas as pl
from jax.experimental.pallas import tpu as pltpu
from jax.sharding import PartitionSpec as P

LANES = 128
HIDDEN = -1e30
NN = (((1,), (0,)), ((), ()))
NT = (((1,), (1,)), ((), ()))
SMALL = pl.CostEstimate(flops=0, bytes_accessed=4096, transcendentals=0)


def round_up(value, multiple):
    return -(-value // multiple) * multiple


def dot(a, b, dims):
    return lax.dot_general(a, b, dims, preferred_element_type=jnp.float32)


def eye_mask(rows):
    shape = (rows, LANES)
    return lax.broadcasted_iota(jnp.int32, shape, 0) == lax.broadcasted_iota(jnp.int32, shape, 1)


def column_to_lanes(column):
    rows = column.shape[0]
    block = min(rows, LANES)
    mask = eye_mask(block)
    return jnp.concatenate(
        [
            jnp.sum(jnp.where(mask, column[at : at + block], 0.0), axis=0, keepdims=True)
            for at in range(0, rows, block)
        ],
        axis=0,
    )


def lanes_to_column(lanes, rows):
    block = min(rows, LANES)
    mask = eye_mask(block)
    return jnp.concatenate(
        [
            jnp.sum(jnp.where(mask, lanes[i : i + 1], 0.0), axis=1, keepdims=True)
            for i in range(lanes.shape[0])
        ],
        axis=0,
    )


def tail_rows(rows):
    return round_up(3 * -(-rows // LANES), 16)


def pack_tail(column):
    lanes = column_to_lanes(column)
    high = lanes.astype(jnp.bfloat16).astype(jnp.float32)
    middle = (lanes - high).astype(jnp.bfloat16).astype(jnp.float32)
    low = lanes - high - middle
    parts = jnp.concatenate([high, middle, low], axis=0)
    spare = tail_rows(column.shape[0]) - parts.shape[0]
    return jnp.concatenate([parts, jnp.zeros((spare, LANES), jnp.float32)], axis=0).astype(
        jnp.bfloat16
    )


def unpack_tail(tail, rows):
    tail = tail.astype(jnp.float32)
    blocks = -(-rows // LANES)
    lanes = tail[:blocks] + tail[blocks : 2 * blocks] + tail[2 * blocks : 3 * blocks]
    return lanes_to_column(lanes, rows)


def in_hbm(array):
    return pltpu.with_memory_space_constraint(array, pltpu.HBM)


def message_kernel(heads, suffix_ref, new_ref, out_ref, here, wide, sems):
    rows, each = suffix_ref.shape[1], new_ref.shape[2]
    total = here.shape[1]
    count = (total - rows) // each
    first = jnp.minimum(lax.axis_index("ctx") * count, new_ref.shape[0] - count)
    copies = [pltpu.make_async_copy(suffix_ref, here.at[:, pl.ds(0, rows)], sems.at[0])]
    for token in range(count):
        there = here.at[:, pl.ds(rows + token * each, each)]
        copies.append(pltpu.make_async_copy(new_ref.at[first + token], there, sems.at[1 + token]))
    for copy in copies:
        copy.start()
    for copy in copies:
        copy.wait()
    for kind in range(2):
        wide[kind] = here[kind].astype(jnp.float32)
        for head in range(heads):
            part = wide[kind, pl.ds(head, total // heads, stride=heads), :]
            out_ref[kind, head] = part.astype(out_ref.dtype)


def build_message(suffix, new, heads, tokens_dev):
    rows = suffix.shape[1] + tokens_dev * new.shape[2]
    size = suffix.shape[2]
    return pl.pallas_call(
        functools.partial(message_kernel, heads),
        in_specs=[pl.BlockSpec(memory_space=pltpu.HBM)] * 2,
        out_shape=jax.ShapeDtypeStruct((2, heads, rows // heads, size), suffix.dtype),
        scratch_shapes=[
            pltpu.VMEM((2, rows, size), suffix.dtype),
            pltpu.VMEM((2, rows, size), jnp.float32),
            pltpu.SemaphoreType.DMA((1 + tokens_dev,)),
        ],
        compiler_params=pltpu.CompilerParams(vmem_limit_bytes=16 << 20),
        cost_estimate=SMALL,
    )(in_hbm(suffix), in_hbm(new))


def iota(shape, axis):
    return lax.broadcasted_iota(jnp.int32, shape, axis)


def lineage_bias(ancestors_ref, lengths_ref, owners, per_owner, suffix_dev, tokens_dev, padded):
    particles = owners * per_owner
    steps = ancestors_ref.shape[0]
    suffix_columns = per_owner * suffix_dev
    each = suffix_columns + per_owner * tokens_dev
    my_owner = lax.axis_index("dom")
    my_shard = lax.axis_index("ctx")
    square = (particles, particles)
    same = iota(square, 0) == iota(square, 1)

    def as_column(row):
        return jnp.sum(jnp.where(same, row, 0), axis=1, keepdims=True)

    unit = same.astype(jnp.float32)
    nothing = jnp.zeros((particles, tokens_dev * particles), jnp.float32)
    state = jnp.concatenate([unit, nothing], axis=1)
    pick = iota((per_owner, particles), 1) == iota((per_owner, particles), 0) + my_owner * per_owner
    pick = pick.astype(jnp.bfloat16)
    mine = []
    for step in range(steps):
        parent = as_column(ancestors_ref[step : step + 1, :])
        move = (parent == iota(square, 1)).astype(jnp.bfloat16)
        state = dot(move, state.astype(jnp.bfloat16), NN)
        blocks = [state[:, :particles]]
        for token in range(tokens_dev):
            written = my_shard * tokens_dev + token
            old = state[:, (1 + token) * particles : (2 + token) * particles]
            blocks.append(jnp.where(written == step, unit, old))
        state = jnp.concatenate(blocks, axis=1)
        mine.append(dot(pick, state.astype(jnp.bfloat16), NN))
    mine = jnp.concatenate(mine, axis=0).astype(jnp.bfloat16)
    lengths = as_column(lengths_ref[...])
    shape = (particles, padded)
    column = iota(shape, 1)
    source = column // each
    owner = lax.rem(my_owner + owners - source, owners)
    inner = column - source * each
    after = inner - suffix_columns
    in_suffix = after < 0
    local = jnp.where(in_suffix, inner // suffix_dev, lax.rem(jnp.maximum(after, 0), per_owner))
    here = (iota(shape, 0) == owner * per_owner + local) & (column < owners * each)
    position = my_shard * suffix_dev + lax.rem(inner, suffix_dev)
    seen = [here & in_suffix & (position < lengths)]
    for token in range(tokens_dev):
        seen.append(here & (after >= token * per_owner) & (after < (token + 1) * per_owner))
    table = jnp.concatenate([s.astype(jnp.bfloat16) for s in seen], axis=0)
    return jnp.where(dot(mine, table, NN) > 0.5, 0.0, HIDDEN)


def split_kernel(
    heads, block, owners, suffix_dev, tokens_dev,
    rows_ref, ancestors_ref, lengths_ref, out_ref, bias_ref, here, wide, sems,
):
    total = out_ref.shape[2]
    places = [(kind, at) for kind in range(2) for at in range(0, total, block)]
    copies = [
        pltpu.make_async_copy(
            rows_ref.at[kind, pl.ds(at * heads, block * heads)],
            here.at[kind, pl.ds(at * heads, block * heads)],
            sems.at[i],
        )
        for i, (kind, at) in enumerate(places)
    ]
    for copy in copies:
        copy.start()
    bias_ref[...] = lineage_bias(
        ancestors_ref,
        lengths_ref,
        owners,
        ancestors_ref.shape[1] // owners,
        suffix_dev,
        tokens_dev,
        bias_ref.shape[1],
    )
    for i, (kind, at) in enumerate(places):
        copies[i].wait()
        wide[i % 2] = here[kind, at * heads : (at + block) * heads].astype(jnp.float32)
        for head in range(heads):
            part = wide[i % 2, pl.ds(head, block, stride=heads), :]
            out_ref[kind, head, at : at + block] = part.astype(out_ref.dtype)


def split_prompt(rows, ancestors, lengths, heads, owners, suffix_dev, tokens_dev):
    total = rows.shape[1] // heads
    block = math.gcd(total, 512)
    size = rows.shape[2]
    steps, particles = ancestors.shape
    padded = round_up(particles * (suffix_dev + tokens_dev), LANES)
    return pl.pallas_call(
        functools.partial(split_kernel, heads, block, owners, suffix_dev, tokens_dev),
        in_specs=[pl.BlockSpec(memory_space=pltpu.HBM)]
        + [pl.BlockSpec(memory_space=pltpu.VMEM)] * 2,
        out_shape=(
            jax.ShapeDtypeStruct((2, heads, total, size), rows.dtype),
            jax.ShapeDtypeStruct((steps * particles // owners, padded), jnp.float32),
        ),
        scratch_shapes=[
            pltpu.VMEM(rows.shape, rows.dtype),
            pltpu.VMEM((2, block * heads, size), jnp.float32),
            pltpu.SemaphoreType.DMA((2 * total // block,)),
        ],
        compiler_params=pltpu.CompilerParams(vmem_limit_bytes=24 << 20),
        cost_estimate=SMALL,
    )(in_hbm(rows), ancestors, lengths.reshape(1, -1))


def with_ones(values):
    return jnp.concatenate([values, jnp.ones_like(values)], axis=1)


def row_peak(scores):
    return jnp.max(scores, axis=1, keepdims=True)


def weigh(scores, factor, offset):
    return jnp.exp2(scores * factor - offset).astype(jnp.bfloat16)


def prompt_sum(q, k_ref, v_ref, i, factor, peak):
    total = k_ref.shape[2]
    block = math.gcd(total, 512)
    together = None
    for at in range(0, total, block):
        scores = dot(q, k_ref[0, i, at : at + block], NT)
        if at == 0:
            top = row_peak(scores)
            offset = (top if peak is None else jnp.maximum(top, peak)) * factor
        part = dot(weigh(scores, factor, offset), with_ones(v_ref[0, i, at : at + block]), NN)
        together = part if together is None else together + part
    return together, offset


def prompt_kernel(factor, q_ref, k_ref, v_ref, together_ref, offset_ref):
    steps, per_owner, _, group, size = q_ref.shape
    q = q_ref[...].reshape(steps * per_owner * group, size)
    together, offset = prompt_sum(q, k_ref, v_ref, 0, factor, None)
    together_ref[...] = together
    offset_ref[...] = jnp.broadcast_to(offset, offset_ref.shape)


def block_specs(queries, prompt, head, count):
    steps, per_owner, _, group, size = queries.shape
    total = prompt.shape[2]
    at = head // count
    return [
        pl.BlockSpec((steps, per_owner, count, group, size), lambda i: (0, 0, at, 0, 0)),
        pl.BlockSpec((1, count, total, size), lambda i: (0, at, 0, 0)),
        pl.BlockSpec((1, count, total, size), lambda i: (1, at, 0, 0)),
    ]


def whole(array):
    return pl.BlockSpec(array.shape, lambda i: (0,) * array.ndim)


def start_head(queries, prompt, head, factor):
    steps, per_owner, _, group, size = queries.shape
    rows = steps * per_owner * group
    shapes = (
        jax.ShapeDtypeStruct((rows, 2 * size), jnp.float32),
        jax.ShapeDtypeStruct((rows, LANES), jnp.float32),
    )
    return pl.pallas_call(
        functools.partial(prompt_kernel, factor),
        grid=(1,),
        in_specs=block_specs(queries, prompt, head, 1),
        out_specs=[whole(s) for s in shapes],
        out_shape=shapes,
        compiler_params=pltpu.CompilerParams(vmem_limit_bytes=24 << 20),
        cost_estimate=SMALL,
    )(queries, prompt, prompt)


def attend_kernel(factor, owners, halves, started, *refs):
    q_ref, k_ref, v_ref, bias_ref = refs[:4]
    row_refs = refs[4 : 4 + owners]
    begun = refs[4 + owners : 4 + owners + 2 * started]
    _, send_ref, keep_ref, sums_ref, out, log_sums = refs[4 + owners + 2 * started :]
    steps, per_owner, count, group, size = q_ref.shape
    padded = bias_ref.shape[1]
    rows = steps * per_owner * group
    half = rows // halves

    def queries_of(i, first, number):
        here = number * per_owner * group
        q = q_ref[pl.ds(first, number), :, i].reshape(here, size)
        at = pl.multiple_of(first * per_owner, per_owner)
        bias = bias_ref[pl.ds(at, number * per_owner), :]
        bias = jnp.broadcast_to(bias[:, None, :], (number * per_owner, group, padded))
        return q, dot(q, suffix_of(i, 0), NT) + bias.reshape(here, padded)

    def suffix_of(i, kind):
        pieces = [ref[kind, i] for ref in row_refs]
        columns = sum(piece.shape[0] for piece in pieces)
        if padded > columns:
            pieces.append(jnp.zeros((padded - columns, size), jnp.bfloat16))
        return jnp.concatenate(pieces, axis=0)

    def store(at, together, offset):
        sums = together[:, size:]
        out[pl.ds(at, sums.shape[0]), :] = together[:, :size] / sums
        log_sums[pl.ds(at, sums.shape[0]), :] = offset + jnp.log2(sums)
        return sums

    for i in range(count):
        q, suffix_scores = queries_of(i, 0, steps)
        if i < started:
            together, offset = begun[2 * i][...], begun[2 * i + 1][:, :1]
        else:
            peak = row_peak(suffix_scores)
            together, offset = prompt_sum(q, k_ref, v_ref, i, factor, peak)
        weight = weigh(suffix_scores, factor, offset)
        together = together + dot(weight, with_ones(suffix_of(i, 1)), NN)
        sums = store(0, together, offset)

        @pl.when(jnp.logical_not(jnp.max(sums) < 2.0**100))
        def _():
            @pl.loop(0, steps)
            def _(step):
                q, suffix_scores = queries_of(i, step, 1)
                scores = dot(q, k_ref[0, i], NT)
                offset = jnp.maximum(row_peak(scores), row_peak(suffix_scores)) * factor
                together = dot(weigh(scores, factor, offset), with_ones(v_ref[0, i]), NN)
                weight = weigh(suffix_scores, factor, offset)
                together = together + dot(weight, with_ones(suffix_of(i, 1)), NN)
                store(pl.multiple_of(step * per_owner * group, per_owner * group), together, offset)

        bit = lax.rem(lax.axis_index("ctx"), 2) if halves == 2 else 0
        there = pl.ds(pl.multiple_of((halves - 1 - bit) * half, half), half)
        send_ref[i, :half] = out[there, :].astype(jnp.bfloat16)
        send_ref[i, half:] = pack_tail(log_sums[there, :][:, :1])
        here = pl.ds(pl.multiple_of(bit * half, half), half)
        keep_ref[i] = out[here, :]
        sums_ref[i] = log_sums[here, :]


def attend(queries, prompt, bias, row_list, head, count, factor, halves, begun, after):
    steps, per_owner, heads, group, size = queries.shape
    rows = steps * per_owner * group
    half = rows // halves
    shapes = (
        jax.ShapeDtypeStruct((count, half + tail_rows(half), size), jnp.bfloat16),
        jax.ShapeDtypeStruct((count, half, size), jnp.float32),
        jax.ShapeDtypeStruct((count, half, LANES), jnp.float32),
    )
    slots = row_list[0].shape[2]
    row_spec = pl.BlockSpec((2, count, slots, size), lambda i: (0, head // count, 0, 0))
    return pl.pallas_call(
        functools.partial(attend_kernel, factor, len(row_list), halves, len(begun) // 2),
        grid=(1,),
        in_specs=[
            *block_specs(queries, prompt, head, count),
            whole(bias),
            *[row_spec] * len(row_list),
            *[whole(b) for b in begun],
            pl.BlockSpec(memory_space=pl.ANY),
        ],
        out_specs=[whole(s) for s in shapes],
        out_shape=shapes,
        scratch_shapes=[
            pltpu.VMEM((rows, size), jnp.float32),
            pltpu.VMEM((rows, LANES), jnp.float32),
        ],
        compiler_params=pltpu.CompilerParams(vmem_limit_bytes=32 << 20),
        cost_estimate=SMALL,
    )(queries, prompt, prompt, bias, *row_list, *begun, after)


def merge(out_a, sum_a, out_b, sum_b):
    top = jnp.maximum(sum_a, sum_b)
    weight_a = jnp.exp2(sum_a - top)
    weight_b = jnp.exp2(sum_b - top)
    total = weight_a + weight_b
    return (out_a * weight_a + out_b * weight_b) / total, top + jnp.log2(total)


def in_vmem(count):
    return [pl.BlockSpec(memory_space=pltpu.VMEM)] * count + [pl.BlockSpec(memory_space=pl.ANY)]


def merge_kernel(level, last, keep_ref, sums_ref, got_ref, _, *outs):
    rows = keep_ref.shape[1]
    for i in range(keep_ref.shape[0]):
        got_sum = unpack_tail(got_ref[i, rows:], rows)
        out, log_sum = merge(
            keep_ref[i], sums_ref[i][:, :1], got_ref[i, :rows].astype(jnp.float32), got_sum
        )
        if last:
            outs[0][i, :rows] = out.astype(jnp.bfloat16)
            outs[0][i, rows:] = pack_tail(log_sum)
        else:
            half = rows // 2
            bit = lax.rem(lax.axis_index("ctx") >> level, 2) == 1
            send, keep, wide = outs

            def choose(first, value):
                return jnp.where(first, value[:half], value[half:])

            send[i, :half] = choose(bit, out).astype(jnp.bfloat16)
            send[i, half:] = pack_tail(choose(bit, log_sum))
            keep[i] = choose(~bit, out)
            wide[i] = jnp.broadcast_to(choose(~bit, log_sum), (half, LANES))


def merge_parts(keep, sums, got, level, last, after):
    count, rows, size = keep.shape
    part = rows if last else rows // 2
    shapes = [jax.ShapeDtypeStruct((count, part + tail_rows(part), size), jnp.bfloat16)]
    if not last:
        shapes.append(jax.ShapeDtypeStruct((count, part, size), jnp.float32))
        shapes.append(jax.ShapeDtypeStruct((count, part, LANES), jnp.float32))
    return pl.pallas_call(
        functools.partial(merge_kernel, level, last),
        in_specs=in_vmem(3),
        out_shape=tuple(shapes),
        compiler_params=pltpu.CompilerParams(vmem_limit_bytes=16 << 20),
        cost_estimate=SMALL,
    )(keep, sums, got, after)


def finish_kernel(mine_ref, got_ref, _, out_ref):
    rows = math.prod(out_ref.shape[1:-1])
    for i in range(mine_ref.shape[0]):
        out, _ = merge(
            mine_ref[i, :rows].astype(jnp.float32),
            unpack_tail(mine_ref[i, rows:], rows),
            got_ref[i, :rows].astype(jnp.float32),
            unpack_tail(got_ref[i, rows:], rows),
        )
        out_ref[i] = out.astype(jnp.bfloat16).reshape(out_ref.shape[1:])


def finish(mine, got, shape, after):
    return pl.pallas_call(
        finish_kernel,
        in_specs=in_vmem(2),
        out_shape=jax.ShapeDtypeStruct(shape, jnp.bfloat16),
        compiler_params=pltpu.CompilerParams(vmem_limit_bytes=16 << 20),
        cost_estimate=SMALL,
    )(mine, got, after)


def place_kernel(levels, plan, *refs):
    *part_refs, out_ref, sems = refs
    copies = []
    for (head, own), ref in zip(plan, part_refs):
        blocks = ref.shape[1]
        bit = lax.rem(lax.axis_index("ctx"), 2) if levels > 1 else 0
        at = (bit if own else 1 - bit) * blocks
        for i in range(ref.shape[0]):
            there = out_ref.at[pl.ds(at, blocks), :, head + i]
            copies.append(pltpu.make_async_copy(ref.at[i], there, sems.at[len(copies)]))
    for copy in copies:
        copy.start()
    for copy in copies:
        copy.wait()


def place(parts, shape, levels):
    arrays = [array for array, _, _ in parts]
    plan = [(head, own) for _, head, own in parts]
    return pl.pallas_call(
        functools.partial(place_kernel, levels, plan),
        in_specs=[pl.BlockSpec(memory_space=pltpu.VMEM)] * len(arrays),
        out_specs=pl.BlockSpec(memory_space=pltpu.HBM),
        out_shape=jax.ShapeDtypeStruct(shape, jnp.bfloat16),
        scratch_shapes=[pltpu.SemaphoreType.DMA((sum(a.shape[0] for a in arrays),))],
        compiler_params=pltpu.CompilerParams(vmem_limit_bytes=16 << 20),
        cost_estimate=SMALL,
    )(*arrays)


def on_device(shards, owners, queries, prompt_cache, suffix_cache, new_kv, ancestors, lengths):
    steps, per_owner, heads, group, size = queries.shape
    suffix_dev = suffix_cache.shape[2]
    shard = lax.axis_index("ctx")
    factor = math.log2(math.e) / math.sqrt(size)
    tokens_dev = -(-steps // shards)
    levels = shards.bit_length() - 1
    halves = 2 if levels > 1 else 1

    def swap(value, bit):
        return lax.ppermute(value, "ctx", [(i, i ^ (1 << bit)) for i in range(shards)])

    mine = build_message(
        suffix_cache.reshape(2, -1, size), new_kv.reshape(steps, 2, -1, size), heads, tokens_dev
    )
    row_list = [mine] + [
        lax.ppermute(mine, "dom", [(i, (i + hop) % owners) for i in range(owners)])
        for hop in range(1, owners)
    ]
    prompt, bias = split_prompt(
        prompt_cache.reshape(2, -1, size), ancestors, lengths, heads, owners, suffix_dev, tokens_dev
    )
    last = [bias]

    def follow(results):
        last[0] = results[0] if isinstance(results, (tuple, list)) else results
        return results

    begun = follow(start_head(queries, prompt, 0, factor))
    first = max(heads // 2, 1)
    chunks = [(0, first)] + [(head, 1) for head in range(first, heads)]
    messages, kept, parts = {}, {}, []

    def run_attend(chunk):
        head, count = chunk
        send, keep, sums = follow(
            attend(
                queries, prompt, bias, row_list, head, count, factor, halves,
                begun if head == 0 else (), last[0],
            )
        )
        kept[chunk] = keep, sums
        messages[chunk] = send, swap(send, 0)

    def run_merges(chunk):
        for level in range(1, levels):
            results = follow(
                merge_parts(
                    *kept[chunk], messages[chunk][1], level, level == levels - 1, last[0]
                )
            )
            send, kept[chunk] = results[0], results[1:]
            messages[chunk] = send, swap(send, level)

    def run_finish(chunk):
        head, count = chunk
        blocks = (steps * per_owner) >> (levels - 1 if levels > 1 else 0)
        done = follow(finish(*messages[chunk], (count, blocks, group, size), last[0]))
        for level in range(levels - 2, 0, -1):
            other = swap(done, level)
            done = jnp.where(
                (shard >> level) % 2 == 1,
                jnp.concatenate([other, done], axis=1),
                jnp.concatenate([done, other], axis=1),
            )
        done = done.reshape(count, steps // halves, per_owner, group, size)
        parts.append((done, head, True))
        if levels > 1:
            parts.append((swap(done, 0), head, False))

    run_attend(chunks[0])
    for before, chunk in zip(chunks, chunks[1:]):
        run_attend(chunk)
        run_merges(before)
    run_merges(chunks[-1])
    for chunk in chunks[:-1]:
        run_finish(chunk)
    run_finish(chunks[-1])
    return place(parts, queries.shape, levels)


def solution(mesh):
    return jax.shard_map(
        functools.partial(on_device, mesh.shape["ctx"], mesh.shape["dom"]),
        mesh=mesh,
        in_specs=(
            P("groups", "dom", "tp", None, None),
            P("groups", "ctx", "tp", None),
            P("groups", "dom", "ctx", "tp", None),
            P("groups", None, "dom", "tp", None),
            P("groups", None),
            P("groups"),
        ),
        out_specs=P("groups", "dom", "tp", None, None),
        check_vma=False,
    )
```

```python
import functools
import math

import jax
import jax.numpy as jnp
from jax import lax
from jax.experimental import pallas as pl
from jax.experimental.pallas import tpu as pltpu
from jax.sharding import PartitionSpec as P

LANES = 128
HIDDEN = -1e30
NN = (((1,), (0,)), ((), ()))
NT = (((1,), (1,)), ((), ()))
SMALL = pl.CostEstimate(flops=0, bytes_accessed=4096, transcendentals=0)


def round_up(value, multiple):
    return -(-value // multiple) * multiple


def dot(a, b, dims):
    return lax.dot_general(a, b, dims, preferred_element_type=jnp.float32)


def eye_mask(rows):
    shape = (rows, LANES)
    return lax.broadcasted_iota(jnp.int32, shape, 0) == lax.broadcasted_iota(jnp.int32, shape, 1)


def column_to_lanes(column):
    rows = column.shape[0]
    block = min(rows, LANES)
    mask = eye_mask(block)
    return jnp.concatenate(
        [
            jnp.sum(jnp.where(mask, column[at : at + block], 0.0), axis=0, keepdims=True)
            for at in range(0, rows, block)
        ],
        axis=0,
    )


def lanes_to_column(lanes, rows):
    block = min(rows, LANES)
    mask = eye_mask(block)
    return jnp.concatenate(
        [
            jnp.sum(jnp.where(mask, lanes[i : i + 1], 0.0), axis=1, keepdims=True)
            for i in range(lanes.shape[0])
        ],
        axis=0,
    )


def tail_rows(rows):
    return round_up(3 * -(-rows // LANES), 16)


def pack_tail(column):
    lanes = column_to_lanes(column)
    high = lanes.astype(jnp.bfloat16).astype(jnp.float32)
    middle = (lanes - high).astype(jnp.bfloat16).astype(jnp.float32)
    low = lanes - high - middle
    parts = jnp.concatenate([high, middle, low], axis=0)
    spare = tail_rows(column.shape[0]) - parts.shape[0]
    return jnp.concatenate([parts, jnp.zeros((spare, LANES), jnp.float32)], axis=0).astype(
        jnp.bfloat16
    )


def unpack_tail(tail, rows):
    tail = tail.astype(jnp.float32)
    blocks = -(-rows // LANES)
    lanes = tail[:blocks] + tail[blocks : 2 * blocks] + tail[2 * blocks : 3 * blocks]
    return lanes_to_column(lanes, rows)


def in_hbm(array):
    return pltpu.with_memory_space_constraint(array, pltpu.HBM)


def message_kernel(
    heads, owners, suffix_dev, tokens_dev,
    suffix_ref, new_ref, prompt_ref, ancestors_ref, lengths_ref,
    out_ref, bias_ref, keys_ref, here, wide, parents, extents, sems,
):
    rows, each = suffix_ref.shape[1], new_ref.shape[2]
    total = here.shape[1]
    first = jnp.minimum(lax.axis_index("ctx") * tokens_dev, new_ref.shape[0] - tokens_dev)
    small = [(ancestors_ref, parents), (lengths_ref, extents)]
    parts = [(suffix_ref, here.at[:, pl.ds(0, rows)])]
    for token in range(tokens_dev):
        parts.append((new_ref.at[first + token], here.at[:, pl.ds(rows + token * each, each)]))
    pairs = small + parts + [(prompt_ref.at[0], keys_ref)]
    copies = [pltpu.make_async_copy(*pair, sems.at[i]) for i, pair in enumerate(pairs)]
    for copy in copies:
        copy.start()
    for copy in copies[: len(small)]:
        copy.wait()
    bias_ref[...] = lineage_bias(
        parents, extents, owners, parents.shape[1] // owners, suffix_dev, tokens_dev,
        bias_ref.shape[1],
    )
    for copy in copies[len(small) : -1]:
        copy.wait()
    for kind in range(2):
        wide[kind] = here[kind].astype(jnp.float32)
        for head in range(heads):
            part = wide[kind, pl.ds(head, total // heads, stride=heads), :]
            out_ref[kind, head] = part.astype(out_ref.dtype)
    copies[-1].wait()


def build_message(suffix, new, prompt, ancestors, lengths, heads, owners, suffix_dev, tokens_dev):
    rows = suffix.shape[1] + tokens_dev * new.shape[2]
    size = suffix.shape[2]
    steps, particles = ancestors.shape
    padded = round_up(particles * (suffix_dev + tokens_dev), LANES)
    operands = (suffix, new, prompt, ancestors, lengths.reshape(1, -1))
    return pl.pallas_call(
        functools.partial(message_kernel, heads, owners, suffix_dev, tokens_dev),
        in_specs=[pl.BlockSpec(memory_space=pltpu.HBM)] * len(operands),
        out_shape=(
            jax.ShapeDtypeStruct((2, heads, rows // heads, size), suffix.dtype),
            jax.ShapeDtypeStruct((steps * particles // owners, padded), jnp.float32),
            jax.ShapeDtypeStruct(prompt.shape[1:], prompt.dtype),
        ),
        scratch_shapes=[
            pltpu.VMEM((2, rows, size), suffix.dtype),
            pltpu.VMEM((2, rows, size), jnp.float32),
            pltpu.VMEM(ancestors.shape, ancestors.dtype),
            pltpu.VMEM((1, particles), lengths.dtype),
            pltpu.SemaphoreType.DMA((4 + tokens_dev,)),
        ],
        compiler_params=pltpu.CompilerParams(vmem_limit_bytes=24 << 20),
        cost_estimate=SMALL,
    )(*[in_hbm(operand) for operand in operands])


def iota(shape, axis):
    return lax.broadcasted_iota(jnp.int32, shape, axis)


def lineage_bias(ancestors_ref, lengths_ref, owners, per_owner, suffix_dev, tokens_dev, padded):
    particles = owners * per_owner
    steps = ancestors_ref.shape[0]
    suffix_columns = per_owner * suffix_dev
    each = suffix_columns + per_owner * tokens_dev
    my_owner = lax.axis_index("dom")
    my_shard = lax.axis_index("ctx")
    square = (particles, particles)
    same = iota(square, 0) == iota(square, 1)

    def as_column(row):
        return jnp.sum(jnp.where(same, row, 0), axis=1, keepdims=True)

    unit = same.astype(jnp.float32)
    nothing = jnp.zeros((particles, tokens_dev * particles), jnp.float32)
    state = jnp.concatenate([unit, nothing], axis=1)
    pick = iota((per_owner, particles), 1) == iota((per_owner, particles), 0) + my_owner * per_owner
    pick = pick.astype(jnp.bfloat16)
    mine = []
    for step in range(steps):
        parent = as_column(ancestors_ref[step : step + 1, :])
        move = (parent == iota(square, 1)).astype(jnp.bfloat16)
        state = dot(move, state.astype(jnp.bfloat16), NN)
        blocks = [state[:, :particles]]
        for token in range(tokens_dev):
            written = my_shard * tokens_dev + token
            old = state[:, (1 + token) * particles : (2 + token) * particles]
            blocks.append(jnp.where(written == step, unit, old))
        state = jnp.concatenate(blocks, axis=1)
        mine.append(dot(pick, state.astype(jnp.bfloat16), NN))
    mine = jnp.concatenate(mine, axis=0).astype(jnp.bfloat16)
    lengths = as_column(lengths_ref[...])
    shape = (particles, padded)
    column = iota(shape, 1)
    source = column // each
    owner = lax.rem(my_owner + owners - source, owners)
    inner = column - source * each
    after = inner - suffix_columns
    in_suffix = after < 0
    local = jnp.where(in_suffix, inner // suffix_dev, lax.rem(jnp.maximum(after, 0), per_owner))
    here = (iota(shape, 0) == owner * per_owner + local) & (column < owners * each)
    position = my_shard * suffix_dev + lax.rem(inner, suffix_dev)
    seen = [here & in_suffix & (position < lengths)]
    for token in range(tokens_dev):
        seen.append(here & (after >= token * per_owner) & (after < (token + 1) * per_owner))
    table = jnp.concatenate([s.astype(jnp.bfloat16) for s in seen], axis=0)
    return jnp.where(dot(mine, table, NN) > 0.5, 0.0, HIDDEN)


def split_kernel(heads, block, rows_ref, keys_ref, out_ref, here, wide, sems):
    total = out_ref.shape[2]
    places = range(0, total, block)
    copies = [
        pltpu.make_async_copy(
            rows_ref.at[1, pl.ds(at * heads, block * heads)],
            here.at[pl.ds(at * heads, block * heads)],
            sems.at[i],
        )
        for i, at in enumerate(places)
    ]
    for copy in copies:
        copy.start()
    for kind, source in enumerate((keys_ref, here)):
        for i, at in enumerate(places):
            if kind == 1:
                copies[i].wait()
            wide[i % 2] = source[at * heads : (at + block) * heads].astype(jnp.float32)
            for head in range(heads):
                part = wide[i % 2, pl.ds(head, block, stride=heads), :]
                out_ref[kind, head, at : at + block] = part.astype(out_ref.dtype)


def split_prompt(rows, keys, heads):
    total = rows.shape[1] // heads
    block = math.gcd(total, 512)
    size = rows.shape[2]
    return pl.pallas_call(
        functools.partial(split_kernel, heads, block),
        in_specs=[
            pl.BlockSpec(memory_space=pltpu.HBM),
            pl.BlockSpec(memory_space=pltpu.VMEM),
        ],
        out_shape=jax.ShapeDtypeStruct((2, heads, total, size), rows.dtype),
        scratch_shapes=[
            pltpu.VMEM(rows.shape[1:], rows.dtype),
            pltpu.VMEM((2, block * heads, size), jnp.float32),
            pltpu.SemaphoreType.DMA((total // block,)),
        ],
        compiler_params=pltpu.CompilerParams(vmem_limit_bytes=24 << 20),
        cost_estimate=SMALL,
    )(in_hbm(rows), keys)


def with_ones(values):
    return jnp.concatenate([values, jnp.ones_like(values)], axis=1)


def row_peak(scores):
    return jnp.max(scores, axis=1, keepdims=True)


def weigh(scores, factor, offset):
    return jnp.exp2(scores * factor - offset).astype(jnp.bfloat16)


def prompt_sum(q, k_ref, v_ref, i, factor, peak):
    total = k_ref.shape[2]
    block = math.gcd(total, 512)
    weights = []
    for at in range(0, total, block):
        scores = dot(q, k_ref[0, i, at : at + block], NT)
        if at == 0:
            top = row_peak(scores)
            offset = (top if peak is None else jnp.maximum(top, peak)) * factor
        weights.append(weigh(scores, factor, offset))
    return dot(jnp.concatenate(weights, axis=1), with_ones(v_ref[0, i]), NN), offset


def prompt_kernel(factor, q_ref, k_ref, v_ref, together_ref, offset_ref):
    steps, per_owner, _, group, size = q_ref.shape
    q = q_ref[...].reshape(steps * per_owner * group, size)
    together, offset = prompt_sum(q, k_ref, v_ref, 0, factor, None)
    together_ref[...] = together
    offset_ref[...] = jnp.broadcast_to(offset, offset_ref.shape)


def block_specs(queries, prompt, head, count):
    steps, per_owner, _, group, size = queries.shape
    total = prompt.shape[2]
    at = head // count
    return [
        pl.BlockSpec((steps, per_owner, count, group, size), lambda i: (0, 0, at, 0, 0)),
        pl.BlockSpec((1, count, total, size), lambda i: (0, at, 0, 0)),
        pl.BlockSpec((1, count, total, size), lambda i: (1, at, 0, 0)),
    ]


def whole(array):
    return pl.BlockSpec(array.shape, lambda i: (0,) * array.ndim)


def start_head(queries, prompt, head, factor):
    steps, per_owner, _, group, size = queries.shape
    rows = steps * per_owner * group
    shapes = (
        jax.ShapeDtypeStruct((rows, 2 * size), jnp.float32),
        jax.ShapeDtypeStruct((rows, LANES), jnp.float32),
    )
    return pl.pallas_call(
        functools.partial(prompt_kernel, factor),
        grid=(1,),
        in_specs=block_specs(queries, prompt, head, 1),
        out_specs=[whole(s) for s in shapes],
        out_shape=shapes,
        compiler_params=pltpu.CompilerParams(vmem_limit_bytes=24 << 20),
        cost_estimate=SMALL,
    )(queries, prompt, prompt)


def attend_kernel(factor, owners, halves, started, *refs):
    q_ref, k_ref, v_ref, bias_ref = refs[:4]
    row_refs = refs[4 : 4 + owners]
    begun = refs[4 + owners : 4 + owners + 2 * started]
    _, send_ref, keep_ref, sums_ref, out, log_sums = refs[4 + owners + 2 * started :]
    steps, per_owner, count, group, size = q_ref.shape
    padded = bias_ref.shape[1]
    rows = steps * per_owner * group
    half = rows // halves

    def queries_of(i, first, number):
        here = number * per_owner * group
        q = q_ref[pl.ds(first, number), :, i].reshape(here, size)
        at = pl.multiple_of(first * per_owner, per_owner)
        bias = bias_ref[pl.ds(at, number * per_owner), :]
        bias = jnp.broadcast_to(bias[:, None, :], (number * per_owner, group, padded))
        return q, dot(q, suffix_of(i, 0), NT) + bias.reshape(here, padded)

    def suffix_of(i, kind):
        pieces = [ref[kind, i] for ref in row_refs]
        columns = sum(piece.shape[0] for piece in pieces)
        if padded > columns:
            pieces.append(jnp.zeros((padded - columns, size), jnp.bfloat16))
        return jnp.concatenate(pieces, axis=0)

    def store(at, together, offset):
        sums = together[:, size:]
        out[pl.ds(at, sums.shape[0]), :] = together[:, :size] / sums
        log_sums[pl.ds(at, sums.shape[0]), :] = offset + jnp.log2(sums)
        return sums

    for i in range(count):
        q, suffix_scores = queries_of(i, 0, steps)
        if i < started:
            together, offset = begun[2 * i][...], begun[2 * i + 1][:, :1]
        else:
            peak = row_peak(suffix_scores)
            together, offset = prompt_sum(q, k_ref, v_ref, i, factor, peak)
        weight = weigh(suffix_scores, factor, offset)
        together = together + dot(weight, with_ones(suffix_of(i, 1)), NN)
        sums = store(0, together, offset)

        @pl.when(jnp.logical_not(jnp.max(sums) < 2.0**100))
        def _():
            @pl.loop(0, steps)
            def _(step):
                q, suffix_scores = queries_of(i, step, 1)
                scores = dot(q, k_ref[0, i], NT)
                offset = jnp.maximum(row_peak(scores), row_peak(suffix_scores)) * factor
                together = dot(weigh(scores, factor, offset), with_ones(v_ref[0, i]), NN)
                weight = weigh(suffix_scores, factor, offset)
                together = together + dot(weight, with_ones(suffix_of(i, 1)), NN)
                store(pl.multiple_of(step * per_owner * group, per_owner * group), together, offset)

        bit = lax.rem(lax.axis_index("ctx"), 2) if halves == 2 else 0
        there = pl.ds(pl.multiple_of((halves - 1 - bit) * half, half), half)
        send_ref[i, :half] = out[there, :].astype(jnp.bfloat16)
        send_ref[i, half:] = pack_tail(log_sums[there, :][:, :1])
        here = pl.ds(pl.multiple_of(bit * half, half), half)
        keep_ref[i] = out[here, :]
        sums_ref[i] = log_sums[here, :]


def attend(queries, prompt, bias, row_list, head, count, factor, halves, begun, after):
    steps, per_owner, heads, group, size = queries.shape
    rows = steps * per_owner * group
    half = rows // halves
    shapes = (
        jax.ShapeDtypeStruct((count, half + tail_rows(half), size), jnp.bfloat16),
        jax.ShapeDtypeStruct((count, half, size), jnp.float32),
        jax.ShapeDtypeStruct((count, half, LANES), jnp.float32),
    )
    slots = row_list[0].shape[2]
    row_spec = pl.BlockSpec((2, count, slots, size), lambda i: (0, head // count, 0, 0))
    return pl.pallas_call(
        functools.partial(attend_kernel, factor, len(row_list), halves, len(begun) // 2),
        grid=(1,),
        in_specs=[
            *block_specs(queries, prompt, head, count),
            whole(bias),
            *[row_spec] * len(row_list),
            *[whole(b) for b in begun],
            pl.BlockSpec(memory_space=pl.ANY),
        ],
        out_specs=[whole(s) for s in shapes],
        out_shape=shapes,
        scratch_shapes=[
            pltpu.VMEM((rows, size), jnp.float32),
            pltpu.VMEM((rows, LANES), jnp.float32),
        ],
        compiler_params=pltpu.CompilerParams(vmem_limit_bytes=32 << 20),
        cost_estimate=SMALL,
    )(queries, prompt, prompt, bias, *row_list, *begun, after)


def merge(out_a, sum_a, out_b, sum_b):
    top = jnp.maximum(sum_a, sum_b)
    weight_a = jnp.exp2(sum_a - top)
    weight_b = jnp.exp2(sum_b - top)
    total = weight_a + weight_b
    return (out_a * weight_a + out_b * weight_b) / total, top + jnp.log2(total)


def in_vmem(count):
    return [pl.BlockSpec(memory_space=pltpu.VMEM)] * count + [pl.BlockSpec(memory_space=pl.ANY)]


def merge_kernel(level, last, keep_ref, sums_ref, got_ref, _, *outs):
    rows = keep_ref.shape[1]
    for i in range(keep_ref.shape[0]):
        got_sum = unpack_tail(got_ref[i, rows:], rows)
        out, log_sum = merge(
            keep_ref[i], sums_ref[i][:, :1], got_ref[i, :rows].astype(jnp.float32), got_sum
        )
        if last:
            outs[0][i, :rows] = out.astype(jnp.bfloat16)
            outs[0][i, rows:] = pack_tail(log_sum)
        else:
            half = rows // 2
            bit = lax.rem(lax.axis_index("ctx") >> level, 2) == 1
            send, keep, wide = outs

            def choose(first, value):
                return jnp.where(first, value[:half], value[half:])

            send[i, :half] = choose(bit, out).astype(jnp.bfloat16)
            send[i, half:] = pack_tail(choose(bit, log_sum))
            keep[i] = choose(~bit, out)
            wide[i] = jnp.broadcast_to(choose(~bit, log_sum), (half, LANES))


def merge_parts(keep, sums, got, level, last, after):
    count, rows, size = keep.shape
    part = rows if last else rows // 2
    shapes = [jax.ShapeDtypeStruct((count, part + tail_rows(part), size), jnp.bfloat16)]
    if not last:
        shapes.append(jax.ShapeDtypeStruct((count, part, size), jnp.float32))
        shapes.append(jax.ShapeDtypeStruct((count, part, LANES), jnp.float32))
    return pl.pallas_call(
        functools.partial(merge_kernel, level, last),
        in_specs=in_vmem(3),
        out_shape=tuple(shapes),
        compiler_params=pltpu.CompilerParams(vmem_limit_bytes=16 << 20),
        cost_estimate=SMALL,
    )(keep, sums, got, after)


def finish_kernel(mine_ref, got_ref, _, out_ref):
    rows = math.prod(out_ref.shape[1:-1])
    for i in range(mine_ref.shape[0]):
        out, _ = merge(
            mine_ref[i, :rows].astype(jnp.float32),
            unpack_tail(mine_ref[i, rows:], rows),
            got_ref[i, :rows].astype(jnp.float32),
            unpack_tail(got_ref[i, rows:], rows),
        )
        out_ref[i] = out.astype(jnp.bfloat16).reshape(out_ref.shape[1:])


def finish(mine, got, shape, after):
    return pl.pallas_call(
        finish_kernel,
        in_specs=in_vmem(2),
        out_shape=jax.ShapeDtypeStruct(shape, jnp.bfloat16),
        compiler_params=pltpu.CompilerParams(vmem_limit_bytes=16 << 20),
        cost_estimate=SMALL,
    )(mine, got, after)


def place_kernel(levels, plan, *refs):
    *part_refs, out_ref, sems = refs
    copies = []
    for (head, own), ref in zip(plan, part_refs):
        blocks = ref.shape[1]
        bit = lax.rem(lax.axis_index("ctx"), 2) if levels > 1 else 0
        at = (bit if own else 1 - bit) * blocks
        for i in range(ref.shape[0]):
            there = out_ref.at[pl.ds(at, blocks), :, head + i]
            copies.append(pltpu.make_async_copy(ref.at[i], there, sems.at[len(copies)]))
    for copy in copies:
        copy.start()
    for copy in copies:
        copy.wait()


def place(parts, shape, levels):
    arrays = [array for array, _, _ in parts]
    plan = [(head, own) for _, head, own in parts]
    return pl.pallas_call(
        functools.partial(place_kernel, levels, plan),
        in_specs=[pl.BlockSpec(memory_space=pltpu.VMEM)] * len(arrays),
        out_specs=pl.BlockSpec(memory_space=pltpu.HBM),
        out_shape=jax.ShapeDtypeStruct(shape, jnp.bfloat16),
        scratch_shapes=[pltpu.SemaphoreType.DMA((sum(a.shape[0] for a in arrays),))],
        compiler_params=pltpu.CompilerParams(vmem_limit_bytes=16 << 20),
        cost_estimate=SMALL,
    )(*arrays)


def on_device(shards, owners, queries, prompt_cache, suffix_cache, new_kv, ancestors, lengths):
    steps, per_owner, heads, group, size = queries.shape
    suffix_dev = suffix_cache.shape[2]
    shard = lax.axis_index("ctx")
    factor = math.log2(math.e) / math.sqrt(size)
    tokens_dev = -(-steps // shards)
    levels = shards.bit_length() - 1
    halves = 2 if levels > 1 else 1

    def swap(value, bit):
        return lax.ppermute(value, "ctx", [(i, i ^ (1 << bit)) for i in range(shards)])

    prompt_rows = prompt_cache.reshape(2, -1, size)
    mine, bias, keys = build_message(
        suffix_cache.reshape(2, -1, size),
        new_kv.reshape(steps, 2, -1, size),
        prompt_rows,
        ancestors,
        lengths,
        heads,
        owners,
        suffix_dev,
        tokens_dev,
    )
    row_list = [mine] + [
        lax.ppermute(mine, "dom", [(i, (i + hop) % owners) for i in range(owners)])
        for hop in range(1, owners)
    ]
    prompt = split_prompt(prompt_rows, keys, heads)
    last = [bias]

    def follow(results):
        last[0] = results[0] if isinstance(results, (tuple, list)) else results
        return results

    begun = follow(start_head(queries, prompt, 0, factor))
    first = max(heads // 2, 1)
    chunks = [(0, first)] + [(head, 1) for head in range(first, heads)]
    messages, kept, parts = {}, {}, []

    def run_attend(chunk):
        head, count = chunk
        send, keep, sums = follow(
            attend(
                queries, prompt, bias, row_list, head, count, factor, halves,
                begun if head == 0 else (), last[0],
            )
        )
        kept[chunk] = keep, sums
        messages[chunk] = send, swap(send, 0)

    def run_merges(chunk):
        for level in range(1, levels):
            results = follow(
                merge_parts(
                    *kept[chunk], messages[chunk][1], level, level == levels - 1, last[0]
                )
            )
            send, kept[chunk] = results[0], results[1:]
            messages[chunk] = send, swap(send, level)

    def run_finish(chunk):
        head, count = chunk
        blocks = (steps * per_owner) >> (levels - 1 if levels > 1 else 0)
        done = follow(finish(*messages[chunk], (count, blocks, group, size), last[0]))
        for level in range(levels - 2, 0, -1):
            other = swap(done, level)
            done = jnp.where(
                (shard >> level) % 2 == 1,
                jnp.concatenate([other, done], axis=1),
                jnp.concatenate([done, other], axis=1),
            )
        done = done.reshape(count, steps // halves, per_owner, group, size)
        parts.append((done, head, True))
        if levels > 1:
            parts.append((swap(done, 0), head, False))

    run_attend(chunks[0])
    for before, chunk in zip(chunks, chunks[1:]):
        run_attend(chunk)
        run_merges(before)
    run_merges(chunks[-1])
    for chunk in chunks[:-1]:
        run_finish(chunk)
    run_finish(chunks[-1])
    return place(parts, queries.shape, levels)


def solution(mesh):
    return jax.shard_map(
        functools.partial(on_device, mesh.shape["ctx"], mesh.shape["dom"]),
        mesh=mesh,
        in_specs=(
            P("groups", "dom", "tp", None, None),
            P("groups", "ctx", "tp", None),
            P("groups", "dom", "ctx", "tp", None),
            P("groups", None, "dom", "tp", None),
            P("groups", None),
            P("groups"),
        ),
        out_specs=P("groups", "dom", "tp", None, None),
        check_vma=False,
    )
```

```python
import functools
import math

import jax
import jax.numpy as jnp
from jax import lax
from jax.experimental import pallas as pl
from jax.experimental.pallas import tpu as pltpu
from jax.sharding import PartitionSpec as P

LANES = 128
HIDDEN = -1e30
NN = (((1,), (0,)), ((), ()))
NT = (((1,), (1,)), ((), ()))
SMALL = pl.CostEstimate(flops=0, bytes_accessed=4096, transcendentals=0)


def round_up(value, multiple):
    return -(-value // multiple) * multiple


def dot(a, b, dims):
    return lax.dot_general(a, b, dims, preferred_element_type=jnp.float32)


def eye_mask(rows):
    shape = (rows, LANES)
    return lax.broadcasted_iota(jnp.int32, shape, 0) == lax.broadcasted_iota(jnp.int32, shape, 1)


def column_to_lanes(column):
    rows = column.shape[0]
    block = min(rows, LANES)
    mask = eye_mask(block)
    return jnp.concatenate(
        [
            jnp.sum(jnp.where(mask, column[at : at + block], 0.0), axis=0, keepdims=True)
            for at in range(0, rows, block)
        ],
        axis=0,
    )


def lanes_to_column(lanes, rows):
    block = min(rows, LANES)
    mask = eye_mask(block)
    return jnp.concatenate(
        [
            jnp.sum(jnp.where(mask, lanes[i : i + 1], 0.0), axis=1, keepdims=True)
            for i in range(lanes.shape[0])
        ],
        axis=0,
    )


def tail_rows(rows):
    return round_up(3 * -(-rows // LANES), 16)


def pack_tail(column):
    lanes = column_to_lanes(column)
    high = lanes.astype(jnp.bfloat16).astype(jnp.float32)
    middle = (lanes - high).astype(jnp.bfloat16).astype(jnp.float32)
    low = lanes - high - middle
    parts = jnp.concatenate([high, middle, low], axis=0)
    spare = tail_rows(column.shape[0]) - parts.shape[0]
    return jnp.concatenate([parts, jnp.zeros((spare, LANES), jnp.float32)], axis=0).astype(
        jnp.bfloat16
    )


def unpack_tail(tail, rows):
    tail = tail.astype(jnp.float32)
    blocks = -(-rows // LANES)
    lanes = tail[:blocks] + tail[blocks : 2 * blocks] + tail[2 * blocks : 3 * blocks]
    return lanes_to_column(lanes, rows)


def in_hbm(array):
    return pltpu.with_memory_space_constraint(array, pltpu.HBM)


def message_kernel(
    heads, tokens_dev, suffix_ref, new_ref, prompt_ref, ancestors_ref, lengths_ref,
    out_ref, keys_ref, parents_ref, extents_ref, here, wide, sems,
):
    rows, each = suffix_ref.shape[1], new_ref.shape[2]
    total = here.shape[1]
    first = jnp.minimum(lax.axis_index("ctx") * tokens_dev, new_ref.shape[0] - tokens_dev)
    pairs = [(suffix_ref, here.at[:, pl.ds(0, rows)])]
    for token in range(tokens_dev):
        pairs.append((new_ref.at[first + token], here.at[:, pl.ds(rows + token * each, each)]))
    parts = len(pairs)
    pairs += [(ancestors_ref, parents_ref), (lengths_ref, extents_ref)]
    pairs.append((prompt_ref.at[0], keys_ref))
    copies = [pltpu.make_async_copy(*pair, sems.at[i]) for i, pair in enumerate(pairs)]
    for copy in copies:
        copy.start()
    for copy in copies[:parts]:
        copy.wait()
    for kind in range(2):
        wide[kind] = here[kind].astype(jnp.float32)
        for head in range(heads):
            part = wide[kind, pl.ds(head, total // heads, stride=heads), :]
            out_ref[kind, head] = part.astype(out_ref.dtype)
    for copy in copies[parts:]:
        copy.wait()


def build_message(suffix, new, prompt, ancestors, lengths, heads, tokens_dev):
    rows = suffix.shape[1] + tokens_dev * new.shape[2]
    size = suffix.shape[2]
    lengths = lengths.reshape(1, -1)
    operands = (suffix, new, prompt, ancestors, lengths)
    return pl.pallas_call(
        functools.partial(message_kernel, heads, tokens_dev),
        in_specs=[pl.BlockSpec(memory_space=pltpu.HBM)] * len(operands),
        out_shape=(
            jax.ShapeDtypeStruct((2, heads, rows // heads, size), suffix.dtype),
            jax.ShapeDtypeStruct(prompt.shape[1:], prompt.dtype),
            jax.ShapeDtypeStruct(ancestors.shape, ancestors.dtype),
            jax.ShapeDtypeStruct(lengths.shape, lengths.dtype),
        ),
        scratch_shapes=[
            pltpu.VMEM((2, rows, size), suffix.dtype),
            pltpu.VMEM((2, rows, size), jnp.float32),
            pltpu.SemaphoreType.DMA((4 + tokens_dev,)),
        ],
        compiler_params=pltpu.CompilerParams(vmem_limit_bytes=24 << 20),
        cost_estimate=SMALL,
    )(*[in_hbm(operand) for operand in operands])


def iota(shape, axis):
    return lax.broadcasted_iota(jnp.int32, shape, axis)


def lineage_bias(ancestors_ref, lengths_ref, owners, per_owner, suffix_dev, tokens_dev, padded):
    particles = owners * per_owner
    steps = ancestors_ref.shape[0]
    suffix_columns = per_owner * suffix_dev
    each = suffix_columns + per_owner * tokens_dev
    my_owner = lax.axis_index("dom")
    my_shard = lax.axis_index("ctx")
    square = (particles, particles)
    same = iota(square, 0) == iota(square, 1)

    def as_column(row):
        return jnp.sum(jnp.where(same, row, 0), axis=1, keepdims=True)

    unit = same.astype(jnp.float32)
    nothing = jnp.zeros((particles, tokens_dev * particles), jnp.float32)
    state = jnp.concatenate([unit, nothing], axis=1)
    pick = iota((per_owner, particles), 1) == iota((per_owner, particles), 0) + my_owner * per_owner
    pick = pick.astype(jnp.bfloat16)
    mine = []
    for step in range(steps):
        parent = as_column(ancestors_ref[step : step + 1, :])
        move = (parent == iota(square, 1)).astype(jnp.bfloat16)
        state = dot(move, state.astype(jnp.bfloat16), NN)
        blocks = [state[:, :particles]]
        for token in range(tokens_dev):
            written = my_shard * tokens_dev + token
            old = state[:, (1 + token) * particles : (2 + token) * particles]
            blocks.append(jnp.where(written == step, unit, old))
        state = jnp.concatenate(blocks, axis=1)
        mine.append(dot(pick, state.astype(jnp.bfloat16), NN))
    mine = jnp.concatenate(mine, axis=0).astype(jnp.bfloat16)
    lengths = as_column(lengths_ref[...])
    shape = (particles, padded)
    column = iota(shape, 1)
    source = column // each
    owner = lax.rem(my_owner + owners - source, owners)
    inner = column - source * each
    after = inner - suffix_columns
    in_suffix = after < 0
    local = jnp.where(in_suffix, inner // suffix_dev, lax.rem(jnp.maximum(after, 0), per_owner))
    here = (iota(shape, 0) == owner * per_owner + local) & (column < owners * each)
    position = my_shard * suffix_dev + lax.rem(inner, suffix_dev)
    seen = [here & in_suffix & (position < lengths)]
    for token in range(tokens_dev):
        seen.append(here & (after >= token * per_owner) & (after < (token + 1) * per_owner))
    table = jnp.concatenate([s.astype(jnp.bfloat16) for s in seen], axis=0)
    return jnp.where(dot(mine, table, NN) > 0.5, 0.0, HIDDEN)


def split_kernel(
    heads, block, owners, suffix_dev, tokens_dev,
    rows_ref, keys_ref, parents_ref, extents_ref, out_ref, bias_ref, here, wide, sems,
):
    total = out_ref.shape[2]
    places = range(0, total, block)
    copies = [
        pltpu.make_async_copy(
            rows_ref.at[1, pl.ds(at * heads, block * heads)],
            here.at[pl.ds(at * heads, block * heads)],
            sems.at[i],
        )
        for i, at in enumerate(places)
    ]
    for copy in copies:
        copy.start()
    for kind, source in enumerate((keys_ref, here)):
        for i, at in enumerate(places):
            if kind == 1:
                copies[i].wait()
            wide[i % 2] = source[at * heads : (at + block) * heads].astype(jnp.float32)
            for head in range(heads):
                part = wide[i % 2, pl.ds(head, block, stride=heads), :]
                out_ref[kind, head, at : at + block] = part.astype(out_ref.dtype)
        if kind == 0:
            bias_ref[...] = lineage_bias(
                parents_ref, extents_ref, owners, parents_ref.shape[1] // owners,
                suffix_dev, tokens_dev, bias_ref.shape[1],
            )


def split_prompt(rows, keys, parents, extents, heads, owners, suffix_dev, tokens_dev):
    total = rows.shape[1] // heads
    block = math.gcd(total, 512)
    size = rows.shape[2]
    steps, particles = parents.shape
    padded = round_up(particles * (suffix_dev + tokens_dev), LANES)
    return pl.pallas_call(
        functools.partial(split_kernel, heads, block, owners, suffix_dev, tokens_dev),
        in_specs=[pl.BlockSpec(memory_space=pltpu.HBM)]
        + [pl.BlockSpec(memory_space=pltpu.VMEM)] * 3,
        out_shape=(
            jax.ShapeDtypeStruct((2, heads, total, size), rows.dtype),
            jax.ShapeDtypeStruct((steps * particles // owners, padded), jnp.float32),
        ),
        scratch_shapes=[
            pltpu.VMEM(rows.shape[1:], rows.dtype),
            pltpu.VMEM((2, block * heads, size), jnp.float32),
            pltpu.SemaphoreType.DMA((total // block,)),
        ],
        compiler_params=pltpu.CompilerParams(vmem_limit_bytes=24 << 20),
        cost_estimate=SMALL,
    )(in_hbm(rows), keys, parents, extents)


def with_ones(values):
    return jnp.concatenate([values, jnp.ones_like(values)], axis=1)


def row_peak(scores):
    return jnp.max(scores, axis=1, keepdims=True)


def weigh(scores, factor, offset):
    return jnp.exp2(scores * factor - offset).astype(jnp.bfloat16)


def prompt_sum(q, k_ref, v_ref, i, factor, peak):
    total = k_ref.shape[2]
    block = math.gcd(total, 512)
    weights = []
    for at in range(0, total, block):
        scores = dot(q, k_ref[0, i, at : at + block], NT)
        if at == 0:
            top = row_peak(scores)
            offset = (top if peak is None else jnp.maximum(top, peak)) * factor
        weights.append(weigh(scores, factor, offset))
    return dot(jnp.concatenate(weights, axis=1), with_ones(v_ref[0, i]), NN), offset


def prompt_kernel(factor, q_ref, k_ref, v_ref, together_ref, offset_ref):
    steps, per_owner, _, group, size = q_ref.shape
    q = q_ref[...].reshape(steps * per_owner * group, size)
    together, offset = prompt_sum(q, k_ref, v_ref, 0, factor, None)
    together_ref[...] = together
    offset_ref[...] = jnp.broadcast_to(offset, offset_ref.shape)


def block_specs(queries, prompt, head, count):
    steps, per_owner, _, group, size = queries.shape
    total = prompt.shape[2]
    at = head // count
    return [
        pl.BlockSpec((steps, per_owner, count, group, size), lambda i: (0, 0, at, 0, 0)),
        pl.BlockSpec((1, count, total, size), lambda i: (0, at, 0, 0)),
        pl.BlockSpec((1, count, total, size), lambda i: (1, at, 0, 0)),
    ]


def whole(array):
    return pl.BlockSpec(array.shape, lambda i: (0,) * array.ndim)


def start_head(queries, prompt, head, factor):
    steps, per_owner, _, group, size = queries.shape
    rows = steps * per_owner * group
    shapes = (
        jax.ShapeDtypeStruct((rows, 2 * size), jnp.float32),
        jax.ShapeDtypeStruct((rows, LANES), jnp.float32),
    )
    return pl.pallas_call(
        functools.partial(prompt_kernel, factor),
        grid=(1,),
        in_specs=block_specs(queries, prompt, head, 1),
        out_specs=[whole(s) for s in shapes],
        out_shape=shapes,
        compiler_params=pltpu.CompilerParams(vmem_limit_bytes=24 << 20),
        cost_estimate=SMALL,
    )(queries, prompt, prompt)


def attend_kernel(factor, owners, halves, started, *refs):
    q_ref, k_ref, v_ref, bias_ref = refs[:4]
    row_refs = refs[4 : 4 + owners]
    begun = refs[4 + owners : 4 + owners + 2 * started]
    _, send_ref, keep_ref, sums_ref, out, log_sums = refs[4 + owners + 2 * started :]
    steps, per_owner, count, group, size = q_ref.shape
    padded = bias_ref.shape[1]
    rows = steps * per_owner * group
    half = rows // halves

    def queries_of(i, first, number):
        here = number * per_owner * group
        q = q_ref[pl.ds(first, number), :, i].reshape(here, size)
        at = pl.multiple_of(first * per_owner, per_owner)
        bias = bias_ref[pl.ds(at, number * per_owner), :]
        bias = jnp.broadcast_to(bias[:, None, :], (number * per_owner, group, padded))
        return q, dot(q, suffix_of(i, 0), NT) + bias.reshape(here, padded)

    def suffix_of(i, kind):
        pieces = [ref[kind, i] for ref in row_refs]
        columns = sum(piece.shape[0] for piece in pieces)
        if padded > columns:
            pieces.append(jnp.zeros((padded - columns, size), jnp.bfloat16))
        return jnp.concatenate(pieces, axis=0)

    def store(at, together, offset):
        sums = together[:, size:]
        out[pl.ds(at, sums.shape[0]), :] = together[:, :size] / sums
        log_sums[pl.ds(at, sums.shape[0]), :] = offset + jnp.log2(sums)
        return sums

    for i in range(count):
        q, suffix_scores = queries_of(i, 0, steps)
        if i < started:
            together, offset = begun[2 * i][...], begun[2 * i + 1][:, :1]
        else:
            peak = row_peak(suffix_scores)
            together, offset = prompt_sum(q, k_ref, v_ref, i, factor, peak)
        weight = weigh(suffix_scores, factor, offset)
        together = together + dot(weight, with_ones(suffix_of(i, 1)), NN)
        sums = store(0, together, offset)

        @pl.when(jnp.logical_not(jnp.max(sums) < 2.0**100))
        def _():
            @pl.loop(0, steps)
            def _(step):
                q, suffix_scores = queries_of(i, step, 1)
                scores = dot(q, k_ref[0, i], NT)
                offset = jnp.maximum(row_peak(scores), row_peak(suffix_scores)) * factor
                together = dot(weigh(scores, factor, offset), with_ones(v_ref[0, i]), NN)
                weight = weigh(suffix_scores, factor, offset)
                together = together + dot(weight, with_ones(suffix_of(i, 1)), NN)
                store(pl.multiple_of(step * per_owner * group, per_owner * group), together, offset)

        bit = lax.rem(lax.axis_index("ctx"), 2) if halves == 2 else 0
        there = pl.ds(pl.multiple_of((halves - 1 - bit) * half, half), half)
        send_ref[i, :half] = out[there, :].astype(jnp.bfloat16)
        send_ref[i, half:] = pack_tail(log_sums[there, :][:, :1])
        here = pl.ds(pl.multiple_of(bit * half, half), half)
        keep_ref[i] = out[here, :]
        sums_ref[i] = log_sums[here, :]


def attend(queries, prompt, bias, row_list, head, count, factor, halves, begun, after):
    steps, per_owner, heads, group, size = queries.shape
    rows = steps * per_owner * group
    half = rows // halves
    shapes = (
        jax.ShapeDtypeStruct((count, half + tail_rows(half), size), jnp.bfloat16),
        jax.ShapeDtypeStruct((count, half, size), jnp.float32),
        jax.ShapeDtypeStruct((count, half, LANES), jnp.float32),
    )
    slots = row_list[0].shape[2]
    row_spec = pl.BlockSpec((2, count, slots, size), lambda i: (0, head // count, 0, 0))
    return pl.pallas_call(
        functools.partial(attend_kernel, factor, len(row_list), halves, len(begun) // 2),
        grid=(1,),
        in_specs=[
            *block_specs(queries, prompt, head, count),
            whole(bias),
            *[row_spec] * len(row_list),
            *[whole(b) for b in begun],
            pl.BlockSpec(memory_space=pl.ANY),
        ],
        out_specs=[whole(s) for s in shapes],
        out_shape=shapes,
        scratch_shapes=[
            pltpu.VMEM((rows, size), jnp.float32),
            pltpu.VMEM((rows, LANES), jnp.float32),
        ],
        compiler_params=pltpu.CompilerParams(vmem_limit_bytes=32 << 20),
        cost_estimate=SMALL,
    )(queries, prompt, prompt, bias, *row_list, *begun, after)


def merge(out_a, sum_a, out_b, sum_b):
    top = jnp.maximum(sum_a, sum_b)
    weight_a = jnp.exp2(sum_a - top)
    weight_b = jnp.exp2(sum_b - top)
    total = weight_a + weight_b
    return (out_a * weight_a + out_b * weight_b) / total, top + jnp.log2(total)


def in_vmem(count):
    return [pl.BlockSpec(memory_space=pltpu.VMEM)] * count + [pl.BlockSpec(memory_space=pl.ANY)]


def merge_kernel(level, pieces, keep_ref, sums_ref, got_ref, _, *outs):
    rows = keep_ref.shape[1]
    half = rows // 2
    places = [(out, i) for out, count in zip(outs, pieces) for i in range(count)]
    for i in range(keep_ref.shape[0]):
        got_sum = unpack_tail(got_ref[i, rows:], rows)
        out, log_sum = merge(
            keep_ref[i], sums_ref[i][:, :1], got_ref[i, :rows].astype(jnp.float32), got_sum
        )
        if pieces:
            there, at = places[i]
            there[at, :rows] = out.astype(jnp.bfloat16)
            there[at, rows:] = pack_tail(log_sum)
        else:
            bit = lax.rem(lax.axis_index("ctx") >> level, 2) == 1
            send, keep, wide = outs

            def choose(first, value):
                return jnp.where(first, value[:half], value[half:])

            send[i, :half] = choose(bit, out).astype(jnp.bfloat16)
            send[i, half:] = pack_tail(choose(bit, log_sum))
            keep[i] = choose(~bit, out)
            wide[i] = jnp.broadcast_to(choose(~bit, log_sum), (half, LANES))


def merge_parts(keep, sums, got, level, pieces, after):
    count, rows, size = keep.shape
    part = rows if pieces else rows // 2
    message = part + tail_rows(part)
    shapes = [jax.ShapeDtypeStruct((n, message, size), jnp.bfloat16) for n in pieces or (count,)]
    if not pieces:
        shapes.append(jax.ShapeDtypeStruct((count, part, size), jnp.float32))
        shapes.append(jax.ShapeDtypeStruct((count, part, LANES), jnp.float32))
    return pl.pallas_call(
        functools.partial(merge_kernel, level, pieces),
        in_specs=in_vmem(3),
        out_shape=tuple(shapes),
        compiler_params=pltpu.CompilerParams(vmem_limit_bytes=16 << 20),
        cost_estimate=SMALL,
    )(keep, sums, got, after)


def finish_kernel(mine_ref, got_ref, _, out_ref):
    rows = math.prod(out_ref.shape[1:-1])
    for i in range(mine_ref.shape[0]):
        out, _ = merge(
            mine_ref[i, :rows].astype(jnp.float32),
            unpack_tail(mine_ref[i, rows:], rows),
            got_ref[i, :rows].astype(jnp.float32),
            unpack_tail(got_ref[i, rows:], rows),
        )
        out_ref[i] = out.astype(jnp.bfloat16).reshape(out_ref.shape[1:])


def finish(mine, got, shape, after):
    return pl.pallas_call(
        finish_kernel,
        in_specs=in_vmem(2),
        out_shape=jax.ShapeDtypeStruct(shape, jnp.bfloat16),
        compiler_params=pltpu.CompilerParams(vmem_limit_bytes=16 << 20),
        cost_estimate=SMALL,
    )(mine, got, after)


def place_kernel(levels, plan, *refs):
    part_refs = refs[: len(plan)]
    out_ref, sems = refs[-2:]
    copies = []
    for (head, own), ref in zip(plan, part_refs):
        blocks = ref.shape[1]
        bit = lax.rem(lax.axis_index("ctx"), 2) if levels > 1 else 0
        at = (bit if own else 1 - bit) * blocks
        for i in range(ref.shape[0]):
            there = out_ref.at[pl.ds(at, blocks), :, head + i]
            copies.append(pltpu.make_async_copy(ref.at[i], there, sems.at[len(copies)]))
    for copy in copies:
        copy.start()
    for copy in copies:
        copy.wait()


def place(out, parts, shape, levels, after):
    arrays = [array for array, _, _ in parts]
    plan = [(head, own) for _, head, own in parts]
    others = [after] if out is None else [after, out]
    return pl.pallas_call(
        functools.partial(place_kernel, levels, plan),
        in_specs=[pl.BlockSpec(memory_space=pltpu.VMEM)] * len(arrays)
        + [pl.BlockSpec(memory_space=pl.ANY), pl.BlockSpec(memory_space=pltpu.HBM)][: len(others)],
        out_specs=pl.BlockSpec(memory_space=pltpu.HBM),
        out_shape=pltpu.HBM(shape, jnp.bfloat16),
        input_output_aliases={} if out is None else {len(arrays) + 1: 0},
        scratch_shapes=[pltpu.SemaphoreType.DMA((sum(a.shape[0] for a in arrays),))],
        compiler_params=pltpu.CompilerParams(vmem_limit_bytes=16 << 20),
        cost_estimate=SMALL,
    )(*arrays, *others)


def on_device(shards, owners, queries, prompt_cache, suffix_cache, new_kv, ancestors, lengths):
    steps, per_owner, heads, group, size = queries.shape
    suffix_dev = suffix_cache.shape[2]
    shard = lax.axis_index("ctx")
    factor = math.log2(math.e) / math.sqrt(size)
    tokens_dev = -(-steps // shards)
    levels = shards.bit_length() - 1
    halves = 2 if levels > 1 else 1

    def swap(value, bit):
        return lax.ppermute(value, "ctx", [(i, i ^ (1 << bit)) for i in range(shards)])

    prompt_rows = prompt_cache.reshape(2, -1, size)
    mine, keys, parents, extents = build_message(
        suffix_cache.reshape(2, -1, size),
        new_kv.reshape(steps, 2, -1, size),
        prompt_rows,
        ancestors,
        lengths,
        heads,
        tokens_dev,
    )
    row_list = [mine] + [
        lax.ppermute(mine, "dom", [(i, (i + hop) % owners) for i in range(owners)])
        for hop in range(1, owners)
    ]
    prompt, bias = split_prompt(
        prompt_rows, keys, parents, extents, heads, owners, suffix_dev, tokens_dev
    )
    last = [bias]

    def follow(results):
        last[0] = results[0] if isinstance(results, (tuple, list)) else results
        return results

    begun = follow(start_head(queries, prompt, 0, factor))
    first = max(heads // 2, 1)
    groups = [(head, min(first, heads - head)) for head in range(0, heads, first)]
    begun_of = {0: begun}
    messages, kept, parts = {}, {}, []

    def run_attend(group):
        head, count = group
        send, keep, sums = follow(
            attend(
                queries, prompt, bias, row_list, head, count, factor, halves,
                begun_of.get(head, ()), last[0],
            )
        )
        kept[group] = keep, sums
        messages[group] = send, swap(send, 0)

    def run_merges(group, sizes):
        head, _ = group
        pieces = [(head + sum(sizes[:i]), size) for i, size in enumerate(sizes)]
        if levels <= 1:
            done, got = messages[group]
            starts = [at - head for at, _ in pieces]
            for piece, at in zip(pieces, starts):
                cut = slice(at, at + piece[1])
                messages[piece] = done[cut], got[cut]
        for level in range(1, levels):
            final = level == levels - 1
            results = follow(
                merge_parts(
                    *kept[group], messages[group][1], level, sizes if final else (), last[0]
                )
            )
            if final:
                for piece, send in zip(pieces, results):
                    messages[piece] = send, swap(send, level)
            else:
                kept[group] = results[1:]
                messages[group] = results[0], swap(results[0], level)
        return pieces

    def run_finish(piece):
        head, count = piece
        blocks = (steps * per_owner) >> (levels - 1 if levels > 1 else 0)
        done = follow(finish(*messages[piece], (count, blocks, group, size), last[0]))
        for level in range(levels - 2, 0, -1):
            other = swap(done, level)
            done = jnp.where(
                (shard >> level) % 2 == 1,
                jnp.concatenate([other, done], axis=1),
                jnp.concatenate([done, other], axis=1),
            )
        done = done.reshape(count, steps // halves, per_owner, group, size)
        mine = (done, head, True)
        return [mine, (swap(done, 0), head, False)] if levels > 1 else [mine]

    for one in groups:
        run_attend(one)
    pieces = run_merges(groups[0], (groups[0][1],))
    for one in groups[1:]:
        pieces += run_merges(one, (1,) * one[1])
    parts = [part for piece in pieces for part in run_finish(piece)]
    early, late = parts[:-1], parts[-1:]
    out = place(None, early, queries.shape, levels, last[0]) if early else None
    return place(out, late, queries.shape, levels, last[0])


def solution(mesh):
    return jax.shard_map(
        functools.partial(on_device, mesh.shape["ctx"], mesh.shape["dom"]),
        mesh=mesh,
        in_specs=(
            P("groups", "dom", "tp", None, None),
            P("groups", "ctx", "tp", None),
            P("groups", "dom", "ctx", "tp", None),
            P("groups", None, "dom", "tp", None),
            P("groups", None),
            P("groups"),
        ),
        out_specs=P("groups", "dom", "tp", None, None),
        check_vma=False,
    )
```

```python
import functools
import math

import jax
import jax.numpy as jnp
from jax import lax
from jax.experimental import pallas as pl
from jax.experimental.pallas import tpu as pltpu
from jax.sharding import PartitionSpec as P

LANES = 128
HIDDEN = -1e30
NN = (((1,), (0,)), ((), ()))
NT = (((1,), (1,)), ((), ()))
SMALL = pl.CostEstimate(flops=0, bytes_accessed=4096, transcendentals=0)


def round_up(value, multiple):
    return -(-value // multiple) * multiple


def dot(a, b, dims):
    return lax.dot_general(a, b, dims, preferred_element_type=jnp.float32)


def eye_mask(rows):
    shape = (rows, LANES)
    return lax.broadcasted_iota(jnp.int32, shape, 0) == lax.broadcasted_iota(jnp.int32, shape, 1)


def column_to_lanes(column):
    rows = column.shape[0]
    block = min(rows, LANES)
    mask = eye_mask(block)
    return jnp.concatenate(
        [
            jnp.sum(jnp.where(mask, column[at : at + block], 0.0), axis=0, keepdims=True)
            for at in range(0, rows, block)
        ],
        axis=0,
    )


def lanes_to_column(lanes, rows):
    block = min(rows, LANES)
    mask = eye_mask(block)
    return jnp.concatenate(
        [
            jnp.sum(jnp.where(mask, lanes[i : i + 1], 0.0), axis=1, keepdims=True)
            for i in range(lanes.shape[0])
        ],
        axis=0,
    )


def tail_rows(rows):
    return round_up(3 * -(-rows // LANES), 16)


def pack_tail(column):
    lanes = column_to_lanes(column)
    high = lanes.astype(jnp.bfloat16).astype(jnp.float32)
    middle = (lanes - high).astype(jnp.bfloat16).astype(jnp.float32)
    low = lanes - high - middle
    parts = jnp.concatenate([high, middle, low], axis=0)
    spare = tail_rows(column.shape[0]) - parts.shape[0]
    return jnp.concatenate([parts, jnp.zeros((spare, LANES), jnp.float32)], axis=0).astype(
        jnp.bfloat16
    )


def unpack_tail(tail, rows):
    tail = tail.astype(jnp.float32)
    blocks = -(-rows // LANES)
    lanes = tail[:blocks] + tail[blocks : 2 * blocks] + tail[2 * blocks : 3 * blocks]
    return lanes_to_column(lanes, rows)


def in_hbm(array):
    return pltpu.with_memory_space_constraint(array, pltpu.HBM)


def message_kernel(
    heads, tokens_dev, suffix_ref, new_ref, prompt_ref, ancestors_ref, lengths_ref,
    out_ref, keys_ref, parents_ref, extents_ref, here, wide, sems,
):
    rows, each = suffix_ref.shape[1], new_ref.shape[2]
    total = here.shape[1]
    first = jnp.minimum(lax.axis_index("ctx") * tokens_dev, new_ref.shape[0] - tokens_dev)
    pairs = [(suffix_ref, here.at[:, pl.ds(0, rows)])]
    for token in range(tokens_dev):
        pairs.append((new_ref.at[first + token], here.at[:, pl.ds(rows + token * each, each)]))
    parts = len(pairs)
    pairs += [(ancestors_ref, parents_ref), (lengths_ref, extents_ref)]
    piece = math.gcd(keys_ref.shape[0], 2048)
    for at in range(0, keys_ref.shape[0], piece):
        pairs.append((prompt_ref.at[0, pl.ds(at, piece)], keys_ref.at[pl.ds(at, piece)]))
    copies = [pltpu.make_async_copy(*pair, sems.at[i]) for i, pair in enumerate(pairs)]
    for copy in copies:
        copy.start()
    for copy in copies[:parts]:
        copy.wait()
    for kind in range(2):
        wide[kind] = here[kind].astype(jnp.float32)
        for head in range(heads):
            part = wide[kind, pl.ds(head, total // heads, stride=heads), :]
            out_ref[kind, head] = part.astype(out_ref.dtype)
    for copy in copies[parts:]:
        copy.wait()


def build_message(suffix, new, prompt, ancestors, lengths, heads, tokens_dev):
    rows = suffix.shape[1] + tokens_dev * new.shape[2]
    size = suffix.shape[2]
    lengths = lengths.reshape(1, -1)
    operands = (suffix, new, prompt, ancestors, lengths)
    return pl.pallas_call(
        functools.partial(message_kernel, heads, tokens_dev),
        in_specs=[pl.BlockSpec(memory_space=pltpu.HBM)] * len(operands),
        out_shape=(
            jax.ShapeDtypeStruct((2, heads, rows // heads, size), suffix.dtype),
            jax.ShapeDtypeStruct(prompt.shape[1:], prompt.dtype),
            jax.ShapeDtypeStruct(ancestors.shape, ancestors.dtype),
            jax.ShapeDtypeStruct(lengths.shape, lengths.dtype),
        ),
        scratch_shapes=[
            pltpu.VMEM((2, rows, size), suffix.dtype),
            pltpu.VMEM((2, rows, size), jnp.float32),
            pltpu.SemaphoreType.DMA((3 + tokens_dev + prompt.shape[1] // math.gcd(prompt.shape[1], 2048),)),
        ],
        compiler_params=pltpu.CompilerParams(vmem_limit_bytes=24 << 20),
        cost_estimate=SMALL,
    )(*[in_hbm(operand) for operand in operands])


def iota(shape, axis):
    return lax.broadcasted_iota(jnp.int32, shape, axis)


def lineage_bias(ancestors_ref, lengths_ref, owners, per_owner, suffix_dev, tokens_dev, padded):
    particles = owners * per_owner
    steps = ancestors_ref.shape[0]
    suffix_columns = per_owner * suffix_dev
    each = suffix_columns + per_owner * tokens_dev
    my_owner = lax.axis_index("dom")
    my_shard = lax.axis_index("ctx")
    square = (particles, particles)
    same = iota(square, 0) == iota(square, 1)

    def as_column(row):
        return jnp.sum(jnp.where(same, row, 0), axis=1, keepdims=True)

    unit = same.astype(jnp.float32)
    nothing = jnp.zeros((particles, tokens_dev * particles), jnp.float32)
    state = jnp.concatenate([unit, nothing], axis=1)
    pick = iota((per_owner, particles), 1) == iota((per_owner, particles), 0) + my_owner * per_owner
    pick = pick.astype(jnp.bfloat16)
    mine = []
    for step in range(steps):
        parent = as_column(ancestors_ref[step : step + 1, :])
        move = (parent == iota(square, 1)).astype(jnp.bfloat16)
        state = dot(move, state.astype(jnp.bfloat16), NN)
        blocks = [state[:, :particles]]
        for token in range(tokens_dev):
            written = my_shard * tokens_dev + token
            old = state[:, (1 + token) * particles : (2 + token) * particles]
            blocks.append(jnp.where(written == step, unit, old))
        state = jnp.concatenate(blocks, axis=1)
        mine.append(dot(pick, state.astype(jnp.bfloat16), NN))
    mine = jnp.concatenate(mine, axis=0).astype(jnp.bfloat16)
    lengths = as_column(lengths_ref[...])
    shape = (particles, padded)
    column = iota(shape, 1)
    source = column // each
    owner = lax.rem(my_owner + owners - source, owners)
    inner = column - source * each
    after = inner - suffix_columns
    in_suffix = after < 0
    local = jnp.where(in_suffix, inner // suffix_dev, lax.rem(jnp.maximum(after, 0), per_owner))
    here = (iota(shape, 0) == owner * per_owner + local) & (column < owners * each)
    position = my_shard * suffix_dev + lax.rem(inner, suffix_dev)
    seen = [here & in_suffix & (position < lengths)]
    for token in range(tokens_dev):
        seen.append(here & (after >= token * per_owner) & (after < (token + 1) * per_owner))
    table = jnp.concatenate([s.astype(jnp.bfloat16) for s in seen], axis=0)
    return jnp.where(dot(mine, table, NN) > 0.5, 0.0, HIDDEN)


def split_kernel(
    heads, block, owners, suffix_dev, tokens_dev,
    rows_ref, keys_ref, parents_ref, extents_ref, out_ref, bias_ref, here, wide, sems,
):
    total = out_ref.shape[2]
    places = range(0, total, block)
    copies = [
        pltpu.make_async_copy(
            rows_ref.at[1, pl.ds(at * heads, block * heads)],
            here.at[pl.ds(at * heads, block * heads)],
            sems.at[i],
        )
        for i, at in enumerate(places)
    ]
    for copy in copies:
        copy.start()
    for kind, source in enumerate((keys_ref, here)):
        for i, at in enumerate(places):
            if kind == 1:
                copies[i].wait()
            wide[i % 2] = source[at * heads : (at + block) * heads].astype(jnp.float32)
            for head in range(heads):
                part = wide[i % 2, pl.ds(head, block, stride=heads), :]
                out_ref[kind, head, at : at + block] = part.astype(out_ref.dtype)
        if kind == 0:
            bias_ref[...] = lineage_bias(
                parents_ref, extents_ref, owners, parents_ref.shape[1] // owners,
                suffix_dev, tokens_dev, bias_ref.shape[1],
            )


def split_prompt(rows, keys, parents, extents, heads, owners, suffix_dev, tokens_dev):
    total = rows.shape[1] // heads
    block = math.gcd(total, 512)
    size = rows.shape[2]
    steps, particles = parents.shape
    padded = round_up(particles * (suffix_dev + tokens_dev), LANES)
    return pl.pallas_call(
        functools.partial(split_kernel, heads, block, owners, suffix_dev, tokens_dev),
        in_specs=[pl.BlockSpec(memory_space=pltpu.HBM)]
        + [pl.BlockSpec(memory_space=pltpu.VMEM)] * 3,
        out_shape=(
            jax.ShapeDtypeStruct((2, heads, total, size), rows.dtype),
            jax.ShapeDtypeStruct((steps * particles // owners, padded), jnp.float32),
        ),
        scratch_shapes=[
            pltpu.VMEM(rows.shape[1:], rows.dtype),
            pltpu.VMEM((2, block * heads, size), jnp.float32),
            pltpu.SemaphoreType.DMA((total // block,)),
        ],
        compiler_params=pltpu.CompilerParams(vmem_limit_bytes=24 << 20),
        cost_estimate=SMALL,
    )(in_hbm(rows), keys, parents, extents)


def with_ones(values):
    return jnp.concatenate([values, jnp.ones_like(values)], axis=1)


def row_peak(scores):
    return jnp.max(scores, axis=1, keepdims=True)


def weigh(scores, factor, offset):
    return jnp.exp2(scores * factor - offset).astype(jnp.bfloat16)


def work_space(rows, total, size):
    half, block = rows // 2, math.gcd(total, 512)
    return [
        pltpu.VMEM((3, half, block), jnp.float32),
        pltpu.VMEM((2, 2, half, math.gcd(total, 2 * block)), jnp.bfloat16),
        pltpu.VMEM((rows, 2 * size), jnp.float32),
    ]


def prompt_sum(q, k_ref, v_ref, i, factor, peak, scores, weights, sums):
    rows, total = q.shape[0], k_ref.shape[2]
    half, block, wide = rows // 2, scores.shape[2], weights.shape[3]
    units = [(at, which) for at in range(0, total, block) for which in range(2)]
    q_of = [q[:half], q[half:]]
    offset_of = [None, None]

    def score(n):
        at, which = units[n]
        scores[n % 3] = dot(q_of[which], k_ref[0, i, at : at + block], NT)

    def weight(n):
        at, which = units[n]
        there = slice(at % wide, at % wide + block)
        weights[which, at // wide % 2, :, there] = weigh(scores[n % 3], factor, offset_of[which])

    def gather(n):
        at, which = units[n]
        end = at + block
        if end % wide:
            return
        values = with_ones(v_ref[0, i, end - wide : end])
        part = dot(weights[which, at // wide % 2], values, NN)
        here = slice(which * half, (which + 1) * half)
        sums[here] = part if end == wide else sums[here] + part

    score(0)
    score(1)
    for which in range(2):
        top = row_peak(scores[which])
        if peak is not None:
            top = jnp.maximum(top, peak[which * half : (which + 1) * half])
        offset_of[which] = top * factor
    for n in range(len(units)):
        if n + 2 < len(units):
            score(n + 2)
        weight(n)
        if n:
            gather(n - 1)
    gather(len(units) - 1)
    return jnp.concatenate(offset_of, axis=0)


def prompt_kernel(factor, q_ref, k_ref, v_ref, together_ref, offset_ref, scores, weights):
    steps, per_owner, _, group, size = q_ref.shape
    q = q_ref[...].reshape(steps * per_owner * group, size)
    offset = prompt_sum(q, k_ref, v_ref, 0, factor, None, scores, weights, together_ref)
    offset_ref[...] = jnp.broadcast_to(offset, offset_ref.shape)


def block_specs(queries, prompt, head, count):
    steps, per_owner, _, group, size = queries.shape
    total = prompt.shape[2]
    at = head // count
    return [
        pl.BlockSpec((steps, per_owner, count, group, size), lambda i: (0, 0, at, 0, 0)),
        pl.BlockSpec((1, count, total, size), lambda i: (0, at, 0, 0)),
        pl.BlockSpec((1, count, total, size), lambda i: (1, at, 0, 0)),
    ]


def whole(array):
    return pl.BlockSpec(array.shape, lambda i: (0,) * array.ndim)


def start_head(queries, prompt, head, factor):
    steps, per_owner, _, group, size = queries.shape
    rows = steps * per_owner * group
    shapes = (
        jax.ShapeDtypeStruct((rows, 2 * size), jnp.float32),
        jax.ShapeDtypeStruct((rows, LANES), jnp.float32),
    )
    return pl.pallas_call(
        functools.partial(prompt_kernel, factor),
        grid=(1,),
        in_specs=block_specs(queries, prompt, head, 1),
        out_specs=[whole(s) for s in shapes],
        out_shape=shapes,
        scratch_shapes=work_space(rows, prompt.shape[2], size)[:2],
        compiler_params=pltpu.CompilerParams(vmem_limit_bytes=24 << 20),
        cost_estimate=SMALL,
    )(queries, prompt, prompt)


def attend_kernel(factor, owners, halves, started, *refs):
    q_ref, k_ref, v_ref, bias_ref = refs[:4]
    row_refs = refs[4 : 4 + owners]
    begun = refs[4 + owners : 4 + owners + 2 * started]
    _, send_ref, keep_ref, sums_ref, out, log_sums, *work = refs[4 + owners + 2 * started :]
    steps, per_owner, count, group, size = q_ref.shape
    padded = bias_ref.shape[1]
    rows = steps * per_owner * group
    half = rows // halves

    def queries_of(i, first, number):
        here = number * per_owner * group
        q = q_ref[pl.ds(first, number), :, i].reshape(here, size)
        at = pl.multiple_of(first * per_owner, per_owner)
        bias = bias_ref[pl.ds(at, number * per_owner), :]
        bias = jnp.broadcast_to(bias[:, None, :], (number * per_owner, group, padded))
        return q, dot(q, suffix_of(i, 0), NT) + bias.reshape(here, padded)

    def suffix_of(i, kind):
        pieces = [ref[kind, i] for ref in row_refs]
        columns = sum(piece.shape[0] for piece in pieces)
        if padded > columns:
            pieces.append(jnp.zeros((padded - columns, size), jnp.bfloat16))
        return jnp.concatenate(pieces, axis=0)

    def store(at, together, offset):
        sums = together[:, size:]
        out[pl.ds(at, sums.shape[0]), :] = together[:, :size] / sums
        log_sums[pl.ds(at, sums.shape[0]), :] = offset + jnp.log2(sums)
        return sums

    for i in range(count):
        q, suffix_scores = queries_of(i, 0, steps)
        if i < started:
            together, offset = begun[2 * i][...], begun[2 * i + 1][:, :1]
        else:
            peak = row_peak(suffix_scores)
            offset = prompt_sum(q, k_ref, v_ref, i, factor, peak, *work)
            together = work[-1][...]
        weight = weigh(suffix_scores, factor, offset)
        together = together + dot(weight, with_ones(suffix_of(i, 1)), NN)
        sums = store(0, together, offset)

        @pl.when(jnp.logical_not(jnp.max(sums) < 2.0**100))
        def _():
            @pl.loop(0, steps)
            def _(step):
                q, suffix_scores = queries_of(i, step, 1)
                scores = dot(q, k_ref[0, i], NT)
                offset = jnp.maximum(row_peak(scores), row_peak(suffix_scores)) * factor
                together = dot(weigh(scores, factor, offset), with_ones(v_ref[0, i]), NN)
                weight = weigh(suffix_scores, factor, offset)
                together = together + dot(weight, with_ones(suffix_of(i, 1)), NN)
                store(pl.multiple_of(step * per_owner * group, per_owner * group), together, offset)

        bit = lax.rem(lax.axis_index("ctx"), 2) if halves == 2 else 0
        there = pl.ds(pl.multiple_of((halves - 1 - bit) * half, half), half)
        send_ref[i, :half] = out[there, :].astype(jnp.bfloat16)
        send_ref[i, half:] = pack_tail(log_sums[there, :][:, :1])
        here = pl.ds(pl.multiple_of(bit * half, half), half)
        keep_ref[i] = out[here, :]
        sums_ref[i] = log_sums[here, :]


def attend(queries, prompt, bias, row_list, head, count, factor, halves, begun, after):
    steps, per_owner, heads, group, size = queries.shape
    rows = steps * per_owner * group
    half = rows // halves
    shapes = (
        jax.ShapeDtypeStruct((count, half + tail_rows(half), size), jnp.bfloat16),
        jax.ShapeDtypeStruct((count, half, size), jnp.float32),
        jax.ShapeDtypeStruct((count, half, LANES), jnp.float32),
    )
    slots = row_list[0].shape[2]
    row_spec = pl.BlockSpec((2, count, slots, size), lambda i: (0, head // count, 0, 0))
    return pl.pallas_call(
        functools.partial(attend_kernel, factor, len(row_list), halves, len(begun) // 2),
        grid=(1,),
        in_specs=[
            *block_specs(queries, prompt, head, count),
            whole(bias),
            *[row_spec] * len(row_list),
            *[whole(b) for b in begun],
            pl.BlockSpec(memory_space=pl.ANY),
        ],
        out_specs=[whole(s) for s in shapes],
        out_shape=shapes,
        scratch_shapes=[
            pltpu.VMEM((rows, size), jnp.float32),
            pltpu.VMEM((rows, LANES), jnp.float32),
            *work_space(rows, prompt.shape[2], size),
        ],
        compiler_params=pltpu.CompilerParams(vmem_limit_bytes=32 << 20),
        cost_estimate=SMALL,
    )(queries, prompt, prompt, bias, *row_list, *begun, after)


def merge(out_a, sum_a, out_b, sum_b):
    top = jnp.maximum(sum_a, sum_b)
    weight_a = jnp.exp2(sum_a - top)
    weight_b = jnp.exp2(sum_b - top)
    total = weight_a + weight_b
    return (out_a * weight_a + out_b * weight_b) / total, top + jnp.log2(total)


def in_vmem(count):
    return [pl.BlockSpec(memory_space=pltpu.VMEM)] * count + [pl.BlockSpec(memory_space=pl.ANY)]


def merge_kernel(level, pieces, keep_ref, sums_ref, got_ref, _, *outs):
    rows = keep_ref.shape[1]
    half = rows // 2
    places = [(out, i) for out, count in zip(outs, pieces) for i in range(count)]
    for i in range(keep_ref.shape[0]):
        got_sum = unpack_tail(got_ref[i, rows:], rows)
        out, log_sum = merge(
            keep_ref[i], sums_ref[i][:, :1], got_ref[i, :rows].astype(jnp.float32), got_sum
        )
        if pieces:
            there, at = places[i]
            there[at, :rows] = out.astype(jnp.bfloat16)
            there[at, rows:] = pack_tail(log_sum)
        else:
            bit = lax.rem(lax.axis_index("ctx") >> level, 2) == 1
            send, keep, wide = outs

            def choose(first, value):
                return jnp.where(first, value[:half], value[half:])

            send[i, :half] = choose(bit, out).astype(jnp.bfloat16)
            send[i, half:] = pack_tail(choose(bit, log_sum))
            keep[i] = choose(~bit, out)
            wide[i] = jnp.broadcast_to(choose(~bit, log_sum), (half, LANES))


def merge_parts(keep, sums, got, level, pieces, after):
    count, rows, size = keep.shape
    part = rows if pieces else rows // 2
    message = part + tail_rows(part)
    shapes = [jax.ShapeDtypeStruct((n, message, size), jnp.bfloat16) for n in pieces or (count,)]
    if not pieces:
        shapes.append(jax.ShapeDtypeStruct((count, part, size), jnp.float32))
        shapes.append(jax.ShapeDtypeStruct((count, part, LANES), jnp.float32))
    return pl.pallas_call(
        functools.partial(merge_kernel, level, pieces),
        in_specs=in_vmem(3),
        out_shape=tuple(shapes),
        compiler_params=pltpu.CompilerParams(vmem_limit_bytes=16 << 20),
        cost_estimate=SMALL,
    )(keep, sums, got, after)


def finish_kernel(mine_ref, got_ref, _, out_ref):
    rows = math.prod(out_ref.shape[1:-1])
    for i in range(mine_ref.shape[0]):
        out, _ = merge(
            mine_ref[i, :rows].astype(jnp.float32),
            unpack_tail(mine_ref[i, rows:], rows),
            got_ref[i, :rows].astype(jnp.float32),
            unpack_tail(got_ref[i, rows:], rows),
        )
        out_ref[i] = out.astype(jnp.bfloat16).reshape(out_ref.shape[1:])


def finish(mine, got, shape, after):
    return pl.pallas_call(
        finish_kernel,
        in_specs=in_vmem(2),
        out_shape=jax.ShapeDtypeStruct(shape, jnp.bfloat16),
        compiler_params=pltpu.CompilerParams(vmem_limit_bytes=16 << 20),
        cost_estimate=SMALL,
    )(mine, got, after)


def place_kernel(levels, plan, *refs):
    part_refs = refs[: len(plan)]
    out_ref, sems = refs[-2:]
    copies = []
    for (head, own), ref in zip(plan, part_refs):
        blocks = ref.shape[1]
        bit = lax.rem(lax.axis_index("ctx"), 2) if levels > 1 else 0
        at = (bit if own else 1 - bit) * blocks
        for i in range(ref.shape[0]):
            there = out_ref.at[pl.ds(at, blocks), :, head + i]
            copies.append(pltpu.make_async_copy(ref.at[i], there, sems.at[len(copies)]))
    for copy in copies:
        copy.start()
    for copy in copies:
        copy.wait()


def place(out, parts, shape, levels, after):
    arrays = [array for array, _, _ in parts]
    plan = [(head, own) for _, head, own in parts]
    others = [after] if out is None else [after, out]
    return pl.pallas_call(
        functools.partial(place_kernel, levels, plan),
        in_specs=[pl.BlockSpec(memory_space=pltpu.VMEM)] * len(arrays)
        + [pl.BlockSpec(memory_space=pl.ANY), pl.BlockSpec(memory_space=pltpu.HBM)][: len(others)],
        out_specs=pl.BlockSpec(memory_space=pltpu.HBM),
        out_shape=pltpu.HBM(shape, jnp.bfloat16),
        input_output_aliases={} if out is None else {len(arrays) + 1: 0},
        scratch_shapes=[pltpu.SemaphoreType.DMA((sum(a.shape[0] for a in arrays),))],
        compiler_params=pltpu.CompilerParams(vmem_limit_bytes=16 << 20),
        cost_estimate=SMALL,
    )(*arrays, *others)


def on_device(shards, owners, queries, prompt_cache, suffix_cache, new_kv, ancestors, lengths):
    steps, per_owner, heads, group, size = queries.shape
    suffix_dev = suffix_cache.shape[2]
    shard = lax.axis_index("ctx")
    factor = math.log2(math.e) / math.sqrt(size)
    tokens_dev = -(-steps // shards)
    levels = shards.bit_length() - 1
    halves = 2 if levels > 1 else 1

    def swap(value, bit):
        return lax.ppermute(value, "ctx", [(i, i ^ (1 << bit)) for i in range(shards)])

    prompt_rows = prompt_cache.reshape(2, -1, size)
    mine, keys, parents, extents = build_message(
        suffix_cache.reshape(2, -1, size),
        new_kv.reshape(steps, 2, -1, size),
        prompt_rows,
        ancestors,
        lengths,
        heads,
        tokens_dev,
    )
    row_list = [mine] + [
        lax.ppermute(mine, "dom", [(i, (i + hop) % owners) for i in range(owners)])
        for hop in range(1, owners)
    ]
    prompt, bias = split_prompt(
        prompt_rows, keys, parents, extents, heads, owners, suffix_dev, tokens_dev
    )
    last = [bias]

    def follow(results):
        last[0] = results[0] if isinstance(results, (tuple, list)) else results
        return results

    begun = follow(start_head(queries, prompt, 0, factor))
    first = max(heads // 2, 1)
    groups = [(head, min(first, heads - head)) for head in range(0, heads, first)]
    begun_of = {0: begun}
    messages, kept, parts = {}, {}, []

    def run_attend(group):
        head, count = group
        send, keep, sums = follow(
            attend(
                queries, prompt, bias, row_list, head, count, factor, halves,
                begun_of.get(head, ()), last[0],
            )
        )
        kept[group] = keep, sums
        messages[group] = send, swap(send, 0)

    def run_merges(group, sizes):
        head, _ = group
        pieces = [(head + sum(sizes[:i]), size) for i, size in enumerate(sizes)]
        if levels <= 1:
            done, got = messages[group]
            starts = [at - head for at, _ in pieces]
            for piece, at in zip(pieces, starts):
                cut = slice(at, at + piece[1])
                messages[piece] = done[cut], got[cut]
        for level in range(1, levels):
            final = level == levels - 1
            results = follow(
                merge_parts(
                    *kept[group], messages[group][1], level, sizes if final else (), last[0]
                )
            )
            if final:
                for piece, send in zip(pieces, results):
                    messages[piece] = send, swap(send, level)
            else:
                kept[group] = results[1:]
                messages[group] = results[0], swap(results[0], level)
        return pieces

    def run_finish(piece):
        head, count = piece
        blocks = (steps * per_owner) >> (levels - 1 if levels > 1 else 0)
        done = follow(finish(*messages[piece], (count, blocks, group, size), last[0]))
        for level in range(levels - 2, 0, -1):
            other = swap(done, level)
            done = jnp.where(
                (shard >> level) % 2 == 1,
                jnp.concatenate([other, done], axis=1),
                jnp.concatenate([done, other], axis=1),
            )
        done = done.reshape(count, steps // halves, per_owner, group, size)
        mine = (done, head, True)
        return [mine, (swap(done, 0), head, False)] if levels > 1 else [mine]

    for one in groups:
        run_attend(one)
    pieces = run_merges(groups[0], (groups[0][1],))
    for one in groups[1:]:
        pieces += run_merges(one, (1,) * one[1])
    parts = [part for piece in pieces for part in run_finish(piece)]
    early, late = parts[:-1], parts[-1:]
    out = place(None, early, queries.shape, levels, last[0]) if early else None
    return place(out, late, queries.shape, levels, last[0])


def solution(mesh):
    return jax.shard_map(
        functools.partial(on_device, mesh.shape["ctx"], mesh.shape["dom"]),
        mesh=mesh,
        in_specs=(
            P("groups", "dom", "tp", None, None),
            P("groups", "ctx", "tp", None),
            P("groups", "dom", "ctx", "tp", None),
            P("groups", None, "dom", "tp", None),
            P("groups", None),
            P("groups"),
        ),
        out_specs=P("groups", "dom", "tp", None, None),
        check_vma=False,
    )
```

```python
import functools
import math

import jax
import jax.numpy as jnp
from jax import lax
from jax.experimental import pallas as pl
from jax.experimental.pallas import tpu as pltpu
from jax.sharding import PartitionSpec as P

LANES = 128
HIDDEN = -1e30
NN = (((1,), (0,)), ((), ()))
NT = (((1,), (1,)), ((), ()))
SMALL = pl.CostEstimate(flops=0, bytes_accessed=4096, transcendentals=0)


def round_up(value, multiple):
    return -(-value // multiple) * multiple


def dot(a, b, dims):
    return lax.dot_general(a, b, dims, preferred_element_type=jnp.float32)


def eye_mask(rows):
    shape = (rows, LANES)
    return lax.broadcasted_iota(jnp.int32, shape, 0) == lax.broadcasted_iota(jnp.int32, shape, 1)


def column_to_lanes(column):
    rows = column.shape[0]
    block = min(rows, LANES)
    mask = eye_mask(block)
    return jnp.concatenate(
        [
            jnp.sum(jnp.where(mask, column[at : at + block], 0.0), axis=0, keepdims=True)
            for at in range(0, rows, block)
        ],
        axis=0,
    )


def lanes_to_column(lanes, rows):
    block = min(rows, LANES)
    mask = eye_mask(block)
    return jnp.concatenate(
        [
            jnp.sum(jnp.where(mask, lanes[i : i + 1], 0.0), axis=1, keepdims=True)
            for i in range(lanes.shape[0])
        ],
        axis=0,
    )


def tail_rows(rows):
    return round_up(3 * -(-rows // LANES), 16)


def pack_tail(column):
    lanes = column_to_lanes(column)
    high = lanes.astype(jnp.bfloat16).astype(jnp.float32)
    middle = (lanes - high).astype(jnp.bfloat16).astype(jnp.float32)
    low = lanes - high - middle
    parts = jnp.concatenate([high, middle, low], axis=0)
    spare = tail_rows(column.shape[0]) - parts.shape[0]
    return jnp.concatenate([parts, jnp.zeros((spare, LANES), jnp.float32)], axis=0).astype(
        jnp.bfloat16
    )


def unpack_tail(tail, rows):
    tail = tail.astype(jnp.float32)
    blocks = -(-rows // LANES)
    lanes = tail[:blocks] + tail[blocks : 2 * blocks] + tail[2 * blocks : 3 * blocks]
    return lanes_to_column(lanes, rows)


def in_hbm(array):
    return pltpu.with_memory_space_constraint(array, pltpu.HBM)


def message_kernel(
    heads, tokens_dev, suffix_ref, new_ref, prompt_ref, ancestors_ref, lengths_ref,
    out_ref, keys_ref, parents_ref, extents_ref, here, wide, sems,
):
    rows, each = suffix_ref.shape[1], new_ref.shape[2]
    total = here.shape[1]
    first = jnp.minimum(lax.axis_index("ctx") * tokens_dev, new_ref.shape[0] - tokens_dev)
    pairs = [(suffix_ref, here.at[:, pl.ds(0, rows)])]
    for token in range(tokens_dev):
        pairs.append((new_ref.at[first + token], here.at[:, pl.ds(rows + token * each, each)]))
    parts = len(pairs)
    pairs += [(ancestors_ref, parents_ref), (lengths_ref, extents_ref)]
    pairs.append((prompt_ref.at[0, pl.ds(0, keys_ref.shape[0])], keys_ref))
    copies = [pltpu.make_async_copy(*pair, sems.at[i]) for i, pair in enumerate(pairs)]
    for copy in copies:
        copy.start()
    for copy in copies[:parts]:
        copy.wait()
    for kind in range(2):
        wide[kind] = here[kind].astype(jnp.float32)
        for head in range(heads):
            part = wide[kind, pl.ds(head, total // heads, stride=heads), :]
            out_ref[kind, head] = part.astype(out_ref.dtype)
    for copy in copies[parts:]:
        copy.wait()


def build_message(suffix, new, prompt, ancestors, lengths, heads, tokens_dev, ahead):
    rows = suffix.shape[1] + tokens_dev * new.shape[2]
    size = suffix.shape[2]
    lengths = lengths.reshape(1, -1)
    operands = (suffix, new, prompt, ancestors, lengths)
    return pl.pallas_call(
        functools.partial(message_kernel, heads, tokens_dev),
        in_specs=[pl.BlockSpec(memory_space=pltpu.HBM)] * len(operands),
        out_shape=(
            jax.ShapeDtypeStruct((2, heads, rows // heads, size), suffix.dtype),
            jax.ShapeDtypeStruct((ahead, size), prompt.dtype),
            jax.ShapeDtypeStruct(ancestors.shape, ancestors.dtype),
            jax.ShapeDtypeStruct(lengths.shape, lengths.dtype),
        ),
        scratch_shapes=[
            pltpu.VMEM((2, rows, size), suffix.dtype),
            pltpu.VMEM((2, rows, size), jnp.float32),
            pltpu.SemaphoreType.DMA((4 + tokens_dev,)),
        ],
        compiler_params=pltpu.CompilerParams(vmem_limit_bytes=24 << 20),
        cost_estimate=SMALL,
    )(*[in_hbm(operand) for operand in operands])


def iota(shape, axis):
    return lax.broadcasted_iota(jnp.int32, shape, axis)


def lineage_bias(ancestors_ref, lengths_ref, owners, per_owner, suffix_dev, tokens_dev, padded):
    particles = owners * per_owner
    steps = ancestors_ref.shape[0]
    suffix_columns = per_owner * suffix_dev
    each = suffix_columns + per_owner * tokens_dev
    my_owner = lax.axis_index("dom")
    my_shard = lax.axis_index("ctx")
    square = (particles, particles)
    same = iota(square, 0) == iota(square, 1)

    def as_column(row):
        return jnp.sum(jnp.where(same, row, 0), axis=1, keepdims=True)

    unit = same.astype(jnp.float32)
    nothing = jnp.zeros((particles, tokens_dev * particles), jnp.float32)
    state = jnp.concatenate([unit, nothing], axis=1)
    pick = iota((per_owner, particles), 1) == iota((per_owner, particles), 0) + my_owner * per_owner
    pick = pick.astype(jnp.bfloat16)
    mine = []
    for step in range(steps):
        parent = as_column(ancestors_ref[step : step + 1, :])
        move = (parent == iota(square, 1)).astype(jnp.bfloat16)
        state = dot(move, state.astype(jnp.bfloat16), NN)
        blocks = [state[:, :particles]]
        for token in range(tokens_dev):
            written = my_shard * tokens_dev + token
            old = state[:, (1 + token) * particles : (2 + token) * particles]
            blocks.append(jnp.where(written == step, unit, old))
        state = jnp.concatenate(blocks, axis=1)
        mine.append(dot(pick, state.astype(jnp.bfloat16), NN))
    mine = jnp.concatenate(mine, axis=0).astype(jnp.bfloat16)
    lengths = as_column(lengths_ref[...])
    shape = (particles, padded)
    column = iota(shape, 1)
    source = column // each
    owner = lax.rem(my_owner + owners - source, owners)
    inner = column - source * each
    after = inner - suffix_columns
    in_suffix = after < 0
    local = jnp.where(in_suffix, inner // suffix_dev, lax.rem(jnp.maximum(after, 0), per_owner))
    here = (iota(shape, 0) == owner * per_owner + local) & (column < owners * each)
    position = my_shard * suffix_dev + lax.rem(inner, suffix_dev)
    seen = [here & in_suffix & (position < lengths)]
    for token in range(tokens_dev):
        seen.append(here & (after >= token * per_owner) & (after < (token + 1) * per_owner))
    table = jnp.concatenate([s.astype(jnp.bfloat16) for s in seen], axis=0)
    return jnp.where(dot(mine, table, NN) > 0.5, 0.0, HIDDEN)


def split_kernel(
    heads, block, owners, suffix_dev, tokens_dev,
    rows_ref, keys_ref, parents_ref, extents_ref, *refs,
):
    out_refs = refs[: 2 * heads]
    bias_ref, here, wide, sems = refs[2 * heads :]
    total = out_refs[0].shape[0]
    places = [(kind, at) for kind in range(2) for at in range(0, total, block)]
    copies = {
        (kind, at): pltpu.make_async_copy(
            rows_ref.at[kind, pl.ds(at * heads, block * heads)],
            here.at[kind, pl.ds(at * heads, block * heads)],
            sems.at[i],
        )
        for i, (kind, at) in enumerate(places)
        if kind or at * heads >= keys_ref.shape[0]
    }
    for copy in copies.values():
        copy.start()
    for kind in range(2):
        for i, at in enumerate(range(0, total, block)):
            there = slice(at * heads, (at + block) * heads)
            if (kind, at) in copies:
                copies[kind, at].wait()
                wide[i % 2] = here[kind, there].astype(jnp.float32)
            else:
                wide[i % 2] = keys_ref[there].astype(jnp.float32)
            for head in range(heads):
                part = wide[i % 2, pl.ds(head, block, stride=heads), :]
                out_refs[kind * heads + head][at : at + block] = part.astype(rows_ref.dtype)
        if kind == 0:
            bias_ref[...] = lineage_bias(
                parents_ref, extents_ref, owners, parents_ref.shape[1] // owners,
                suffix_dev, tokens_dev, bias_ref.shape[1],
            )


def split_prompt(rows, keys, parents, extents, heads, owners, suffix_dev, tokens_dev):
    total = rows.shape[1] // heads
    block = math.gcd(total, 512)
    size = rows.shape[2]
    steps, particles = parents.shape
    padded = round_up(particles * (suffix_dev + tokens_dev), LANES)
    return pl.pallas_call(
        functools.partial(split_kernel, heads, block, owners, suffix_dev, tokens_dev),
        in_specs=[pl.BlockSpec(memory_space=pltpu.HBM)]
        + [pl.BlockSpec(memory_space=pltpu.VMEM)] * 3,
        out_shape=(
            *[jax.ShapeDtypeStruct((total, size), rows.dtype)] * (2 * heads),
            jax.ShapeDtypeStruct((steps * particles // owners, padded), jnp.float32),
        ),
        scratch_shapes=[
            pltpu.VMEM(rows.shape, rows.dtype),
            pltpu.VMEM((2, block * heads, size), jnp.float32),
            pltpu.SemaphoreType.DMA((2 * total // block,)),
        ],
        compiler_params=pltpu.CompilerParams(vmem_limit_bytes=24 << 20),
        cost_estimate=SMALL,
    )(in_hbm(rows), keys, parents, extents)


def with_ones(values):
    return jnp.concatenate([values, jnp.ones_like(values)], axis=1)


def row_peak(scores):
    return jnp.max(scores, axis=1, keepdims=True)


def weigh(scores, factor, offset):
    return jnp.exp2(scores * factor - offset).astype(jnp.bfloat16)


def work_space(rows, total, size):
    half, block = rows // 2, math.gcd(total, 512)
    return [
        pltpu.VMEM((3, half, block), jnp.float32),
        pltpu.VMEM((2, 2, half, math.gcd(total, 2 * block)), jnp.bfloat16),
        pltpu.VMEM((rows, 2 * size), jnp.float32),
    ]


def prompt_sum(q, k_ref, v_ref, factor, peak, scores, weights, sums):
    rows, total = q.shape[0], k_ref.shape[0]
    half, block, wide = rows // 2, scores.shape[2], weights.shape[3]
    units = [(at, which) for at in range(0, total, block) for which in range(2)]
    q_of = [q[:half], q[half:]]
    offset_of = [None, None]

    def score(n):
        at, which = units[n]
        scores[n % 3] = dot(q_of[which], k_ref[at : at + block], NT)

    def weight(n):
        at, which = units[n]
        there = slice(at % wide, at % wide + block)
        weights[which, at // wide % 2, :, there] = weigh(scores[n % 3], factor, offset_of[which])

    def gather(n):
        at, which = units[n]
        end = at + block
        if end % wide:
            return
        values = with_ones(v_ref[end - wide : end])
        part = dot(weights[which, at // wide % 2], values, NN)
        here = slice(which * half, (which + 1) * half)
        sums[here] = part if end == wide else sums[here] + part

    score(0)
    score(1)
    for which in range(2):
        top = row_peak(scores[which])
        if peak is not None:
            top = jnp.maximum(top, peak[which * half : (which + 1) * half])
        offset_of[which] = top * factor
    for n in range(len(units)):
        if n + 2 < len(units):
            score(n + 2)
        weight(n)
        if n:
            gather(n - 1)
    gather(len(units) - 1)
    return jnp.concatenate(offset_of, axis=0)


def prompt_kernel(head, factor, q_ref, k_ref, v_ref, together_ref, offset_ref, scores, weights):
    steps, per_owner, _, group, size = q_ref.shape
    q = q_ref[:, :, head].reshape(steps * per_owner * group, size)
    offset = prompt_sum(q, k_ref, v_ref, factor, None, scores, weights, together_ref)
    offset_ref[...] = jnp.broadcast_to(offset, offset_ref.shape)


def in_vmem(count, ordered=True):
    last = [pl.BlockSpec(memory_space=pl.ANY)] if ordered else []
    return [pl.BlockSpec(memory_space=pltpu.VMEM)] * count + last


def start_head(queries, keys, values, head, factor):
    steps, per_owner, _, group, size = queries.shape
    rows = steps * per_owner * group
    return pl.pallas_call(
        functools.partial(prompt_kernel, head, factor),
        in_specs=in_vmem(3, False),
        out_shape=(
            jax.ShapeDtypeStruct((rows, 2 * size), jnp.float32),
            jax.ShapeDtypeStruct((rows, LANES), jnp.float32),
        ),
        scratch_shapes=work_space(rows, keys.shape[0], size)[:2],
        compiler_params=pltpu.CompilerParams(vmem_limit_bytes=24 << 20),
        cost_estimate=SMALL,
    )(queries, keys, values)


def attend_kernel(head, factor, owners, halves, started, *refs):
    q_ref, k_ref, v_ref, bias_ref = refs[:4]
    row_refs = refs[4 : 4 + owners]
    begun = refs[4 + owners : 4 + owners + 2 * started]
    _, send_ref, keep_ref, sums_ref, out, log_sums, *work = refs[4 + owners + 2 * started :]
    steps, per_owner, _, group, size = q_ref.shape
    padded = bias_ref.shape[1]
    rows = steps * per_owner * group
    half = rows // halves

    def queries_of(first, number):
        here = number * per_owner * group
        q = q_ref[pl.ds(first, number), :, head].reshape(here, size)
        at = pl.multiple_of(first * per_owner, per_owner)
        bias = bias_ref[pl.ds(at, number * per_owner), :]
        bias = jnp.broadcast_to(bias[:, None, :], (number * per_owner, group, padded))
        return q, dot(q, suffix_of(0), NT) + bias.reshape(here, padded)

    def suffix_of(kind):
        pieces = [ref[kind, head] for ref in row_refs]
        columns = sum(piece.shape[0] for piece in pieces)
        if padded > columns:
            pieces.append(jnp.zeros((padded - columns, size), jnp.bfloat16))
        return jnp.concatenate(pieces, axis=0)

    def store(at, together, offset):
        sums = together[:, size:]
        out[pl.ds(at, sums.shape[0]), :] = together[:, :size] / sums
        log_sums[pl.ds(at, sums.shape[0]), :] = offset + jnp.log2(sums)
        return sums

    q, suffix_scores = queries_of(0, steps)
    if started:
        together, offset = begun[0][...], begun[1][:, :1]
    else:
        peak = row_peak(suffix_scores)
        offset = prompt_sum(q, k_ref, v_ref, factor, peak, *work)
        together = work[-1][...]
    weight = weigh(suffix_scores, factor, offset)
    together = together + dot(weight, with_ones(suffix_of(1)), NN)
    sums = store(0, together, offset)

    @pl.when(jnp.logical_not(jnp.max(sums) < 2.0**100))
    def _():
        @pl.loop(0, steps)
        def _(step):
            q, suffix_scores = queries_of(step, 1)
            scores = dot(q, k_ref[...], NT)
            offset = jnp.maximum(row_peak(scores), row_peak(suffix_scores)) * factor
            together = dot(weigh(scores, factor, offset), with_ones(v_ref[...]), NN)
            weight = weigh(suffix_scores, factor, offset)
            together = together + dot(weight, with_ones(suffix_of(1)), NN)
            store(pl.multiple_of(step * per_owner * group, per_owner * group), together, offset)

    bit = lax.rem(lax.axis_index("ctx"), 2) if halves == 2 else 0
    there = pl.ds(pl.multiple_of((halves - 1 - bit) * half, half), half)
    send_ref[0, :half] = out[there, :].astype(jnp.bfloat16)
    send_ref[0, half:] = pack_tail(log_sums[there, :][:, :1])
    here = pl.ds(pl.multiple_of(bit * half, half), half)
    keep_ref[0] = out[here, :]
    sums_ref[0] = log_sums[here, :]


def attend(queries, keys, values, bias, row_list, head, factor, halves, begun, after):
    steps, per_owner, heads, group, size = queries.shape
    rows = steps * per_owner * group
    half = rows // halves
    operands = (queries, keys, values, bias, *row_list, *begun)
    return pl.pallas_call(
        functools.partial(attend_kernel, head, factor, len(row_list), halves, len(begun) // 2),
        in_specs=in_vmem(len(operands)),
        out_shape=(
            jax.ShapeDtypeStruct((1, half + tail_rows(half), size), jnp.bfloat16),
            jax.ShapeDtypeStruct((1, half, size), jnp.float32),
            jax.ShapeDtypeStruct((1, half, LANES), jnp.float32),
        ),
        scratch_shapes=[
            pltpu.VMEM((rows, size), jnp.float32),
            pltpu.VMEM((rows, LANES), jnp.float32),
            *work_space(rows, keys.shape[0], size),
        ],
        compiler_params=pltpu.CompilerParams(vmem_limit_bytes=32 << 20),
        cost_estimate=SMALL,
    )(*operands, after)


def merge(out_a, sum_a, out_b, sum_b):
    top = jnp.maximum(sum_a, sum_b)
    weight_a = jnp.exp2(sum_a - top)
    weight_b = jnp.exp2(sum_b - top)
    total = weight_a + weight_b
    return (out_a * weight_a + out_b * weight_b) / total, top + jnp.log2(total)


def merge_kernel(level, pieces, keep_ref, sums_ref, got_ref, _, *outs):
    rows = keep_ref.shape[1]
    half = rows // 2
    places = [(out, i) for out, count in zip(outs, pieces) for i in range(count)]
    for i in range(keep_ref.shape[0]):
        got_sum = unpack_tail(got_ref[i, rows:], rows)
        out, log_sum = merge(
            keep_ref[i], sums_ref[i][:, :1], got_ref[i, :rows].astype(jnp.float32), got_sum
        )
        if pieces:
            there, at = places[i]
            there[at, :rows] = out.astype(jnp.bfloat16)
            there[at, rows:] = pack_tail(log_sum)
        else:
            bit = lax.rem(lax.axis_index("ctx") >> level, 2) == 1
            send, keep, wide = outs

            def choose(first, value):
                return jnp.where(first, value[:half], value[half:])

            send[i, :half] = choose(bit, out).astype(jnp.bfloat16)
            send[i, half:] = pack_tail(choose(bit, log_sum))
            keep[i] = choose(~bit, out)
            wide[i] = jnp.broadcast_to(choose(~bit, log_sum), (half, LANES))


def merge_parts(keep, sums, got, level, pieces, after):
    count, rows, size = keep.shape
    part = rows if pieces else rows // 2
    message = part + tail_rows(part)
    shapes = [jax.ShapeDtypeStruct((n, message, size), jnp.bfloat16) for n in pieces or (count,)]
    if not pieces:
        shapes.append(jax.ShapeDtypeStruct((count, part, size), jnp.float32))
        shapes.append(jax.ShapeDtypeStruct((count, part, LANES), jnp.float32))
    return pl.pallas_call(
        functools.partial(merge_kernel, level, pieces),
        in_specs=in_vmem(3),
        out_shape=tuple(shapes),
        compiler_params=pltpu.CompilerParams(vmem_limit_bytes=16 << 20),
        cost_estimate=SMALL,
    )(keep, sums, got, after)


def finish_kernel(ready, *refs):
    *part_refs, _, out_ref = refs
    rows = math.prod(out_ref.shape[1:-1])
    at = 0
    for ref in part_refs[:ready]:
        out_ref[at : at + ref.shape[0]] = ref[...]
        at += ref.shape[0]
    pair_refs = part_refs[ready:]
    for mine_ref, got_ref in zip(pair_refs[::2], pair_refs[1::2]):
        for i in range(mine_ref.shape[0]):
            out, _ = merge(
                mine_ref[i, :rows].astype(jnp.float32),
                unpack_tail(mine_ref[i, rows:], rows),
                got_ref[i, :rows].astype(jnp.float32),
                unpack_tail(got_ref[i, rows:], rows),
            )
            out_ref[at] = out.astype(jnp.bfloat16).reshape(out_ref.shape[1:])
            at += 1


def finish(ready, pair, shape, after):
    arrays = (*ready, *pair)
    return pl.pallas_call(
        functools.partial(finish_kernel, len(ready)),
        in_specs=in_vmem(len(arrays)),
        out_shape=jax.ShapeDtypeStruct(shape, jnp.bfloat16),
        compiler_params=pltpu.CompilerParams(vmem_limit_bytes=16 << 20),
        cost_estimate=SMALL,
    )(*arrays, after)


def place_kernel(levels, plan, *refs):
    part_refs = refs[: len(plan)]
    out_ref, sems = refs[-2:]
    copies = []
    for (head, own), ref in zip(plan, part_refs):
        blocks = ref.shape[1]
        bit = lax.rem(lax.axis_index("ctx"), 2) if levels > 1 else 0
        at = (bit if own else 1 - bit) * blocks
        for i in range(ref.shape[0]):
            there = out_ref.at[pl.ds(at, blocks), :, head + i]
            copies.append(pltpu.make_async_copy(ref.at[i], there, sems.at[len(copies)]))
    for copy in copies:
        copy.start()
    for copy in copies:
        copy.wait()


def place(out, parts, shape, levels, after):
    arrays = [array for array, _, _ in parts]
    plan = [(head, own) for _, head, own in parts]
    others = [after] if out is None else [after, out]
    return pl.pallas_call(
        functools.partial(place_kernel, levels, plan),
        in_specs=[pl.BlockSpec(memory_space=pltpu.VMEM)] * len(arrays)
        + [pl.BlockSpec(memory_space=pl.ANY), pl.BlockSpec(memory_space=pltpu.HBM)][: len(others)],
        out_specs=pl.BlockSpec(memory_space=pltpu.HBM),
        out_shape=pltpu.HBM(shape, jnp.bfloat16),
        input_output_aliases={} if out is None else {len(arrays) + 1: 0},
        scratch_shapes=[pltpu.SemaphoreType.DMA((sum(a.shape[0] for a in arrays),))],
        compiler_params=pltpu.CompilerParams(vmem_limit_bytes=16 << 20),
        cost_estimate=SMALL,
    )(*arrays, *others)


def on_device(shards, owners, queries, prompt_cache, suffix_cache, new_kv, ancestors, lengths):
    steps, per_owner, heads, group, size = queries.shape
    suffix_dev = suffix_cache.shape[2]
    shard = lax.axis_index("ctx")
    factor = math.log2(math.e) / math.sqrt(size)
    tokens_dev = -(-steps // shards)
    levels = shards.bit_length() - 1
    halves = 2 if levels > 1 else 1

    def swap(value, bit):
        return lax.ppermute(value, "ctx", [(i, i ^ (1 << bit)) for i in range(shards)])

    prompt_rows = prompt_cache.reshape(2, -1, size)
    mine, keys, parents, extents = build_message(
        suffix_cache.reshape(2, -1, size),
        new_kv.reshape(steps, 2, -1, size),
        prompt_rows,
        ancestors,
        lengths,
        heads,
        tokens_dev,
        math.gcd(prompt_rows.shape[1] // 2, 512 * heads),
    )
    row_list = [mine] + [
        lax.ppermute(mine, "dom", [(i, (i + hop) % owners) for i in range(owners)])
        for hop in range(1, owners)
    ]
    *prompt, bias = split_prompt(
        prompt_rows, keys, parents, extents, heads, owners, suffix_dev, tokens_dev
    )
    last = [bias]

    def follow(results):
        last[0] = results[0] if isinstance(results, (tuple, list)) else results
        return results

    begun_of = {0: follow(start_head(queries, prompt[0], prompt[heads], 0, factor))}
    messages, kept, parts = {}, {}, []

    def run_attend(group):
        head, _ = group
        send, keep, sums = follow(
            attend(
                queries, prompt[head], prompt[heads + head], bias, row_list, head, factor, halves,
                begun_of.get(head, ()), last[0],
            )
        )
        kept[group] = keep, sums
        messages[group] = send, swap(send, 0)

    def run_merges(group, sizes):
        head, _ = group
        pieces = [(head + sum(sizes[:i]), size) for i, size in enumerate(sizes)]
        if levels <= 1:
            done, got = messages[group]
            starts = [at - head for at, _ in pieces]
            for piece, at in zip(pieces, starts):
                cut = slice(at, at + piece[1])
                messages[piece] = done[cut], got[cut]
        for level in range(1, levels):
            final = level == levels - 1
            results = follow(
                merge_parts(
                    *kept[group], messages[group][1], level, sizes if final else (), last[0]
                )
            )
            if final:
                for piece, send in zip(pieces, results):
                    messages[piece] = send, swap(send, level)
            else:
                kept[group] = results[1:]
                messages[group] = results[0], swap(results[0], level)
        return pieces

    blocks = (steps * per_owner) >> (levels - 1 if levels > 1 else 0)

    def run_finish(piece, ready=()):
        count = len(ready) + 1
        return follow(finish(ready, messages[piece], (count, blocks, group, size), last[0]))

    def run_gather(head, done):
        count = done.shape[0]
        for level in range(levels - 2, 0, -1):
            other = swap(done, level)
            done = jnp.where(
                (shard >> level) % 2 == 1,
                jnp.concatenate([other, done], axis=1),
                jnp.concatenate([done, other], axis=1),
            )
        done = done.reshape(count, steps // halves, per_owner, group, size)
        parts.append((done, head, True))
        if levels > 1:
            parts.append((swap(done, 0), head, False))

    waiting = []
    for head in range(0, heads, 2):
        both = [(one, 1) for one in range(head, min(head + 2, heads))]
        ready = ()
        for one in both:
            run_attend(one)
            if waiting:
                ready = (run_finish(waiting.pop(0), ready),)
                if not waiting:
                    run_gather(head - ready[0].shape[0], ready[0])
        for one in both:
            run_merges(one, (1,))
        waiting = both
    for one in waiting:
        run_gather(one[0], run_finish(one))
    early, late = parts[:-1], parts[-1:]
    out = place(None, early, queries.shape, levels, last[0]) if early else None
    return place(out, late, queries.shape, levels, last[0])


def solution(mesh):
    return jax.shard_map(
        functools.partial(on_device, mesh.shape["ctx"], mesh.shape["dom"]),
        mesh=mesh,
        in_specs=(
            P("groups", "dom", "tp", None, None),
            P("groups", "ctx", "tp", None),
            P("groups", "dom", "ctx", "tp", None),
            P("groups", None, "dom", "tp", None),
            P("groups", None),
            P("groups"),
        ),
        out_specs=P("groups", "dom", "tp", None, None),
        check_vma=False,
    )
```

```python
import functools
import math

import jax
import jax.numpy as jnp
from jax import lax
from jax.experimental import pallas as pl
from jax.experimental.pallas import tpu as pltpu
from jax.sharding import PartitionSpec as P

LANES = 128
HIDDEN = -1e30
NN = (((1,), (0,)), ((), ()))
NT = (((1,), (1,)), ((), ()))
SMALL = pl.CostEstimate(flops=0, bytes_accessed=4096, transcendentals=0)


def round_up(value, multiple):
    return -(-value // multiple) * multiple


def dot(a, b, dims):
    return lax.dot_general(a, b, dims, preferred_element_type=jnp.float32)


def eye_mask(rows):
    shape = (rows, LANES)
    return lax.broadcasted_iota(jnp.int32, shape, 0) == lax.broadcasted_iota(jnp.int32, shape, 1)


def column_to_lanes(column):
    rows = column.shape[0]
    block = min(rows, LANES)
    mask = eye_mask(block)
    return jnp.concatenate(
        [
            jnp.sum(jnp.where(mask, column[at : at + block], 0.0), axis=0, keepdims=True)
            for at in range(0, rows, block)
        ],
        axis=0,
    )


def lanes_to_column(lanes, rows):
    block = min(rows, LANES)
    mask = eye_mask(block)
    return jnp.concatenate(
        [
            jnp.sum(jnp.where(mask, lanes[i : i + 1], 0.0), axis=1, keepdims=True)
            for i in range(lanes.shape[0])
        ],
        axis=0,
    )


def tail_rows(rows):
    return round_up(3 * -(-rows // LANES), 16)


def pack_tail(column):
    lanes = column_to_lanes(column)
    high = lanes.astype(jnp.bfloat16).astype(jnp.float32)
    middle = (lanes - high).astype(jnp.bfloat16).astype(jnp.float32)
    low = lanes - high - middle
    parts = jnp.concatenate([high, middle, low], axis=0)
    spare = tail_rows(column.shape[0]) - parts.shape[0]
    return jnp.concatenate([parts, jnp.zeros((spare, LANES), jnp.float32)], axis=0).astype(
        jnp.bfloat16
    )


def unpack_tail(tail, rows):
    tail = tail.astype(jnp.float32)
    blocks = -(-rows // LANES)
    lanes = tail[:blocks] + tail[blocks : 2 * blocks] + tail[2 * blocks : 3 * blocks]
    return lanes_to_column(lanes, rows)


def in_hbm(array):
    return pltpu.with_memory_space_constraint(array, pltpu.HBM)


def message_kernel(
    heads, suffix_ref, new_ref, ancestors_ref, lengths_ref,
    out_ref, parents_ref, extents_ref, here, wide, sems,
):
    steps, each = new_ref.shape[0], new_ref.shape[2]
    total = here.shape[1]
    is_last = lax.axis_index("ctx") == lax.axis_size("ctx") - 1
    suffix_copy = pltpu.make_async_copy(suffix_ref, here, sems.at[0])
    token_copies = [
        pltpu.make_async_copy(
            new_ref.at[step], here.at[:, pl.ds(step * each, each)], sems.at[1 + step]
        )
        for step in range(steps)
    ]
    small = [
        pltpu.make_async_copy(ancestors_ref, parents_ref, sems.at[1 + steps]),
        pltpu.make_async_copy(lengths_ref, extents_ref, sems.at[2 + steps]),
    ]
    for copy in small:
        copy.start()

    @pl.when(is_last)
    def _():
        for copy in token_copies:
            copy.start()
        for copy in token_copies:
            copy.wait()

    @pl.when(jnp.logical_not(is_last))
    def _():
        suffix_copy.start()
        suffix_copy.wait()

    for kind in range(2):
        wide[kind] = here[kind].astype(jnp.float32)
        for head in range(heads):
            part = wide[kind, pl.ds(head, total // heads, stride=heads), :]
            out_ref[kind, head] = part.astype(out_ref.dtype)
    for copy in small:
        copy.wait()


def build_message(suffix, new, ancestors, lengths, heads):
    _, rows, size = suffix.shape
    lengths = lengths.reshape(1, -1)
    operands = (suffix, new, ancestors, lengths)
    return pl.pallas_call(
        functools.partial(message_kernel, heads),
        in_specs=[pl.BlockSpec(memory_space=pltpu.HBM)] * len(operands),
        out_shape=(
            jax.ShapeDtypeStruct((2, heads, rows // heads, size), suffix.dtype),
            jax.ShapeDtypeStruct(ancestors.shape, ancestors.dtype),
            jax.ShapeDtypeStruct(lengths.shape, lengths.dtype),
        ),
        scratch_shapes=[
            pltpu.VMEM(suffix.shape, suffix.dtype),
            pltpu.VMEM(suffix.shape, jnp.float32),
            pltpu.SemaphoreType.DMA((3 + new.shape[0],)),
        ],
        compiler_params=pltpu.CompilerParams(vmem_limit_bytes=24 << 20),
        cost_estimate=SMALL,
    )(*[in_hbm(operand) for operand in operands])


def iota(shape, axis):
    return lax.broadcasted_iota(jnp.int32, shape, axis)


def lineage_bias(ancestors_ref, lengths_ref, states, owners, suffix_dev):
    steps, particles = ancestors_ref.shape
    per_owner = particles // owners
    each = per_owner * suffix_dev
    my_owner = lax.axis_index("dom")
    my_shard = lax.axis_index("ctx")
    is_last = my_shard == lax.axis_size("ctx") - 1
    square = (particles, particles)
    same = iota(square, 0) == iota(square, 1)

    def as_column(row):
        return jnp.sum(jnp.where(same, row, 0), axis=1, keepdims=True)

    products = {}
    for step in range(steps):
        parent = as_column(ancestors_ref[step : step + 1, :])
        products[step - 1, step] = (parent == iota(square, 1)).astype(jnp.bfloat16)
    for length in range(2, steps + 1):
        for step in range(length - 1, steps):
            after = step - length
            middle = (step + after + 1) // 2
            both = dot(products[middle, step], products[after, middle], NN)
            products[after, step] = both.astype(jnp.bfloat16)
    for step in range(steps):
        states[step, :, :particles] = products[-1, step].astype(jnp.float32)
        for token in range(steps):
            here = slice((1 + token) * particles, (2 + token) * particles)
            if token < step:
                states[step, :, here] = products[token, step].astype(jnp.float32)
            else:
                states[step, :, here] = same.astype(jnp.float32) * float(token == step)
    rows = pl.ds(pl.multiple_of(my_owner * per_owner, per_owner), per_owner)
    mine = jnp.concatenate([states[step, rows, :] for step in range(steps)], axis=0)
    mine = mine.astype(jnp.bfloat16)
    lengths = as_column(lengths_ref[...])
    shape = (particles, owners * each)
    column = iota(shape, 1)
    source = column // each
    first = lax.rem(my_owner + owners - source, owners) * per_owner
    inner = column - source * each
    position = my_shard * suffix_dev + lax.rem(inner, suffix_dev)
    by_particle = iota(shape, 0) == first + inner // suffix_dev
    by_token = iota(shape, 0) == first + lax.rem(inner, per_owner)
    seen = [by_particle & (position < lengths) & jnp.logical_not(is_last)]
    seen += [by_token & (inner // per_owner == token) & is_last for token in range(steps)]
    table = jnp.concatenate([s.astype(jnp.bfloat16) for s in seen], axis=0)
    return jnp.where(dot(mine, table, NN) > 0.5, 0.0, HIDDEN)


def split_kernel(
    heads, block, owners, suffix_dev,
    rows_ref, parents_ref, extents_ref, *refs,
):
    out_refs = refs[: 2 * heads]
    bias_ref, here, wide, states, sems = refs[2 * heads :]
    total = out_refs[0].shape[0]
    places = [(kind, at) for kind in range(2) for at in range(0, total, block)]
    copies = [
        pltpu.make_async_copy(
            rows_ref.at[kind, pl.ds(at * heads, block * heads)],
            here.at[kind, pl.ds(at * heads, block * heads)],
            sems.at[i],
        )
        for i, (kind, at) in enumerate(places)
    ]
    for copy in copies:
        copy.start()
    bias_ref[...] = lineage_bias(parents_ref, extents_ref, states, owners, suffix_dev)
    for i, (kind, at) in enumerate(places):
        copies[i].wait()
        wide[i % 2] = here[kind, at * heads : (at + block) * heads].astype(jnp.float32)
        for head in range(heads):
            part = wide[i % 2, pl.ds(head, block, stride=heads), :]
            out_refs[kind * heads + head][at : at + block] = part.astype(rows_ref.dtype)


def split_prompt(rows, parents, extents, heads, owners, suffix_dev):
    total = rows.shape[1] // heads
    block = math.gcd(total, 512)
    size = rows.shape[2]
    steps, particles = parents.shape
    return pl.pallas_call(
        functools.partial(split_kernel, heads, block, owners, suffix_dev),
        in_specs=[pl.BlockSpec(memory_space=pltpu.HBM)]
        + [pl.BlockSpec(memory_space=pltpu.VMEM)] * 2,
        out_shape=(
            *[jax.ShapeDtypeStruct((total, size), rows.dtype)] * (2 * heads),
            jax.ShapeDtypeStruct(
                (steps * particles // owners, particles * suffix_dev), jnp.float32
            ),
        ),
        scratch_shapes=[
            pltpu.VMEM(rows.shape, rows.dtype),
            pltpu.VMEM((2, block * heads, size), jnp.float32),
            pltpu.VMEM((steps, particles, (1 + steps) * particles), jnp.float32),
            pltpu.SemaphoreType.DMA((2 * total // block,)),
        ],
        compiler_params=pltpu.CompilerParams(vmem_limit_bytes=24 << 20),
        cost_estimate=SMALL,
    )(in_hbm(rows), parents, extents)


def with_ones(values):
    return jnp.concatenate([values, jnp.ones_like(values)], axis=1)


def row_peak(scores):
    return jnp.max(scores, axis=1, keepdims=True)


def weigh(scores, factor, offset):
    return jnp.exp2(scores * factor - offset).astype(jnp.bfloat16)


def work_space(streams, rows, total, size):
    block = math.gcd(total, 1024)
    return [
        pltpu.VMEM((3, rows, block), jnp.float32),
        pltpu.VMEM((streams, 2, rows, block), jnp.bfloat16),
        pltpu.VMEM((streams * rows, 2 * size), jnp.float32),
    ]


def prompt_sum(streams, factor, scores, weights, sums):
    rows, total = streams[0][0].shape[0], streams[0][1].shape[0]
    block, wide = scores.shape[2], weights.shape[3]
    units = [(at, i) for at in range(0, total, block) for i in range(len(streams))]
    offsets = [None] * len(streams)

    def score(n):
        at, i = units[n]
        scores[n % 3] = dot(streams[i][0], streams[i][1][at : at + block], NT)

    def weight(n):
        at, i = units[n]
        if at == 0:
            top = row_peak(scores[n % 3])
            peak = streams[i][3]
            offsets[i] = (top if peak is None else jnp.maximum(top, peak)) * factor
        there = slice(at % wide, at % wide + block)
        weights[i, at // wide % 2, :, there] = weigh(scores[n % 3], factor, offsets[i])

    def gather(n):
        at, i = units[n]
        end = at + block
        if end % wide:
            return
        part = dot(weights[i, at // wide % 2], with_ones(streams[i][2][end - wide : end]), NN)
        here = slice(i * rows, (i + 1) * rows)
        sums[here] = part if end == wide else sums[here] + part

    score(0)
    score(1)
    for n in range(len(units)):
        if n + 2 < len(units):
            score(n + 2)
        weight(n)
        if n:
            gather(n - 1)
    gather(len(units) - 1)
    return offsets


def first_step(q_ref, kept):
    bit = lax.rem(lax.axis_index("ctx"), 2)
    return (bit if kept else 1 - bit) * (q_ref.shape[0] // 2)


def queries_of(q_ref, head, first, number):
    _, per_owner, _, group, size = q_ref.shape
    return q_ref[pl.ds(first, number), :, head].reshape(number * per_owner * group, size)


def prompt_kernel(heads, kept, factor, q_ref, *refs):
    k_refs, v_refs = refs[: len(heads)], refs[len(heads) : 2 * len(heads)]
    together_ref, offset_ref, scores, weights = refs[2 * len(heads) :]
    first, number = first_step(q_ref, kept), q_ref.shape[0] // 2
    streams = [
        (queries_of(q_ref, head, first, number), k_ref, v_ref, None)
        for head, k_ref, v_ref in zip(heads, k_refs, v_refs)
    ]
    offsets = prompt_sum(streams, factor, scores, weights, together_ref)
    offset = jnp.concatenate(offsets, axis=0)
    offset_ref[...] = jnp.broadcast_to(offset, offset_ref.shape)


def in_vmem(count, ordered=True):
    last = [pl.BlockSpec(memory_space=pl.ANY)] if ordered else []
    return [pl.BlockSpec(memory_space=pltpu.VMEM)] * count + last


def begin(queries, prompt, heads, kept, factor):
    steps, per_owner, _, group, size = queries.shape
    rows = steps * per_owner * group // 2
    keys, values = prompt
    space = work_space(len(heads), rows, keys[0].shape[0], size)
    return pl.pallas_call(
        functools.partial(prompt_kernel, heads, kept, factor),
        in_specs=in_vmem(1 + 2 * len(heads), False),
        out_shape=(
            jax.ShapeDtypeStruct((len(heads) * rows, 2 * size), jnp.float32),
            jax.ShapeDtypeStruct((len(heads) * rows, LANES), jnp.float32),
        ),
        scratch_shapes=space[:2],
        compiler_params=pltpu.CompilerParams(vmem_limit_bytes=24 << 20),
        cost_estimate=SMALL,
    )(queries, *[keys[head] for head in heads], *[values[head] for head in heads])


def attend_kernel(heads, kept, factor, owners, started, *refs):
    count = len(heads)
    q_ref, bias_ref = refs[:2]
    row_refs = refs[2 : 2 + owners]
    refs = refs[2 + owners :]
    k_refs, v_refs, refs = refs[:count], refs[count : 2 * count], refs[2 * count :]
    begun, refs = refs[: 2 * started], refs[2 * started + 1 :]
    if kept:
        out, log_sums, *work = refs
    else:
        send_ref, out, log_sums, *work = refs
    steps, per_owner, _, group, size = q_ref.shape
    columns = bias_ref.shape[1]
    number = steps // 2
    rows = number * per_owner * group
    start = first_step(q_ref, kept)

    def suffix_of(head, kind):
        return jnp.concatenate([ref[kind, head] for ref in row_refs], axis=0)

    def suffix_scores(q, head, first, number):
        at = pl.multiple_of(first * per_owner, per_owner)
        bias = bias_ref[pl.ds(at, number * per_owner), :]
        bias = jnp.broadcast_to(bias[:, None, :], (number * per_owner, group, columns))
        return dot(q, suffix_of(head, 0), NT) + bias.reshape(number * per_owner * group, columns)

    def store(i, at, together, offset):
        sums = together[:, size:]
        out[i, pl.ds(at, sums.shape[0]), :] = together[:, :size] / sums
        log_sums[i, pl.ds(at, sums.shape[0]), :] = offset + jnp.log2(sums)
        return sums

    queries = [queries_of(q_ref, head, start, number) for head in heads]
    extras = [suffix_scores(q, head, start, number) for q, head in zip(queries, heads)]
    if started:
        offsets = [begun[1][i * rows : (i + 1) * rows, :1] for i in range(count)]
        togethers = begun[0]
    else:
        streams = [(q, k, v, row_peak(e)) for q, k, v, e in zip(queries, k_refs, v_refs, extras)]
        offsets = prompt_sum(streams, factor, *work)
        togethers = work[-1]
    worst = []
    for i, head in enumerate(heads):
        weight = weigh(extras[i], factor, offsets[i])
        together = togethers[i * rows : (i + 1) * rows]
        together = together + dot(weight, with_ones(suffix_of(head, 1)), NN)
        worst.append(jnp.max(store(i, 0, together, offsets[i])))

    for i, head in enumerate(heads):

        @pl.when(jnp.logical_not(worst[i] < 2.0**100))
        def _():
            @pl.loop(0, number)
            def _(step):
                q = queries_of(q_ref, head, start + step, 1)
                extra = suffix_scores(q, head, start + step, 1)
                scores = dot(q, k_refs[i][...], NT)
                offset = jnp.maximum(row_peak(scores), row_peak(extra)) * factor
                weight = weigh(scores, factor, offset)
                together = dot(weight, with_ones(v_refs[i][...]), NN)
                weight = weigh(extra, factor, offset)
                together = together + dot(weight, with_ones(suffix_of(head, 1)), NN)
                here = per_owner * group
                store(i, pl.multiple_of(step * here, here), together, offset)

        if not kept:
            send_ref[i, :rows] = out[i].astype(jnp.bfloat16)
            send_ref[i, rows:] = pack_tail(log_sums[i, :, :1])


def attend(queries, prompt, bias, row_list, heads, kept, factor, begun, after):
    steps, per_owner, _, group, size = queries.shape
    rows = steps * per_owner * group // 2
    count = len(heads)
    keys, values = prompt
    operands = (
        queries, bias, *row_list,
        *[keys[head] for head in heads], *[values[head] for head in heads], *begun,
    )
    parts = [((count, rows, size), jnp.float32), ((count, rows, LANES), jnp.float32)]
    send = jax.ShapeDtypeStruct((count, rows + tail_rows(rows), size), jnp.bfloat16)
    space = work_space(count, rows, keys[0].shape[0], size)
    return pl.pallas_call(
        functools.partial(
            attend_kernel, heads, kept, factor, len(row_list), len(begun) // 2
        ),
        in_specs=in_vmem(len(operands)),
        out_shape=tuple(jax.ShapeDtypeStruct(*part) for part in parts) if kept else send,
        scratch_shapes=[*([] if kept else [pltpu.VMEM(*part) for part in parts]), *space],
        compiler_params=pltpu.CompilerParams(vmem_limit_bytes=32 << 20),
        cost_estimate=SMALL,
    )(*operands, after)


def merge(out_a, sum_a, out_b, sum_b):
    top = jnp.maximum(sum_a, sum_b)
    weight_a = jnp.exp2(sum_a - top)
    weight_b = jnp.exp2(sum_b - top)
    total = weight_a + weight_b
    return (out_a * weight_a + out_b * weight_b) / total, top + jnp.log2(total)


def merge_kernel(level, pieces, keep_ref, sums_ref, got_ref, _, *outs):
    rows = keep_ref.shape[1]
    half = rows // 2
    places = [(out, i) for out, count in zip(outs, pieces) for i in range(count)]
    for i in range(keep_ref.shape[0]):
        got_sum = unpack_tail(got_ref[i, rows:], rows)
        out, log_sum = merge(
            keep_ref[i], sums_ref[i][:, :1], got_ref[i, :rows].astype(jnp.float32), got_sum
        )
        if pieces:
            there, at = places[i]
            there[at, :rows] = out.astype(jnp.bfloat16)
            there[at, rows:] = pack_tail(log_sum)
        else:
            bit = lax.rem(lax.axis_index("ctx") >> level, 2) == 1
            send, keep, wide = outs

            def choose(first, value):
                return jnp.where(first, value[:half], value[half:])

            send[i, :half] = choose(bit, out).astype(jnp.bfloat16)
            send[i, half:] = pack_tail(choose(bit, log_sum))
            keep[i] = choose(~bit, out)
            wide[i] = jnp.broadcast_to(choose(~bit, log_sum), (half, LANES))


def merge_parts(keep, sums, got, level, pieces, after):
    count, rows, size = keep.shape
    part = rows if pieces else rows // 2
    message = part + tail_rows(part)
    shapes = [jax.ShapeDtypeStruct((n, message, size), jnp.bfloat16) for n in pieces or (count,)]
    if not pieces:
        shapes.append(jax.ShapeDtypeStruct((count, part, size), jnp.float32))
        shapes.append(jax.ShapeDtypeStruct((count, part, LANES), jnp.float32))
    return pl.pallas_call(
        functools.partial(merge_kernel, level, pieces),
        in_specs=in_vmem(3),
        out_shape=tuple(shapes),
        compiler_params=pltpu.CompilerParams(vmem_limit_bytes=16 << 20),
        cost_estimate=SMALL,
    )(keep, sums, got, after)


def finish_kernel(*refs):
    *pair_refs, _, out_ref = refs
    rows = math.prod(out_ref.shape[1:-1])
    at = 0
    for mine_ref, got_ref in zip(pair_refs[::2], pair_refs[1::2]):
        for i in range(mine_ref.shape[0]):
            out, _ = merge(
                mine_ref[i, :rows].astype(jnp.float32),
                unpack_tail(mine_ref[i, rows:], rows),
                got_ref[i, :rows].astype(jnp.float32),
                unpack_tail(got_ref[i, rows:], rows),
            )
            out_ref[at] = out.astype(jnp.bfloat16).reshape(out_ref.shape[1:])
            at += 1


def finish(pairs, shape, after):
    arrays = [array for pair in pairs for array in pair]
    return pl.pallas_call(
        finish_kernel,
        in_specs=in_vmem(len(arrays)),
        out_shape=jax.ShapeDtypeStruct(shape, jnp.bfloat16),
        compiler_params=pltpu.CompilerParams(vmem_limit_bytes=16 << 20),
        cost_estimate=SMALL,
    )(*arrays, after)


def place_kernel(levels, plan, *refs):
    part_refs = refs[: len(plan)]
    out_ref, sems = refs[-2:]
    copies = []
    for (head, own), ref in zip(plan, part_refs):
        blocks = ref.shape[1]
        bit = lax.rem(lax.axis_index("ctx"), 2) if levels > 1 else 0
        at = (bit if own else 1 - bit) * blocks
        for i in range(ref.shape[0]):
            there = out_ref.at[pl.ds(at, blocks), :, head + i]
            copies.append(pltpu.make_async_copy(ref.at[i], there, sems.at[len(copies)]))
    for copy in copies:
        copy.start()
    for copy in copies:
        copy.wait()


def place(out, parts, shape, levels, after):
    arrays = [array for array, _, _ in parts]
    plan = [(head, own) for _, head, own in parts]
    others = [after] if out is None else [after, out]
    return pl.pallas_call(
        functools.partial(place_kernel, levels, plan),
        in_specs=[pl.BlockSpec(memory_space=pltpu.VMEM)] * len(arrays)
        + [pl.BlockSpec(memory_space=pl.ANY), pl.BlockSpec(memory_space=pltpu.HBM)][: len(others)],
        out_specs=pl.BlockSpec(memory_space=pltpu.HBM),
        out_shape=pltpu.HBM(shape, jnp.bfloat16),
        input_output_aliases={} if out is None else {len(arrays) + 1: 0},
        scratch_shapes=[pltpu.SemaphoreType.DMA((sum(a.shape[0] for a in arrays),))],
        compiler_params=pltpu.CompilerParams(vmem_limit_bytes=16 << 20),
        cost_estimate=SMALL,
    )(*arrays, *others)


def on_device(shards, owners, queries, prompt_cache, suffix_cache, new_kv, ancestors, lengths):
    steps, per_owner, heads, group, size = queries.shape
    suffix_dev = suffix_cache.shape[2]
    shard = lax.axis_index("ctx")
    factor = math.log2(math.e) / math.sqrt(size)
    levels = shards.bit_length() - 1
    if shards != 1 << levels or levels < 2 or steps % 2 or suffix_dev != steps:
        raise ValueError("unsupported sizes")

    def swap(value, bit):
        return lax.ppermute(value, "ctx", [(i, i ^ (1 << bit)) for i in range(shards)])

    prompt_rows = prompt_cache.reshape(2, -1, size)
    mine, parents, extents = build_message(
        suffix_cache.reshape(2, -1, size),
        new_kv.reshape(steps, 2, -1, size),
        ancestors,
        lengths,
        heads,
    )
    row_list = [mine] + [
        lax.ppermute(mine, "dom", [(i, (i + hop) % owners) for i in range(owners)])
        for hop in range(1, owners)
    ]
    *prompt, bias = split_prompt(
        prompt_rows, parents, extents, heads, owners, suffix_dev
    )
    prompt = prompt[:heads], prompt[heads:]
    last = [bias]

    def follow(results):
        last[0] = results[0] if isinstance(results, (tuple, list)) else results
        return results

    messages = {}
    blocks = steps * per_owner >> (levels - 1)

    def run_attend(group, kept, begun=()):
        return follow(
            attend(queries, prompt, bias, row_list, group, kept, factor, begun, last[0])
        )

    def run_merges(group, got, parts, sizes):
        for level in range(1, levels):
            final = level == levels - 1
            results = follow(merge_parts(*parts, got, level, sizes if final else (), last[0]))
            if not final:
                got, parts = swap(results[0], level), results[1:]
        return [(send, swap(send, levels - 1)) for send in results]

    parts = []

    def run_finish(pairs):
        count = sum(send.shape[0] for send, _ in pairs)
        return follow(finish(pairs, (count, blocks, group, size), last[0]))

    def run_gather(head, done):
        count = done.shape[0]
        for level in range(levels - 2, 0, -1):
            other = swap(done, level)
            done = jnp.where(
                (shard >> level) % 2 == 1,
                jnp.concatenate([other, done], axis=1),
                jnp.concatenate([done, other], axis=1),
            )
        done = done.reshape(count, steps // 2, per_owner, group, size)
        parts.append((done, head, True))
        parts.append((swap(done, 0), head, False))

    first = max(heads // 2, 1)
    groups = [tuple(range(heads))[at : at + first] for at in range(0, heads, first)]
    begun = follow(begin(queries, prompt, groups[0], False, factor))
    arrived = []
    for number, one in enumerate(groups):
        arrived.append(swap(run_attend(one, False, () if number else begun), 0))
    pairs = []
    for number, one in enumerate(groups):
        sizes = (1,) * len(one) if number else (len(one),)
        pairs += run_merges(one, arrived[number], run_attend(one, True), sizes)
    head = 0
    for pair in pairs:
        run_gather(head, run_finish([pair]))
        head += pair[0].shape[0]
    late = [parts[-3], parts[-1]] if len(parts) > 4 else parts[-1:]
    early = [part for part in parts if not any(part is one for one in late)]
    out = place(None, early, queries.shape, levels, last[0]) if early else None
    return place(out, late, queries.shape, levels, last[0])


def solution(mesh):
    return jax.shard_map(
        functools.partial(on_device, mesh.shape["ctx"], mesh.shape["dom"]),
        mesh=mesh,
        in_specs=(
            P("groups", "dom", "tp", None, None),
            P("groups", "ctx", "tp", None),
            P("groups", "dom", "ctx", "tp", None),
            P("groups", None, "dom", "tp", None),
            P("groups", None),
            P("groups"),
        ),
        out_specs=P("groups", "dom", "tp", None, None),
        check_vma=False,
    )
```

```python
import functools
import math

import jax
import jax.numpy as jnp
from jax import lax
from jax.experimental import pallas as pl
from jax.experimental.pallas import tpu as pltpu
from jax.sharding import PartitionSpec as P

LANES = 128
HIDDEN = -1e30
NN = (((1,), (0,)), ((), ()))
NT = (((1,), (1,)), ((), ()))
SMALL = pl.CostEstimate(flops=0, bytes_accessed=4096, transcendentals=0)


def round_up(value, multiple):
    return -(-value // multiple) * multiple


def dot(a, b, dims):
    return lax.dot_general(a, b, dims, preferred_element_type=jnp.float32)


def eye_mask(rows):
    shape = (rows, LANES)
    return lax.broadcasted_iota(jnp.int32, shape, 0) == lax.broadcasted_iota(jnp.int32, shape, 1)


def column_to_lanes(column):
    rows = column.shape[0]
    block = min(rows, LANES)
    mask = eye_mask(block)
    return jnp.concatenate(
        [
            jnp.sum(jnp.where(mask, column[at : at + block], 0.0), axis=0, keepdims=True)
            for at in range(0, rows, block)
        ],
        axis=0,
    )


def lanes_to_column(lanes, rows):
    block = min(rows, LANES)
    mask = eye_mask(block)
    return jnp.concatenate(
        [
            jnp.sum(jnp.where(mask, lanes[i : i + 1], 0.0), axis=1, keepdims=True)
            for i in range(lanes.shape[0])
        ],
        axis=0,
    )


def tail_rows(rows):
    return round_up(3 * -(-rows // LANES), 16)


def pack_tail(column):
    lanes = column_to_lanes(column)
    high = lanes.astype(jnp.bfloat16).astype(jnp.float32)
    middle = (lanes - high).astype(jnp.bfloat16).astype(jnp.float32)
    low = lanes - high - middle
    parts = jnp.concatenate([high, middle, low], axis=0)
    spare = tail_rows(column.shape[0]) - parts.shape[0]
    return jnp.concatenate([parts, jnp.zeros((spare, LANES), jnp.float32)], axis=0).astype(
        jnp.bfloat16
    )


def unpack_tail(tail, rows):
    tail = tail.astype(jnp.float32)
    blocks = -(-rows // LANES)
    lanes = tail[:blocks] + tail[blocks : 2 * blocks] + tail[2 * blocks : 3 * blocks]
    return lanes_to_column(lanes, rows)


def in_hbm(array):
    return pltpu.with_memory_space_constraint(array, pltpu.HBM)


def message_kernel(
    heads, suffix_ref, new_ref, ancestors_ref, lengths_ref,
    out_ref, parents_ref, extents_ref, here, wide, sems,
):
    steps, each = new_ref.shape[0], new_ref.shape[2]
    total = here.shape[1]
    is_last = lax.axis_index("ctx") == lax.axis_size("ctx") - 1
    suffix_copy = pltpu.make_async_copy(suffix_ref, here, sems.at[0])
    token_copies = [
        pltpu.make_async_copy(
            new_ref.at[step], here.at[:, pl.ds(step * each, each)], sems.at[1 + step]
        )
        for step in range(steps)
    ]
    small = [
        pltpu.make_async_copy(ancestors_ref, parents_ref, sems.at[1 + steps]),
        pltpu.make_async_copy(lengths_ref, extents_ref, sems.at[2 + steps]),
    ]
    for copy in small:
        copy.start()

    @pl.when(is_last)
    def _():
        for copy in token_copies:
            copy.start()
        for copy in token_copies:
            copy.wait()

    @pl.when(jnp.logical_not(is_last))
    def _():
        suffix_copy.start()
        suffix_copy.wait()

    for kind in range(2):
        wide[kind] = here[kind].astype(jnp.float32)
        for head in range(heads):
            part = wide[kind, pl.ds(head, total // heads, stride=heads), :]
            out_ref[kind, head] = part.astype(out_ref.dtype)
    for copy in small:
        copy.wait()


def build_message(suffix, new, ancestors, lengths, heads):
    _, rows, size = suffix.shape
    lengths = lengths.reshape(1, -1)
    operands = (suffix, new, ancestors, lengths)
    return pl.pallas_call(
        functools.partial(message_kernel, heads),
        in_specs=[pl.BlockSpec(memory_space=pltpu.HBM)] * len(operands),
        out_shape=(
            jax.ShapeDtypeStruct((2, heads, rows // heads, size), suffix.dtype),
            jax.ShapeDtypeStruct(ancestors.shape, ancestors.dtype),
            jax.ShapeDtypeStruct(lengths.shape, lengths.dtype),
        ),
        scratch_shapes=[
            pltpu.VMEM(suffix.shape, suffix.dtype),
            pltpu.VMEM(suffix.shape, jnp.float32),
            pltpu.SemaphoreType.DMA((3 + new.shape[0],)),
        ],
        compiler_params=pltpu.CompilerParams(vmem_limit_bytes=24 << 20),
        cost_estimate=SMALL,
    )(*[in_hbm(operand) for operand in operands])


def iota(shape, axis):
    return lax.broadcasted_iota(jnp.int32, shape, axis)


def lineage_bias(ancestors_ref, lengths_ref, states, owners, suffix_dev):
    steps, particles = ancestors_ref.shape
    per_owner = particles // owners
    each = per_owner * suffix_dev
    my_owner = lax.axis_index("dom")
    my_shard = lax.axis_index("ctx")
    is_last = my_shard == lax.axis_size("ctx") - 1
    square = (particles, particles)
    same = iota(square, 0) == iota(square, 1)

    def as_column(row):
        return jnp.sum(jnp.where(same, row, 0), axis=1, keepdims=True)

    products = {}
    for step in range(steps):
        parent = as_column(ancestors_ref[step : step + 1, :])
        products[step - 1, step] = (parent == iota(square, 1)).astype(jnp.bfloat16)
    for length in range(2, steps + 1):
        for step in range(length - 1, steps):
            after = step - length
            middle = (step + after + 1) // 2
            both = dot(products[middle, step], products[after, middle], NN)
            products[after, step] = both.astype(jnp.bfloat16)
    for step in range(steps):
        states[step, :, :particles] = products[-1, step].astype(jnp.float32)
        for token in range(steps):
            here = slice((1 + token) * particles, (2 + token) * particles)
            if token < step:
                states[step, :, here] = products[token, step].astype(jnp.float32)
            else:
                states[step, :, here] = same.astype(jnp.float32) * float(token == step)
    rows = pl.ds(pl.multiple_of(my_owner * per_owner, per_owner), per_owner)
    mine = jnp.concatenate([states[step, rows, :] for step in range(steps)], axis=0)
    mine = mine.astype(jnp.bfloat16)
    lengths = as_column(lengths_ref[...])
    shape = (particles, owners * each)
    column = iota(shape, 1)
    source = column // each
    first = lax.rem(my_owner + owners - source, owners) * per_owner
    inner = column - source * each
    position = my_shard * suffix_dev + lax.rem(inner, suffix_dev)
    by_particle = iota(shape, 0) == first + inner // suffix_dev
    by_token = iota(shape, 0) == first + lax.rem(inner, per_owner)
    seen = [by_particle & (position < lengths) & jnp.logical_not(is_last)]
    seen += [by_token & (inner // per_owner == token) & is_last for token in range(steps)]
    table = jnp.concatenate([s.astype(jnp.bfloat16) for s in seen], axis=0)
    return jnp.where(dot(mine, table, NN) > 0.5, 0.0, HIDDEN)


def split_kernel(
    heads, block, owners, suffix_dev,
    rows_ref, parents_ref, extents_ref, *refs,
):
    out_refs = refs[: 2 * heads]
    bias_ref, here, wide, states, sems = refs[2 * heads :]
    total = out_refs[0].shape[0]
    places = [(kind, at) for kind in range(2) for at in range(0, total, block)]
    copies = [
        pltpu.make_async_copy(
            rows_ref.at[kind, pl.ds(at * heads, block * heads)],
            here.at[kind, pl.ds(at * heads, block * heads)],
            sems.at[i],
        )
        for i, (kind, at) in enumerate(places)
    ]
    for copy in copies:
        copy.start()
    bias_ref[...] = lineage_bias(parents_ref, extents_ref, states, owners, suffix_dev)
    for i, (kind, at) in enumerate(places):
        copies[i].wait()
        wide[i % 2] = here[kind, at * heads : (at + block) * heads].astype(jnp.float32)
        for head in range(heads):
            part = wide[i % 2, pl.ds(head, block, stride=heads), :]
            out_refs[kind * heads + head][at : at + block] = part.astype(rows_ref.dtype)


def split_prompt(rows, parents, extents, heads, owners, suffix_dev):
    total = rows.shape[1] // heads
    block = math.gcd(total, 512)
    size = rows.shape[2]
    steps, particles = parents.shape
    return pl.pallas_call(
        functools.partial(split_kernel, heads, block, owners, suffix_dev),
        in_specs=[pl.BlockSpec(memory_space=pltpu.HBM)]
        + [pl.BlockSpec(memory_space=pltpu.VMEM)] * 2,
        out_shape=(
            *[jax.ShapeDtypeStruct((total, size), rows.dtype)] * (2 * heads),
            jax.ShapeDtypeStruct(
                (steps * particles // owners, particles * suffix_dev), jnp.float32
            ),
        ),
        scratch_shapes=[
            pltpu.VMEM(rows.shape, rows.dtype),
            pltpu.VMEM((2, block * heads, size), jnp.float32),
            pltpu.VMEM((steps, particles, (1 + steps) * particles), jnp.float32),
            pltpu.SemaphoreType.DMA((2 * total // block,)),
        ],
        compiler_params=pltpu.CompilerParams(vmem_limit_bytes=24 << 20),
        cost_estimate=SMALL,
    )(in_hbm(rows), parents, extents)


def with_ones(values):
    return jnp.concatenate([values, jnp.ones_like(values)], axis=1)


def row_peak(scores):
    return jnp.max(scores, axis=1, keepdims=True)


def weigh(scores, factor, offset):
    return jnp.exp2(scores * factor - offset).astype(jnp.bfloat16)


def work_space(streams, rows, total, size):
    block = math.gcd(total, 512)
    return [
        pltpu.VMEM((3, rows, block), jnp.float32),
        pltpu.VMEM((streams, 2, rows, math.gcd(total, 2 * block)), jnp.bfloat16),
        pltpu.VMEM((streams * rows, 2 * size), jnp.float32),
    ]


def prompt_sum(streams, factor, scores, weights, sums):
    rows, total = streams[0][0].shape[0], streams[0][1].shape[0]
    block, wide = scores.shape[2], weights.shape[3]
    units = [(at, i) for at in range(0, total, block) for i in range(len(streams))]
    offsets = [None] * len(streams)

    def score(n):
        at, i = units[n]
        scores[n % 3] = dot(streams[i][0], streams[i][1][at : at + block], NT)

    def weight(n):
        at, i = units[n]
        if at == 0:
            top = row_peak(scores[n % 3])
            peak = streams[i][3]
            offsets[i] = (top if peak is None else jnp.maximum(top, peak)) * factor
        there = slice(at % wide, at % wide + block)
        weights[i, at // wide % 2, :, there] = weigh(scores[n % 3], factor, offsets[i])

    def gather(n):
        at, i = units[n]
        end = at + block
        if end % wide:
            return
        part = dot(weights[i, at // wide % 2], with_ones(streams[i][2][end - wide : end]), NN)
        here = slice(i * rows, (i + 1) * rows)
        sums[here] = part if end == wide else sums[here] + part

    score(0)
    score(1)
    for n in range(len(units)):
        if n + 2 < len(units):
            score(n + 2)
        weight(n)
        if n:
            gather(n - 1)
    gather(len(units) - 1)
    return offsets


def first_step(q_ref, kept):
    bit = lax.rem(lax.axis_index("ctx"), 2)
    return (bit if kept else 1 - bit) * (q_ref.shape[0] // 2)


def queries_of(q_ref, head, first, number):
    _, per_owner, _, group, size = q_ref.shape
    return q_ref[pl.ds(first, number), :, head].reshape(number * per_owner * group, size)


def prompt_kernel(heads, kept, factor, q_ref, *refs):
    k_refs, v_refs = refs[: len(heads)], refs[len(heads) : 2 * len(heads)]
    together_ref, offset_ref, scores, weights = refs[2 * len(heads) :]
    first, number = first_step(q_ref, kept), q_ref.shape[0] // 2
    streams = [
        (queries_of(q_ref, head, first, number), k_ref, v_ref, None)
        for head, k_ref, v_ref in zip(heads, k_refs, v_refs)
    ]
    offsets = prompt_sum(streams, factor, scores, weights, together_ref)
    offset = jnp.concatenate(offsets, axis=0)
    offset_ref[...] = jnp.broadcast_to(offset, offset_ref.shape)


def in_vmem(count, ordered=True):
    last = [pl.BlockSpec(memory_space=pl.ANY)] if ordered else []
    return [pl.BlockSpec(memory_space=pltpu.VMEM)] * count + last


def begin(queries, prompt, heads, kept, factor):
    steps, per_owner, _, group, size = queries.shape
    rows = steps * per_owner * group // 2
    keys, values = prompt
    space = work_space(len(heads), rows, keys[0].shape[0], size)
    return pl.pallas_call(
        functools.partial(prompt_kernel, heads, kept, factor),
        in_specs=in_vmem(1 + 2 * len(heads), False),
        out_shape=(
            jax.ShapeDtypeStruct((len(heads) * rows, 2 * size), jnp.float32),
            jax.ShapeDtypeStruct((len(heads) * rows, LANES), jnp.float32),
        ),
        scratch_shapes=space[:2],
        compiler_params=pltpu.CompilerParams(vmem_limit_bytes=24 << 20),
        cost_estimate=SMALL,
    )(queries, *[keys[head] for head in heads], *[values[head] for head in heads])


def attend_kernel(heads, kept, factor, owners, started, *refs):
    count = len(heads)
    q_ref, bias_ref = refs[:2]
    row_refs = refs[2 : 2 + owners]
    refs = refs[2 + owners :]
    k_refs, v_refs, refs = refs[:count], refs[count : 2 * count], refs[2 * count :]
    begun, refs = refs[: 2 * started], refs[2 * started + 1 :]
    if kept:
        out, log_sums, *work = refs
    else:
        send_ref, out, log_sums, *work = refs
    steps, per_owner, _, group, size = q_ref.shape
    columns = bias_ref.shape[1]
    number = steps // 2
    rows = number * per_owner * group
    start = first_step(q_ref, kept)

    def suffix_of(head, kind):
        return jnp.concatenate([ref[kind, head] for ref in row_refs], axis=0)

    def suffix_scores(q, head, first, number):
        at = pl.multiple_of(first * per_owner, per_owner)
        bias = bias_ref[pl.ds(at, number * per_owner), :]
        bias = jnp.broadcast_to(bias[:, None, :], (number * per_owner, group, columns))
        return dot(q, suffix_of(head, 0), NT) + bias.reshape(number * per_owner * group, columns)

    def store(i, at, together, offset):
        sums = together[:, size:]
        out[i, pl.ds(at, sums.shape[0]), :] = together[:, :size] / sums
        log_sums[i, pl.ds(at, sums.shape[0]), :] = offset + jnp.log2(sums)
        return sums

    queries = [queries_of(q_ref, head, start, number) for head in heads]
    extras = [suffix_scores(q, head, start, number) for q, head in zip(queries, heads)]
    if started:
        offsets = [begun[1][i * rows : (i + 1) * rows, :1] for i in range(count)]
        togethers = begun[0]
    else:
        streams = [(q, k, v, row_peak(e)) for q, k, v, e in zip(queries, k_refs, v_refs, extras)]
        offsets = prompt_sum(streams, factor, *work)
        togethers = work[-1]
    worst = []
    for i, head in enumerate(heads):
        weight = weigh(extras[i], factor, offsets[i])
        together = togethers[i * rows : (i + 1) * rows]
        together = together + dot(weight, with_ones(suffix_of(head, 1)), NN)
        worst.append(jnp.max(store(i, 0, together, offsets[i])))

    for i, head in enumerate(heads):

        @pl.when(jnp.logical_not(worst[i] < 2.0**100))
        def _():
            @pl.loop(0, number)
            def _(step):
                q = queries_of(q_ref, head, start + step, 1)
                extra = suffix_scores(q, head, start + step, 1)
                scores = dot(q, k_refs[i][...], NT)
                offset = jnp.maximum(row_peak(scores), row_peak(extra)) * factor
                weight = weigh(scores, factor, offset)
                together = dot(weight, with_ones(v_refs[i][...]), NN)
                weight = weigh(extra, factor, offset)
                together = together + dot(weight, with_ones(suffix_of(head, 1)), NN)
                here = per_owner * group
                store(i, pl.multiple_of(step * here, here), together, offset)

        if not kept:
            send_ref[i, :rows] = out[i].astype(jnp.bfloat16)
            send_ref[i, rows:] = pack_tail(log_sums[i, :, :1])


def attend(queries, prompt, bias, row_list, heads, kept, factor, begun, after):
    steps, per_owner, _, group, size = queries.shape
    rows = steps * per_owner * group // 2
    count = len(heads)
    keys, values = prompt
    operands = (
        queries, bias, *row_list,
        *[keys[head] for head in heads], *[values[head] for head in heads], *begun,
    )
    parts = [((count, rows, size), jnp.float32), ((count, rows, LANES), jnp.float32)]
    send = jax.ShapeDtypeStruct((count, rows + tail_rows(rows), size), jnp.bfloat16)
    space = work_space(count, rows, keys[0].shape[0], size)
    return pl.pallas_call(
        functools.partial(
            attend_kernel, heads, kept, factor, len(row_list), len(begun) // 2
        ),
        in_specs=in_vmem(len(operands)),
        out_shape=tuple(jax.ShapeDtypeStruct(*part) for part in parts) if kept else send,
        scratch_shapes=[*([] if kept else [pltpu.VMEM(*part) for part in parts]), *space],
        compiler_params=pltpu.CompilerParams(vmem_limit_bytes=32 << 20),
        cost_estimate=SMALL,
    )(*operands, after)


def merge(out_a, sum_a, out_b, sum_b):
    top = jnp.maximum(sum_a, sum_b)
    weight_a = jnp.exp2(sum_a - top)
    weight_b = jnp.exp2(sum_b - top)
    total = weight_a + weight_b
    return (out_a * weight_a + out_b * weight_b) / total, top + jnp.log2(total)


def merge_kernel(level, last, keep_ref, sums_ref, got_ref, _, *outs):
    rows = keep_ref.shape[1]
    half = rows // 2
    for at, i in enumerate(last or range(keep_ref.shape[0])):
        got_sum = unpack_tail(got_ref[i, rows:], rows)
        out, log_sum = merge(
            keep_ref[i], sums_ref[i][:, :1], got_ref[i, :rows].astype(jnp.float32), got_sum
        )
        if last:
            outs[at][0, :rows] = out.astype(jnp.bfloat16)
            outs[at][0, rows:] = pack_tail(log_sum)
        else:
            bit = lax.rem(lax.axis_index("ctx") >> level, 2) == 1
            send, keep, wide = outs

            def choose(first, value):
                return jnp.where(first, value[:half], value[half:])

            send[i, :half] = choose(bit, out).astype(jnp.bfloat16)
            send[i, half:] = pack_tail(choose(bit, log_sum))
            keep[i] = choose(~bit, out)
            wide[i] = jnp.broadcast_to(choose(~bit, log_sum), (half, LANES))


def merge_parts(keep, sums, got, level, last, after):
    count, rows, size = keep.shape
    part = rows if last else rows // 2
    message = (part + tail_rows(part), size)
    if last:
        shapes = [jax.ShapeDtypeStruct((1, *message), jnp.bfloat16)] * len(last)
    else:
        shapes = [
            jax.ShapeDtypeStruct((count, *message), jnp.bfloat16),
            jax.ShapeDtypeStruct((count, part, size), jnp.float32),
            jax.ShapeDtypeStruct((count, part, LANES), jnp.float32),
        ]
    return pl.pallas_call(
        functools.partial(merge_kernel, level, last),
        in_specs=in_vmem(3),
        out_shape=tuple(shapes),
        compiler_params=pltpu.CompilerParams(vmem_limit_bytes=16 << 20),
        cost_estimate=SMALL,
    )(keep, sums, got, after)


def finish_kernel(ready, *refs):
    *part_refs, mine_ref, got_ref, _, out_ref = refs
    rows = math.prod(out_ref.shape[1:-1])
    if ready:
        out_ref[: out_ref.shape[0] - 1] = part_refs[0][...]
    out, _ = merge(
        mine_ref[0, :rows].astype(jnp.float32),
        unpack_tail(mine_ref[0, rows:], rows),
        got_ref[0, :rows].astype(jnp.float32),
        unpack_tail(got_ref[0, rows:], rows),
    )
    out_ref[out_ref.shape[0] - 1] = out.astype(jnp.bfloat16).reshape(out_ref.shape[1:])


def finish(ready, pair, shape, after):
    arrays = (*ready, *pair)
    return pl.pallas_call(
        functools.partial(finish_kernel, len(ready)),
        in_specs=in_vmem(len(arrays)),
        out_shape=jax.ShapeDtypeStruct(shape, jnp.bfloat16),
        compiler_params=pltpu.CompilerParams(vmem_limit_bytes=16 << 20),
        cost_estimate=SMALL,
    )(*arrays, after)


def place_kernel(levels, plan, *refs):
    part_refs = refs[: len(plan)]
    out_ref, sems = refs[-2:]
    copies = []
    for (head, own), ref in zip(plan, part_refs):
        blocks = ref.shape[1]
        bit = lax.rem(lax.axis_index("ctx"), 2) if levels > 1 else 0
        at = (bit if own else 1 - bit) * blocks
        for i in range(ref.shape[0]):
            there = out_ref.at[pl.ds(at, blocks), :, head + i]
            copies.append(pltpu.make_async_copy(ref.at[i], there, sems.at[len(copies)]))
    for copy in copies:
        copy.start()
    for copy in copies:
        copy.wait()


def place(out, parts, shape, levels, after):
    arrays = [array for array, _, _ in parts]
    plan = [(head, own) for _, head, own in parts]
    others = [after] if out is None else [after, out]
    return pl.pallas_call(
        functools.partial(place_kernel, levels, plan),
        in_specs=[pl.BlockSpec(memory_space=pltpu.VMEM)] * len(arrays)
        + [pl.BlockSpec(memory_space=pl.ANY), pl.BlockSpec(memory_space=pltpu.HBM)][: len(others)],
        out_specs=pl.BlockSpec(memory_space=pltpu.HBM),
        out_shape=pltpu.HBM(shape, jnp.bfloat16),
        input_output_aliases={} if out is None else {len(arrays) + 1: 0},
        scratch_shapes=[pltpu.SemaphoreType.DMA((sum(a.shape[0] for a in arrays),))],
        compiler_params=pltpu.CompilerParams(vmem_limit_bytes=16 << 20),
        cost_estimate=SMALL,
    )(*arrays, *others)


def on_device(shards, owners, queries, prompt_cache, suffix_cache, new_kv, ancestors, lengths):
    steps, per_owner, heads, group, size = queries.shape
    suffix_dev = suffix_cache.shape[2]
    shard = lax.axis_index("ctx")
    factor = math.log2(math.e) / math.sqrt(size)
    levels = shards.bit_length() - 1
    if shards != 1 << levels or levels < 2 or steps % 2 or suffix_dev != steps:
        raise ValueError("unsupported sizes")

    def swap(value, bit):
        return lax.ppermute(value, "ctx", [(i, i ^ (1 << bit)) for i in range(shards)])

    prompt_rows = prompt_cache.reshape(2, -1, size)
    mine, parents, extents = build_message(
        suffix_cache.reshape(2, -1, size),
        new_kv.reshape(steps, 2, -1, size),
        ancestors,
        lengths,
        heads,
    )
    row_list = [mine] + [
        lax.ppermute(mine, "dom", [(i, (i + hop) % owners) for i in range(owners)])
        for hop in range(1, owners)
    ]
    *prompt, bias = split_prompt(
        prompt_rows, parents, extents, heads, owners, suffix_dev
    )
    prompt = prompt[:heads], prompt[heads:]
    last = [bias]

    def follow(results):
        last[0] = results[0] if isinstance(results, (tuple, list)) else results
        return results

    messages = {}
    blocks = steps * per_owner >> (levels - 1)

    def run_attend(group, kept, begun=()):
        return follow(
            attend(queries, prompt, bias, row_list, group, kept, factor, begun, last[0])
        )

    def run_halvings(got, kept):
        for level in range(1, levels - 1):
            send, *kept = follow(merge_parts(*kept, got, level, (), last[0]))
            got = swap(send, level)
        return (*kept, got)

    def run_exchange(held, which):
        results = follow(merge_parts(*held, levels - 1, which, last[0]))
        return [(send, swap(send, levels - 1)) for send in results]

    parts = []

    def run_finish(pair, ready=()):
        count = 1 + sum(one.shape[0] for one in ready)
        return follow(finish(ready, pair, (count, blocks, group, size), last[0]))

    def run_gather(head, done):
        count = done.shape[0]
        for level in range(levels - 2, 0, -1):
            other = swap(done, level)
            done = jnp.where(
                (shard >> level) % 2 == 1,
                jnp.concatenate([other, done], axis=1),
                jnp.concatenate([done, other], axis=1),
            )
        done = done.reshape(count, steps // 2, per_owner, group, size)
        parts.append((done, head, True))
        parts.append((swap(done, 0), head, False))

    first = max(heads // 2, 1)
    groups = [tuple(range(heads))[at : at + first] for at in range(0, heads, first)]
    begun = follow(begin(queries, prompt, groups[0], False, factor))
    arrived = []
    for number, one in enumerate(groups):
        arrived.append(swap(run_attend(one, False, () if number else begun), 0))
    ready = ()
    held = run_halvings(arrived[0], run_attend(groups[0], True))
    pairs = run_exchange(held, (0,))
    later = [run_attend(one, True) for one in groups[1:]]
    for i in range(1, len(groups[0])):
        pairs += run_exchange(held, (i,))
        ready = (run_finish(pairs.pop(0), ready),)
    others = []
    for number, (one, kept) in enumerate(zip(groups[1:], later)):
        held = run_halvings(arrived[1 + number], kept)
        others += run_exchange(held, tuple(range(len(one))))
    for pair in pairs:
        ready = (run_finish(pair, ready),)
    run_gather(0, ready[0])
    for i, pair in enumerate(others):
        run_gather(len(groups[0]) + i, run_finish(pair))
    late = [parts[-3], parts[-1]] if len(parts) > 4 else parts[-1:]
    early = [part for part in parts if not any(part is one for one in late)]
    out = place(None, early, queries.shape, levels, last[0]) if early else None
    return place(out, late, queries.shape, levels, last[0])


def solution(mesh):
    return jax.shard_map(
        functools.partial(on_device, mesh.shape["ctx"], mesh.shape["dom"]),
        mesh=mesh,
        in_specs=(
            P("groups", "dom", "tp", None, None),
            P("groups", "ctx", "tp", None),
            P("groups", "dom", "ctx", "tp", None),
            P("groups", None, "dom", "tp", None),
            P("groups", None),
            P("groups"),
        ),
        out_specs=P("groups", "dom", "tp", None, None),
        check_vma=False,
    )
```

```python
import functools
import math

import jax
import jax.numpy as jnp
from jax import lax
from jax.experimental import pallas as pl
from jax.experimental.pallas import tpu as pltpu
from jax.sharding import PartitionSpec as P

LANES = 128
HIDDEN = -1e30
NN = (((1,), (0,)), ((), ()))
NT = (((1,), (1,)), ((), ()))
SMALL = pl.CostEstimate(flops=0, bytes_accessed=4096, transcendentals=0)


def round_up(value, multiple):
    return -(-value // multiple) * multiple


def dot(a, b, dims):
    return lax.dot_general(a, b, dims, preferred_element_type=jnp.float32)


def eye_mask(rows):
    shape = (rows, LANES)
    return lax.broadcasted_iota(jnp.int32, shape, 0) == lax.broadcasted_iota(jnp.int32, shape, 1)


def column_to_lanes(column):
    rows = column.shape[0]
    block = min(rows, LANES)
    mask = eye_mask(block)
    return jnp.concatenate(
        [
            jnp.sum(jnp.where(mask, column[at : at + block], 0.0), axis=0, keepdims=True)
            for at in range(0, rows, block)
        ],
        axis=0,
    )


def lanes_to_column(lanes, rows):
    block = min(rows, LANES)
    mask = eye_mask(block)
    return jnp.concatenate(
        [
            jnp.sum(jnp.where(mask, lanes[i : i + 1], 0.0), axis=1, keepdims=True)
            for i in range(lanes.shape[0])
        ],
        axis=0,
    )


def tail_rows(rows):
    return round_up(3 * -(-rows // LANES), 16)


def pack_tail(column):
    lanes = column_to_lanes(column)
    high = lanes.astype(jnp.bfloat16).astype(jnp.float32)
    middle = (lanes - high).astype(jnp.bfloat16).astype(jnp.float32)
    low = lanes - high - middle
    parts = jnp.concatenate([high, middle, low], axis=0)
    spare = tail_rows(column.shape[0]) - parts.shape[0]
    return jnp.concatenate([parts, jnp.zeros((spare, LANES), jnp.float32)], axis=0).astype(
        jnp.bfloat16
    )


def unpack_tail(tail, rows):
    tail = tail.astype(jnp.float32)
    blocks = -(-rows // LANES)
    lanes = tail[:blocks] + tail[blocks : 2 * blocks] + tail[2 * blocks : 3 * blocks]
    return lanes_to_column(lanes, rows)


def in_hbm(array):
    return pltpu.with_memory_space_constraint(array, pltpu.HBM)


def message_kernel(
    heads, suffix_ref, new_ref, ancestors_ref, lengths_ref,
    out_ref, parents_ref, extents_ref, here, wide, sems,
):
    steps, each = new_ref.shape[0], new_ref.shape[2]
    total = here.shape[1]
    is_last = lax.axis_index("ctx") == lax.axis_size("ctx") - 1
    suffix_copy = pltpu.make_async_copy(suffix_ref, here, sems.at[0])
    token_copies = [
        pltpu.make_async_copy(
            new_ref.at[step], here.at[:, pl.ds(step * each, each)], sems.at[1 + step]
        )
        for step in range(steps)
    ]
    small = [
        pltpu.make_async_copy(ancestors_ref, parents_ref, sems.at[1 + steps]),
        pltpu.make_async_copy(lengths_ref, extents_ref, sems.at[2 + steps]),
    ]
    for copy in small:
        copy.start()

    @pl.when(is_last)
    def _():
        for copy in token_copies:
            copy.start()
        for copy in token_copies:
            copy.wait()

    @pl.when(jnp.logical_not(is_last))
    def _():
        suffix_copy.start()
        suffix_copy.wait()

    for kind in range(2):
        wide[kind] = here[kind].astype(jnp.float32)
        for head in range(heads):
            part = wide[kind, pl.ds(head, total // heads, stride=heads), :]
            out_ref[kind, head] = part.astype(out_ref.dtype)
    for copy in small:
        copy.wait()


def build_message(suffix, new, ancestors, lengths, heads):
    _, rows, size = suffix.shape
    lengths = lengths.reshape(1, -1)
    operands = (suffix, new, ancestors, lengths)
    return pl.pallas_call(
        functools.partial(message_kernel, heads),
        in_specs=[pl.BlockSpec(memory_space=pltpu.HBM)] * len(operands),
        out_shape=(
            jax.ShapeDtypeStruct((2, heads, rows // heads, size), suffix.dtype),
            jax.ShapeDtypeStruct(ancestors.shape, ancestors.dtype),
            jax.ShapeDtypeStruct(lengths.shape, lengths.dtype),
        ),
        scratch_shapes=[
            pltpu.VMEM(suffix.shape, suffix.dtype),
            pltpu.VMEM(suffix.shape, jnp.float32),
            pltpu.SemaphoreType.DMA((3 + new.shape[0],)),
        ],
        compiler_params=pltpu.CompilerParams(vmem_limit_bytes=24 << 20),
        cost_estimate=SMALL,
    )(*[in_hbm(operand) for operand in operands])


def iota(shape, axis):
    return lax.broadcasted_iota(jnp.int32, shape, axis)


def lineage_bias(ancestors_ref, lengths_ref, states, owners, suffix_dev):
    steps, particles = ancestors_ref.shape
    per_owner = particles // owners
    each = per_owner * suffix_dev
    my_owner = lax.axis_index("dom")
    my_shard = lax.axis_index("ctx")
    is_last = my_shard == lax.axis_size("ctx") - 1
    square = (particles, particles)
    same = iota(square, 0) == iota(square, 1)

    def as_column(row):
        return jnp.sum(jnp.where(same, row, 0), axis=1, keepdims=True)

    products = {}
    for step in range(steps):
        parent = as_column(ancestors_ref[step : step + 1, :])
        products[step - 1, step] = (parent == iota(square, 1)).astype(jnp.bfloat16)
    for length in range(2, steps + 1):
        for step in range(length - 1, steps):
            after = step - length
            middle = (step + after + 1) // 2
            both = dot(products[middle, step], products[after, middle], NN)
            products[after, step] = both.astype(jnp.bfloat16)
    for step in range(steps):
        states[step, :, :particles] = products[-1, step].astype(jnp.float32)
        for token in range(steps):
            here = slice((1 + token) * particles, (2 + token) * particles)
            if token < step:
                states[step, :, here] = products[token, step].astype(jnp.float32)
            else:
                states[step, :, here] = same.astype(jnp.float32) * float(token == step)
    rows = pl.ds(pl.multiple_of(my_owner * per_owner, per_owner), per_owner)
    mine = jnp.concatenate([states[step, rows, :] for step in range(steps)], axis=0)
    mine = mine.astype(jnp.bfloat16)
    lengths = as_column(lengths_ref[...])
    shape = (particles, owners * each)
    column = iota(shape, 1)
    source = column // each
    first = lax.rem(my_owner + owners - source, owners) * per_owner
    inner = column - source * each
    position = my_shard * suffix_dev + lax.rem(inner, suffix_dev)
    by_particle = iota(shape, 0) == first + inner // suffix_dev
    by_token = iota(shape, 0) == first + lax.rem(inner, per_owner)
    seen = [by_particle & (position < lengths) & jnp.logical_not(is_last)]
    seen += [by_token & (inner // per_owner == token) & is_last for token in range(steps)]
    table = jnp.concatenate([s.astype(jnp.bfloat16) for s in seen], axis=0)
    return jnp.where(dot(mine, table, NN) > 0.5, 0.0, HIDDEN)


def split_kernel(
    heads, block, owners, suffix_dev,
    rows_ref, parents_ref, extents_ref, *refs,
):
    out_refs = refs[: 2 * heads]
    bias_ref, here, wide, states, sems = refs[2 * heads :]
    total = out_refs[0].shape[0]
    places = [(kind, at) for kind in range(2) for at in range(0, total, block)]
    copies = [
        pltpu.make_async_copy(
            rows_ref.at[kind, pl.ds(at * heads, block * heads)],
            here.at[kind, pl.ds(at * heads, block * heads)],
            sems.at[i],
        )
        for i, (kind, at) in enumerate(places)
    ]
    for copy in copies:
        copy.start()
    bias_ref[...] = lineage_bias(parents_ref, extents_ref, states, owners, suffix_dev)
    for i, (kind, at) in enumerate(places):
        copies[i].wait()
        wide[i % 2] = here[kind, at * heads : (at + block) * heads].astype(jnp.float32)
        for head in range(heads):
            part = wide[i % 2, pl.ds(head, block, stride=heads), :]
            out_refs[kind * heads + head][at : at + block] = part.astype(rows_ref.dtype)


def split_prompt(rows, parents, extents, heads, owners, suffix_dev):
    total = rows.shape[1] // heads
    block = math.gcd(total, 512)
    size = rows.shape[2]
    steps, particles = parents.shape
    return pl.pallas_call(
        functools.partial(split_kernel, heads, block, owners, suffix_dev),
        in_specs=[pl.BlockSpec(memory_space=pltpu.HBM)]
        + [pl.BlockSpec(memory_space=pltpu.VMEM)] * 2,
        out_shape=(
            *[jax.ShapeDtypeStruct((total, size), rows.dtype)] * (2 * heads),
            jax.ShapeDtypeStruct(
                (steps * particles // owners, particles * suffix_dev), jnp.float32
            ),
        ),
        scratch_shapes=[
            pltpu.VMEM(rows.shape, rows.dtype),
            pltpu.VMEM((2, block * heads, size), jnp.float32),
            pltpu.VMEM((steps, particles, (1 + steps) * particles), jnp.float32),
            pltpu.SemaphoreType.DMA((2 * total // block,)),
        ],
        compiler_params=pltpu.CompilerParams(vmem_limit_bytes=24 << 20),
        cost_estimate=SMALL,
    )(in_hbm(rows), parents, extents)


def with_ones(values):
    return jnp.concatenate([values, jnp.ones_like(values)], axis=1)


def row_peak(scores):
    return jnp.max(scores, axis=1, keepdims=True)


def weigh(scores, factor, offset):
    return jnp.exp2(scores * factor - offset).astype(jnp.bfloat16)


def work_space(streams, rows, total, size):
    block = math.gcd(total, 512)
    return [
        pltpu.VMEM((3, rows, block), jnp.float32),
        pltpu.VMEM((streams, 2, rows, math.gcd(total, 2 * block)), jnp.bfloat16),
        pltpu.VMEM((streams * rows, 2 * size), jnp.float32),
    ]


def prompt_sum(streams, factor, scores, weights, sums):
    rows, total = streams[0][0].shape[0], streams[0][1].shape[0]
    block, wide = scores.shape[2], weights.shape[3]
    units = [(at, i) for at in range(0, total, block) for i in range(len(streams))]
    offsets = [None] * len(streams)

    def score(n):
        at, i = units[n]
        scores[n % 3] = dot(streams[i][0], streams[i][1][at : at + block], NT)

    def weight(n):
        at, i = units[n]
        if at == 0:
            top = row_peak(scores[n % 3])
            peak = streams[i][3]
            offsets[i] = (top if peak is None else jnp.maximum(top, peak)) * factor
        there = slice(at % wide, at % wide + block)
        weights[i, at // wide % 2, :, there] = weigh(scores[n % 3], factor, offsets[i])

    def gather(n):
        at, i = units[n]
        end = at + block
        if end % wide:
            return
        part = dot(weights[i, at // wide % 2], with_ones(streams[i][2][end - wide : end]), NN)
        here = slice(i * rows, (i + 1) * rows)
        sums[here] = part if end == wide else sums[here] + part

    score(0)
    score(1)
    for n in range(len(units)):
        if n + 2 < len(units):
            score(n + 2)
        weight(n)
        if n:
            gather(n - 1)
    gather(len(units) - 1)
    return offsets


def first_step(q_ref, kept):
    bit = lax.rem(lax.axis_index("ctx"), 2)
    return (bit if kept else 1 - bit) * (q_ref.shape[0] // 2)


def queries_of(q_ref, head, first, number):
    _, per_owner, _, group, size = q_ref.shape
    return q_ref[pl.ds(first, number), :, head].reshape(number * per_owner * group, size)


def prompt_kernel(heads, kept, factor, q_ref, *refs):
    k_refs, v_refs = refs[: len(heads)], refs[len(heads) : 2 * len(heads)]
    together_ref, offset_ref, scores, weights = refs[2 * len(heads) :]
    first, number = first_step(q_ref, kept), q_ref.shape[0] // 2
    streams = [
        (queries_of(q_ref, head, first, number), k_ref, v_ref, None)
        for head, k_ref, v_ref in zip(heads, k_refs, v_refs)
    ]
    offsets = prompt_sum(streams, factor, scores, weights, together_ref)
    offset = jnp.concatenate(offsets, axis=0)
    offset_ref[...] = jnp.broadcast_to(offset, offset_ref.shape)


def in_vmem(count, ordered=True):
    last = [pl.BlockSpec(memory_space=pl.ANY)] if ordered else []
    return [pl.BlockSpec(memory_space=pltpu.VMEM)] * count + last


def begin(queries, prompt, heads, kept, factor):
    steps, per_owner, _, group, size = queries.shape
    rows = steps * per_owner * group // 2
    keys, values = prompt
    space = work_space(len(heads), rows, keys[0].shape[0], size)
    return pl.pallas_call(
        functools.partial(prompt_kernel, heads, kept, factor),
        in_specs=in_vmem(1 + 2 * len(heads), False),
        out_shape=(
            jax.ShapeDtypeStruct((len(heads) * rows, 2 * size), jnp.float32),
            jax.ShapeDtypeStruct((len(heads) * rows, LANES), jnp.float32),
        ),
        scratch_shapes=space[:2],
        compiler_params=pltpu.CompilerParams(vmem_limit_bytes=24 << 20),
        cost_estimate=SMALL,
    )(queries, *[keys[head] for head in heads], *[values[head] for head in heads])


def attend_kernel(heads, kept, factor, owners, started, *refs):
    count = len(heads)
    q_ref, bias_ref = refs[:2]
    row_refs = refs[2 : 2 + owners]
    refs = refs[2 + owners :]
    k_refs, v_refs, refs = refs[:count], refs[count : 2 * count], refs[2 * count :]
    begun, refs = refs[: 2 * started], refs[2 * started + 1 :]
    if kept:
        out, log_sums, *work = refs
    else:
        send_ref, out, log_sums, *work = refs
    steps, per_owner, _, group, size = q_ref.shape
    columns = bias_ref.shape[1]
    number = steps // 2
    rows = number * per_owner * group
    start = first_step(q_ref, kept)

    def suffix_of(head, kind):
        return jnp.concatenate([ref[kind, head] for ref in row_refs], axis=0)

    def suffix_scores(q, head, first, number):
        at = pl.multiple_of(first * per_owner, per_owner)
        bias = bias_ref[pl.ds(at, number * per_owner), :]
        bias = jnp.broadcast_to(bias[:, None, :], (number * per_owner, group, columns))
        return dot(q, suffix_of(head, 0), NT) + bias.reshape(number * per_owner * group, columns)

    def store(i, at, together, offset):
        sums = together[:, size:]
        out[i, pl.ds(at, sums.shape[0]), :] = together[:, :size] / sums
        log_sums[i, pl.ds(at, sums.shape[0]), :] = offset + jnp.log2(sums)
        return sums

    queries = [queries_of(q_ref, head, start, number) for head in heads]
    extras = [suffix_scores(q, head, start, number) for q, head in zip(queries, heads)]
    if started:
        offsets = [begun[1][i * rows : (i + 1) * rows, :1] for i in range(count)]
        togethers = begun[0]
    else:
        streams = [(q, k, v, row_peak(e)) for q, k, v, e in zip(queries, k_refs, v_refs, extras)]
        offsets = prompt_sum(streams, factor, *work)
        togethers = work[-1]
    worst = []
    for i, head in enumerate(heads):
        weight = weigh(extras[i], factor, offsets[i])
        together = togethers[i * rows : (i + 1) * rows]
        together = together + dot(weight, with_ones(suffix_of(head, 1)), NN)
        worst.append(jnp.max(store(i, 0, together, offsets[i])))

    for i, head in enumerate(heads):

        @pl.when(jnp.logical_not(worst[i] < 2.0**100))
        def _():
            @pl.loop(0, number)
            def _(step):
                q = queries_of(q_ref, head, start + step, 1)
                extra = suffix_scores(q, head, start + step, 1)
                scores = dot(q, k_refs[i][...], NT)
                offset = jnp.maximum(row_peak(scores), row_peak(extra)) * factor
                weight = weigh(scores, factor, offset)
                together = dot(weight, with_ones(v_refs[i][...]), NN)
                weight = weigh(extra, factor, offset)
                together = together + dot(weight, with_ones(suffix_of(head, 1)), NN)
                here = per_owner * group
                store(i, pl.multiple_of(step * here, here), together, offset)

        if not kept:
            send_ref[i, :rows] = out[i].astype(jnp.bfloat16)
            send_ref[i, rows:] = pack_tail(log_sums[i, :, :1])


def attend(queries, prompt, bias, row_list, heads, kept, factor, begun, after):
    steps, per_owner, _, group, size = queries.shape
    rows = steps * per_owner * group // 2
    count = len(heads)
    keys, values = prompt
    operands = (
        queries, bias, *row_list,
        *[keys[head] for head in heads], *[values[head] for head in heads], *begun,
    )
    parts = [((count, rows, size), jnp.float32), ((count, rows, LANES), jnp.float32)]
    send = jax.ShapeDtypeStruct((count, rows + tail_rows(rows), size), jnp.bfloat16)
    space = work_space(count, rows, keys[0].shape[0], size)
    return pl.pallas_call(
        functools.partial(
            attend_kernel, heads, kept, factor, len(row_list), len(begun) // 2
        ),
        in_specs=in_vmem(len(operands)),
        out_shape=tuple(jax.ShapeDtypeStruct(*part) for part in parts) if kept else send,
        scratch_shapes=[*([] if kept else [pltpu.VMEM(*part) for part in parts]), *space],
        compiler_params=pltpu.CompilerParams(vmem_limit_bytes=32 << 20),
        cost_estimate=SMALL,
    )(*operands, after)


def merge(out_a, sum_a, out_b, sum_b):
    top = jnp.maximum(sum_a, sum_b)
    weight_a = jnp.exp2(sum_a - top)
    weight_b = jnp.exp2(sum_b - top)
    total = weight_a + weight_b
    return (out_a * weight_a + out_b * weight_b) / total, top + jnp.log2(total)


def merge_kernel(level, pieces, keep_ref, sums_ref, got_ref, _, *outs):
    rows = keep_ref.shape[1]
    half = rows // 2
    places = [(out, i) for out, count in zip(outs, pieces) for i in range(count)]
    for i in range(keep_ref.shape[0]):
        got_sum = unpack_tail(got_ref[i, rows:], rows)
        out, log_sum = merge(
            keep_ref[i], sums_ref[i][:, :1], got_ref[i, :rows].astype(jnp.float32), got_sum
        )
        if pieces:
            there, at = places[i]
            there[at, :rows] = out.astype(jnp.bfloat16)
            there[at, rows:] = pack_tail(log_sum)
        else:
            bit = lax.rem(lax.axis_index("ctx") >> level, 2) == 1
            send, keep, wide = outs

            def choose(first, value):
                return jnp.where(first, value[:half], value[half:])

            send[i, :half] = choose(bit, out).astype(jnp.bfloat16)
            send[i, half:] = pack_tail(choose(bit, log_sum))
            keep[i] = choose(~bit, out)
            wide[i] = jnp.broadcast_to(choose(~bit, log_sum), (half, LANES))


def merge_parts(keep, sums, got, level, pieces, after):
    count, rows, size = keep.shape
    part = rows if pieces else rows // 2
    message = part + tail_rows(part)
    shapes = [jax.ShapeDtypeStruct((n, message, size), jnp.bfloat16) for n in pieces or (count,)]
    if not pieces:
        shapes.append(jax.ShapeDtypeStruct((count, part, size), jnp.float32))
        shapes.append(jax.ShapeDtypeStruct((count, part, LANES), jnp.float32))
    return pl.pallas_call(
        functools.partial(merge_kernel, level, pieces),
        in_specs=in_vmem(3),
        out_shape=tuple(shapes),
        compiler_params=pltpu.CompilerParams(vmem_limit_bytes=16 << 20),
        cost_estimate=SMALL,
    )(keep, sums, got, after)


def finish_kernel(*refs):
    *pair_refs, _, out_ref = refs
    rows = math.prod(out_ref.shape[1:-1])
    at = 0
    for mine_ref, got_ref in zip(pair_refs[::2], pair_refs[1::2]):
        for i in range(mine_ref.shape[0]):
            out, _ = merge(
                mine_ref[i, :rows].astype(jnp.float32),
                unpack_tail(mine_ref[i, rows:], rows),
                got_ref[i, :rows].astype(jnp.float32),
                unpack_tail(got_ref[i, rows:], rows),
            )
            out_ref[at] = out.astype(jnp.bfloat16).reshape(out_ref.shape[1:])
            at += 1


def finish(pairs, shape, after):
    arrays = [array for pair in pairs for array in pair]
    return pl.pallas_call(
        finish_kernel,
        in_specs=in_vmem(len(arrays)),
        out_shape=jax.ShapeDtypeStruct(shape, jnp.bfloat16),
        compiler_params=pltpu.CompilerParams(vmem_limit_bytes=16 << 20),
        cost_estimate=SMALL,
    )(*arrays, after)


def place_kernel(levels, plan, *refs):
    part_refs = refs[: len(plan)]
    out_ref, sems = refs[-2:]
    copies = []
    for (head, own), ref in zip(plan, part_refs):
        blocks = ref.shape[1]
        bit = lax.rem(lax.axis_index("ctx"), 2) if levels > 1 else 0
        at = (bit if own else 1 - bit) * blocks
        for i in range(ref.shape[0]):
            there = out_ref.at[pl.ds(at, blocks), :, head + i]
            copies.append(pltpu.make_async_copy(ref.at[i], there, sems.at[len(copies)]))
    for copy in copies:
        copy.start()
    for copy in copies:
        copy.wait()


def place(out, parts, shape, levels, after):
    arrays = [array for array, _, _ in parts]
    plan = [(head, own) for _, head, own in parts]
    others = [after] if out is None else [after, out]
    return pl.pallas_call(
        functools.partial(place_kernel, levels, plan),
        in_specs=[pl.BlockSpec(memory_space=pltpu.VMEM)] * len(arrays)
        + [pl.BlockSpec(memory_space=pl.ANY), pl.BlockSpec(memory_space=pltpu.HBM)][: len(others)],
        out_specs=pl.BlockSpec(memory_space=pltpu.HBM),
        out_shape=pltpu.HBM(shape, jnp.bfloat16),
        input_output_aliases={} if out is None else {len(arrays) + 1: 0},
        scratch_shapes=[pltpu.SemaphoreType.DMA((sum(a.shape[0] for a in arrays),))],
        compiler_params=pltpu.CompilerParams(vmem_limit_bytes=16 << 20),
        cost_estimate=SMALL,
    )(*arrays, *others)


def on_device(shards, owners, queries, prompt_cache, suffix_cache, new_kv, ancestors, lengths):
    steps, per_owner, heads, group, size = queries.shape
    suffix_dev = suffix_cache.shape[2]
    shard = lax.axis_index("ctx")
    factor = math.log2(math.e) / math.sqrt(size)
    levels = shards.bit_length() - 1
    if shards != 1 << levels or levels < 2 or steps % 2 or suffix_dev != steps:
        raise ValueError("unsupported sizes")

    def swap(value, bit):
        return lax.ppermute(value, "ctx", [(i, i ^ (1 << bit)) for i in range(shards)])

    prompt_rows = prompt_cache.reshape(2, -1, size)
    mine, parents, extents = build_message(
        suffix_cache.reshape(2, -1, size),
        new_kv.reshape(steps, 2, -1, size),
        ancestors,
        lengths,
        heads,
    )
    row_list = [mine] + [
        lax.ppermute(mine, "dom", [(i, (i + hop) % owners) for i in range(owners)])
        for hop in range(1, owners)
    ]
    *prompt, bias = split_prompt(
        prompt_rows, parents, extents, heads, owners, suffix_dev
    )
    prompt = prompt[:heads], prompt[heads:]
    last = [bias]

    def follow(results):
        last[0] = results[0] if isinstance(results, (tuple, list)) else results
        return results

    messages = {}
    blocks = steps * per_owner >> (levels - 1)

    def run_attend(group, kept, begun=()):
        return follow(
            attend(queries, prompt, bias, row_list, group, kept, factor, begun, last[0])
        )

    def run_merges(group, got, parts, sizes):
        for level in range(1, levels):
            final = level == levels - 1
            results = follow(merge_parts(*parts, got, level, sizes if final else (), last[0]))
            if not final:
                got, parts = swap(results[0], level), results[1:]
        return [(send, swap(send, levels - 1)) for send in results]

    parts = []

    def run_finish(pairs):
        count = sum(send.shape[0] for send, _ in pairs)
        return follow(finish(pairs, (count, blocks, group, size), last[0]))

    def run_gather(head, done):
        count = done.shape[0]
        for level in range(levels - 2, 0, -1):
            other = swap(done, level)
            done = jnp.where(
                (shard >> level) % 2 == 1,
                jnp.concatenate([other, done], axis=1),
                jnp.concatenate([done, other], axis=1),
            )
        done = done.reshape(count, steps // 2, per_owner, group, size)
        parts.append((done, head, True))
        parts.append((swap(done, 0), head, False))

    first = max(heads // 2, 1)
    groups = [tuple(range(heads))[at : at + first] for at in range(0, heads, first)]
    begun = follow(begin(queries, prompt, groups[0], False, factor))
    arrived = []
    for number, one in enumerate(groups):
        arrived.append(swap(run_attend(one, False, () if number else begun), 0))
    pairs = []
    for number, one in enumerate(groups):
        sizes = (1,) * len(one) if number else (len(one),)
        pairs += run_merges(one, arrived[number], run_attend(one, True), sizes)
    head = 0
    for pair in pairs:
        run_gather(head, run_finish([pair]))
        head += pair[0].shape[0]
    late = [parts[-3], parts[-1]] if len(parts) > 4 else parts[-1:]
    early = [part for part in parts if not any(part is one for one in late)]
    out = place(None, early, queries.shape, levels, last[0]) if early else None
    return place(out, late, queries.shape, levels, last[0])


def solution(mesh):
    return jax.shard_map(
        functools.partial(on_device, mesh.shape["ctx"], mesh.shape["dom"]),
        mesh=mesh,
        in_specs=(
            P("groups", "dom", "tp", None, None),
            P("groups", "ctx", "tp", None),
            P("groups", "dom", "ctx", "tp", None),
            P("groups", None, "dom", "tp", None),
            P("groups", None),
            P("groups"),
        ),
        out_specs=P("groups", "dom", "tp", None, None),
        check_vma=False,
    )
```

```python
import functools
import math

import jax
import jax.numpy as jnp
from jax import lax
from jax.experimental import pallas as pl
from jax.experimental.pallas import tpu as pltpu
from jax.sharding import PartitionSpec as P

LANES = 128
HIDDEN = -1e30
NN = (((1,), (0,)), ((), ()))
NT = (((1,), (1,)), ((), ()))
SMALL = pl.CostEstimate(flops=0, bytes_accessed=4096, transcendentals=0)


def round_up(value, multiple):
    return -(-value // multiple) * multiple


def dot(a, b, dims):
    return lax.dot_general(a, b, dims, preferred_element_type=jnp.float32)


def eye_mask(rows):
    shape = (rows, LANES)
    return lax.broadcasted_iota(jnp.int32, shape, 0) == lax.broadcasted_iota(jnp.int32, shape, 1)


def column_to_lanes(column):
    rows = column.shape[0]
    block = min(rows, LANES)
    mask = eye_mask(block)
    return jnp.concatenate(
        [
            jnp.sum(jnp.where(mask, column[at : at + block], 0.0), axis=0, keepdims=True)
            for at in range(0, rows, block)
        ],
        axis=0,
    )


def lanes_to_column(lanes, rows):
    block = min(rows, LANES)
    mask = eye_mask(block)
    return jnp.concatenate(
        [
            jnp.sum(jnp.where(mask, lanes[i : i + 1], 0.0), axis=1, keepdims=True)
            for i in range(lanes.shape[0])
        ],
        axis=0,
    )


def tail_rows(rows):
    return round_up(3 * -(-rows // LANES), 16)


def message_shape(rows, size):
    return rows + tail_rows(rows), size


def pack_tail(column):
    lanes = column_to_lanes(column)
    high = lanes.astype(jnp.bfloat16).astype(jnp.float32)
    middle = (lanes - high).astype(jnp.bfloat16).astype(jnp.float32)
    low = lanes - high - middle
    parts = jnp.concatenate([high, middle, low], axis=0)
    spare = tail_rows(column.shape[0]) - parts.shape[0]
    return jnp.concatenate([parts, jnp.zeros((spare, LANES), jnp.float32)], axis=0).astype(
        jnp.bfloat16
    )


def unpack_tail(tail, rows):
    tail = tail.astype(jnp.float32)
    blocks = -(-rows // LANES)
    lanes = tail[:blocks] + tail[blocks : 2 * blocks] + tail[2 * blocks : 3 * blocks]
    return lanes_to_column(lanes, rows)


def in_hbm(array):
    return pltpu.with_memory_space_constraint(array, pltpu.HBM)


def message_kernel(
    heads, suffix_ref, new_ref, ancestors_ref, lengths_ref,
    out_ref, parents_ref, extents_ref, here, wide, sems,
):
    steps, each = new_ref.shape[0], new_ref.shape[2]
    total = here.shape[1]
    is_last = lax.axis_index("ctx") == lax.axis_size("ctx") - 1
    suffix_copy = pltpu.make_async_copy(suffix_ref, here, sems.at[0])
    token_copies = [
        pltpu.make_async_copy(
            new_ref.at[step], here.at[:, pl.ds(step * each, each)], sems.at[1 + step]
        )
        for step in range(steps)
    ]
    small = [
        pltpu.make_async_copy(ancestors_ref, parents_ref, sems.at[1 + steps]),
        pltpu.make_async_copy(lengths_ref, extents_ref, sems.at[2 + steps]),
    ]
    for copy in small:
        copy.start()

    @pl.when(is_last)
    def _():
        for copy in token_copies:
            copy.start()
        for copy in token_copies:
            copy.wait()

    @pl.when(jnp.logical_not(is_last))
    def _():
        suffix_copy.start()
        suffix_copy.wait()

    for kind in range(2):
        wide[kind] = here[kind].astype(jnp.float32)
        for head in range(heads):
            part = wide[kind, pl.ds(head, total // heads, stride=heads), :]
            out_ref[kind, head] = part.astype(out_ref.dtype)
    for copy in small:
        copy.wait()


def build_message(suffix, new, ancestors, lengths, heads):
    _, rows, size = suffix.shape
    lengths = lengths.reshape(1, -1)
    operands = (suffix, new, ancestors, lengths)
    return pl.pallas_call(
        functools.partial(message_kernel, heads),
        in_specs=[pl.BlockSpec(memory_space=pltpu.HBM)] * len(operands),
        out_shape=(
            jax.ShapeDtypeStruct((2, heads, rows // heads, size), suffix.dtype),
            jax.ShapeDtypeStruct(ancestors.shape, ancestors.dtype),
            jax.ShapeDtypeStruct(lengths.shape, lengths.dtype),
        ),
        scratch_shapes=[
            pltpu.VMEM(suffix.shape, suffix.dtype),
            pltpu.VMEM(suffix.shape, jnp.float32),
            pltpu.SemaphoreType.DMA((3 + new.shape[0],)),
        ],
        compiler_params=pltpu.CompilerParams(vmem_limit_bytes=24 << 20),
        cost_estimate=SMALL,
    )(*[in_hbm(operand) for operand in operands])


def iota(shape, axis):
    return lax.broadcasted_iota(jnp.int32, shape, axis)


def lineage_bias(ancestors_ref, lengths_ref, states, owners, suffix_dev):
    steps, particles = ancestors_ref.shape
    per_owner = particles // owners
    each = per_owner * suffix_dev
    my_owner = lax.axis_index("dom")
    my_shard = lax.axis_index("ctx")
    is_last = my_shard == lax.axis_size("ctx") - 1
    square = (particles, particles)
    same = iota(square, 0) == iota(square, 1)

    def as_column(row):
        return jnp.sum(jnp.where(same, row, 0), axis=1, keepdims=True)

    products = {}
    for step in range(steps):
        parent = as_column(ancestors_ref[step : step + 1, :])
        products[step - 1, step] = (parent == iota(square, 1)).astype(jnp.bfloat16)
    for length in range(2, steps + 1):
        for step in range(length - 1, steps):
            after = step - length
            middle = (step + after + 1) // 2
            both = dot(products[middle, step], products[after, middle], NN)
            products[after, step] = both.astype(jnp.bfloat16)
    for step in range(steps):
        states[step, :, :particles] = products[-1, step].astype(jnp.float32)
        for token in range(steps):
            here = slice((1 + token) * particles, (2 + token) * particles)
            if token < step:
                states[step, :, here] = products[token, step].astype(jnp.float32)
            else:
                states[step, :, here] = same.astype(jnp.float32) * float(token == step)
    rows = pl.ds(pl.multiple_of(my_owner * per_owner, per_owner), per_owner)
    mine = jnp.concatenate([states[step, rows, :] for step in range(steps)], axis=0)
    mine = mine.astype(jnp.bfloat16)
    lengths = as_column(lengths_ref[...])
    shape = (particles, owners * each)
    column = iota(shape, 1)
    source = column // each
    first = lax.rem(my_owner + owners - source, owners) * per_owner
    inner = column - source * each
    position = my_shard * suffix_dev + lax.rem(inner, suffix_dev)
    by_particle = iota(shape, 0) == first + inner // suffix_dev
    by_token = iota(shape, 0) == first + lax.rem(inner, per_owner)
    seen = [by_particle & (position < lengths) & jnp.logical_not(is_last)]
    seen += [by_token & (inner // per_owner == token) & is_last for token in range(steps)]
    table = jnp.concatenate([s.astype(jnp.bfloat16) for s in seen], axis=0)
    return jnp.where(dot(mine, table, NN) > 0.5, 0.0, HIDDEN)


def split_kernel(
    heads, block, owners, suffix_dev,
    rows_ref, parents_ref, extents_ref, *refs,
):
    out_refs = refs[: 2 * heads]
    bias_ref, here, wide, states, sems = refs[2 * heads :]
    total = out_refs[0].shape[0]
    places = [(kind, at) for kind in range(2) for at in range(0, total, block)]
    copies = [
        pltpu.make_async_copy(
            rows_ref.at[kind, pl.ds(at * heads, block * heads)],
            here.at[kind, pl.ds(at * heads, block * heads)],
            sems.at[i],
        )
        for i, (kind, at) in enumerate(places)
    ]
    for copy in copies:
        copy.start()
    bias_ref[...] = lineage_bias(parents_ref, extents_ref, states, owners, suffix_dev)
    for i, (kind, at) in enumerate(places):
        copies[i].wait()
        wide[i % 2] = here[kind, at * heads : (at + block) * heads].astype(jnp.float32)
        for head in range(heads):
            part = wide[i % 2, pl.ds(head, block, stride=heads), :]
            out_refs[kind * heads + head][at : at + block] = part.astype(rows_ref.dtype)


def split_prompt(rows, parents, extents, heads, owners, suffix_dev):
    total = rows.shape[1] // heads
    block = math.gcd(total, 512)
    size = rows.shape[2]
    steps, particles = parents.shape
    return pl.pallas_call(
        functools.partial(split_kernel, heads, block, owners, suffix_dev),
        in_specs=[pl.BlockSpec(memory_space=pltpu.HBM)]
        + [pl.BlockSpec(memory_space=pltpu.VMEM)] * 2,
        out_shape=(
            *[jax.ShapeDtypeStruct((total, size), rows.dtype)] * (2 * heads),
            jax.ShapeDtypeStruct(
                (steps * particles // owners, particles * suffix_dev), jnp.float32
            ),
        ),
        scratch_shapes=[
            pltpu.VMEM(rows.shape, rows.dtype),
            pltpu.VMEM((2, block * heads, size), jnp.float32),
            pltpu.VMEM((steps, particles, (1 + steps) * particles), jnp.float32),
            pltpu.SemaphoreType.DMA((2 * total // block,)),
        ],
        compiler_params=pltpu.CompilerParams(vmem_limit_bytes=24 << 20),
        cost_estimate=SMALL,
    )(in_hbm(rows), parents, extents)


def with_ones(values):
    return jnp.concatenate([values, jnp.ones_like(values)], axis=1)


def row_peak(scores):
    return jnp.max(scores, axis=1, keepdims=True)


def weigh(scores, factor, offset):
    return jnp.exp2(scores * factor - offset).astype(jnp.bfloat16)


def work_space(streams, rows, total, size):
    block = math.gcd(total, 512)
    return [
        pltpu.VMEM((3, rows, block), jnp.float32),
        pltpu.VMEM((streams, 2, rows, math.gcd(total, 2 * block)), jnp.bfloat16),
        pltpu.VMEM((streams * rows, 2 * size), jnp.float32),
    ]


def prompt_sum(streams, factor, scores, weights, sums):
    rows, total = streams[0][0].shape[0], streams[0][1].shape[0]
    block, wide = scores.shape[2], weights.shape[3]
    units = [(at, i) for at in range(0, total, block) for i in range(len(streams))]
    offsets = [None] * len(streams)

    def score(n):
        at, i = units[n]
        scores[n % 3] = dot(streams[i][0], streams[i][1][at : at + block], NT)

    def weight(n):
        at, i = units[n]
        if at == 0:
            top = row_peak(scores[n % 3])
            peak = streams[i][3]
            offsets[i] = (top if peak is None else jnp.maximum(top, peak)) * factor
        there = slice(at % wide, at % wide + block)
        weights[i, at // wide % 2, :, there] = weigh(scores[n % 3], factor, offsets[i])

    def gather(n):
        at, i = units[n]
        end = at + block
        if end % wide:
            return
        part = dot(weights[i, at // wide % 2], with_ones(streams[i][2][end - wide : end]), NN)
        here = slice(i * rows, (i + 1) * rows)
        sums[here] = part if end == wide else sums[here] + part

    score(0)
    score(1)
    for n in range(len(units)):
        if n + 2 < len(units):
            score(n + 2)
        weight(n)
        if n:
            gather(n - 1)
    gather(len(units) - 1)
    return offsets


def first_step(q_ref, kept):
    bit = lax.rem(lax.axis_index("ctx"), 2)
    return (bit if kept else 1 - bit) * (q_ref.shape[0] // 2)


def queries_of(q_ref, head, first, number):
    _, per_owner, _, group, size = q_ref.shape
    return q_ref[pl.ds(first, number), :, head].reshape(number * per_owner * group, size)


def prompt_kernel(heads, kept, factor, q_ref, *refs):
    k_refs, v_refs = refs[: len(heads)], refs[len(heads) : 2 * len(heads)]
    together_ref, offset_ref, scores, weights = refs[2 * len(heads) :]
    first, number = first_step(q_ref, kept), q_ref.shape[0] // 2
    streams = [
        (queries_of(q_ref, head, first, number), k_ref, v_ref, None)
        for head, k_ref, v_ref in zip(heads, k_refs, v_refs)
    ]
    offsets = prompt_sum(streams, factor, scores, weights, together_ref)
    offset = jnp.concatenate(offsets, axis=0)
    offset_ref[...] = jnp.broadcast_to(offset, offset_ref.shape)


def in_vmem(count, ordered=True):
    last = [pl.BlockSpec(memory_space=pl.ANY)] if ordered else []
    return [pl.BlockSpec(memory_space=pltpu.VMEM)] * count + last


def begin(queries, prompt, heads, kept, factor):
    steps, per_owner, _, group, size = queries.shape
    rows = steps * per_owner * group // 2
    keys, values = prompt
    space = work_space(len(heads), rows, keys[0].shape[0], size)
    return pl.pallas_call(
        functools.partial(prompt_kernel, heads, kept, factor),
        in_specs=in_vmem(1 + 2 * len(heads), False),
        out_shape=(
            jax.ShapeDtypeStruct((len(heads) * rows, 2 * size), jnp.float32),
            jax.ShapeDtypeStruct((len(heads) * rows, LANES), jnp.float32),
        ),
        scratch_shapes=space[:2],
        compiler_params=pltpu.CompilerParams(vmem_limit_bytes=24 << 20),
        cost_estimate=SMALL,
    )(queries, *[keys[head] for head in heads], *[values[head] for head in heads])


def attend_kernel(heads, kept, factor, owners, started, *refs):
    count = len(heads)
    q_ref, bias_ref = refs[:2]
    row_refs = refs[2 : 2 + owners]
    refs = refs[2 + owners :]
    k_refs, v_refs, refs = refs[:count], refs[count : 2 * count], refs[2 * count :]
    begun, refs = refs[: 2 * started], refs[2 * started + 1 :]
    if kept:
        out, log_sums, *work = refs
    else:
        send_ref, out, log_sums, *work = refs
    steps, per_owner, _, group, size = q_ref.shape
    columns = bias_ref.shape[1]
    number = steps // 2
    rows = number * per_owner * group
    start = first_step(q_ref, kept)

    def suffix_of(head, kind):
        return jnp.concatenate([ref[kind, head] for ref in row_refs], axis=0)

    def suffix_scores(q, head, first, number):
        at = pl.multiple_of(first * per_owner, per_owner)
        bias = bias_ref[pl.ds(at, number * per_owner), :]
        bias = jnp.broadcast_to(bias[:, None, :], (number * per_owner, group, columns))
        return dot(q, suffix_of(head, 0), NT) + bias.reshape(number * per_owner * group, columns)

    def store(i, at, together, offset):
        sums = together[:, size:]
        out[i, pl.ds(at, sums.shape[0]), :] = together[:, :size] / sums
        log_sums[i, pl.ds(at, sums.shape[0]), :] = offset + jnp.log2(sums)
        return sums

    queries = [queries_of(q_ref, head, start, number) for head in heads]
    extras = [suffix_scores(q, head, start, number) for q, head in zip(queries, heads)]
    if started:
        offsets = [begun[1][i * rows : (i + 1) * rows, :1] for i in range(count)]
        togethers = begun[0]
    else:
        streams = [(q, k, v, row_peak(e)) for q, k, v, e in zip(queries, k_refs, v_refs, extras)]
        offsets = prompt_sum(streams, factor, *work)
        togethers = work[-1]
    worst = []
    for i, head in enumerate(heads):
        weight = weigh(extras[i], factor, offsets[i])
        together = togethers[i * rows : (i + 1) * rows]
        together = together + dot(weight, with_ones(suffix_of(head, 1)), NN)
        worst.append(jnp.max(store(i, 0, together, offsets[i])))

    for i, head in enumerate(heads):

        @pl.when(jnp.logical_not(worst[i] < 2.0**100))
        def _():
            @pl.loop(0, number)
            def _(step):
                q = queries_of(q_ref, head, start + step, 1)
                extra = suffix_scores(q, head, start + step, 1)
                scores = dot(q, k_refs[i][...], NT)
                offset = jnp.maximum(row_peak(scores), row_peak(extra)) * factor
                weight = weigh(scores, factor, offset)
                together = dot(weight, with_ones(v_refs[i][...]), NN)
                weight = weigh(extra, factor, offset)
                together = together + dot(weight, with_ones(suffix_of(head, 1)), NN)
                here = per_owner * group
                store(i, pl.multiple_of(step * here, here), together, offset)

    if not kept:
        for i in range(count):
            send_ref[i * rows : (i + 1) * rows] = out[i].astype(jnp.bfloat16)
        column = jnp.concatenate([log_sums[i, :, :1] for i in range(count)], axis=0)
        send_ref[count * rows :] = pack_tail(column)


def attend(queries, prompt, bias, row_list, heads, kept, factor, begun, after):
    steps, per_owner, _, group, size = queries.shape
    rows = steps * per_owner * group // 2
    count = len(heads)
    keys, values = prompt
    operands = (
        queries, bias, *row_list,
        *[keys[head] for head in heads], *[values[head] for head in heads], *begun,
    )
    parts = [((count, rows, size), jnp.float32), ((count, rows, LANES), jnp.float32)]
    send = jax.ShapeDtypeStruct(message_shape(count * rows, size), jnp.bfloat16)
    space = work_space(count, rows, keys[0].shape[0], size)
    return pl.pallas_call(
        functools.partial(
            attend_kernel, heads, kept, factor, len(row_list), len(begun) // 2
        ),
        in_specs=in_vmem(len(operands)),
        out_shape=tuple(jax.ShapeDtypeStruct(*part) for part in parts) if kept else send,
        scratch_shapes=[*([] if kept else [pltpu.VMEM(*part) for part in parts]), *space],
        compiler_params=pltpu.CompilerParams(vmem_limit_bytes=32 << 20),
        cost_estimate=SMALL,
    )(*operands, after)


def merge(out_a, sum_a, out_b, sum_b):
    top = jnp.maximum(sum_a, sum_b)
    weight_a = jnp.exp2(sum_a - top)
    weight_b = jnp.exp2(sum_b - top)
    total = weight_a + weight_b
    return (out_a * weight_a + out_b * weight_b) / total, top + jnp.log2(total)


def merge_kernel(level, last, keep_ref, sums_ref, got_ref, _, *outs):
    count, rows = keep_ref.shape[:2]
    got_sums = unpack_tail(got_ref[count * rows :], count * rows)
    merged = []
    for i in range(count):
        here = slice(i * rows, (i + 1) * rows)
        got = got_ref[here].astype(jnp.float32)
        merged.append(merge(keep_ref[i], sums_ref[i][:, :1], got, got_sums[here]))
    part = rows if last else rows // 2
    bit = lax.rem(lax.axis_index("ctx") >> level, 2) == 1

    def choose(first, value):
        return value if last else jnp.where(first, value[:part], value[part:])

    send = outs[0]
    for i, (out, _) in enumerate(merged):
        send[i * part : (i + 1) * part] = choose(bit, out).astype(jnp.bfloat16)
    send[count * part :] = pack_tail(
        jnp.concatenate([choose(bit, log_sum) for _, log_sum in merged], axis=0)
    )
    if not last:
        _, keep, wide = outs
        for i, (out, log_sum) in enumerate(merged):
            keep[i] = choose(~bit, out)
            wide[i] = jnp.broadcast_to(choose(~bit, log_sum), (part, LANES))


def merge_parts(keep, sums, got, level, last, after):
    count, rows, size = keep.shape
    part = rows if last else rows // 2
    shapes = [jax.ShapeDtypeStruct(message_shape(count * part, size), jnp.bfloat16)]
    if not last:
        shapes.append(jax.ShapeDtypeStruct((count, part, size), jnp.float32))
        shapes.append(jax.ShapeDtypeStruct((count, part, LANES), jnp.float32))
    return pl.pallas_call(
        functools.partial(merge_kernel, level, last),
        in_specs=in_vmem(3),
        out_shape=tuple(shapes),
        compiler_params=pltpu.CompilerParams(vmem_limit_bytes=16 << 20),
        cost_estimate=SMALL,
    )(keep, sums, got, after)


def finish_kernel(mine_ref, got_ref, _, out_ref):
    count, rows = out_ref.shape[0], math.prod(out_ref.shape[1:-1])
    mine_sums = unpack_tail(mine_ref[count * rows :], count * rows)
    got_sums = unpack_tail(got_ref[count * rows :], count * rows)
    for i in range(count):
        here = slice(i * rows, (i + 1) * rows)
        out, _ = merge(
            mine_ref[here].astype(jnp.float32),
            mine_sums[here],
            got_ref[here].astype(jnp.float32),
            got_sums[here],
        )
        out_ref[i] = out.astype(jnp.bfloat16).reshape(out_ref.shape[1:])


def finish(mine, got, shape, after):
    return pl.pallas_call(
        finish_kernel,
        in_specs=in_vmem(2),
        out_shape=jax.ShapeDtypeStruct(shape, jnp.bfloat16),
        compiler_params=pltpu.CompilerParams(vmem_limit_bytes=16 << 20),
        cost_estimate=SMALL,
    )(mine, got, after)


def place_kernel(levels, plan, *refs):
    part_refs = refs[: len(plan)]
    out_ref, sems = refs[-2:]
    copies = []
    for (head, own), ref in zip(plan, part_refs):
        blocks = ref.shape[1]
        bit = lax.rem(lax.axis_index("ctx"), 2) if levels > 1 else 0
        at = (bit if own else 1 - bit) * blocks
        for i in range(ref.shape[0]):
            there = out_ref.at[pl.ds(at, blocks), :, head + i]
            copies.append(pltpu.make_async_copy(ref.at[i], there, sems.at[len(copies)]))
    for copy in copies:
        copy.start()
    for copy in copies:
        copy.wait()


def place(out, parts, shape, levels, after):
    arrays = [array for array, _, _ in parts]
    plan = [(head, own) for _, head, own in parts]
    others = [after] if out is None else [after, out]
    return pl.pallas_call(
        functools.partial(place_kernel, levels, plan),
        in_specs=[pl.BlockSpec(memory_space=pltpu.VMEM)] * len(arrays)
        + [pl.BlockSpec(memory_space=pl.ANY), pl.BlockSpec(memory_space=pltpu.HBM)][: len(others)],
        out_specs=pl.BlockSpec(memory_space=pltpu.HBM),
        out_shape=pltpu.HBM(shape, jnp.bfloat16),
        input_output_aliases={} if out is None else {len(arrays) + 1: 0},
        scratch_shapes=[pltpu.SemaphoreType.DMA((sum(a.shape[0] for a in arrays),))],
        compiler_params=pltpu.CompilerParams(vmem_limit_bytes=16 << 20),
        cost_estimate=SMALL,
    )(*arrays, *others)


def on_device(shards, owners, queries, prompt_cache, suffix_cache, new_kv, ancestors, lengths):
    steps, per_owner, heads, group, size = queries.shape
    suffix_dev = suffix_cache.shape[2]
    shard = lax.axis_index("ctx")
    factor = math.log2(math.e) / math.sqrt(size)
    levels = shards.bit_length() - 1
    if shards != 1 << levels or levels < 2 or steps % 2 or suffix_dev != steps:
        raise ValueError("unsupported sizes")

    def swap(value, bit):
        return lax.ppermute(value, "ctx", [(i, i ^ (1 << bit)) for i in range(shards)])

    prompt_rows = prompt_cache.reshape(2, -1, size)
    mine, parents, extents = build_message(
        suffix_cache.reshape(2, -1, size),
        new_kv.reshape(steps, 2, -1, size),
        ancestors,
        lengths,
        heads,
    )
    row_list = [mine] + [
        lax.ppermute(mine, "dom", [(i, (i + hop) % owners) for i in range(owners)])
        for hop in range(1, owners)
    ]
    *prompt, bias = split_prompt(
        prompt_rows, parents, extents, heads, owners, suffix_dev
    )
    prompt = prompt[:heads], prompt[heads:]
    last = [bias]

    def follow(results):
        last[0] = results[0] if isinstance(results, (tuple, list)) else results
        return results

    messages = {}
    blocks = steps * per_owner >> (levels - 1)

    def run_attend(group, kept, begun=()):
        return follow(
            attend(queries, prompt, bias, row_list, group, kept, factor, begun, last[0])
        )

    def run_merges(got, parts):
        for level in range(1, levels):
            send, *parts = follow(merge_parts(*parts, got, level, level == levels - 1, last[0]))
            got = swap(send, level)
        return send, got

    parts = []

    def run_finish(count, send, got):
        return follow(finish(send, got, (count, blocks, group, size), last[0]))

    def run_gather(head, done):
        count = done.shape[0]
        for level in range(levels - 2, 0, -1):
            other = swap(done, level)
            done = jnp.where(
                (shard >> level) % 2 == 1,
                jnp.concatenate([other, done], axis=1),
                jnp.concatenate([done, other], axis=1),
            )
        done = done.reshape(count, steps // 2, per_owner, group, size)
        parts.append((done, head, True))
        parts.append((swap(done, 0), head, False))

    first = max(heads // 2, 1)
    groups = [tuple(range(heads))[at : at + first] for at in range(0, heads, first)]
    begun = follow(begin(queries, prompt, groups[0], False, factor))
    arrived = []
    for number, one in enumerate(groups):
        arrived.append(swap(run_attend(one, False, () if number else begun), 0))
    pairs = [run_merges(got, run_attend(one, True)) for one, got in zip(groups, arrived)]
    for one, pair in zip(groups, pairs):
        run_gather(one[0], run_finish(len(one), *pair))
    late = parts[-1:]
    early = [part for part in parts if not any(part is one for one in late)]
    out = place(None, early, queries.shape, levels, last[0]) if early else None
    return place(out, late, queries.shape, levels, last[0])


def solution(mesh):
    return jax.shard_map(
        functools.partial(on_device, mesh.shape["ctx"], mesh.shape["dom"]),
        mesh=mesh,
        in_specs=(
            P("groups", "dom", "tp", None, None),
            P("groups", "ctx", "tp", None),
            P("groups", "dom", "ctx", "tp", None),
            P("groups", None, "dom", "tp", None),
            P("groups", None),
            P("groups"),
        ),
        out_specs=P("groups", "dom", "tp", None, None),
        check_vma=False,
    )
```

```python
import functools
import math

import jax
import jax.numpy as jnp
from jax import lax
from jax.experimental import pallas as pl
from jax.experimental.pallas import tpu as pltpu
from jax.sharding import PartitionSpec as P

LANES = 128
HIDDEN = -1e30
NN = (((1,), (0,)), ((), ()))
NT = (((1,), (1,)), ((), ()))
SMALL = pl.CostEstimate(flops=0, bytes_accessed=4096, transcendentals=0)


def round_up(value, multiple):
    return -(-value // multiple) * multiple


def dot(a, b, dims):
    return lax.dot_general(a, b, dims, preferred_element_type=jnp.float32)


def eye_mask(rows):
    shape = (rows, LANES)
    return lax.broadcasted_iota(jnp.int32, shape, 0) == lax.broadcasted_iota(jnp.int32, shape, 1)


def column_to_lanes(column):
    rows = column.shape[0]
    block = min(rows, LANES)
    mask = eye_mask(block)
    return jnp.concatenate(
        [
            jnp.sum(jnp.where(mask, column[at : at + block], 0.0), axis=0, keepdims=True)
            for at in range(0, rows, block)
        ],
        axis=0,
    )


def lanes_to_column(lanes, rows):
    block = min(rows, LANES)
    mask = eye_mask(block)
    return jnp.concatenate(
        [
            jnp.sum(jnp.where(mask, lanes[i : i + 1], 0.0), axis=1, keepdims=True)
            for i in range(lanes.shape[0])
        ],
        axis=0,
    )


def tail_rows(rows):
    return round_up(3 * -(-rows // LANES), 16)


def message_shape(rows, size):
    return rows + tail_rows(rows), size


def pack_tail(column):
    lanes = column_to_lanes(column)
    high = lanes.astype(jnp.bfloat16).astype(jnp.float32)
    middle = (lanes - high).astype(jnp.bfloat16).astype(jnp.float32)
    low = lanes - high - middle
    parts = jnp.concatenate([high, middle, low], axis=0)
    spare = tail_rows(column.shape[0]) - parts.shape[0]
    return jnp.concatenate([parts, jnp.zeros((spare, LANES), jnp.float32)], axis=0).astype(
        jnp.bfloat16
    )


def unpack_tail(tail, rows):
    tail = tail.astype(jnp.float32)
    blocks = -(-rows // LANES)
    lanes = tail[:blocks] + tail[blocks : 2 * blocks] + tail[2 * blocks : 3 * blocks]
    return lanes_to_column(lanes, rows)


def in_hbm(array):
    return pltpu.with_memory_space_constraint(array, pltpu.HBM)


def message_kernel(
    heads, suffix_ref, new_ref, ancestors_ref, lengths_ref,
    out_ref, parents_ref, extents_ref, here, wide, sems,
):
    steps, each = new_ref.shape[0], new_ref.shape[2]
    total = here.shape[1]
    is_last = lax.axis_index("ctx") == lax.axis_size("ctx") - 1
    suffix_copy = pltpu.make_async_copy(suffix_ref, here, sems.at[0])
    token_copies = [
        pltpu.make_async_copy(
            new_ref.at[step], here.at[:, pl.ds(step * each, each)], sems.at[1 + step]
        )
        for step in range(steps)
    ]
    small = [
        pltpu.make_async_copy(ancestors_ref, parents_ref, sems.at[1 + steps]),
        pltpu.make_async_copy(lengths_ref, extents_ref, sems.at[2 + steps]),
    ]
    for copy in small:
        copy.start()

    @pl.when(is_last)
    def _():
        for copy in token_copies:
            copy.start()
        for copy in token_copies:
            copy.wait()

    @pl.when(jnp.logical_not(is_last))
    def _():
        suffix_copy.start()
        suffix_copy.wait()

    for kind in range(2):
        wide[kind] = here[kind].astype(jnp.float32)
        for head in range(heads):
            part = wide[kind, pl.ds(head, total // heads, stride=heads), :]
            out_ref[kind, head] = part.astype(out_ref.dtype)
    for copy in small:
        copy.wait()


def build_message(suffix, new, ancestors, lengths, heads):
    _, rows, size = suffix.shape
    lengths = lengths.reshape(1, -1)
    operands = (suffix, new, ancestors, lengths)
    return pl.pallas_call(
        functools.partial(message_kernel, heads),
        in_specs=[pl.BlockSpec(memory_space=pltpu.HBM)] * len(operands),
        out_shape=(
            jax.ShapeDtypeStruct((2, heads, rows // heads, size), suffix.dtype),
            jax.ShapeDtypeStruct(ancestors.shape, ancestors.dtype),
            jax.ShapeDtypeStruct(lengths.shape, lengths.dtype),
        ),
        scratch_shapes=[
            pltpu.VMEM(suffix.shape, suffix.dtype),
            pltpu.VMEM(suffix.shape, jnp.float32),
            pltpu.SemaphoreType.DMA((3 + new.shape[0],)),
        ],
        compiler_params=pltpu.CompilerParams(vmem_limit_bytes=24 << 20),
        cost_estimate=SMALL,
    )(*[in_hbm(operand) for operand in operands])


def iota(shape, axis):
    return lax.broadcasted_iota(jnp.int32, shape, axis)


def lineage_bias(ancestors_ref, lengths_ref, states, owners, suffix_dev):
    steps, particles = ancestors_ref.shape
    per_owner = particles // owners
    each = per_owner * suffix_dev
    my_owner = lax.axis_index("dom")
    my_shard = lax.axis_index("ctx")
    is_last = my_shard == lax.axis_size("ctx") - 1
    square = (particles, particles)
    same = iota(square, 0) == iota(square, 1)

    def as_column(row):
        return jnp.sum(jnp.where(same, row, 0), axis=1, keepdims=True)

    products = {}
    for step in range(steps):
        parent = as_column(ancestors_ref[step : step + 1, :])
        products[step - 1, step] = (parent == iota(square, 1)).astype(jnp.bfloat16)
    for length in range(2, steps + 1):
        for step in range(length - 1, steps):
            after = step - length
            middle = (step + after + 1) // 2
            both = dot(products[middle, step], products[after, middle], NN)
            products[after, step] = both.astype(jnp.bfloat16)
    for step in range(steps):
        states[step, :, :particles] = products[-1, step].astype(jnp.float32)
        for token in range(steps):
            here = slice((1 + token) * particles, (2 + token) * particles)
            if token < step:
                states[step, :, here] = products[token, step].astype(jnp.float32)
            else:
                states[step, :, here] = same.astype(jnp.float32) * float(token == step)
    rows = pl.ds(pl.multiple_of(my_owner * per_owner, per_owner), per_owner)
    mine = jnp.concatenate([states[step, rows, :] for step in range(steps)], axis=0)
    mine = mine.astype(jnp.bfloat16)
    lengths = as_column(lengths_ref[...])
    shape = (particles, owners * each)
    column = iota(shape, 1)
    source = column // each
    first = lax.rem(my_owner + owners - source, owners) * per_owner
    inner = column - source * each
    position = my_shard * suffix_dev + lax.rem(inner, suffix_dev)
    by_particle = iota(shape, 0) == first + inner // suffix_dev
    by_token = iota(shape, 0) == first + lax.rem(inner, per_owner)
    seen = [by_particle & (position < lengths) & jnp.logical_not(is_last)]
    seen += [by_token & (inner // per_owner == token) & is_last for token in range(steps)]
    table = jnp.concatenate([s.astype(jnp.bfloat16) for s in seen], axis=0)
    return jnp.where(dot(mine, table, NN) > 0.5, 0.0, HIDDEN)


def split_kernel(
    heads, block, owners, suffix_dev,
    rows_ref, parents_ref, extents_ref, *refs,
):
    out_refs = refs[: 2 * heads]
    bias_ref, here, wide, states, sems = refs[2 * heads :]
    total = out_refs[0].shape[0]
    places = [(kind, at) for kind in range(2) for at in range(0, total, block)]
    copies = [
        pltpu.make_async_copy(
            rows_ref.at[kind, pl.ds(at * heads, block * heads)],
            here.at[kind, pl.ds(at * heads, block * heads)],
            sems.at[i],
        )
        for i, (kind, at) in enumerate(places)
    ]
    for copy in copies:
        copy.start()
    bias_ref[...] = lineage_bias(parents_ref, extents_ref, states, owners, suffix_dev)
    for i, (kind, at) in enumerate(places):
        copies[i].wait()
        wide[i % 2] = here[kind, at * heads : (at + block) * heads].astype(jnp.float32)
        for head in range(heads):
            part = wide[i % 2, pl.ds(head, block, stride=heads), :]
            out_refs[kind * heads + head][at : at + block] = part.astype(rows_ref.dtype)


def split_prompt(rows, parents, extents, heads, owners, suffix_dev):
    total = rows.shape[1] // heads
    block = math.gcd(total, 512)
    size = rows.shape[2]
    steps, particles = parents.shape
    return pl.pallas_call(
        functools.partial(split_kernel, heads, block, owners, suffix_dev),
        in_specs=[pl.BlockSpec(memory_space=pltpu.HBM)]
        + [pl.BlockSpec(memory_space=pltpu.VMEM)] * 2,
        out_shape=(
            *[jax.ShapeDtypeStruct((total, size), rows.dtype)] * (2 * heads),
            jax.ShapeDtypeStruct(
                (steps * particles // owners, particles * suffix_dev), jnp.float32
            ),
        ),
        scratch_shapes=[
            pltpu.VMEM(rows.shape, rows.dtype),
            pltpu.VMEM((2, block * heads, size), jnp.float32),
            pltpu.VMEM((steps, particles, (1 + steps) * particles), jnp.float32),
            pltpu.SemaphoreType.DMA((2 * total // block,)),
        ],
        compiler_params=pltpu.CompilerParams(vmem_limit_bytes=24 << 20),
        cost_estimate=SMALL,
    )(in_hbm(rows), parents, extents)


def row_peak(scores):
    return jnp.max(scores, axis=1, keepdims=True)


def weigh(scores, factor, offset):
    return jnp.exp2(scores * factor - offset)


def by_lane(weight):
    return sum(weight[:, at : at + LANES] for at in range(0, weight.shape[1], LANES))


def work_space(streams, rows, total, size):
    block = math.gcd(total, 512)
    return [
        pltpu.VMEM((3, rows, block), jnp.float32),
        pltpu.VMEM((streams, 2, rows, math.gcd(total, 2 * block)), jnp.bfloat16),
        pltpu.VMEM((streams * rows, size), jnp.float32),
        pltpu.VMEM((streams * rows, LANES), jnp.float32),
    ]


def prompt_sum(streams, factor, scores, weights, sums, totals):
    rows, total = streams[0][0].shape[0], streams[0][1].shape[0]
    block, wide = scores.shape[2], weights.shape[3]
    units = [(at, i) for at in range(0, total, block) for i in range(len(streams))]
    offsets = [None] * len(streams)

    def score(n):
        at, i = units[n]
        scores[n % 3] = dot(streams[i][0], streams[i][1][at : at + block], NT)

    def weight(n):
        at, i = units[n]
        if at == 0:
            top = row_peak(scores[n % 3])
            peak = streams[i][3]
            offsets[i] = (top if peak is None else jnp.maximum(top, peak)) * factor
        there = slice(at % wide, at % wide + block)
        here = slice(i * rows, (i + 1) * rows)
        weight = weigh(scores[n % 3], factor, offsets[i])
        totals[here] = by_lane(weight) if at == 0 else totals[here] + by_lane(weight)
        weights[i, at // wide % 2, :, there] = weight.astype(jnp.bfloat16)

    def gather(n):
        at, i = units[n]
        end = at + block
        if end % wide:
            return
        part = dot(weights[i, at // wide % 2], streams[i][2][end - wide : end], NN)
        here = slice(i * rows, (i + 1) * rows)
        sums[here] = part if end == wide else sums[here] + part

    score(0)
    score(1)
    for n in range(len(units)):
        if n + 2 < len(units):
            score(n + 2)
        weight(n)
        if n:
            gather(n - 1)
    gather(len(units) - 1)
    return offsets


def first_step(q_ref, kept):
    bit = lax.rem(lax.axis_index("ctx"), 2)
    return (bit if kept else 1 - bit) * (q_ref.shape[0] // 2)


def queries_of(q_ref, head, first, number):
    _, per_owner, _, group, size = q_ref.shape
    return q_ref[pl.ds(first, number), :, head].reshape(number * per_owner * group, size)


def prompt_kernel(heads, kept, factor, q_ref, *refs):
    k_refs, v_refs = refs[: len(heads)], refs[len(heads) : 2 * len(heads)]
    sums_ref, totals_ref, offset_ref, scores, weights = refs[2 * len(heads) :]
    first, number = first_step(q_ref, kept), q_ref.shape[0] // 2
    streams = [
        (queries_of(q_ref, head, first, number), k_ref, v_ref, None)
        for head, k_ref, v_ref in zip(heads, k_refs, v_refs)
    ]
    offsets = prompt_sum(streams, factor, scores, weights, sums_ref, totals_ref)
    offset = jnp.concatenate(offsets, axis=0)
    offset_ref[...] = jnp.broadcast_to(offset, offset_ref.shape)


def in_vmem(count, ordered=True):
    last = [pl.BlockSpec(memory_space=pl.ANY)] if ordered else []
    return [pl.BlockSpec(memory_space=pltpu.VMEM)] * count + last


def begin(queries, prompt, heads, kept, factor):
    steps, per_owner, _, group, size = queries.shape
    rows = steps * per_owner * group // 2
    keys, values = prompt
    space = work_space(len(heads), rows, keys[0].shape[0], size)
    return pl.pallas_call(
        functools.partial(prompt_kernel, heads, kept, factor),
        in_specs=in_vmem(1 + 2 * len(heads), False),
        out_shape=(
            jax.ShapeDtypeStruct((len(heads) * rows, size), jnp.float32),
            *[jax.ShapeDtypeStruct((len(heads) * rows, LANES), jnp.float32)] * 2,
        ),
        scratch_shapes=space[:2],
        compiler_params=pltpu.CompilerParams(vmem_limit_bytes=24 << 20),
        cost_estimate=SMALL,
    )(queries, *[keys[head] for head in heads], *[values[head] for head in heads])


def attend_kernel(heads, kept, factor, owners, started, *refs):
    count = len(heads)
    q_ref, bias_ref = refs[:2]
    row_refs = refs[2 : 2 + owners]
    refs = refs[2 + owners :]
    k_refs, v_refs, refs = refs[:count], refs[count : 2 * count], refs[2 * count :]
    begun, refs = refs[: 3 * started], refs[3 * started + 1 :]
    if kept:
        out, log_sums, *work = refs
    else:
        send_ref, out, log_sums, *work = refs
    steps, per_owner, _, group, size = q_ref.shape
    columns = bias_ref.shape[1]
    number = steps // 2
    rows = number * per_owner * group
    start = first_step(q_ref, kept)

    def suffix_of(head, kind):
        return jnp.concatenate([ref[kind, head] for ref in row_refs], axis=0)

    def suffix_scores(q, head, first, number):
        at = pl.multiple_of(first * per_owner, per_owner)
        bias = bias_ref[pl.ds(at, number * per_owner), :]
        bias = jnp.broadcast_to(bias[:, None, :], (number * per_owner, group, columns))
        return dot(q, suffix_of(head, 0), NT) + bias.reshape(number * per_owner * group, columns)

    def store(i, at, sums, total, offset):
        total = jnp.sum(total, axis=1, keepdims=True)
        here = pl.ds(at, sums.shape[0])
        out[i, here, :] = sums / total
        log_sums[i, here, :] = jnp.broadcast_to(offset + jnp.log2(total), (sums.shape[0], LANES))
        return total

    queries = [queries_of(q_ref, head, start, number) for head in heads]
    extras = [suffix_scores(q, head, start, number) for q, head in zip(queries, heads)]
    if started:
        offsets = [begun[2][i * rows : (i + 1) * rows, :1] for i in range(count)]
        sums, totals = begun[:2]
    else:
        streams = [(q, k, v, row_peak(e)) for q, k, v, e in zip(queries, k_refs, v_refs, extras)]
        offsets = prompt_sum(streams, factor, *work)
        sums, totals = work[-2:]
    worst = []
    for i, head in enumerate(heads):
        here = slice(i * rows, (i + 1) * rows)
        weight = weigh(extras[i], factor, offsets[i])
        total = totals[here] + by_lane(weight)
        both = sums[here] + dot(weight.astype(jnp.bfloat16), suffix_of(head, 1), NN)
        worst.append(jnp.max(store(i, 0, both, total, offsets[i])))

    for i, head in enumerate(heads):

        @pl.when(jnp.logical_not(worst[i] < 2.0**100))
        def _():
            @pl.loop(0, number)
            def _(step):
                q = queries_of(q_ref, head, start + step, 1)
                extra = suffix_scores(q, head, start + step, 1)
                scores = dot(q, k_refs[i][...], NT)
                offset = jnp.maximum(row_peak(scores), row_peak(extra)) * factor
                weight = weigh(scores, factor, offset)
                both = dot(weight.astype(jnp.bfloat16), v_refs[i][...], NN)
                total = by_lane(weight)
                weight = weigh(extra, factor, offset)
                both = both + dot(weight.astype(jnp.bfloat16), suffix_of(head, 1), NN)
                here = per_owner * group
                at = pl.multiple_of(step * here, here)
                store(i, at, both, total + by_lane(weight), offset)

    if not kept:
        for i in range(count):
            send_ref[i * rows : (i + 1) * rows] = out[i].astype(jnp.bfloat16)
        column = jnp.concatenate([log_sums[i, :, :1] for i in range(count)], axis=0)
        send_ref[count * rows :] = pack_tail(column)


def attend(queries, prompt, bias, row_list, heads, kept, factor, begun, after):
    steps, per_owner, _, group, size = queries.shape
    rows = steps * per_owner * group // 2
    count = len(heads)
    keys, values = prompt
    operands = (
        queries, bias, *row_list,
        *[keys[head] for head in heads], *[values[head] for head in heads], *begun,
    )
    parts = [((count, rows, size), jnp.float32), ((count, rows, LANES), jnp.float32)]
    send = jax.ShapeDtypeStruct(message_shape(count * rows, size), jnp.bfloat16)
    space = work_space(count, rows, keys[0].shape[0], size)
    return pl.pallas_call(
        functools.partial(
            attend_kernel, heads, kept, factor, len(row_list), len(begun) // 3
        ),
        in_specs=in_vmem(len(operands)),
        out_shape=tuple(jax.ShapeDtypeStruct(*part) for part in parts) if kept else send,
        scratch_shapes=[*([] if kept else [pltpu.VMEM(*part) for part in parts]), *space],
        compiler_params=pltpu.CompilerParams(vmem_limit_bytes=32 << 20),
        cost_estimate=SMALL,
    )(*operands, after)


def merge(out_a, sum_a, out_b, sum_b):
    top = jnp.maximum(sum_a, sum_b)
    weight_a = jnp.exp2(sum_a - top)
    weight_b = jnp.exp2(sum_b - top)
    total = weight_a + weight_b
    return (out_a * weight_a + out_b * weight_b) / total, top + jnp.log2(total)


def merge_kernel(level, last, keep_ref, sums_ref, got_ref, _, *outs):
    count, rows = keep_ref.shape[:2]
    got_sums = unpack_tail(got_ref[count * rows :], count * rows)
    merged = []
    for i in range(count):
        here = slice(i * rows, (i + 1) * rows)
        got = got_ref[here].astype(jnp.float32)
        merged.append(merge(keep_ref[i], sums_ref[i][:, :1], got, got_sums[here]))
    part = rows if last else rows // 2
    bit = lax.rem(lax.axis_index("ctx") >> level, 2) == 1

    def choose(first, value):
        return value if last else jnp.where(first, value[:part], value[part:])

    send = outs[0]
    for i, (out, _) in enumerate(merged):
        send[i * part : (i + 1) * part] = choose(bit, out).astype(jnp.bfloat16)
    send[count * part :] = pack_tail(
        jnp.concatenate([choose(bit, log_sum) for _, log_sum in merged], axis=0)
    )
    if not last:
        _, keep, wide = outs
        for i, (out, log_sum) in enumerate(merged):
            keep[i] = choose(~bit, out)
            wide[i] = jnp.broadcast_to(choose(~bit, log_sum), (part, LANES))


def merge_parts(keep, sums, got, level, last, after):
    count, rows, size = keep.shape
    part = rows if last else rows // 2
    shapes = [jax.ShapeDtypeStruct(message_shape(count * part, size), jnp.bfloat16)]
    if not last:
        shapes.append(jax.ShapeDtypeStruct((count, part, size), jnp.float32))
        shapes.append(jax.ShapeDtypeStruct((count, part, LANES), jnp.float32))
    return pl.pallas_call(
        functools.partial(merge_kernel, level, last),
        in_specs=in_vmem(3),
        out_shape=tuple(shapes),
        compiler_params=pltpu.CompilerParams(vmem_limit_bytes=16 << 20),
        cost_estimate=SMALL,
    )(keep, sums, got, after)


def finish_kernel(mine_ref, got_ref, _, out_ref):
    count, rows = out_ref.shape[0], math.prod(out_ref.shape[1:-1])
    mine_sums = unpack_tail(mine_ref[count * rows :], count * rows)
    got_sums = unpack_tail(got_ref[count * rows :], count * rows)
    for i in range(count):
        here = slice(i * rows, (i + 1) * rows)
        out, _ = merge(
            mine_ref[here].astype(jnp.float32),
            mine_sums[here],
            got_ref[here].astype(jnp.float32),
            got_sums[here],
        )
        out_ref[i] = out.astype(jnp.bfloat16).reshape(out_ref.shape[1:])


def finish(mine, got, shape, after):
    return pl.pallas_call(
        finish_kernel,
        in_specs=in_vmem(2),
        out_shape=jax.ShapeDtypeStruct(shape, jnp.bfloat16),
        compiler_params=pltpu.CompilerParams(vmem_limit_bytes=16 << 20),
        cost_estimate=SMALL,
    )(mine, got, after)


def place_kernel(levels, plan, *refs):
    part_refs = refs[: len(plan)]
    out_ref, sems = refs[-2:]
    copies = []
    for (head, own), ref in zip(plan, part_refs):
        blocks = ref.shape[1]
        bit = lax.rem(lax.axis_index("ctx"), 2) if levels > 1 else 0
        at = (bit if own else 1 - bit) * blocks
        for i in range(ref.shape[0]):
            there = out_ref.at[pl.ds(at, blocks), :, head + i]
            copies.append(pltpu.make_async_copy(ref.at[i], there, sems.at[len(copies)]))
    for copy in copies:
        copy.start()
    for copy in copies:
        copy.wait()


def place(out, parts, shape, levels, after):
    arrays = [array for array, _, _ in parts]
    plan = [(head, own) for _, head, own in parts]
    others = [after] if out is None else [after, out]
    return pl.pallas_call(
        functools.partial(place_kernel, levels, plan),
        in_specs=[pl.BlockSpec(memory_space=pltpu.VMEM)] * len(arrays)
        + [pl.BlockSpec(memory_space=pl.ANY), pl.BlockSpec(memory_space=pltpu.HBM)][: len(others)],
        out_specs=pl.BlockSpec(memory_space=pltpu.HBM),
        out_shape=pltpu.HBM(shape, jnp.bfloat16),
        input_output_aliases={} if out is None else {len(arrays) + 1: 0},
        scratch_shapes=[pltpu.SemaphoreType.DMA((sum(a.shape[0] for a in arrays),))],
        compiler_params=pltpu.CompilerParams(vmem_limit_bytes=16 << 20),
        cost_estimate=SMALL,
    )(*arrays, *others)


def on_device(shards, owners, queries, prompt_cache, suffix_cache, new_kv, ancestors, lengths):
    steps, per_owner, heads, group, size = queries.shape
    suffix_dev = suffix_cache.shape[2]
    shard = lax.axis_index("ctx")
    factor = math.log2(math.e) / math.sqrt(size)
    levels = shards.bit_length() - 1
    if shards != 1 << levels or levels < 2 or steps % 2 or suffix_dev != steps:
        raise ValueError("unsupported sizes")

    def swap(value, bit):
        return lax.ppermute(value, "ctx", [(i, i ^ (1 << bit)) for i in range(shards)])

    prompt_rows = prompt_cache.reshape(2, -1, size)
    mine, parents, extents = build_message(
        suffix_cache.reshape(2, -1, size),
        new_kv.reshape(steps, 2, -1, size),
        ancestors,
        lengths,
        heads,
    )
    row_list = [mine] + [
        lax.ppermute(mine, "dom", [(i, (i + hop) % owners) for i in range(owners)])
        for hop in range(1, owners)
    ]
    *prompt, bias = split_prompt(
        prompt_rows, parents, extents, heads, owners, suffix_dev
    )
    prompt = prompt[:heads], prompt[heads:]
    last = [bias]

    def follow(results):
        last[0] = results[0] if isinstance(results, (tuple, list)) else results
        return results

    messages = {}
    blocks = steps * per_owner >> (levels - 1)

    def run_attend(group, kept, begun=()):
        return follow(
            attend(queries, prompt, bias, row_list, group, kept, factor, begun, last[0])
        )

    def run_merges(got, parts):
        for level in range(1, levels):
            send, *parts = follow(merge_parts(*parts, got, level, level == levels - 1, last[0]))
            got = swap(send, level)
        return send, got

    parts = []

    def run_finish(count, send, got):
        return follow(finish(send, got, (count, blocks, group, size), last[0]))

    def run_gather(head, done):
        count = done.shape[0]
        for level in range(levels - 2, 0, -1):
            other = swap(done, level)
            done = jnp.where(
                (shard >> level) % 2 == 1,
                jnp.concatenate([other, done], axis=1),
                jnp.concatenate([done, other], axis=1),
            )
        done = done.reshape(count, steps // 2, per_owner, group, size)
        parts.append((done, head, True))
        parts.append((swap(done, 0), head, False))

    first = max(heads // 2, 1)
    groups = [tuple(range(heads))[at : at + first] for at in range(0, heads, first)]
    begun = follow(begin(queries, prompt, groups[0], False, factor))
    arrived = []
    for number, one in enumerate(groups):
        arrived.append(swap(run_attend(one, False, () if number else begun), 0))
    pairs = [run_merges(got, run_attend(one, True)) for one, got in zip(groups, arrived)]
    for one, pair in zip(groups, pairs):
        run_gather(one[0], run_finish(len(one), *pair))
    late = parts[-1:]
    early = [part for part in parts if not any(part is one for one in late)]
    out = place(None, early, queries.shape, levels, last[0]) if early else None
    return place(out, late, queries.shape, levels, last[0])


def solution(mesh):
    return jax.shard_map(
        functools.partial(on_device, mesh.shape["ctx"], mesh.shape["dom"]),
        mesh=mesh,
        in_specs=(
            P("groups", "dom", "tp", None, None),
            P("groups", "ctx", "tp", None),
            P("groups", "dom", "ctx", "tp", None),
            P("groups", None, "dom", "tp", None),
            P("groups", None),
            P("groups"),
        ),
        out_specs=P("groups", "dom", "tp", None, None),
        check_vma=False,
    )
```

```python
import functools
import math

import jax
import jax.numpy as jnp
from jax import lax
from jax.experimental import pallas as pl
from jax.experimental.pallas import tpu as pltpu
from jax.sharding import PartitionSpec as P

LANES = 128
HIDDEN = -1e30
NN = (((1,), (0,)), ((), ()))
NT = (((1,), (1,)), ((), ()))
SMALL = pl.CostEstimate(flops=0, bytes_accessed=4096, transcendentals=0)


def round_up(value, multiple):
    return -(-value // multiple) * multiple


def dot(a, b, dims):
    return lax.dot_general(a, b, dims, preferred_element_type=jnp.float32)


def eye_mask(rows):
    shape = (rows, LANES)
    return lax.broadcasted_iota(jnp.int32, shape, 0) == lax.broadcasted_iota(jnp.int32, shape, 1)


def column_to_lanes(column):
    rows = column.shape[0]
    block = min(rows, LANES)
    mask = eye_mask(block)
    return jnp.concatenate(
        [
            jnp.sum(jnp.where(mask, column[at : at + block], 0.0), axis=0, keepdims=True)
            for at in range(0, rows, block)
        ],
        axis=0,
    )


def lanes_to_column(lanes, rows):
    block = min(rows, LANES)
    mask = eye_mask(block)
    return jnp.concatenate(
        [
            jnp.sum(jnp.where(mask, lanes[i : i + 1], 0.0), axis=1, keepdims=True)
            for i in range(lanes.shape[0])
        ],
        axis=0,
    )


def tail_rows(rows):
    return round_up(3 * -(-rows // LANES), 16)


def message_shape(rows, size):
    return rows + tail_rows(rows), size


def pack_tail(column):
    lanes = column_to_lanes(column)
    high = lanes.astype(jnp.bfloat16).astype(jnp.float32)
    middle = (lanes - high).astype(jnp.bfloat16).astype(jnp.float32)
    low = lanes - high - middle
    parts = jnp.concatenate([high, middle, low], axis=0)
    spare = tail_rows(column.shape[0]) - parts.shape[0]
    return jnp.concatenate([parts, jnp.zeros((spare, LANES), jnp.float32)], axis=0).astype(
        jnp.bfloat16
    )


def unpack_tail(tail, rows):
    tail = tail.astype(jnp.float32)
    blocks = -(-rows // LANES)
    lanes = tail[:blocks] + tail[blocks : 2 * blocks] + tail[2 * blocks : 3 * blocks]
    return lanes_to_column(lanes, rows)


def in_hbm(array):
    return pltpu.with_memory_space_constraint(array, pltpu.HBM)


def message_kernel(
    heads, suffix_ref, new_ref, ancestors_ref, lengths_ref,
    out_ref, parents_ref, extents_ref, here, wide, sems,
):
    steps, each = new_ref.shape[0], new_ref.shape[2]
    total = here.shape[1]
    is_last = lax.axis_index("ctx") == lax.axis_size("ctx") - 1
    suffix_copy = pltpu.make_async_copy(suffix_ref, here, sems.at[0])
    token_copies = [
        pltpu.make_async_copy(
            new_ref.at[step], here.at[:, pl.ds(step * each, each)], sems.at[1 + step]
        )
        for step in range(steps)
    ]
    small = [
        pltpu.make_async_copy(ancestors_ref, parents_ref, sems.at[1 + steps]),
        pltpu.make_async_copy(lengths_ref, extents_ref, sems.at[2 + steps]),
    ]
    for copy in small:
        copy.start()

    @pl.when(is_last)
    def _():
        for copy in token_copies:
            copy.start()
        for copy in token_copies:
            copy.wait()

    @pl.when(jnp.logical_not(is_last))
    def _():
        suffix_copy.start()
        suffix_copy.wait()

    for kind in range(2):
        wide[kind] = here[kind].astype(jnp.float32)
        for head in range(heads):
            part = wide[kind, pl.ds(head, total // heads, stride=heads), :]
            out_ref[kind, head] = part.astype(out_ref.dtype)
    for copy in small:
        copy.wait()


def build_message(suffix, new, ancestors, lengths, heads):
    _, rows, size = suffix.shape
    lengths = lengths.reshape(1, -1)
    operands = (suffix, new, ancestors, lengths)
    return pl.pallas_call(
        functools.partial(message_kernel, heads),
        in_specs=[pl.BlockSpec(memory_space=pltpu.HBM)] * len(operands),
        out_shape=(
            jax.ShapeDtypeStruct((2, heads, rows // heads, size), suffix.dtype),
            jax.ShapeDtypeStruct(ancestors.shape, ancestors.dtype),
            jax.ShapeDtypeStruct(lengths.shape, lengths.dtype),
        ),
        scratch_shapes=[
            pltpu.VMEM(suffix.shape, suffix.dtype),
            pltpu.VMEM(suffix.shape, jnp.float32),
            pltpu.SemaphoreType.DMA((3 + new.shape[0],)),
        ],
        compiler_params=pltpu.CompilerParams(vmem_limit_bytes=24 << 20),
        cost_estimate=SMALL,
    )(*[in_hbm(operand) for operand in operands])


def iota(shape, axis):
    return lax.broadcasted_iota(jnp.int32, shape, axis)


def lineage_bias(ancestors_ref, lengths_ref, states, owners, suffix_dev):
    steps, particles = ancestors_ref.shape
    per_owner = particles // owners
    each = per_owner * suffix_dev
    my_owner = lax.axis_index("dom")
    my_shard = lax.axis_index("ctx")
    is_last = my_shard == lax.axis_size("ctx") - 1
    square = (particles, particles)
    same = iota(square, 0) == iota(square, 1)

    def as_column(row):
        return jnp.sum(jnp.where(same, row, 0), axis=1, keepdims=True)

    products = {}
    for step in range(steps):
        parent = as_column(ancestors_ref[step : step + 1, :])
        products[step - 1, step] = (parent == iota(square, 1)).astype(jnp.bfloat16)
    for length in range(2, steps + 1):
        for step in range(length - 1, steps):
            after = step - length
            middle = (step + after + 1) // 2
            both = dot(products[middle, step], products[after, middle], NN)
            products[after, step] = both.astype(jnp.bfloat16)
    for step in range(steps):
        states[step, :, :particles] = products[-1, step].astype(jnp.float32)
        for token in range(steps):
            here = slice((1 + token) * particles, (2 + token) * particles)
            if token < step:
                states[step, :, here] = products[token, step].astype(jnp.float32)
            else:
                states[step, :, here] = same.astype(jnp.float32) * float(token == step)
    rows = pl.ds(pl.multiple_of(my_owner * per_owner, per_owner), per_owner)
    mine = jnp.concatenate([states[step, rows, :] for step in range(steps)], axis=0)
    mine = mine.astype(jnp.bfloat16)
    lengths = as_column(lengths_ref[...])
    shape = (particles, owners * each)
    column = iota(shape, 1)
    source = column // each
    first = lax.rem(my_owner + owners - source, owners) * per_owner
    inner = column - source * each
    position = my_shard * suffix_dev + lax.rem(inner, suffix_dev)
    by_particle = iota(shape, 0) == first + inner // suffix_dev
    by_token = iota(shape, 0) == first + lax.rem(inner, per_owner)
    seen = [by_particle & (position < lengths) & jnp.logical_not(is_last)]
    seen += [by_token & (inner // per_owner == token) & is_last for token in range(steps)]
    table = jnp.concatenate([s.astype(jnp.bfloat16) for s in seen], axis=0)
    return jnp.where(dot(mine, table, NN) > 0.5, 0.0, HIDDEN)


def split_kernel(
    heads, block, owners, suffix_dev,
    rows_ref, parents_ref, extents_ref, *refs,
):
    out_refs = refs[: 2 * heads]
    bias_ref, here, wide, states, sems = refs[2 * heads :]
    total = out_refs[0].shape[0]
    places = [(kind, at) for kind in range(2) for at in range(0, total, block)]
    copies = [
        pltpu.make_async_copy(
            rows_ref.at[kind, pl.ds(at * heads, block * heads)],
            here.at[kind, pl.ds(at * heads, block * heads)],
            sems.at[i],
        )
        for i, (kind, at) in enumerate(places)
    ]
    for copy in copies:
        copy.start()
    bias_ref[...] = lineage_bias(parents_ref, extents_ref, states, owners, suffix_dev)
    for i, (kind, at) in enumerate(places):
        copies[i].wait()
        wide[i % 2] = here[kind, at * heads : (at + block) * heads].astype(jnp.float32)
        for head in range(heads):
            part = wide[i % 2, pl.ds(head, block, stride=heads), :]
            out_refs[kind * heads + head][at : at + block] = part.astype(rows_ref.dtype)


def split_prompt(rows, parents, extents, heads, owners, suffix_dev):
    total = rows.shape[1] // heads
    block = math.gcd(total, 512)
    size = rows.shape[2]
    steps, particles = parents.shape
    return pl.pallas_call(
        functools.partial(split_kernel, heads, block, owners, suffix_dev),
        in_specs=[pl.BlockSpec(memory_space=pltpu.HBM)]
        + [pl.BlockSpec(memory_space=pltpu.VMEM)] * 2,
        out_shape=(
            *[jax.ShapeDtypeStruct((total, size), rows.dtype)] * (2 * heads),
            jax.ShapeDtypeStruct(
                (steps * particles // owners, particles * suffix_dev), jnp.float32
            ),
        ),
        scratch_shapes=[
            pltpu.VMEM(rows.shape, rows.dtype),
            pltpu.VMEM((2, block * heads, size), jnp.float32),
            pltpu.VMEM((steps, particles, (1 + steps) * particles), jnp.float32),
            pltpu.SemaphoreType.DMA((2 * total // block,)),
        ],
        compiler_params=pltpu.CompilerParams(vmem_limit_bytes=24 << 20),
        cost_estimate=SMALL,
    )(in_hbm(rows), parents, extents)


def with_ones(values):
    return jnp.concatenate([values, jnp.ones_like(values)], axis=1)


def row_peak(scores):
    return jnp.max(scores, axis=1, keepdims=True)


def weigh(scores, factor, offset):
    return jnp.exp2(scores * factor - offset).astype(jnp.bfloat16)


def work_space(streams, rows, total, size):
    block = math.gcd(total, 512)
    return [
        pltpu.VMEM((3, rows, block), jnp.float32),
        pltpu.VMEM((streams, 2, rows, math.gcd(total, 2 * block)), jnp.bfloat16),
        pltpu.VMEM((streams * rows, 2 * size), jnp.float32),
    ]


def prompt_sum(streams, factor, scores, weights, sums):
    rows, total = streams[0][0].shape[0], streams[0][1].shape[0]
    block, wide = scores.shape[2], weights.shape[3]
    units = [(at, i) for at in range(0, total, block) for i in range(len(streams))]
    offsets = [None] * len(streams)

    def score(n):
        at, i = units[n]
        scores[n % 3] = dot(streams[i][0], streams[i][1][at : at + block], NT)

    def weight(n):
        at, i = units[n]
        if at == 0:
            top = row_peak(scores[n % 3])
            peak = streams[i][3]
            offsets[i] = (top if peak is None else jnp.maximum(top, peak)) * factor
        there = slice(at % wide, at % wide + block)
        weights[i, at // wide % 2, :, there] = weigh(scores[n % 3], factor, offsets[i])

    def gather(n):
        at, i = units[n]
        end = at + block
        if end % wide:
            return
        part = dot(weights[i, at // wide % 2], with_ones(streams[i][2][end - wide : end]), NN)
        here = slice(i * rows, (i + 1) * rows)
        sums[here] = part if end == wide else sums[here] + part

    score(0)
    score(1)
    for n in range(len(units)):
        if n + 2 < len(units):
            score(n + 2)
        weight(n)
        if n:
            gather(n - 1)
    gather(len(units) - 1)
    return offsets


def half_bit(level):
    shard = lax.axis_index("ctx")
    return lax.rem((shard >> level) + (shard >> (level + 1)), 2)


def first_step(q_ref, kept):
    bit = half_bit(0)
    return (bit if kept else 1 - bit) * (q_ref.shape[0] // 2)


def queries_of(q_ref, head, first, number):
    _, per_owner, _, group, size = q_ref.shape
    return q_ref[pl.ds(first, number), :, head].reshape(number * per_owner * group, size)


def prompt_kernel(heads, kept, factor, q_ref, *refs):
    k_refs, v_refs = refs[: len(heads)], refs[len(heads) : 2 * len(heads)]
    together_ref, offset_ref, scores, weights = refs[2 * len(heads) :]
    first, number = first_step(q_ref, kept), q_ref.shape[0] // 2
    streams = [
        (queries_of(q_ref, head, first, number), k_ref, v_ref, None)
        for head, k_ref, v_ref in zip(heads, k_refs, v_refs)
    ]
    offsets = prompt_sum(streams, factor, scores, weights, together_ref)
    offset = jnp.concatenate(offsets, axis=0)
    offset_ref[...] = jnp.broadcast_to(offset, offset_ref.shape)


def in_vmem(count, ordered=True):
    last = [pl.BlockSpec(memory_space=pl.ANY)] if ordered else []
    return [pl.BlockSpec(memory_space=pltpu.VMEM)] * count + last


def begin(queries, prompt, heads, kept, factor):
    steps, per_owner, _, group, size = queries.shape
    rows = steps * per_owner * group // 2
    keys, values = prompt
    space = work_space(len(heads), rows, keys[0].shape[0], size)
    return pl.pallas_call(
        functools.partial(prompt_kernel, heads, kept, factor),
        in_specs=in_vmem(1 + 2 * len(heads), False),
        out_shape=(
            jax.ShapeDtypeStruct((len(heads) * rows, 2 * size), jnp.float32),
            jax.ShapeDtypeStruct((len(heads) * rows, LANES), jnp.float32),
        ),
        scratch_shapes=space[:2],
        compiler_params=pltpu.CompilerParams(vmem_limit_bytes=24 << 20),
        cost_estimate=SMALL,
    )(queries, *[keys[head] for head in heads], *[values[head] for head in heads])


def attend_kernel(heads, kept, factor, owners, started, *refs):
    count = len(heads)
    q_ref, bias_ref = refs[:2]
    row_refs = refs[2 : 2 + owners]
    refs = refs[2 + owners :]
    k_refs, v_refs, refs = refs[:count], refs[count : 2 * count], refs[2 * count :]
    begun, refs = refs[: 2 * started], refs[2 * started + 1 :]
    if kept:
        out, log_sums, *work = refs
    else:
        send_ref, out, log_sums, *work = refs
    steps, per_owner, _, group, size = q_ref.shape
    columns = bias_ref.shape[1]
    number = steps // 2
    rows = number * per_owner * group
    start = first_step(q_ref, kept)

    def suffix_of(head, kind):
        return jnp.concatenate([ref[kind, head] for ref in row_refs], axis=0)

    def suffix_scores(q, head, first, number):
        at = pl.multiple_of(first * per_owner, per_owner)
        bias = bias_ref[pl.ds(at, number * per_owner), :]
        bias = jnp.broadcast_to(bias[:, None, :], (number * per_owner, group, columns))
        return dot(q, suffix_of(head, 0), NT) + bias.reshape(number * per_owner * group, columns)

    def store(i, at, together, offset):
        sums = together[:, size:]
        out[i, pl.ds(at, sums.shape[0]), :] = together[:, :size] / sums
        log_sums[i, pl.ds(at, sums.shape[0]), :] = offset + jnp.log2(sums)
        return sums

    queries = [queries_of(q_ref, head, start, number) for head in heads]
    extras = [suffix_scores(q, head, start, number) for q, head in zip(queries, heads)]
    if started:
        offsets = [begun[1][i * rows : (i + 1) * rows, :1] for i in range(count)]
        togethers = begun[0]
    else:
        streams = [(q, k, v, row_peak(e)) for q, k, v, e in zip(queries, k_refs, v_refs, extras)]
        offsets = prompt_sum(streams, factor, *work)
        togethers = work[-1]
    worst = []
    for i, head in enumerate(heads):
        weight = weigh(extras[i], factor, offsets[i])
        together = togethers[i * rows : (i + 1) * rows]
        together = together + dot(weight, with_ones(suffix_of(head, 1)), NN)
        worst.append(jnp.max(store(i, 0, together, offsets[i])))

    for i, head in enumerate(heads):

        @pl.when(jnp.logical_not(worst[i] < 2.0**100))
        def _():
            @pl.loop(0, number)
            def _(step):
                q = queries_of(q_ref, head, start + step, 1)
                extra = suffix_scores(q, head, start + step, 1)
                scores = dot(q, k_refs[i][...], NT)
                offset = jnp.maximum(row_peak(scores), row_peak(extra)) * factor
                weight = weigh(scores, factor, offset)
                together = dot(weight, with_ones(v_refs[i][...]), NN)
                weight = weigh(extra, factor, offset)
                together = together + dot(weight, with_ones(suffix_of(head, 1)), NN)
                here = per_owner * group
                store(i, pl.multiple_of(step * here, here), together, offset)

    if not kept:
        for i in range(count):
            send_ref[i * rows : (i + 1) * rows] = out[i].astype(jnp.bfloat16)
        column = jnp.concatenate([log_sums[i, :, :1] for i in range(count)], axis=0)
        send_ref[count * rows :] = pack_tail(column)


def attend(queries, prompt, bias, row_list, heads, kept, factor, begun, after):
    steps, per_owner, _, group, size = queries.shape
    rows = steps * per_owner * group // 2
    count = len(heads)
    keys, values = prompt
    operands = (
        queries, bias, *row_list,
        *[keys[head] for head in heads], *[values[head] for head in heads], *begun,
    )
    parts = [((count, rows, size), jnp.float32), ((count, rows, LANES), jnp.float32)]
    send = jax.ShapeDtypeStruct(message_shape(count * rows, size), jnp.bfloat16)
    space = work_space(count, rows, keys[0].shape[0], size)
    return pl.pallas_call(
        functools.partial(
            attend_kernel, heads, kept, factor, len(row_list), len(begun) // 2
        ),
        in_specs=in_vmem(len(operands)),
        out_shape=tuple(jax.ShapeDtypeStruct(*part) for part in parts) if kept else send,
        scratch_shapes=[*([] if kept else [pltpu.VMEM(*part) for part in parts]), *space],
        compiler_params=pltpu.CompilerParams(vmem_limit_bytes=32 << 20),
        cost_estimate=SMALL,
    )(*operands, after)


def merge(out_a, sum_a, out_b, sum_b):
    top = jnp.maximum(sum_a, sum_b)
    weight_a = jnp.exp2(sum_a - top)
    weight_b = jnp.exp2(sum_b - top)
    total = weight_a + weight_b
    return (out_a * weight_a + out_b * weight_b) / total, top + jnp.log2(total)


def merge_kernel(level, last, keep_ref, sums_ref, got_ref, _, *outs):
    count, rows = keep_ref.shape[:2]
    got_sums = unpack_tail(got_ref[count * rows :], count * rows)
    merged = []
    for i in range(count):
        here = slice(i * rows, (i + 1) * rows)
        got = got_ref[here].astype(jnp.float32)
        merged.append(merge(keep_ref[i], sums_ref[i][:, :1], got, got_sums[here]))
    part = rows if last else rows // 2
    bit = half_bit(level) == 1

    def choose(first, value):
        return value if last else jnp.where(first, value[:part], value[part:])

    send = outs[0]
    for i, (out, _) in enumerate(merged):
        send[i * part : (i + 1) * part] = choose(bit, out).astype(jnp.bfloat16)
    send[count * part :] = pack_tail(
        jnp.concatenate([choose(bit, log_sum) for _, log_sum in merged], axis=0)
    )
    if not last:
        _, keep, wide = outs
        for i, (out, log_sum) in enumerate(merged):
            keep[i] = choose(~bit, out)
            wide[i] = jnp.broadcast_to(choose(~bit, log_sum), (part, LANES))


def merge_parts(keep, sums, got, level, last, after):
    count, rows, size = keep.shape
    part = rows if last else rows // 2
    shapes = [jax.ShapeDtypeStruct(message_shape(count * part, size), jnp.bfloat16)]
    if not last:
        shapes.append(jax.ShapeDtypeStruct((count, part, size), jnp.float32))
        shapes.append(jax.ShapeDtypeStruct((count, part, LANES), jnp.float32))
    return pl.pallas_call(
        functools.partial(merge_kernel, level, last),
        in_specs=in_vmem(3),
        out_shape=tuple(shapes),
        compiler_params=pltpu.CompilerParams(vmem_limit_bytes=16 << 20),
        cost_estimate=SMALL,
    )(keep, sums, got, after)


def finish_kernel(mine_ref, got_ref, _, out_ref):
    count, rows = out_ref.shape[0], math.prod(out_ref.shape[1:-1])
    mine_sums = unpack_tail(mine_ref[count * rows :], count * rows)
    got_sums = unpack_tail(got_ref[count * rows :], count * rows)
    for i in range(count):
        here = slice(i * rows, (i + 1) * rows)
        out, _ = merge(
            mine_ref[here].astype(jnp.float32),
            mine_sums[here],
            got_ref[here].astype(jnp.float32),
            got_sums[here],
        )
        out_ref[i] = out.astype(jnp.bfloat16).reshape(out_ref.shape[1:])


def finish(mine, got, shape, after):
    return pl.pallas_call(
        finish_kernel,
        in_specs=in_vmem(2),
        out_shape=jax.ShapeDtypeStruct(shape, jnp.bfloat16),
        compiler_params=pltpu.CompilerParams(vmem_limit_bytes=16 << 20),
        cost_estimate=SMALL,
    )(mine, got, after)


def place_kernel(levels, plan, *refs):
    part_refs = refs[: len(plan)]
    out_ref, sems = refs[-2:]
    copies = []
    for (head, own), ref in zip(plan, part_refs):
        blocks = ref.shape[1]
        bit = half_bit(0)
        at = (bit if own else 1 - bit) * blocks
        for i in range(ref.shape[0]):
            there = out_ref.at[pl.ds(at, blocks), :, head + i]
            copies.append(pltpu.make_async_copy(ref.at[i], there, sems.at[len(copies)]))
    for copy in copies:
        copy.start()
    for copy in copies:
        copy.wait()


def place(out, parts, shape, levels, after):
    arrays = [array for array, _, _ in parts]
    plan = [(head, own) for _, head, own in parts]
    others = [after] if out is None else [after, out]
    return pl.pallas_call(
        functools.partial(place_kernel, levels, plan),
        in_specs=[pl.BlockSpec(memory_space=pltpu.VMEM)] * len(arrays)
        + [pl.BlockSpec(memory_space=pl.ANY), pl.BlockSpec(memory_space=pltpu.HBM)][: len(others)],
        out_specs=pl.BlockSpec(memory_space=pltpu.HBM),
        out_shape=pltpu.HBM(shape, jnp.bfloat16),
        input_output_aliases={} if out is None else {len(arrays) + 1: 0},
        scratch_shapes=[pltpu.SemaphoreType.DMA((sum(a.shape[0] for a in arrays),))],
        compiler_params=pltpu.CompilerParams(vmem_limit_bytes=16 << 20),
        cost_estimate=SMALL,
    )(*arrays, *others)


def on_device(shards, owners, queries, prompt_cache, suffix_cache, new_kv, ancestors, lengths):
    steps, per_owner, heads, group, size = queries.shape
    suffix_dev = suffix_cache.shape[2]
    factor = math.log2(math.e) / math.sqrt(size)
    levels = shards.bit_length() - 1
    if shards != 1 << levels or levels < 2 or steps % 2 or suffix_dev != steps:
        raise ValueError("unsupported sizes")

    def swap(value, bit):
        return lax.ppermute(value, "ctx", [(i, i ^ ((2 << bit) - 1)) for i in range(shards)])

    prompt_rows = prompt_cache.reshape(2, -1, size)
    mine, parents, extents = build_message(
        suffix_cache.reshape(2, -1, size),
        new_kv.reshape(steps, 2, -1, size),
        ancestors,
        lengths,
        heads,
    )
    row_list = [mine] + [
        lax.ppermute(mine, "dom", [(i, (i + hop) % owners) for i in range(owners)])
        for hop in range(1, owners)
    ]
    *prompt, bias = split_prompt(
        prompt_rows, parents, extents, heads, owners, suffix_dev
    )
    prompt = prompt[:heads], prompt[heads:]
    last = [bias]

    def follow(results):
        last[0] = results[0] if isinstance(results, (tuple, list)) else results
        return results

    messages = {}
    blocks = steps * per_owner >> (levels - 1)

    def run_attend(group, kept, begun=()):
        return follow(
            attend(queries, prompt, bias, row_list, group, kept, factor, begun, last[0])
        )

    def run_merges(got, parts):
        for level in range(1, levels):
            send, *parts = follow(merge_parts(*parts, got, level, level == levels - 1, last[0]))
            got = swap(send, level)
        return send, got

    parts = []

    def run_finish(count, send, got):
        return follow(finish(send, got, (count, blocks, group, size), last[0]))

    def run_gather(head, done):
        count = done.shape[0]
        for level in range(levels - 2, 0, -1):
            other = swap(done, level)
            done = jnp.where(
                half_bit(level) == 1,
                jnp.concatenate([other, done], axis=1),
                jnp.concatenate([done, other], axis=1),
            )
        done = done.reshape(count, steps // 2, per_owner, group, size)
        parts.append((done, head, True))
        parts.append((swap(done, 0), head, False))

    first = max(heads // 2, 1)
    groups = [tuple(range(heads))[at : at + first] for at in range(0, heads, first)]
    begun = follow(begin(queries, prompt, groups[0], False, factor))
    arrived = []
    for number, one in enumerate(groups):
        arrived.append(swap(run_attend(one, False, () if number else begun), 0))
    pairs = [run_merges(got, run_attend(one, True)) for one, got in zip(groups, arrived)]
    for one, pair in zip(groups, pairs):
        run_gather(one[0], run_finish(len(one), *pair))
    late = parts[-1:]
    early = [part for part in parts if not any(part is one for one in late)]
    out = place(None, early, queries.shape, levels, last[0]) if early else None
    return place(out, late, queries.shape, levels, last[0])


def solution(mesh):
    return jax.shard_map(
        functools.partial(on_device, mesh.shape["ctx"], mesh.shape["dom"]),
        mesh=mesh,
        in_specs=(
            P("groups", "dom", "tp", None, None),
            P("groups", "ctx", "tp", None),
            P("groups", "dom", "ctx", "tp", None),
            P("groups", None, "dom", "tp", None),
            P("groups", None),
            P("groups"),
        ),
        out_specs=P("groups", "dom", "tp", None, None),
        check_vma=False,
    )
```

```python
import functools
import math

import jax
import jax.numpy as jnp
from jax import lax
from jax.experimental import pallas as pl
from jax.experimental.pallas import tpu as pltpu
from jax.sharding import PartitionSpec as P

LANES = 128
HIDDEN = -1e30
NN = (((1,), (0,)), ((), ()))
NT = (((1,), (1,)), ((), ()))
SMALL = pl.CostEstimate(flops=0, bytes_accessed=4096, transcendentals=0)


def round_up(value, multiple):
    return -(-value // multiple) * multiple


def dot(a, b, dims):
    return lax.dot_general(a, b, dims, preferred_element_type=jnp.float32)


def eye_mask(rows):
    shape = (rows, LANES)
    return lax.broadcasted_iota(jnp.int32, shape, 0) == lax.broadcasted_iota(jnp.int32, shape, 1)


def column_to_lanes(column):
    rows = column.shape[0]
    block = min(rows, LANES)
    mask = eye_mask(block)
    return jnp.concatenate(
        [
            jnp.sum(jnp.where(mask, column[at : at + block], 0.0), axis=0, keepdims=True)
            for at in range(0, rows, block)
        ],
        axis=0,
    )


def lanes_to_column(lanes, rows):
    block = min(rows, LANES)
    mask = eye_mask(block)
    return jnp.concatenate(
        [
            jnp.sum(jnp.where(mask, lanes[i : i + 1], 0.0), axis=1, keepdims=True)
            for i in range(lanes.shape[0])
        ],
        axis=0,
    )


def tail_rows(rows):
    return round_up(3 * -(-rows // LANES), 16)


def message_shape(rows, size):
    return rows + tail_rows(rows), size


def pack_tail(column):
    lanes = column_to_lanes(column)
    high = lanes.astype(jnp.bfloat16).astype(jnp.float32)
    middle = (lanes - high).astype(jnp.bfloat16).astype(jnp.float32)
    low = lanes - high - middle
    parts = jnp.concatenate([high, middle, low], axis=0)
    spare = tail_rows(column.shape[0]) - parts.shape[0]
    return jnp.concatenate([parts, jnp.zeros((spare, LANES), jnp.float32)], axis=0).astype(
        jnp.bfloat16
    )


def unpack_tail(tail, rows):
    tail = tail.astype(jnp.float32)
    blocks = -(-rows // LANES)
    lanes = tail[:blocks] + tail[blocks : 2 * blocks] + tail[2 * blocks : 3 * blocks]
    return lanes_to_column(lanes, rows)


def in_hbm(array):
    return pltpu.with_memory_space_constraint(array, pltpu.HBM)


def message_kernel(
    heads, suffix_ref, new_ref, ancestors_ref, lengths_ref,
    out_ref, parents_ref, extents_ref, here, wide, sems,
):
    steps, each = new_ref.shape[0], new_ref.shape[2]
    total = here.shape[1]
    is_last = lax.axis_index("ctx") == lax.axis_size("ctx") - 1
    suffix_copy = pltpu.make_async_copy(suffix_ref, here, sems.at[0])
    token_copies = [
        pltpu.make_async_copy(
            new_ref.at[step], here.at[:, pl.ds(step * each, each)], sems.at[1 + step]
        )
        for step in range(steps)
    ]
    small = [
        pltpu.make_async_copy(ancestors_ref, parents_ref, sems.at[1 + steps]),
        pltpu.make_async_copy(lengths_ref, extents_ref, sems.at[2 + steps]),
    ]
    for copy in small:
        copy.start()

    @pl.when(is_last)
    def _():
        for copy in token_copies:
            copy.start()
        for copy in token_copies:
            copy.wait()

    @pl.when(jnp.logical_not(is_last))
    def _():
        suffix_copy.start()
        suffix_copy.wait()

    for kind in range(2):
        wide[kind] = here[kind].astype(jnp.float32)
        for head in range(heads):
            part = wide[kind, pl.ds(head, total // heads, stride=heads), :]
            out_ref[kind, head] = part.astype(out_ref.dtype)
    for copy in small:
        copy.wait()


def build_message(suffix, new, ancestors, lengths, heads):
    _, rows, size = suffix.shape
    lengths = lengths.reshape(1, -1)
    operands = (suffix, new, ancestors, lengths)
    return pl.pallas_call(
        functools.partial(message_kernel, heads),
        in_specs=[pl.BlockSpec(memory_space=pltpu.HBM)] * len(operands),
        out_shape=(
            jax.ShapeDtypeStruct((2, heads, rows // heads, size), suffix.dtype),
            jax.ShapeDtypeStruct(ancestors.shape, ancestors.dtype),
            jax.ShapeDtypeStruct(lengths.shape, lengths.dtype),
        ),
        scratch_shapes=[
            pltpu.VMEM(suffix.shape, suffix.dtype),
            pltpu.VMEM(suffix.shape, jnp.float32),
            pltpu.SemaphoreType.DMA((3 + new.shape[0],)),
        ],
        compiler_params=pltpu.CompilerParams(vmem_limit_bytes=24 << 20),
        cost_estimate=SMALL,
    )(*[in_hbm(operand) for operand in operands])


def iota(shape, axis):
    return lax.broadcasted_iota(jnp.int32, shape, axis)


def lineage_bias(ancestors_ref, lengths_ref, states, owners, suffix_dev):
    steps, particles = ancestors_ref.shape
    per_owner = particles // owners
    each = per_owner * suffix_dev
    my_owner = lax.axis_index("dom")
    my_shard = lax.axis_index("ctx")
    is_last = my_shard == lax.axis_size("ctx") - 1
    square = (particles, particles)
    same = iota(square, 0) == iota(square, 1)

    def as_column(row):
        return jnp.sum(jnp.where(same, row, 0), axis=1, keepdims=True)

    products = {}
    for step in range(steps):
        parent = as_column(ancestors_ref[step : step + 1, :])
        products[step - 1, step] = (parent == iota(square, 1)).astype(jnp.bfloat16)
    for length in range(2, steps + 1):
        for step in range(length - 1, steps):
            after = step - length
            middle = (step + after + 1) // 2
            both = dot(products[middle, step], products[after, middle], NN)
            products[after, step] = both.astype(jnp.bfloat16)
    for step in range(steps):
        states[step, :, :particles] = products[-1, step].astype(jnp.float32)
        for token in range(steps):
            here = slice((1 + token) * particles, (2 + token) * particles)
            if token < step:
                states[step, :, here] = products[token, step].astype(jnp.float32)
            else:
                states[step, :, here] = same.astype(jnp.float32) * float(token == step)
    rows = pl.ds(pl.multiple_of(my_owner * per_owner, per_owner), per_owner)
    mine = jnp.concatenate([states[step, rows, :] for step in range(steps)], axis=0)
    mine = mine.astype(jnp.bfloat16)
    lengths = as_column(lengths_ref[...])
    shape = (particles, owners * each)
    column = iota(shape, 1)
    source = column // each
    first = lax.rem(my_owner + owners - source, owners) * per_owner
    inner = column - source * each
    position = my_shard * suffix_dev + lax.rem(inner, suffix_dev)
    by_particle = iota(shape, 0) == first + inner // suffix_dev
    by_token = iota(shape, 0) == first + lax.rem(inner, per_owner)
    seen = [by_particle & (position < lengths) & jnp.logical_not(is_last)]
    seen += [by_token & (inner // per_owner == token) & is_last for token in range(steps)]
    table = jnp.concatenate([s.astype(jnp.bfloat16) for s in seen], axis=0)
    return jnp.where(dot(mine, table, NN) > 0.5, 0.0, HIDDEN)


def split_kernel(
    heads, block, owners, suffix_dev,
    rows_ref, parents_ref, extents_ref, *refs,
):
    out_refs = refs[: 2 * heads]
    bias_ref, here, wide, states, sems = refs[2 * heads :]
    total = out_refs[0].shape[0]
    places = [(kind, at) for kind in range(2) for at in range(0, total, block)]
    copies = [
        pltpu.make_async_copy(
            rows_ref.at[kind, pl.ds(at * heads, block * heads)],
            here.at[kind, pl.ds(at * heads, block * heads)],
            sems.at[i],
        )
        for i, (kind, at) in enumerate(places)
    ]
    for copy in copies:
        copy.start()
    bias_ref[...] = lineage_bias(parents_ref, extents_ref, states, owners, suffix_dev)
    for i, (kind, at) in enumerate(places):
        copies[i].wait()
        wide[i % 2] = here[kind, at * heads : (at + block) * heads].astype(jnp.float32)
        for head in range(heads):
            part = wide[i % 2, pl.ds(head, block, stride=heads), :]
            out_refs[kind * heads + head][at : at + block] = part.astype(rows_ref.dtype)


def split_prompt(rows, parents, extents, heads, owners, suffix_dev):
    total = rows.shape[1] // heads
    block = math.gcd(total, 512)
    size = rows.shape[2]
    steps, particles = parents.shape
    return pl.pallas_call(
        functools.partial(split_kernel, heads, block, owners, suffix_dev),
        in_specs=[pl.BlockSpec(memory_space=pltpu.HBM)]
        + [pl.BlockSpec(memory_space=pltpu.VMEM)] * 2,
        out_shape=(
            *[jax.ShapeDtypeStruct((total, size), rows.dtype)] * (2 * heads),
            jax.ShapeDtypeStruct(
                (steps * particles // owners, particles * suffix_dev), jnp.float32
            ),
        ),
        scratch_shapes=[
            pltpu.VMEM(rows.shape, rows.dtype),
            pltpu.VMEM((2, block * heads, size), jnp.float32),
            pltpu.VMEM((steps, particles, (1 + steps) * particles), jnp.float32),
            pltpu.SemaphoreType.DMA((2 * total // block,)),
        ],
        compiler_params=pltpu.CompilerParams(vmem_limit_bytes=24 << 20),
        cost_estimate=SMALL,
    )(in_hbm(rows), parents, extents)


def with_ones(values):
    return jnp.concatenate([values, jnp.ones_like(values)], axis=1)


def row_peak(scores):
    return jnp.max(scores, axis=1, keepdims=True)


def weigh(scores, factor, offset):
    return jnp.exp2(scores * factor - offset).astype(jnp.bfloat16)


def work_space(streams, rows, total, size):
    block = math.gcd(total, 512)
    return [
        pltpu.VMEM((3, rows, block), jnp.float32),
        pltpu.VMEM((streams, 2, rows, math.gcd(total, 2 * block)), jnp.bfloat16),
        pltpu.VMEM((streams * rows, 2 * size), jnp.float32),
    ]


def prompt_sum(streams, factor, scores, weights, sums):
    rows, total = streams[0][0].shape[0], streams[0][1].shape[0]
    block, wide = scores.shape[2], weights.shape[3]
    units = [(at, i) for at in range(0, total, block) for i in range(len(streams))]
    offsets = [None] * len(streams)

    def score(n):
        at, i = units[n]
        scores[n % 3] = dot(streams[i][0], streams[i][1][at : at + block], NT)

    def weight(n):
        at, i = units[n]
        if at == 0:
            top = row_peak(scores[n % 3])
            peak = streams[i][3]
            offsets[i] = (top if peak is None else jnp.maximum(top, peak)) * factor
        there = slice(at % wide, at % wide + block)
        weights[i, at // wide % 2, :, there] = weigh(scores[n % 3], factor, offsets[i])

    def gather(n):
        at, i = units[n]
        end = at + block
        if end % wide:
            return
        part = dot(weights[i, at // wide % 2], with_ones(streams[i][2][end - wide : end]), NN)
        here = slice(i * rows, (i + 1) * rows)
        sums[here] = part if end == wide else sums[here] + part

    score(0)
    score(1)
    for n in range(len(units)):
        if n + 2 < len(units):
            score(n + 2)
        weight(n)
        if n:
            gather(n - 1)
    gather(len(units) - 1)
    return offsets


def half_bit(level):
    shard = lax.axis_index("ctx")
    return lax.rem((shard >> level) + (shard >> (level + 1)), 2)


def first_step(q_ref, kept):
    bit = half_bit(0)
    return (bit if kept else 1 - bit) * (q_ref.shape[0] // 2)


def queries_of(q_ref, head, first, number):
    _, per_owner, _, group, size = q_ref.shape
    return q_ref[pl.ds(first, number), :, head].reshape(number * per_owner * group, size)


def prompt_kernel(heads, kept, factor, q_ref, *refs):
    k_refs, v_refs = refs[: len(heads)], refs[len(heads) : 2 * len(heads)]
    together_ref, offset_ref, scores, weights = refs[2 * len(heads) :]
    first, number = first_step(q_ref, kept), q_ref.shape[0] // 2
    streams = [
        (queries_of(q_ref, head, first, number), k_ref, v_ref, None)
        for head, k_ref, v_ref in zip(heads, k_refs, v_refs)
    ]
    offsets = prompt_sum(streams, factor, scores, weights, together_ref)
    offset = jnp.concatenate(offsets, axis=0)
    offset_ref[...] = jnp.broadcast_to(offset, offset_ref.shape)


def in_vmem(count, ordered=True):
    last = [pl.BlockSpec(memory_space=pl.ANY)] if ordered else []
    return [pl.BlockSpec(memory_space=pltpu.VMEM)] * count + last


def begin(queries, prompt, heads, kept, factor):
    steps, per_owner, _, group, size = queries.shape
    rows = steps * per_owner * group // 2
    keys, values = prompt
    space = work_space(len(heads), rows, keys[0].shape[0], size)
    return pl.pallas_call(
        functools.partial(prompt_kernel, heads, kept, factor),
        in_specs=in_vmem(1 + 2 * len(heads), False),
        out_shape=(
            jax.ShapeDtypeStruct((len(heads) * rows, 2 * size), jnp.float32),
            jax.ShapeDtypeStruct((len(heads) * rows, LANES), jnp.float32),
        ),
        scratch_shapes=space[:2],
        compiler_params=pltpu.CompilerParams(vmem_limit_bytes=24 << 20),
        cost_estimate=SMALL,
    )(queries, *[keys[head] for head in heads], *[values[head] for head in heads])


def attend_kernel(heads, kept, factor, owners, started, *refs):
    count = len(heads)
    q_ref, bias_ref = refs[:2]
    row_refs = refs[2 : 2 + owners]
    refs = refs[2 + owners :]
    k_refs, v_refs, refs = refs[:count], refs[count : 2 * count], refs[2 * count :]
    begun, refs = refs[: 2 * started], refs[2 * started + 1 :]
    if kept:
        out, log_sums, *work = refs
    else:
        send_ref, out, log_sums, *work = refs
    steps, per_owner, _, group, size = q_ref.shape
    columns = bias_ref.shape[1]
    number = steps // 2
    rows = number * per_owner * group
    start = first_step(q_ref, kept)

    def suffix_of(head, kind):
        return jnp.concatenate([ref[kind, head] for ref in row_refs], axis=0)

    def suffix_scores(q, head, first, number):
        at = pl.multiple_of(first * per_owner, per_owner)
        bias = bias_ref[pl.ds(at, number * per_owner), :]
        bias = jnp.broadcast_to(bias[:, None, :], (number * per_owner, group, columns))
        return dot(q, suffix_of(head, 0), NT) + bias.reshape(number * per_owner * group, columns)

    def store(i, at, together, offset):
        sums = together[:, size:]
        out[i, pl.ds(at, sums.shape[0]), :] = together[:, :size] / sums
        log_sums[i, pl.ds(at, sums.shape[0]), :] = offset + jnp.log2(sums)
        return sums

    queries = [queries_of(q_ref, head, start, number) for head in heads]
    extras = [suffix_scores(q, head, start, number) for q, head in zip(queries, heads)]
    if started:
        offsets = [begun[1][i * rows : (i + 1) * rows, :1] for i in range(count)]
        togethers = begun[0]
    else:
        streams = [(q, k, v, row_peak(e)) for q, k, v, e in zip(queries, k_refs, v_refs, extras)]
        offsets = prompt_sum(streams, factor, *work)
        togethers = work[-1]
    worst = []
    for i, head in enumerate(heads):
        weight = weigh(extras[i], factor, offsets[i])
        together = togethers[i * rows : (i + 1) * rows]
        together = together + dot(weight, with_ones(suffix_of(head, 1)), NN)
        worst.append(jnp.max(store(i, 0, together, offsets[i])))

    for i, head in enumerate(heads):

        @pl.when(jnp.logical_not(worst[i] < 2.0**100))
        def _():
            @pl.loop(0, number)
            def _(step):
                q = queries_of(q_ref, head, start + step, 1)
                extra = suffix_scores(q, head, start + step, 1)
                scores = dot(q, k_refs[i][...], NT)
                offset = jnp.maximum(row_peak(scores), row_peak(extra)) * factor
                weight = weigh(scores, factor, offset)
                together = dot(weight, with_ones(v_refs[i][...]), NN)
                weight = weigh(extra, factor, offset)
                together = together + dot(weight, with_ones(suffix_of(head, 1)), NN)
                here = per_owner * group
                store(i, pl.multiple_of(step * here, here), together, offset)

    if not kept:
        for i in range(count):
            send_ref[i * rows : (i + 1) * rows] = out[i].astype(jnp.bfloat16)
        column = jnp.concatenate([log_sums[i, :, :1] for i in range(count)], axis=0)
        send_ref[count * rows :] = pack_tail(column)


def attend(queries, prompt, bias, row_list, heads, kept, factor, begun, after):
    steps, per_owner, _, group, size = queries.shape
    rows = steps * per_owner * group // 2
    count = len(heads)
    keys, values = prompt
    operands = (
        queries, bias, *row_list,
        *[keys[head] for head in heads], *[values[head] for head in heads], *begun,
    )
    parts = [((count, rows, size), jnp.float32), ((count, rows, LANES), jnp.float32)]
    send = jax.ShapeDtypeStruct(message_shape(count * rows, size), jnp.bfloat16)
    space = work_space(count, rows, keys[0].shape[0], size)
    return pl.pallas_call(
        functools.partial(
            attend_kernel, heads, kept, factor, len(row_list), len(begun) // 2
        ),
        in_specs=in_vmem(len(operands)),
        out_shape=tuple(jax.ShapeDtypeStruct(*part) for part in parts) if kept else send,
        scratch_shapes=[*([] if kept else [pltpu.VMEM(*part) for part in parts]), *space],
        compiler_params=pltpu.CompilerParams(vmem_limit_bytes=32 << 20),
        cost_estimate=SMALL,
    )(*operands, after)


def merge(out_a, sum_a, out_b, sum_b):
    top = jnp.maximum(sum_a, sum_b)
    weight_a = jnp.exp2(sum_a - top)
    weight_b = jnp.exp2(sum_b - top)
    total = weight_a + weight_b
    return (out_a * weight_a + out_b * weight_b) / total, top + jnp.log2(total)


def merge_kernel(level, last, keep_ref, sums_ref, got_ref, _, *outs):
    count, rows = keep_ref.shape[:2]
    got_sums = unpack_tail(got_ref[count * rows :], count * rows)
    merged = []
    for i in range(count):
        here = slice(i * rows, (i + 1) * rows)
        got = got_ref[here].astype(jnp.float32)
        merged.append(merge(keep_ref[i], sums_ref[i][:, :1], got, got_sums[here]))
    part = rows if last else rows // 2
    bit = half_bit(level) == 1

    def choose(first, value):
        return value if last else jnp.where(first, value[:part], value[part:])

    send = outs[0]
    for i, (out, _) in enumerate(merged):
        send[i * part : (i + 1) * part] = choose(bit, out).astype(jnp.bfloat16)
    send[count * part :] = pack_tail(
        jnp.concatenate([choose(bit, log_sum) for _, log_sum in merged], axis=0)
    )
    if not last:
        _, keep, wide = outs
        for i, (out, log_sum) in enumerate(merged):
            keep[i] = choose(~bit, out)
            wide[i] = jnp.broadcast_to(choose(~bit, log_sum), (part, LANES))


def merge_parts(keep, sums, got, level, last, after):
    count, rows, size = keep.shape
    part = rows if last else rows // 2
    shapes = [jax.ShapeDtypeStruct(message_shape(count * part, size), jnp.bfloat16)]
    if not last:
        shapes.append(jax.ShapeDtypeStruct((count, part, size), jnp.float32))
        shapes.append(jax.ShapeDtypeStruct((count, part, LANES), jnp.float32))
    return pl.pallas_call(
        functools.partial(merge_kernel, level, last),
        in_specs=in_vmem(3),
        out_shape=tuple(shapes),
        compiler_params=pltpu.CompilerParams(vmem_limit_bytes=16 << 20),
        cost_estimate=SMALL,
    )(keep, sums, got, after)


def finish_kernel(mine_ref, got_ref, _, out_ref):
    count, rows = out_ref.shape[0], math.prod(out_ref.shape[1:-1])
    mine_sums = unpack_tail(mine_ref[count * rows :], count * rows)
    got_sums = unpack_tail(got_ref[count * rows :], count * rows)
    for i in range(count):
        here = slice(i * rows, (i + 1) * rows)
        out, _ = merge(
            mine_ref[here].astype(jnp.float32),
            mine_sums[here],
            got_ref[here].astype(jnp.float32),
            got_sums[here],
        )
        out_ref[i] = out.astype(jnp.bfloat16).reshape(out_ref.shape[1:])


def finish(mine, got, shape, after):
    return pl.pallas_call(
        finish_kernel,
        in_specs=in_vmem(2),
        out_shape=jax.ShapeDtypeStruct(shape, jnp.bfloat16),
        compiler_params=pltpu.CompilerParams(vmem_limit_bytes=16 << 20),
        cost_estimate=SMALL,
    )(mine, got, after)


def place_kernel(levels, plan, *refs):
    part_refs = refs[: len(plan)]
    out_ref, sems = refs[-2:]
    copies = []
    for (head, own), ref in zip(plan, part_refs):
        blocks = ref.shape[1]
        bit = half_bit(0)
        at = (bit if own else 1 - bit) * blocks
        for i in range(ref.shape[0]):
            there = out_ref.at[pl.ds(at, blocks), :, head + i]
            copies.append(pltpu.make_async_copy(ref.at[i], there, sems.at[len(copies)]))
    for copy in copies:
        copy.start()
    for copy in copies:
        copy.wait()


def place(out, parts, shape, levels, after):
    arrays = [array for array, _, _ in parts]
    plan = [(head, own) for _, head, own in parts]
    others = [after] if out is None else [after, out]
    return pl.pallas_call(
        functools.partial(place_kernel, levels, plan),
        in_specs=[pl.BlockSpec(memory_space=pltpu.VMEM)] * len(arrays)
        + [pl.BlockSpec(memory_space=pl.ANY), pl.BlockSpec(memory_space=pltpu.HBM)][: len(others)],
        out_specs=pl.BlockSpec(memory_space=pltpu.HBM),
        out_shape=pltpu.HBM(shape, jnp.bfloat16),
        input_output_aliases={} if out is None else {len(arrays) + 1: 0},
        scratch_shapes=[pltpu.SemaphoreType.DMA((sum(a.shape[0] for a in arrays),))],
        compiler_params=pltpu.CompilerParams(vmem_limit_bytes=16 << 20),
        cost_estimate=SMALL,
    )(*arrays, *others)


def on_device(shards, owners, queries, prompt_cache, suffix_cache, new_kv, ancestors, lengths):
    steps, per_owner, heads, group, size = queries.shape
    suffix_dev = suffix_cache.shape[2]
    factor = math.log2(math.e) / math.sqrt(size)
    levels = shards.bit_length() - 1
    if shards != 1 << levels or levels < 2 or steps % 2 or suffix_dev != steps:
        raise ValueError("unsupported sizes")

    def swap(value, bit):
        return lax.ppermute(value, "ctx", [(i, i ^ ((2 << bit) - 1)) for i in range(shards)])

    prompt_rows = prompt_cache.reshape(2, -1, size)
    mine, parents, extents = build_message(
        suffix_cache.reshape(2, -1, size),
        new_kv.reshape(steps, 2, -1, size),
        ancestors,
        lengths,
        heads,
    )
    row_list = [mine] + [
        lax.ppermute(mine, "dom", [(i, (i + hop) % owners) for i in range(owners)])
        for hop in range(1, owners)
    ]
    *prompt, bias = split_prompt(
        prompt_rows, parents, extents, heads, owners, suffix_dev
    )
    prompt = prompt[:heads], prompt[heads:]
    last = [bias]

    def follow(results):
        last[0] = results[0] if isinstance(results, (tuple, list)) else results
        return results

    messages = {}
    blocks = steps * per_owner >> (levels - 1)

    def run_attend(group, kept, begun=()):
        return follow(
            attend(queries, prompt, bias, row_list, group, kept, factor, begun, last[0])
        )

    def run_merges(got, parts):
        for level in range(1, levels):
            send, *parts = follow(merge_parts(*parts, got, level, level == levels - 1, last[0]))
            got = swap(send, level)
        return send, got

    parts = []

    def run_finish(count, send, got):
        return follow(finish(send, got, (count, blocks, group, size), last[0]))

    def run_gather(head, done):
        count = done.shape[0]
        for level in range(levels - 2, 0, -1):
            other = swap(done, level)
            done = jnp.where(
                half_bit(level) == 1,
                jnp.concatenate([other, done], axis=1),
                jnp.concatenate([done, other], axis=1),
            )
        done = done.reshape(count, steps // 2, per_owner, group, size)
        parts.append((done, head, True))
        parts.append((swap(done, 0), head, False))

    first = max(heads // 2, 1)
    groups = [tuple(range(heads))[at : at + first] for at in range(0, heads, first)]
    begun = follow(begin(queries, prompt, groups[0], False, factor))
    arrived, kept = [], []
    for number, one in enumerate(groups):
        arrived.append(swap(run_attend(one, False, () if number else begun), 0))
        if not number:
            kept.append(run_attend(one, True))
    pairs = []
    for number, one in enumerate(groups):
        if number:
            kept.append(run_attend(one, True))
        pairs.append(run_merges(arrived[number], kept[number]))
    for one, pair in zip(groups, pairs):
        run_gather(one[0], run_finish(len(one), *pair))
    late = parts[-1:]
    early = [part for part in parts if not any(part is one for one in late)]
    out = place(None, early, queries.shape, levels, last[0]) if early else None
    return place(out, late, queries.shape, levels, last[0])


def solution(mesh):
    return jax.shard_map(
        functools.partial(on_device, mesh.shape["ctx"], mesh.shape["dom"]),
        mesh=mesh,
        in_specs=(
            P("groups", "dom", "tp", None, None),
            P("groups", "ctx", "tp", None),
            P("groups", "dom", "ctx", "tp", None),
            P("groups", None, "dom", "tp", None),
            P("groups", None),
            P("groups"),
        ),
        out_specs=P("groups", "dom", "tp", None, None),
        check_vma=False,
    )
```

```python
import functools
import math

import jax
import jax.numpy as jnp
from jax import lax
from jax.experimental import pallas as pl
from jax.experimental.pallas import tpu as pltpu
from jax.sharding import PartitionSpec as P

LANES = 128
HIDDEN = -1e30
NN = (((1,), (0,)), ((), ()))
NT = (((1,), (1,)), ((), ()))
SMALL = pl.CostEstimate(flops=0, bytes_accessed=4096, transcendentals=0)


def round_up(value, multiple):
    return -(-value // multiple) * multiple


def dot(a, b, dims):
    return lax.dot_general(a, b, dims, preferred_element_type=jnp.float32)


def eye_mask(rows):
    shape = (rows, LANES)
    return lax.broadcasted_iota(jnp.int32, shape, 0) == lax.broadcasted_iota(jnp.int32, shape, 1)


def column_to_lanes(column):
    rows = column.shape[0]
    block = min(rows, LANES)
    mask = eye_mask(block)
    return jnp.concatenate(
        [
            jnp.sum(jnp.where(mask, column[at : at + block], 0.0), axis=0, keepdims=True)
            for at in range(0, rows, block)
        ],
        axis=0,
    )


def lanes_to_column(lanes, rows):
    block = min(rows, LANES)
    mask = eye_mask(block)
    return jnp.concatenate(
        [
            jnp.sum(jnp.where(mask, lanes[i : i + 1], 0.0), axis=1, keepdims=True)
            for i in range(lanes.shape[0])
        ],
        axis=0,
    )


def tail_rows(rows):
    return round_up(3 * -(-rows // LANES), 16)


def message_shape(rows, size):
    return rows + tail_rows(rows), size


def pack_tail(column):
    lanes = column_to_lanes(column)
    high = lanes.astype(jnp.bfloat16).astype(jnp.float32)
    middle = (lanes - high).astype(jnp.bfloat16).astype(jnp.float32)
    low = lanes - high - middle
    parts = jnp.concatenate([high, middle, low], axis=0)
    spare = tail_rows(column.shape[0]) - parts.shape[0]
    return jnp.concatenate([parts, jnp.zeros((spare, LANES), jnp.float32)], axis=0).astype(
        jnp.bfloat16
    )


def unpack_tail(tail, rows):
    tail = tail.astype(jnp.float32)
    blocks = -(-rows // LANES)
    lanes = tail[:blocks] + tail[blocks : 2 * blocks] + tail[2 * blocks : 3 * blocks]
    return lanes_to_column(lanes, rows)


def in_hbm(array):
    return pltpu.with_memory_space_constraint(array, pltpu.HBM)


def message_kernel(
    heads, suffix_ref, new_ref, ancestors_ref, lengths_ref, prompt_ref,
    out_ref, parents_ref, extents_ref, keys_ref, here, wide, sems,
):
    steps, each = new_ref.shape[0], new_ref.shape[2]
    total = here.shape[1]
    is_last = lax.axis_index("ctx") == lax.axis_size("ctx") - 1
    suffix_copy = pltpu.make_async_copy(suffix_ref, here, sems.at[0])
    token_copies = [
        pltpu.make_async_copy(
            new_ref.at[step], here.at[:, pl.ds(step * each, each)], sems.at[1 + step]
        )
        for step in range(steps)
    ]
    small = [
        pltpu.make_async_copy(ancestors_ref, parents_ref, sems.at[1 + steps]),
        pltpu.make_async_copy(lengths_ref, extents_ref, sems.at[2 + steps]),
        pltpu.make_async_copy(
            prompt_ref.at[0, pl.ds(0, keys_ref.shape[0])], keys_ref, sems.at[3 + steps]
        ),
    ]

    @pl.when(is_last)
    def _():
        for copy in token_copies + small:
            copy.start()
        for copy in token_copies:
            copy.wait()

    @pl.when(jnp.logical_not(is_last))
    def _():
        for copy in [suffix_copy] + small:
            copy.start()
        suffix_copy.wait()

    for kind in range(2):
        wide[kind] = here[kind].astype(jnp.float32)
        for head in range(heads):
            part = wide[kind, pl.ds(head, total // heads, stride=heads), :]
            out_ref[kind, head] = part.astype(out_ref.dtype)
    for copy in small:
        copy.wait()


def build_message(suffix, new, ancestors, lengths, prompt, heads, ahead):
    _, rows, size = suffix.shape
    lengths = lengths.reshape(1, -1)
    operands = (suffix, new, ancestors, lengths, prompt)
    return pl.pallas_call(
        functools.partial(message_kernel, heads),
        in_specs=[pl.BlockSpec(memory_space=pltpu.HBM)] * len(operands),
        out_shape=(
            jax.ShapeDtypeStruct((2, heads, rows // heads, size), suffix.dtype),
            jax.ShapeDtypeStruct(ancestors.shape, ancestors.dtype),
            jax.ShapeDtypeStruct(lengths.shape, lengths.dtype),
            jax.ShapeDtypeStruct((ahead, size), prompt.dtype),
        ),
        scratch_shapes=[
            pltpu.VMEM(suffix.shape, suffix.dtype),
            pltpu.VMEM(suffix.shape, jnp.float32),
            pltpu.SemaphoreType.DMA((4 + new.shape[0],)),
        ],
        compiler_params=pltpu.CompilerParams(vmem_limit_bytes=24 << 20),
        cost_estimate=SMALL,
    )(*[in_hbm(operand) for operand in operands])


def iota(shape, axis):
    return lax.broadcasted_iota(jnp.int32, shape, axis)


def lineage_bias(ancestors_ref, lengths_ref, states, owners, suffix_dev):
    steps, particles = ancestors_ref.shape
    per_owner = particles // owners
    each = per_owner * suffix_dev
    my_owner = lax.axis_index("dom")
    my_shard = lax.axis_index("ctx")
    is_last = my_shard == lax.axis_size("ctx") - 1
    square = (particles, particles)
    same = iota(square, 0) == iota(square, 1)

    def as_column(row):
        return jnp.sum(jnp.where(same, row, 0), axis=1, keepdims=True)

    products = {}
    for step in range(steps):
        parent = as_column(ancestors_ref[step : step + 1, :])
        products[step - 1, step] = (parent == iota(square, 1)).astype(jnp.bfloat16)
    for length in range(2, steps + 1):
        for step in range(length - 1, steps):
            after = step - length
            middle = (step + after + 1) // 2
            both = dot(products[middle, step], products[after, middle], NN)
            products[after, step] = both.astype(jnp.bfloat16)
    for step in range(steps):
        states[step, :, :particles] = products[-1, step].astype(jnp.float32)
        for token in range(steps):
            here = slice((1 + token) * particles, (2 + token) * particles)
            if token < step:
                states[step, :, here] = products[token, step].astype(jnp.float32)
            else:
                states[step, :, here] = same.astype(jnp.float32) * float(token == step)
    rows = pl.ds(pl.multiple_of(my_owner * per_owner, per_owner), per_owner)
    mine = jnp.concatenate([states[step, rows, :] for step in range(steps)], axis=0)
    mine = mine.astype(jnp.bfloat16)
    lengths = as_column(lengths_ref[...])
    shape = (particles, owners * each)
    column = iota(shape, 1)
    source = column // each
    first = lax.rem(my_owner + owners - source, owners) * per_owner
    inner = column - source * each
    position = my_shard * suffix_dev + lax.rem(inner, suffix_dev)
    by_particle = iota(shape, 0) == first + inner // suffix_dev
    by_token = iota(shape, 0) == first + lax.rem(inner, per_owner)
    seen = [by_particle & (position < lengths) & jnp.logical_not(is_last)]
    seen += [by_token & (inner // per_owner == token) & is_last for token in range(steps)]
    table = jnp.concatenate([s.astype(jnp.bfloat16) for s in seen], axis=0)
    return jnp.where(dot(mine, table, NN) > 0.5, 0.0, HIDDEN)


def split_kernel(
    heads, block, owners, suffix_dev,
    rows_ref, keys_ref, parents_ref, extents_ref, *refs,
):
    out_refs = refs[: 2 * heads]
    bias_ref, here, wide, states, sems = refs[2 * heads :]
    total = out_refs[0].shape[0]
    places = [(kind, at) for kind in range(2) for at in range(0, total, block)]
    ahead = keys_ref.shape[0] // (heads * block)
    copies = [
        pltpu.make_async_copy(
            rows_ref.at[kind, pl.ds(at * heads, block * heads)],
            here.at[kind, pl.ds(at * heads, block * heads)],
            sems.at[i],
        )
        for i, (kind, at) in enumerate(places)
    ]
    for copy in copies[ahead:]:
        copy.start()
    bias_ref[...] = lineage_bias(parents_ref, extents_ref, states, owners, suffix_dev)
    for i, (kind, at) in enumerate(places):
        there = slice(at * heads, (at + block) * heads)
        if i < ahead:
            wide[i % 2] = keys_ref[there].astype(jnp.float32)
        else:
            copies[i].wait()
            wide[i % 2] = here[kind, there].astype(jnp.float32)
        for head in range(heads):
            part = wide[i % 2, pl.ds(head, block, stride=heads), :]
            out_refs[kind * heads + head][at : at + block] = part.astype(rows_ref.dtype)


def split_prompt(rows, keys, parents, extents, heads, owners, suffix_dev):
    total = rows.shape[1] // heads
    block = math.gcd(total, 512)
    size = rows.shape[2]
    steps, particles = parents.shape
    return pl.pallas_call(
        functools.partial(split_kernel, heads, block, owners, suffix_dev),
        in_specs=[pl.BlockSpec(memory_space=pltpu.HBM)]
        + [pl.BlockSpec(memory_space=pltpu.VMEM)] * 3,
        out_shape=(
            *[jax.ShapeDtypeStruct((total, size), rows.dtype)] * (2 * heads),
            jax.ShapeDtypeStruct(
                (steps * particles // owners, particles * suffix_dev), jnp.float32
            ),
        ),
        scratch_shapes=[
            pltpu.VMEM(rows.shape, rows.dtype),
            pltpu.VMEM((2, block * heads, size), jnp.float32),
            pltpu.VMEM((steps, particles, (1 + steps) * particles), jnp.float32),
            pltpu.SemaphoreType.DMA((2 * total // block,)),
        ],
        compiler_params=pltpu.CompilerParams(vmem_limit_bytes=24 << 20),
        cost_estimate=SMALL,
    )(in_hbm(rows), keys, parents, extents)


def with_ones(values):
    return jnp.concatenate([values, jnp.ones_like(values)], axis=1)


def row_peak(scores):
    return jnp.max(scores, axis=1, keepdims=True)


def weigh(scores, factor, offset):
    return jnp.exp2(scores * factor - offset).astype(jnp.bfloat16)


def work_space(streams, rows, total, size):
    block = math.gcd(total, 512)
    return [
        pltpu.VMEM((3, rows, block), jnp.float32),
        pltpu.VMEM((streams, 2, rows, math.gcd(total, 2 * block)), jnp.bfloat16),
        pltpu.VMEM((streams * rows, 2 * size), jnp.float32),
    ]


def prompt_sum(streams, factor, scores, weights, sums):
    rows, total = streams[0][0].shape[0], streams[0][1].shape[0]
    block, wide = scores.shape[2], weights.shape[3]
    units = [(at, i) for at in range(0, total, block) for i in range(len(streams))]
    offsets = [None] * len(streams)

    def score(n):
        at, i = units[n]
        scores[n % 3] = dot(streams[i][0], streams[i][1][at : at + block], NT)

    def weight(n):
        at, i = units[n]
        if at == 0:
            top = row_peak(scores[n % 3])
            peak = streams[i][3]
            offsets[i] = (top if peak is None else jnp.maximum(top, peak)) * factor
        there = slice(at % wide, at % wide + block)
        weights[i, at // wide % 2, :, there] = weigh(scores[n % 3], factor, offsets[i])

    def gather(n):
        at, i = units[n]
        end = at + block
        if end % wide:
            return
        part = dot(weights[i, at // wide % 2], with_ones(streams[i][2][end - wide : end]), NN)
        here = slice(i * rows, (i + 1) * rows)
        sums[here] = part if end == wide else sums[here] + part

    score(0)
    score(1)
    for n in range(len(units)):
        if n + 2 < len(units):
            score(n + 2)
        weight(n)
        if n:
            gather(n - 1)
    gather(len(units) - 1)
    return offsets


def half_bit(level):
    shard = lax.axis_index("ctx")
    return lax.rem((shard >> level) + (shard >> (level + 1)), 2)


def first_step(q_ref, kept):
    bit = half_bit(0)
    return (bit if kept else 1 - bit) * (q_ref.shape[0] // 2)


def queries_of(q_ref, head, first, number):
    _, per_owner, _, group, size = q_ref.shape
    return q_ref[pl.ds(first, number), :, head].reshape(number * per_owner * group, size)


def prompt_kernel(heads, kept, factor, q_ref, *refs):
    k_refs, v_refs = refs[: len(heads)], refs[len(heads) : 2 * len(heads)]
    together_ref, offset_ref, scores, weights = refs[2 * len(heads) :]
    first, number = first_step(q_ref, kept), q_ref.shape[0] // 2
    streams = [
        (queries_of(q_ref, head, first, number), k_ref, v_ref, None)
        for head, k_ref, v_ref in zip(heads, k_refs, v_refs)
    ]
    offsets = prompt_sum(streams, factor, scores, weights, together_ref)
    offset = jnp.concatenate(offsets, axis=0)
    offset_ref[...] = jnp.broadcast_to(offset, offset_ref.shape)


def in_vmem(count, ordered=True):
    last = [pl.BlockSpec(memory_space=pl.ANY)] if ordered else []
    return [pl.BlockSpec(memory_space=pltpu.VMEM)] * count + last


def begin(queries, prompt, heads, kept, factor):
    steps, per_owner, _, group, size = queries.shape
    rows = steps * per_owner * group // 2
    keys, values = prompt
    space = work_space(len(heads), rows, keys[0].shape[0], size)
    return pl.pallas_call(
        functools.partial(prompt_kernel, heads, kept, factor),
        in_specs=in_vmem(1 + 2 * len(heads), False),
        out_shape=(
            jax.ShapeDtypeStruct((len(heads) * rows, 2 * size), jnp.float32),
            jax.ShapeDtypeStruct((len(heads) * rows, LANES), jnp.float32),
        ),
        scratch_shapes=space[:2],
        compiler_params=pltpu.CompilerParams(vmem_limit_bytes=24 << 20),
        cost_estimate=SMALL,
    )(queries, *[keys[head] for head in heads], *[values[head] for head in heads])


def attend_kernel(heads, kept, factor, owners, started, *refs):
    count = len(heads)
    q_ref, bias_ref = refs[:2]
    row_refs = refs[2 : 2 + owners]
    refs = refs[2 + owners :]
    k_refs, v_refs, refs = refs[:count], refs[count : 2 * count], refs[2 * count :]
    begun, refs = refs[: 2 * started], refs[2 * started + 1 :]
    if kept:
        out, log_sums, *work = refs
    else:
        send_ref, log_sums, *work = refs
    steps, per_owner, _, group, size = q_ref.shape
    columns = bias_ref.shape[1]
    number = steps // 2
    rows = number * per_owner * group
    start = first_step(q_ref, kept)

    def suffix_of(head, kind):
        return jnp.concatenate([ref[kind, head] for ref in row_refs], axis=0)

    def suffix_scores(q, head, first, number):
        at = pl.multiple_of(first * per_owner, per_owner)
        bias = bias_ref[pl.ds(at, number * per_owner), :]
        bias = jnp.broadcast_to(bias[:, None, :], (number * per_owner, group, columns))
        return dot(q, suffix_of(head, 0), NT) + bias.reshape(number * per_owner * group, columns)

    def store(i, at, together, offset):
        sums = together[:, size:]
        result = together[:, :size] / sums
        if kept:
            out[i, pl.ds(at, sums.shape[0]), :] = result
        else:
            there = pl.ds(pl.multiple_of(i * rows + at, LANES), sums.shape[0])
            send_ref[there, :] = result.astype(jnp.bfloat16)
        log_sums[i, pl.ds(at, sums.shape[0]), :] = offset + jnp.log2(sums)
        return sums

    queries = [queries_of(q_ref, head, start, number) for head in heads]
    extras = [suffix_scores(q, head, start, number) for q, head in zip(queries, heads)]
    if started:
        offsets = [begun[1][i * rows : (i + 1) * rows, :1] for i in range(count)]
        togethers = begun[0]
    else:
        streams = [(q, k, v, row_peak(e)) for q, k, v, e in zip(queries, k_refs, v_refs, extras)]
        offsets = prompt_sum(streams, factor, *work)
        togethers = work[-1]
    worst = []
    for i, head in enumerate(heads):
        weight = weigh(extras[i], factor, offsets[i])
        together = togethers[i * rows : (i + 1) * rows]
        together = together + dot(weight, with_ones(suffix_of(head, 1)), NN)
        worst.append(jnp.max(store(i, 0, together, offsets[i])))

    for i, head in enumerate(heads):

        @pl.when(jnp.logical_not(worst[i] < 2.0**100))
        def _():
            @pl.loop(0, number)
            def _(step):
                q = queries_of(q_ref, head, start + step, 1)
                extra = suffix_scores(q, head, start + step, 1)
                scores = dot(q, k_refs[i][...], NT)
                offset = jnp.maximum(row_peak(scores), row_peak(extra)) * factor
                weight = weigh(scores, factor, offset)
                together = dot(weight, with_ones(v_refs[i][...]), NN)
                weight = weigh(extra, factor, offset)
                together = together + dot(weight, with_ones(suffix_of(head, 1)), NN)
                here = per_owner * group
                store(i, pl.multiple_of(step * here, here), together, offset)

    if not kept:
        column = jnp.concatenate([log_sums[i, :, :1] for i in range(count)], axis=0)
        send_ref[count * rows :] = pack_tail(column)


def attend(queries, prompt, bias, row_list, heads, kept, factor, begun, after):
    steps, per_owner, _, group, size = queries.shape
    rows = steps * per_owner * group // 2
    count = len(heads)
    keys, values = prompt
    operands = (
        queries, bias, *row_list,
        *[keys[head] for head in heads], *[values[head] for head in heads], *begun,
    )
    parts = [((count, rows, size), jnp.float32), ((count, rows, LANES), jnp.float32)]
    send = jax.ShapeDtypeStruct(message_shape(count * rows, size), jnp.bfloat16)
    space = work_space(count, rows, keys[0].shape[0], size)
    return pl.pallas_call(
        functools.partial(
            attend_kernel, heads, kept, factor, len(row_list), len(begun) // 2
        ),
        in_specs=in_vmem(len(operands)),
        out_shape=tuple(jax.ShapeDtypeStruct(*part) for part in parts) if kept else send,
        scratch_shapes=[*([] if kept else [pltpu.VMEM(*parts[1])]), *space],
        compiler_params=pltpu.CompilerParams(vmem_limit_bytes=32 << 20),
        cost_estimate=SMALL,
    )(*operands, after)


def merge(out_a, sum_a, out_b, sum_b):
    top = jnp.maximum(sum_a, sum_b)
    weight_a = jnp.exp2(sum_a - top)
    weight_b = jnp.exp2(sum_b - top)
    total = weight_a + weight_b
    return (out_a * weight_a + out_b * weight_b) / total, top + jnp.log2(total)


def merge_kernel(level, last, keep_ref, sums_ref, got_ref, _, *outs):
    count, rows = keep_ref.shape[:2]
    got_sums = unpack_tail(got_ref[count * rows :], count * rows)
    merged = []
    for i in range(count):
        here = slice(i * rows, (i + 1) * rows)
        got = got_ref[here].astype(jnp.float32)
        merged.append(merge(keep_ref[i], sums_ref[i][:, :1], got, got_sums[here]))
    part = rows if last else rows // 2
    bit = half_bit(level) == 1

    def choose(first, value):
        return value if last else jnp.where(first, value[:part], value[part:])

    send = outs[0]
    for i, (out, _) in enumerate(merged):
        send[i * part : (i + 1) * part] = choose(bit, out).astype(jnp.bfloat16)
    send[count * part :] = pack_tail(
        jnp.concatenate([choose(bit, log_sum) for _, log_sum in merged], axis=0)
    )
    if not last:
        _, keep, wide = outs
        for i, (out, log_sum) in enumerate(merged):
            keep[i] = choose(~bit, out)
            wide[i] = jnp.broadcast_to(choose(~bit, log_sum), (part, LANES))


def merge_parts(keep, sums, got, level, last, after):
    count, rows, size = keep.shape
    part = rows if last else rows // 2
    shapes = [jax.ShapeDtypeStruct(message_shape(count * part, size), jnp.bfloat16)]
    if not last:
        shapes.append(jax.ShapeDtypeStruct((count, part, size), jnp.float32))
        shapes.append(jax.ShapeDtypeStruct((count, part, LANES), jnp.float32))
    return pl.pallas_call(
        functools.partial(merge_kernel, level, last),
        in_specs=in_vmem(3),
        out_shape=tuple(shapes),
        compiler_params=pltpu.CompilerParams(vmem_limit_bytes=16 << 20),
        cost_estimate=SMALL,
    )(keep, sums, got, after)


def finish_kernel(mine_ref, got_ref, _, out_ref):
    count, rows = out_ref.shape[0], math.prod(out_ref.shape[1:-1])
    mine_sums = unpack_tail(mine_ref[count * rows :], count * rows)
    got_sums = unpack_tail(got_ref[count * rows :], count * rows)
    for i in range(count):
        here = slice(i * rows, (i + 1) * rows)
        out, _ = merge(
            mine_ref[here].astype(jnp.float32),
            mine_sums[here],
            got_ref[here].astype(jnp.float32),
            got_sums[here],
        )
        out_ref[i] = out.astype(jnp.bfloat16).reshape(out_ref.shape[1:])


def finish(mine, got, shape, after):
    return pl.pallas_call(
        finish_kernel,
        in_specs=in_vmem(2),
        out_shape=jax.ShapeDtypeStruct(shape, jnp.bfloat16),
        compiler_params=pltpu.CompilerParams(vmem_limit_bytes=16 << 20),
        cost_estimate=SMALL,
    )(mine, got, after)


def place_kernel(levels, plan, *refs):
    part_refs = refs[: len(plan)]
    out_ref, sems = refs[-2:]
    copies = []
    for (head, own), ref in zip(plan, part_refs):
        blocks = ref.shape[1]
        bit = half_bit(0)
        at = (bit if own else 1 - bit) * blocks
        for i in range(ref.shape[0]):
            there = out_ref.at[pl.ds(at, blocks), :, head + i]
            copies.append(pltpu.make_async_copy(ref.at[i], there, sems.at[len(copies)]))
    for copy in copies:
        copy.start()
    for copy in copies:
        copy.wait()


def place(out, parts, shape, levels, after):
    arrays = [array for array, _, _ in parts]
    plan = [(head, own) for _, head, own in parts]
    others = [after] if out is None else [after, out]
    return pl.pallas_call(
        functools.partial(place_kernel, levels, plan),
        in_specs=[pl.BlockSpec(memory_space=pltpu.VMEM)] * len(arrays)
        + [pl.BlockSpec(memory_space=pl.ANY), pl.BlockSpec(memory_space=pltpu.HBM)][: len(others)],
        out_specs=pl.BlockSpec(memory_space=pltpu.HBM),
        out_shape=pltpu.HBM(shape, jnp.bfloat16),
        input_output_aliases={} if out is None else {len(arrays) + 1: 0},
        scratch_shapes=[pltpu.SemaphoreType.DMA((sum(a.shape[0] for a in arrays),))],
        compiler_params=pltpu.CompilerParams(vmem_limit_bytes=16 << 20),
        cost_estimate=SMALL,
    )(*arrays, *others)


def on_device(shards, owners, queries, prompt_cache, suffix_cache, new_kv, ancestors, lengths):
    steps, per_owner, heads, group, size = queries.shape
    suffix_dev = suffix_cache.shape[2]
    factor = math.log2(math.e) / math.sqrt(size)
    levels = shards.bit_length() - 1
    if shards != 1 << levels or levels < 2 or steps % 2 or suffix_dev != steps:
        raise ValueError("unsupported sizes")

    def swap(value, bit):
        return lax.ppermute(value, "ctx", [(i, i ^ ((2 << bit) - 1)) for i in range(shards)])

    prompt_rows = prompt_cache.reshape(2, -1, size)
    mine, parents, extents, keys = build_message(
        suffix_cache.reshape(2, -1, size),
        new_kv.reshape(steps, 2, -1, size),
        ancestors,
        lengths,
        prompt_rows,
        heads,
        math.gcd(prompt_rows.shape[1] // 4, 1024 * heads),
    )
    row_list = [mine] + [
        lax.ppermute(mine, "dom", [(i, (i + hop) % owners) for i in range(owners)])
        for hop in range(1, owners)
    ]
    *prompt, bias = split_prompt(
        prompt_rows, keys, parents, extents, heads, owners, suffix_dev
    )
    prompt = prompt[:heads], prompt[heads:]
    last = [bias]

    def follow(results):
        last[0] = results[0] if isinstance(results, (tuple, list)) else results
        return results

    messages = {}
    blocks = steps * per_owner >> (levels - 1)

    def run_attend(group, kept, begun=()):
        return follow(
            attend(queries, prompt, bias, row_list, group, kept, factor, begun, last[0])
        )

    def run_merges(got, parts):
        for level in range(1, levels):
            send, *parts = follow(merge_parts(*parts, got, level, level == levels - 1, last[0]))
            got = swap(send, level)
        return send, got

    parts = []

    def run_finish(count, send, got):
        return follow(finish(send, got, (count, blocks, group, size), last[0]))

    def run_gather(head, done):
        count = done.shape[0]
        for level in range(levels - 2, 0, -1):
            other = swap(done, level)
            done = jnp.where(
                half_bit(level) == 1,
                jnp.concatenate([other, done], axis=1),
                jnp.concatenate([done, other], axis=1),
            )
        done = done.reshape(count, steps // 2, per_owner, group, size)
        parts.append((done, head, True))
        parts.append((swap(done, 0), head, False))

    first = max(heads // 2, 1)
    groups = [tuple(range(heads))[at : at + first] for at in range(0, heads, first)]
    begun = follow(begin(queries, prompt, groups[0], False, factor))
    arrived, kept = [], []
    for number, one in enumerate(groups):
        arrived.append(swap(run_attend(one, False, () if number else begun), 0))
        if not number:
            kept.append(run_attend(one, True))
    pairs = []
    for number, one in enumerate(groups):
        if number:
            kept.append(run_attend(one, True))
        pairs.append(run_merges(arrived[number], kept[number]))
    for one, pair in zip(groups, pairs):
        run_gather(one[0], run_finish(len(one), *pair))
    late = parts[-1:]
    early = [part for part in parts if not any(part is one for one in late)]
    out = place(None, early, queries.shape, levels, last[0]) if early else None
    return place(out, late, queries.shape, levels, last[0])


def solution(mesh):
    return jax.shard_map(
        functools.partial(on_device, mesh.shape["ctx"], mesh.shape["dom"]),
        mesh=mesh,
        in_specs=(
            P("groups", "dom", "tp", None, None),
            P("groups", "ctx", "tp", None),
            P("groups", "dom", "ctx", "tp", None),
            P("groups", None, "dom", "tp", None),
            P("groups", None),
            P("groups"),
        ),
        out_specs=P("groups", "dom", "tp", None, None),
        check_vma=False,
    )
```

```python
import functools
import math

import jax
import jax.numpy as jnp
from jax import lax
from jax.experimental import pallas as pl
from jax.experimental.pallas import tpu as pltpu
from jax.sharding import PartitionSpec as P

LANES = 128
HIDDEN = -1e30
NN = (((1,), (0,)), ((), ()))
NT = (((1,), (1,)), ((), ()))
SMALL = pl.CostEstimate(flops=0, bytes_accessed=4096, transcendentals=0)


def round_up(value, multiple):
    return -(-value // multiple) * multiple


def dot(a, b, dims):
    return lax.dot_general(a, b, dims, preferred_element_type=jnp.float32)


def eye_mask(rows):
    shape = (rows, LANES)
    return lax.broadcasted_iota(jnp.int32, shape, 0) == lax.broadcasted_iota(jnp.int32, shape, 1)


def column_to_lanes(column):
    rows = column.shape[0]
    block = min(rows, LANES)
    mask = eye_mask(block)
    return jnp.concatenate(
        [
            jnp.sum(jnp.where(mask, column[at : at + block], 0.0), axis=0, keepdims=True)
            for at in range(0, rows, block)
        ],
        axis=0,
    )


def lanes_to_column(lanes, rows):
    block = min(rows, LANES)
    mask = eye_mask(block)
    return jnp.concatenate(
        [
            jnp.sum(jnp.where(mask, lanes[i : i + 1], 0.0), axis=1, keepdims=True)
            for i in range(lanes.shape[0])
        ],
        axis=0,
    )


def tail_rows(rows):
    return round_up(3 * -(-rows // LANES), 16)


def message_shape(rows, size):
    return rows + tail_rows(rows), size


def pack_tail(lanes, rows):
    high = lanes.astype(jnp.bfloat16).astype(jnp.float32)
    middle = (lanes - high).astype(jnp.bfloat16).astype(jnp.float32)
    low = lanes - high - middle
    parts = jnp.concatenate([high, middle, low], axis=0)
    spare = tail_rows(rows) - parts.shape[0]
    return jnp.concatenate([parts, jnp.zeros((spare, LANES), jnp.float32)], axis=0).astype(
        jnp.bfloat16
    )


def unpack_tail(tail, rows):
    tail = tail.astype(jnp.float32)
    blocks = -(-rows // LANES)
    return tail[:blocks] + tail[blocks : 2 * blocks] + tail[2 * blocks : 3 * blocks]


def in_hbm(array):
    return pltpu.with_memory_space_constraint(array, pltpu.HBM)


def message_kernel(
    heads, suffix_ref, new_ref, ancestors_ref, lengths_ref, prompt_ref,
    out_ref, parents_ref, extents_ref, keys_ref, here, wide, sems,
):
    steps, each = new_ref.shape[0], new_ref.shape[2]
    total = here.shape[1]
    is_last = lax.axis_index("ctx") == lax.axis_size("ctx") - 1
    suffix_copy = pltpu.make_async_copy(suffix_ref, here, sems.at[0])
    token_copies = [
        pltpu.make_async_copy(
            new_ref.at[step], here.at[:, pl.ds(step * each, each)], sems.at[1 + step]
        )
        for step in range(steps)
    ]
    small = [
        pltpu.make_async_copy(ancestors_ref, parents_ref, sems.at[1 + steps]),
        pltpu.make_async_copy(lengths_ref, extents_ref, sems.at[2 + steps]),
        pltpu.make_async_copy(
            prompt_ref.at[0, pl.ds(0, keys_ref.shape[0])], keys_ref, sems.at[3 + steps]
        ),
    ]

    @pl.when(is_last)
    def _():
        for copy in token_copies + small:
            copy.start()
        for copy in token_copies:
            copy.wait()

    @pl.when(jnp.logical_not(is_last))
    def _():
        for copy in [suffix_copy] + small:
            copy.start()
        suffix_copy.wait()

    for kind in range(2):
        wide[kind] = here[kind].astype(jnp.float32)
        for head in range(heads):
            part = wide[kind, pl.ds(head, total // heads, stride=heads), :]
            out_ref[kind, head] = part.astype(out_ref.dtype)
    for copy in small:
        copy.wait()


def build_message(suffix, new, ancestors, lengths, prompt, heads, ahead):
    _, rows, size = suffix.shape
    lengths = lengths.reshape(1, -1)
    operands = (suffix, new, ancestors, lengths, prompt)
    return pl.pallas_call(
        functools.partial(message_kernel, heads),
        in_specs=[pl.BlockSpec(memory_space=pltpu.HBM)] * len(operands),
        out_shape=(
            jax.ShapeDtypeStruct((2, heads, rows // heads, size), suffix.dtype),
            jax.ShapeDtypeStruct(ancestors.shape, ancestors.dtype),
            jax.ShapeDtypeStruct(lengths.shape, lengths.dtype),
            jax.ShapeDtypeStruct((ahead, size), prompt.dtype),
        ),
        scratch_shapes=[
            pltpu.VMEM(suffix.shape, suffix.dtype),
            pltpu.VMEM(suffix.shape, jnp.float32),
            pltpu.SemaphoreType.DMA((4 + new.shape[0],)),
        ],
        compiler_params=pltpu.CompilerParams(vmem_limit_bytes=24 << 20),
        cost_estimate=SMALL,
    )(*[in_hbm(operand) for operand in operands])


def iota(shape, axis):
    return lax.broadcasted_iota(jnp.int32, shape, axis)


def lineage_bias(ancestors_ref, lengths_ref, states, owners, suffix_dev):
    steps, particles = ancestors_ref.shape
    per_owner = particles // owners
    each = per_owner * suffix_dev
    my_owner = lax.axis_index("dom")
    my_shard = lax.axis_index("ctx")
    is_last = my_shard == lax.axis_size("ctx") - 1
    square = (particles, particles)
    same = iota(square, 0) == iota(square, 1)

    def as_column(row):
        return jnp.sum(jnp.where(same, row, 0), axis=1, keepdims=True)

    products = {}
    for step in range(steps):
        parent = as_column(ancestors_ref[step : step + 1, :])
        products[step - 1, step] = (parent == iota(square, 1)).astype(jnp.bfloat16)
    for length in range(2, steps + 1):
        for step in range(length - 1, steps):
            after = step - length
            middle = (step + after + 1) // 2
            both = dot(products[middle, step], products[after, middle], NN)
            products[after, step] = both.astype(jnp.bfloat16)
    for step in range(steps):
        states[step, :, :particles] = products[-1, step].astype(jnp.float32)
        for token in range(steps):
            here = slice((1 + token) * particles, (2 + token) * particles)
            if token < step:
                states[step, :, here] = products[token, step].astype(jnp.float32)
            else:
                states[step, :, here] = same.astype(jnp.float32) * float(token == step)
    rows = pl.ds(pl.multiple_of(my_owner * per_owner, per_owner), per_owner)
    mine = jnp.concatenate([states[step, rows, :] for step in range(steps)], axis=0)
    mine = mine.astype(jnp.bfloat16)
    lengths = as_column(lengths_ref[...])
    shape = (particles, owners * each)
    column = iota(shape, 1)
    source = column // each
    first = lax.rem(my_owner + owners - source, owners) * per_owner
    inner = column - source * each
    position = my_shard * suffix_dev + lax.rem(inner, suffix_dev)
    by_particle = iota(shape, 0) == first + inner // suffix_dev
    by_token = iota(shape, 0) == first + lax.rem(inner, per_owner)
    seen = [by_particle & (position < lengths) & jnp.logical_not(is_last)]
    seen += [by_token & (inner // per_owner == token) & is_last for token in range(steps)]
    table = jnp.concatenate([s.astype(jnp.bfloat16) for s in seen], axis=0)
    return jnp.where(dot(mine, table, NN) > 0.5, 0.0, HIDDEN)


def split_kernel(
    heads, block, owners, suffix_dev,
    rows_ref, keys_ref, parents_ref, extents_ref, *refs,
):
    out_refs = refs[: 2 * heads]
    bias_ref, here, wide, states, sems = refs[2 * heads :]
    total = out_refs[0].shape[0]
    places = [(kind, at) for kind in range(2) for at in range(0, total, block)]
    ahead = keys_ref.shape[0] // (heads * block)
    copies = [
        pltpu.make_async_copy(
            rows_ref.at[kind, pl.ds(at * heads, block * heads)],
            here.at[kind, pl.ds(at * heads, block * heads)],
            sems.at[i],
        )
        for i, (kind, at) in enumerate(places)
    ]
    for copy in copies[ahead:]:
        copy.start()
    bias_ref[...] = lineage_bias(parents_ref, extents_ref, states, owners, suffix_dev)
    for i, (kind, at) in enumerate(places):
        there = slice(at * heads, (at + block) * heads)
        if i < ahead:
            wide[i % 2] = keys_ref[there].astype(jnp.float32)
        else:
            copies[i].wait()
            wide[i % 2] = here[kind, there].astype(jnp.float32)
        for head in range(heads):
            part = wide[i % 2, pl.ds(head, block, stride=heads), :]
            out_refs[kind * heads + head][at : at + block] = part.astype(rows_ref.dtype)


def split_prompt(rows, keys, parents, extents, heads, owners, suffix_dev):
    total = rows.shape[1] // heads
    block = math.gcd(total, 512)
    size = rows.shape[2]
    steps, particles = parents.shape
    return pl.pallas_call(
        functools.partial(split_kernel, heads, block, owners, suffix_dev),
        in_specs=[pl.BlockSpec(memory_space=pltpu.HBM)]
        + [pl.BlockSpec(memory_space=pltpu.VMEM)] * 3,
        out_shape=(
            *[jax.ShapeDtypeStruct((total, size), rows.dtype)] * (2 * heads),
            jax.ShapeDtypeStruct(
                (steps * particles // owners, particles * suffix_dev), jnp.float32
            ),
        ),
        scratch_shapes=[
            pltpu.VMEM(rows.shape, rows.dtype),
            pltpu.VMEM((2, block * heads, size), jnp.float32),
            pltpu.VMEM((steps, particles, (1 + steps) * particles), jnp.float32),
            pltpu.SemaphoreType.DMA((2 * total // block,)),
        ],
        compiler_params=pltpu.CompilerParams(vmem_limit_bytes=24 << 20),
        cost_estimate=SMALL,
    )(in_hbm(rows), keys, parents, extents)


def with_ones(values):
    return jnp.concatenate([values, jnp.ones_like(values)], axis=1)


def row_peak(scores):
    return jnp.max(scores, axis=1, keepdims=True)


def weigh(scores, factor, offset):
    return jnp.exp2(scores * factor - offset).astype(jnp.bfloat16)


def work_space(streams, rows, total, size):
    block = math.gcd(total, 512)
    return [
        pltpu.VMEM((3, rows, block), jnp.float32),
        pltpu.VMEM((streams, 2, rows, math.gcd(total, 2 * block)), jnp.bfloat16),
        pltpu.VMEM((streams * rows, 2 * size), jnp.float32),
    ]


def prompt_sum(streams, factor, scores, weights, sums):
    rows, total = streams[0][0].shape[0], streams[0][1].shape[0]
    block, wide = scores.shape[2], weights.shape[3]
    units = [(at, i) for at in range(0, total, block) for i in range(len(streams))]
    offsets = [None] * len(streams)

    def score(n):
        at, i = units[n]
        scores[n % 3] = dot(streams[i][0], streams[i][1][at : at + block], NT)

    def weight(n):
        at, i = units[n]
        if at == 0:
            top = row_peak(scores[n % 3])
            peak = streams[i][3]
            offsets[i] = (top if peak is None else jnp.maximum(top, peak)) * factor
        there = slice(at % wide, at % wide + block)
        weights[i, at // wide % 2, :, there] = weigh(scores[n % 3], factor, offsets[i])

    def gather(n):
        at, i = units[n]
        end = at + block
        if end % wide:
            return
        part = dot(weights[i, at // wide % 2], with_ones(streams[i][2][end - wide : end]), NN)
        here = slice(i * rows, (i + 1) * rows)
        sums[here] = part if end == wide else sums[here] + part

    score(0)
    score(1)
    for n in range(len(units)):
        if n + 2 < len(units):
            score(n + 2)
        weight(n)
        if n:
            gather(n - 1)
    gather(len(units) - 1)
    return offsets


def half_bit(level):
    shard = lax.axis_index("ctx")
    return lax.rem((shard >> level) + (shard >> (level + 1)), 2)


def first_step(q_ref, kept):
    bit = half_bit(0)
    return (bit if kept else 1 - bit) * (q_ref.shape[0] // 2)


def queries_of(q_ref, head, first, number):
    _, per_owner, _, group, size = q_ref.shape
    return q_ref[pl.ds(first, number), :, head].reshape(number * per_owner * group, size)


def prompt_kernel(heads, kept, factor, q_ref, *refs):
    k_refs, v_refs = refs[: len(heads)], refs[len(heads) : 2 * len(heads)]
    together_ref, offset_ref, scores, weights = refs[2 * len(heads) :]
    first, number = first_step(q_ref, kept), q_ref.shape[0] // 2
    streams = [
        (queries_of(q_ref, head, first, number), k_ref, v_ref, None)
        for head, k_ref, v_ref in zip(heads, k_refs, v_refs)
    ]
    offsets = prompt_sum(streams, factor, scores, weights, together_ref)
    offset = jnp.concatenate(offsets, axis=0)
    offset_ref[...] = jnp.broadcast_to(offset, offset_ref.shape)


def in_vmem(count, ordered=True):
    last = [pl.BlockSpec(memory_space=pl.ANY)] if ordered else []
    return [pl.BlockSpec(memory_space=pltpu.VMEM)] * count + last


def begin(queries, prompt, heads, kept, factor):
    steps, per_owner, _, group, size = queries.shape
    rows = steps * per_owner * group // 2
    keys, values = prompt
    space = work_space(len(heads), rows, keys[0].shape[0], size)
    return pl.pallas_call(
        functools.partial(prompt_kernel, heads, kept, factor),
        in_specs=in_vmem(1 + 2 * len(heads), False),
        out_shape=(
            jax.ShapeDtypeStruct((len(heads) * rows, 2 * size), jnp.float32),
            jax.ShapeDtypeStruct((len(heads) * rows, LANES), jnp.float32),
        ),
        scratch_shapes=space[:2],
        compiler_params=pltpu.CompilerParams(vmem_limit_bytes=24 << 20),
        cost_estimate=SMALL,
    )(queries, *[keys[head] for head in heads], *[values[head] for head in heads])


def attend_kernel(heads, kept, factor, owners, started, *refs):
    count = len(heads)
    q_ref, bias_ref = refs[:2]
    row_refs = refs[2 : 2 + owners]
    refs = refs[2 + owners :]
    k_refs, v_refs, refs = refs[:count], refs[count : 2 * count], refs[2 * count :]
    begun, refs = refs[: 2 * started], refs[2 * started + 1 :]
    if kept:
        out, log_sums, *work = refs
    else:
        send_ref, log_sums, *work = refs
    steps, per_owner, _, group, size = q_ref.shape
    columns = bias_ref.shape[1]
    number = steps // 2
    rows = number * per_owner * group
    start = first_step(q_ref, kept)

    def suffix_of(head, kind):
        return jnp.concatenate([ref[kind, head] for ref in row_refs], axis=0)

    def suffix_scores(q, head, first, number):
        at = pl.multiple_of(first * per_owner, per_owner)
        bias = bias_ref[pl.ds(at, number * per_owner), :]
        bias = jnp.broadcast_to(bias[:, None, :], (number * per_owner, group, columns))
        return dot(q, suffix_of(head, 0), NT) + bias.reshape(number * per_owner * group, columns)

    def store(i, at, together, offset):
        sums = together[:, size:]
        result = together[:, :size] / sums
        if kept:
            out[i, pl.ds(at, sums.shape[0]), :] = result
        else:
            there = pl.ds(pl.multiple_of(i * rows + at, LANES), sums.shape[0])
            send_ref[there, :] = result.astype(jnp.bfloat16)
        log_sums[i, pl.ds(at, sums.shape[0]), :] = offset + jnp.log2(sums)
        return sums

    queries = [queries_of(q_ref, head, start, number) for head in heads]
    extras = [suffix_scores(q, head, start, number) for q, head in zip(queries, heads)]
    if started:
        offsets = [begun[1][i * rows : (i + 1) * rows, :1] for i in range(count)]
        togethers = begun[0]
    else:
        streams = [(q, k, v, row_peak(e)) for q, k, v, e in zip(queries, k_refs, v_refs, extras)]
        offsets = prompt_sum(streams, factor, *work)
        togethers = work[-1]
    worst = []
    for i, head in enumerate(heads):
        weight = weigh(extras[i], factor, offsets[i])
        together = togethers[i * rows : (i + 1) * rows]
        together = together + dot(weight, with_ones(suffix_of(head, 1)), NN)
        worst.append(jnp.max(store(i, 0, together, offsets[i])))

    for i, head in enumerate(heads):

        @pl.when(jnp.logical_not(worst[i] < 2.0**100))
        def _():
            @pl.loop(0, number)
            def _(step):
                q = queries_of(q_ref, head, start + step, 1)
                extra = suffix_scores(q, head, start + step, 1)
                scores = dot(q, k_refs[i][...], NT)
                offset = jnp.maximum(row_peak(scores), row_peak(extra)) * factor
                weight = weigh(scores, factor, offset)
                together = dot(weight, with_ones(v_refs[i][...]), NN)
                weight = weigh(extra, factor, offset)
                together = together + dot(weight, with_ones(suffix_of(head, 1)), NN)
                here = per_owner * group
                store(i, pl.multiple_of(step * here, here), together, offset)

    if not kept:
        column = jnp.concatenate([log_sums[i, :, :1] for i in range(count)], axis=0)
        send_ref[count * rows :] = pack_tail(column_to_lanes(column), count * rows)


def attend(queries, prompt, bias, row_list, heads, kept, factor, begun, after):
    steps, per_owner, _, group, size = queries.shape
    rows = steps * per_owner * group // 2
    count = len(heads)
    keys, values = prompt
    operands = (
        queries, bias, *row_list,
        *[keys[head] for head in heads], *[values[head] for head in heads], *begun,
    )
    parts = [((count, rows, size), jnp.float32), ((count, rows, LANES), jnp.float32)]
    send = jax.ShapeDtypeStruct(message_shape(count * rows, size), jnp.bfloat16)
    space = work_space(count, rows, keys[0].shape[0], size)
    return pl.pallas_call(
        functools.partial(
            attend_kernel, heads, kept, factor, len(row_list), len(begun) // 2
        ),
        in_specs=in_vmem(len(operands)),
        out_shape=tuple(jax.ShapeDtypeStruct(*part) for part in parts) if kept else send,
        scratch_shapes=[*([] if kept else [pltpu.VMEM(*parts[1])]), *space],
        compiler_params=pltpu.CompilerParams(vmem_limit_bytes=32 << 20),
        cost_estimate=SMALL,
    )(*operands, after)


def merge_weights(sums_a, sums_b, rows):
    top = jnp.maximum(sums_a, sums_b)
    weight_a = jnp.exp2(sums_a - top)
    weight_b = jnp.exp2(sums_b - top)
    total = weight_a + weight_b
    weights = [lanes_to_column(weight / total, rows) for weight in (weight_a, weight_b)]
    return *weights, top + jnp.log2(total)


def merge_kernel(level, last, keep_ref, sums_ref, got_ref, _, *outs):
    count, rows = keep_ref.shape[:2]
    column = jnp.concatenate([sums_ref[i][:, :1] for i in range(count)], axis=0)
    got_sums = unpack_tail(got_ref[count * rows :], count * rows)
    mine, other, log_sums = merge_weights(column_to_lanes(column), got_sums, count * rows)
    merged = []
    for i in range(count):
        here = slice(i * rows, (i + 1) * rows)
        merged.append(keep_ref[i] * mine[here] + got_ref[here].astype(jnp.float32) * other[here])
    send = outs[0]
    if last:
        for i, out in enumerate(merged):
            send[i * rows : (i + 1) * rows] = out.astype(jnp.bfloat16)
        send[count * rows :] = pack_tail(log_sums, count * rows)
        return
    _, keep, wide = outs
    part = rows // 2
    bit = half_bit(level) == 1
    column = lanes_to_column(log_sums, count * rows)
    leaving = []
    for i, out in enumerate(merged):
        halves = [slice(0, part), slice(part, rows)]
        sums = column[i * rows : (i + 1) * rows]
        first, second = (out[half] for half in halves)
        send[i * part : (i + 1) * part] = jnp.where(bit, first, second).astype(jnp.bfloat16)
        keep[i] = jnp.where(bit, second, first)
        first, second = (sums[half] for half in halves)
        leaving.append(jnp.where(bit, first, second))
        wide[i] = jnp.broadcast_to(jnp.where(bit, second, first), (part, LANES))
    leaving = jnp.concatenate(leaving, axis=0)
    send[count * part :] = pack_tail(column_to_lanes(leaving), count * part)


def merge_parts(keep, sums, got, level, last, after):
    count, rows, size = keep.shape
    part = rows if last else rows // 2
    shapes = [jax.ShapeDtypeStruct(message_shape(count * part, size), jnp.bfloat16)]
    if not last:
        shapes.append(jax.ShapeDtypeStruct((count, part, size), jnp.float32))
        shapes.append(jax.ShapeDtypeStruct((count, part, LANES), jnp.float32))
    return pl.pallas_call(
        functools.partial(merge_kernel, level, last),
        in_specs=in_vmem(3),
        out_shape=tuple(shapes),
        compiler_params=pltpu.CompilerParams(vmem_limit_bytes=16 << 20),
        cost_estimate=SMALL,
    )(keep, sums, got, after)


def finish_kernel(mine_ref, got_ref, _, out_ref):
    count, rows = out_ref.shape[0], math.prod(out_ref.shape[1:-1])
    sums = [unpack_tail(ref[count * rows :], count * rows) for ref in (mine_ref, got_ref)]
    mine, other, _ = merge_weights(*sums, count * rows)
    for i in range(count):
        here = slice(i * rows, (i + 1) * rows)
        out = mine_ref[here].astype(jnp.float32) * mine[here]
        out = out + got_ref[here].astype(jnp.float32) * other[here]
        out_ref[i] = out.astype(jnp.bfloat16).reshape(out_ref.shape[1:])


def finish(mine, got, shape, after):
    return pl.pallas_call(
        finish_kernel,
        in_specs=in_vmem(2),
        out_shape=jax.ShapeDtypeStruct(shape, jnp.bfloat16),
        compiler_params=pltpu.CompilerParams(vmem_limit_bytes=16 << 20),
        cost_estimate=SMALL,
    )(mine, got, after)


def place_kernel(levels, plan, *refs):
    part_refs = refs[: len(plan)]
    out_ref, sems = refs[-2:]
    copies = []
    for (head, own), ref in zip(plan, part_refs):
        blocks = ref.shape[1]
        bit = half_bit(0)
        at = (bit if own else 1 - bit) * blocks
        for i in range(ref.shape[0]):
            there = out_ref.at[pl.ds(at, blocks), :, head + i]
            copies.append(pltpu.make_async_copy(ref.at[i], there, sems.at[len(copies)]))
    for copy in copies:
        copy.start()
    for copy in copies:
        copy.wait()


def place(out, parts, shape, levels, after):
    arrays = [array for array, _, _ in parts]
    plan = [(head, own) for _, head, own in parts]
    others = [after] if out is None else [after, out]
    return pl.pallas_call(
        functools.partial(place_kernel, levels, plan),
        in_specs=[pl.BlockSpec(memory_space=pltpu.VMEM)] * len(arrays)
        + [pl.BlockSpec(memory_space=pl.ANY), pl.BlockSpec(memory_space=pltpu.HBM)][: len(others)],
        out_specs=pl.BlockSpec(memory_space=pltpu.HBM),
        out_shape=pltpu.HBM(shape, jnp.bfloat16),
        input_output_aliases={} if out is None else {len(arrays) + 1: 0},
        scratch_shapes=[pltpu.SemaphoreType.DMA((sum(a.shape[0] for a in arrays),))],
        compiler_params=pltpu.CompilerParams(vmem_limit_bytes=16 << 20),
        cost_estimate=SMALL,
    )(*arrays, *others)


def on_device(shards, owners, queries, prompt_cache, suffix_cache, new_kv, ancestors, lengths):
    steps, per_owner, heads, group, size = queries.shape
    suffix_dev = suffix_cache.shape[2]
    factor = math.log2(math.e) / math.sqrt(size)
    levels = shards.bit_length() - 1
    if shards != 1 << levels or levels < 2 or steps % 2 or suffix_dev != steps:
        raise ValueError("unsupported sizes")

    def swap(value, bit):
        return lax.ppermute(value, "ctx", [(i, i ^ ((2 << bit) - 1)) for i in range(shards)])

    prompt_rows = prompt_cache.reshape(2, -1, size)
    mine, parents, extents, keys = build_message(
        suffix_cache.reshape(2, -1, size),
        new_kv.reshape(steps, 2, -1, size),
        ancestors,
        lengths,
        prompt_rows,
        heads,
        math.gcd(prompt_rows.shape[1] // 4, 1024 * heads),
    )
    row_list = [mine] + [
        lax.ppermute(mine, "dom", [(i, (i + hop) % owners) for i in range(owners)])
        for hop in range(1, owners)
    ]
    *prompt, bias = split_prompt(
        prompt_rows, keys, parents, extents, heads, owners, suffix_dev
    )
    prompt = prompt[:heads], prompt[heads:]
    last = [bias]

    def follow(results):
        last[0] = results[0] if isinstance(results, (tuple, list)) else results
        return results

    messages = {}
    blocks = steps * per_owner >> (levels - 1)

    def run_attend(group, kept, begun=()):
        return follow(
            attend(queries, prompt, bias, row_list, group, kept, factor, begun, last[0])
        )

    def run_merges(got, parts):
        for level in range(1, levels):
            send, *parts = follow(merge_parts(*parts, got, level, level == levels - 1, last[0]))
            got = swap(send, level)
        return send, got

    parts = []

    def run_finish(count, send, got):
        return follow(finish(send, got, (count, blocks, group, size), last[0]))

    def run_gather(head, done):
        count = done.shape[0]
        for level in range(levels - 2, 0, -1):
            other = swap(done, level)
            done = jnp.where(
                half_bit(level) == 1,
                jnp.concatenate([other, done], axis=1),
                jnp.concatenate([done, other], axis=1),
            )
        done = done.reshape(count, steps // 2, per_owner, group, size)
        parts.append((done, head, True))
        parts.append((swap(done, 0), head, False))

    first = max(heads // 2, 1)
    groups = [tuple(range(heads))[at : at + first] for at in range(0, heads, first)]
    begun = follow(begin(queries, prompt, groups[0], False, factor))
    arrived, kept = [], []
    for number, one in enumerate(groups):
        arrived.append(swap(run_attend(one, False, () if number else begun), 0))
        if not number:
            kept.append(run_attend(one, True))
    pairs = []
    for number, one in enumerate(groups):
        if number:
            kept.append(run_attend(one, True))
        pairs.append(run_merges(arrived[number], kept[number]))
    for one, pair in zip(groups, pairs):
        run_gather(one[0], run_finish(len(one), *pair))
    late = parts[-1:]
    early = [part for part in parts if not any(part is one for one in late)]
    out = place(None, early, queries.shape, levels, last[0]) if early else None
    return place(out, late, queries.shape, levels, last[0])


def solution(mesh):
    return jax.shard_map(
        functools.partial(on_device, mesh.shape["ctx"], mesh.shape["dom"]),
        mesh=mesh,
        in_specs=(
            P("groups", "dom", "tp", None, None),
            P("groups", "ctx", "tp", None),
            P("groups", "dom", "ctx", "tp", None),
            P("groups", None, "dom", "tp", None),
            P("groups", None),
            P("groups"),
        ),
        out_specs=P("groups", "dom", "tp", None, None),
        check_vma=False,
    )
```

```python
import functools
import math

import jax
import jax.numpy as jnp
from jax import lax
from jax.experimental import pallas as pl
from jax.experimental.pallas import tpu as pltpu
from jax.sharding import PartitionSpec as P

LANES = 128
HIDDEN = -1e30
NN = (((1,), (0,)), ((), ()))
NT = (((1,), (1,)), ((), ()))
SMALL = pl.CostEstimate(flops=0, bytes_accessed=4096, transcendentals=0)


def round_up(value, multiple):
    return -(-value // multiple) * multiple


def dot(a, b, dims):
    return lax.dot_general(a, b, dims, preferred_element_type=jnp.float32)


def eye_mask(rows):
    shape = (rows, LANES)
    return lax.broadcasted_iota(jnp.int32, shape, 0) == lax.broadcasted_iota(jnp.int32, shape, 1)


def column_to_lanes(column):
    rows = column.shape[0]
    block = min(rows, LANES)
    mask = eye_mask(block)
    return jnp.concatenate(
        [
            jnp.sum(jnp.where(mask, column[at : at + block], 0.0), axis=0, keepdims=True)
            for at in range(0, rows, block)
        ],
        axis=0,
    )


def lanes_to_column(lanes, rows):
    block = min(rows, LANES)
    mask = eye_mask(block)
    return jnp.concatenate(
        [
            jnp.sum(jnp.where(mask, lanes[i : i + 1], 0.0), axis=1, keepdims=True)
            for i in range(lanes.shape[0])
        ],
        axis=0,
    )


def tail_rows(rows):
    return round_up(3 * -(-rows // LANES), 16)


def message_shape(rows, size):
    return rows + tail_rows(rows), size


def pack_tail(lanes, rows):
    high = lanes.astype(jnp.bfloat16).astype(jnp.float32)
    middle = (lanes - high).astype(jnp.bfloat16).astype(jnp.float32)
    low = lanes - high - middle
    parts = jnp.concatenate([high, middle, low], axis=0)
    spare = tail_rows(rows) - parts.shape[0]
    return jnp.concatenate([parts, jnp.zeros((spare, LANES), jnp.float32)], axis=0).astype(
        jnp.bfloat16
    )


def unpack_tail(tail, rows):
    tail = tail.astype(jnp.float32)
    blocks = -(-rows // LANES)
    return tail[:blocks] + tail[blocks : 2 * blocks] + tail[2 * blocks : 3 * blocks]


def in_hbm(array):
    return pltpu.with_memory_space_constraint(array, pltpu.HBM)


def message_kernel(
    heads, suffix_ref, new_ref, ancestors_ref, lengths_ref, prompt_ref,
    out_ref, parents_ref, extents_ref, keys_ref, here, wide, sems,
):
    steps, each = new_ref.shape[0], new_ref.shape[2]
    total = here.shape[1]
    is_last = lax.axis_index("ctx") == lax.axis_size("ctx") - 1
    suffix_copy = pltpu.make_async_copy(suffix_ref, here, sems.at[0])
    token_copies = [
        pltpu.make_async_copy(
            new_ref.at[step], here.at[:, pl.ds(step * each, each)], sems.at[1 + step]
        )
        for step in range(steps)
    ]
    small = [
        pltpu.make_async_copy(ancestors_ref, parents_ref, sems.at[1 + steps]),
        pltpu.make_async_copy(lengths_ref, extents_ref, sems.at[2 + steps]),
        pltpu.make_async_copy(
            prompt_ref.at[0, pl.ds(0, keys_ref.shape[0])], keys_ref, sems.at[3 + steps]
        ),
    ]

    @pl.when(is_last)
    def _():
        for copy in token_copies + small:
            copy.start()
        for copy in token_copies:
            copy.wait()

    @pl.when(jnp.logical_not(is_last))
    def _():
        for copy in [suffix_copy] + small:
            copy.start()
        suffix_copy.wait()

    for kind in range(2):
        wide[kind] = here[kind].astype(jnp.float32)
        for head in range(heads):
            part = wide[kind, pl.ds(head, total // heads, stride=heads), :]
            out_ref[kind, head] = part.astype(out_ref.dtype)
    for copy in small:
        copy.wait()


def build_message(suffix, new, ancestors, lengths, prompt, heads, ahead):
    _, rows, size = suffix.shape
    lengths = lengths.reshape(1, -1)
    operands = (suffix, new, ancestors, lengths, prompt)
    return pl.pallas_call(
        functools.partial(message_kernel, heads),
        in_specs=[pl.BlockSpec(memory_space=pltpu.HBM)] * len(operands),
        out_shape=(
            jax.ShapeDtypeStruct((2, heads, rows // heads, size), suffix.dtype),
            jax.ShapeDtypeStruct(ancestors.shape, ancestors.dtype),
            jax.ShapeDtypeStruct(lengths.shape, lengths.dtype),
            jax.ShapeDtypeStruct((ahead, size), prompt.dtype),
        ),
        scratch_shapes=[
            pltpu.VMEM(suffix.shape, suffix.dtype),
            pltpu.VMEM(suffix.shape, jnp.float32),
            pltpu.SemaphoreType.DMA((4 + new.shape[0],)),
        ],
        compiler_params=pltpu.CompilerParams(vmem_limit_bytes=24 << 20),
        cost_estimate=SMALL,
    )(*[in_hbm(operand) for operand in operands])


def iota(shape, axis):
    return lax.broadcasted_iota(jnp.int32, shape, axis)


def lineage_bias(ancestors_ref, lengths_ref, states, owners, suffix_dev):
    steps, particles = ancestors_ref.shape
    per_owner = particles // owners
    each = per_owner * suffix_dev
    my_owner = lax.axis_index("dom")
    my_shard = lax.axis_index("ctx")
    is_last = my_shard == lax.axis_size("ctx") - 1
    square = (particles, particles)
    same = iota(square, 0) == iota(square, 1)

    def as_column(row):
        return jnp.sum(jnp.where(same, row, 0), axis=1, keepdims=True)

    products = {}
    for step in range(steps):
        parent = as_column(ancestors_ref[step : step + 1, :])
        products[step - 1, step] = (parent == iota(square, 1)).astype(jnp.bfloat16)
    for length in range(2, steps + 1):
        for step in range(length - 1, steps):
            after = step - length
            middle = (step + after + 1) // 2
            both = dot(products[middle, step], products[after, middle], NN)
            products[after, step] = both.astype(jnp.bfloat16)
    for step in range(steps):
        states[step, :, :particles] = products[-1, step].astype(jnp.float32)
        for token in range(steps):
            here = slice((1 + token) * particles, (2 + token) * particles)
            if token < step:
                states[step, :, here] = products[token, step].astype(jnp.float32)
            else:
                states[step, :, here] = same.astype(jnp.float32) * float(token == step)
    rows = pl.ds(pl.multiple_of(my_owner * per_owner, per_owner), per_owner)
    mine = jnp.concatenate([states[step, rows, :] for step in range(steps)], axis=0)
    mine = mine.astype(jnp.bfloat16)
    lengths = as_column(lengths_ref[...])
    shape = (particles, owners * each)
    column = iota(shape, 1)
    source = column // each
    first = lax.rem(my_owner + owners - source, owners) * per_owner
    inner = column - source * each
    position = my_shard * suffix_dev + lax.rem(inner, suffix_dev)
    by_particle = iota(shape, 0) == first + inner // suffix_dev
    by_token = iota(shape, 0) == first + lax.rem(inner, per_owner)
    seen = [by_particle & (position < lengths) & jnp.logical_not(is_last)]
    seen += [by_token & (inner // per_owner == token) & is_last for token in range(steps)]
    table = jnp.concatenate([s.astype(jnp.bfloat16) for s in seen], axis=0)
    return jnp.where(dot(mine, table, NN) > 0.5, 0.0, HIDDEN)


def split_kernel(
    heads, block, owners, suffix_dev,
    rows_ref, keys_ref, parents_ref, extents_ref, *refs,
):
    out_refs = refs[: 2 * heads]
    bias_ref, here, wide, states, sems = refs[2 * heads :]
    total = out_refs[0].shape[0]
    places = [(kind, at) for kind in range(2) for at in range(0, total, block)]
    ahead = keys_ref.shape[0] // (heads * block)
    copies = [
        pltpu.make_async_copy(
            rows_ref.at[kind, pl.ds(at * heads, block * heads)],
            here.at[kind, pl.ds(at * heads, block * heads)],
            sems.at[i],
        )
        for i, (kind, at) in enumerate(places)
    ]
    for copy in copies[ahead:]:
        copy.start()
    bias_ref[...] = lineage_bias(parents_ref, extents_ref, states, owners, suffix_dev)
    for i, (kind, at) in enumerate(places):
        there = slice(at * heads, (at + block) * heads)
        if i < ahead:
            wide[i % 2] = keys_ref[there].astype(jnp.float32)
        else:
            copies[i].wait()
            wide[i % 2] = here[kind, there].astype(jnp.float32)
        for head in range(heads):
            part = wide[i % 2, pl.ds(head, block, stride=heads), :]
            out_refs[kind * heads + head][at : at + block] = part.astype(rows_ref.dtype)


def split_prompt(rows, keys, parents, extents, heads, owners, suffix_dev):
    total = rows.shape[1] // heads
    block = math.gcd(total, 512)
    size = rows.shape[2]
    steps, particles = parents.shape
    return pl.pallas_call(
        functools.partial(split_kernel, heads, block, owners, suffix_dev),
        in_specs=[pl.BlockSpec(memory_space=pltpu.HBM)]
        + [pl.BlockSpec(memory_space=pltpu.VMEM)] * 3,
        out_shape=(
            *[jax.ShapeDtypeStruct((total, size), rows.dtype)] * (2 * heads),
            jax.ShapeDtypeStruct(
                (steps * particles // owners, particles * suffix_dev), jnp.float32
            ),
        ),
        scratch_shapes=[
            pltpu.VMEM(rows.shape, rows.dtype),
            pltpu.VMEM((2, block * heads, size), jnp.float32),
            pltpu.VMEM((steps, particles, (1 + steps) * particles), jnp.float32),
            pltpu.SemaphoreType.DMA((2 * total // block,)),
        ],
        compiler_params=pltpu.CompilerParams(vmem_limit_bytes=24 << 20),
        cost_estimate=SMALL,
    )(in_hbm(rows), keys, parents, extents)


def with_ones(values):
    return jnp.concatenate([values, jnp.ones_like(values)], axis=1)


def row_peak(scores):
    return jnp.max(scores, axis=1, keepdims=True)


def weigh(scores, factor, offset):
    return jnp.exp2(scores * factor - offset).astype(jnp.bfloat16)


def work_space(streams, rows, total, size):
    block = math.gcd(total, 512)
    return [
        pltpu.VMEM((3, rows, block), jnp.float32),
        pltpu.VMEM((streams, 2, rows, math.gcd(total, 2 * block)), jnp.bfloat16),
        pltpu.VMEM((streams * rows, 2 * size), jnp.float32),
    ]


def prompt_sum(streams, factor, scores, weights, sums):
    rows, total = streams[0][0].shape[0], streams[0][1].shape[0]
    block, wide = scores.shape[2], weights.shape[3]
    units = [(at, i) for at in range(0, total, block) for i in range(len(streams))]
    offsets = [None] * len(streams)

    def score(n):
        at, i = units[n]
        scores[n % 3] = dot(streams[i][0], streams[i][1][at : at + block], NT)

    def weight(n):
        at, i = units[n]
        if at == 0:
            top = row_peak(scores[n % 3])
            peak = streams[i][3]
            offsets[i] = (top if peak is None else jnp.maximum(top, peak)) * factor
        there = slice(at % wide, at % wide + block)
        weights[i, at // wide % 2, :, there] = weigh(scores[n % 3], factor, offsets[i])

    def gather(n):
        at, i = units[n]
        end = at + block
        if end % wide:
            return
        part = dot(weights[i, at // wide % 2], with_ones(streams[i][2][end - wide : end]), NN)
        here = slice(i * rows, (i + 1) * rows)
        sums[here] = part if end == wide else sums[here] + part

    score(0)
    score(1)
    for n in range(len(units)):
        if n + 2 < len(units):
            score(n + 2)
        weight(n)
        if n:
            gather(n - 1)
    gather(len(units) - 1)
    return offsets


def half_bit(level):
    shard = lax.axis_index("ctx")
    return lax.rem((shard >> level) + (shard >> (level + 1)), 2)


def first_step(q_ref, kept):
    bit = half_bit(0)
    return (bit if kept else 1 - bit) * (q_ref.shape[0] // 2)


def queries_of(q_ref, head, first, number):
    _, per_owner, _, group, size = q_ref.shape
    return q_ref[pl.ds(first, number), :, head].reshape(number * per_owner * group, size)


def prompt_kernel(heads, kept, factor, q_ref, *refs):
    k_refs, v_refs = refs[: len(heads)], refs[len(heads) : 2 * len(heads)]
    together_ref, offset_ref, scores, weights = refs[2 * len(heads) :]
    first, number = first_step(q_ref, kept), q_ref.shape[0] // 2
    streams = [
        (queries_of(q_ref, head, first, number), k_ref, v_ref, None)
        for head, k_ref, v_ref in zip(heads, k_refs, v_refs)
    ]
    offsets = prompt_sum(streams, factor, scores, weights, together_ref)
    offset = jnp.concatenate(offsets, axis=0)
    offset_ref[...] = jnp.broadcast_to(offset, offset_ref.shape)


def in_vmem(count, ordered=True):
    last = [pl.BlockSpec(memory_space=pl.ANY)] if ordered else []
    return [pl.BlockSpec(memory_space=pltpu.VMEM)] * count + last


def begin(queries, prompt, heads, kept, factor):
    steps, per_owner, _, group, size = queries.shape
    rows = steps * per_owner * group // 2
    keys, values = prompt
    space = work_space(len(heads), rows, keys[0].shape[0], size)
    return pl.pallas_call(
        functools.partial(prompt_kernel, heads, kept, factor),
        in_specs=in_vmem(1 + 2 * len(heads), False),
        out_shape=(
            jax.ShapeDtypeStruct((len(heads) * rows, 2 * size), jnp.float32),
            jax.ShapeDtypeStruct((len(heads) * rows, LANES), jnp.float32),
        ),
        scratch_shapes=space[:2],
        compiler_params=pltpu.CompilerParams(vmem_limit_bytes=24 << 20),
        cost_estimate=SMALL,
    )(queries, *[keys[head] for head in heads], *[values[head] for head in heads])


def attend_kernel(heads, kept, factor, owners, started, *refs):
    count = len(heads)
    q_ref, bias_ref = refs[:2]
    row_refs = refs[2 : 2 + owners]
    refs = refs[2 + owners :]
    k_refs, v_refs, refs = refs[:count], refs[count : 2 * count], refs[2 * count :]
    begun, refs = refs[: 2 * started], refs[2 * started + 1 :]
    if kept:
        out, log_sums, *work = refs
    else:
        send_ref, log_sums, *work = refs
    steps, per_owner, _, group, size = q_ref.shape
    columns = bias_ref.shape[1]
    number = steps // 2
    rows = number * per_owner * group
    start = first_step(q_ref, kept)

    def suffix_of(head, kind):
        return jnp.concatenate([ref[kind, head] for ref in row_refs], axis=0)

    def suffix_scores(q, head, first, number):
        at = pl.multiple_of(first * per_owner, per_owner)
        bias = bias_ref[pl.ds(at, number * per_owner), :]
        bias = jnp.broadcast_to(bias[:, None, :], (number * per_owner, group, columns))
        return dot(q, suffix_of(head, 0), NT) + bias.reshape(number * per_owner * group, columns)

    def store(i, at, together, offset):
        sums = together[:, size:]
        result = together[:, :size] / sums
        if kept:
            out[i, pl.ds(at, sums.shape[0]), :] = result
        else:
            there = pl.ds(pl.multiple_of(i * rows + at, LANES), sums.shape[0])
            send_ref[there, :] = result.astype(jnp.bfloat16)
        log_sums[i, pl.ds(at, sums.shape[0]), :] = offset + jnp.log2(sums)
        return sums

    queries = [queries_of(q_ref, head, start, number) for head in heads]
    extras = [suffix_scores(q, head, start, number) for q, head in zip(queries, heads)]
    if started:
        offsets = [begun[1][i * rows : (i + 1) * rows, :1] for i in range(count)]
        togethers = begun[0]
    else:
        streams = [(q, k, v, row_peak(e)) for q, k, v, e in zip(queries, k_refs, v_refs, extras)]
        offsets = prompt_sum(streams, factor, *work)
        togethers = work[-1]
    worst = []
    for i, head in enumerate(heads):
        weight = weigh(extras[i], factor, offsets[i])
        together = togethers[i * rows : (i + 1) * rows]
        together = together + dot(weight, with_ones(suffix_of(head, 1)), NN)
        worst.append(jnp.max(store(i, 0, together, offsets[i])))

    for i, head in enumerate(heads):

        @pl.when(jnp.logical_not(worst[i] < 2.0**100))
        def _():
            @pl.loop(0, number)
            def _(step):
                q = queries_of(q_ref, head, start + step, 1)
                extra = suffix_scores(q, head, start + step, 1)
                scores = dot(q, k_refs[i][...], NT)
                offset = jnp.maximum(row_peak(scores), row_peak(extra)) * factor
                weight = weigh(scores, factor, offset)
                together = dot(weight, with_ones(v_refs[i][...]), NN)
                weight = weigh(extra, factor, offset)
                together = together + dot(weight, with_ones(suffix_of(head, 1)), NN)
                here = per_owner * group
                store(i, pl.multiple_of(step * here, here), together, offset)

    if not kept:
        column = jnp.concatenate([log_sums[i] for i in range(count)], axis=0)
        send_ref[count * rows :] = pack_tail(column_to_lanes(column), count * rows)


def attend(queries, prompt, bias, row_list, heads, kept, factor, begun, after):
    steps, per_owner, _, group, size = queries.shape
    rows = steps * per_owner * group // 2
    count = len(heads)
    keys, values = prompt
    operands = (
        queries, bias, *row_list,
        *[keys[head] for head in heads], *[values[head] for head in heads], *begun,
    )
    parts = [((count, rows, size), jnp.float32), ((count, rows, LANES), jnp.float32)]
    send = jax.ShapeDtypeStruct(message_shape(count * rows, size), jnp.bfloat16)
    space = work_space(count, rows, keys[0].shape[0], size)
    return pl.pallas_call(
        functools.partial(
            attend_kernel, heads, kept, factor, len(row_list), len(begun) // 2
        ),
        in_specs=in_vmem(len(operands)),
        out_shape=tuple(jax.ShapeDtypeStruct(*part) for part in parts) if kept else send,
        scratch_shapes=[*([] if kept else [pltpu.VMEM(*parts[1])]), *space],
        compiler_params=pltpu.CompilerParams(vmem_limit_bytes=32 << 20),
        cost_estimate=SMALL,
    )(*operands, after)


def merge_weights(sums_a, sums_b, rows):
    top = jnp.maximum(sums_a, sums_b)
    weight_a = jnp.exp2(sums_a - top)
    weight_b = jnp.exp2(sums_b - top)
    total = weight_a + weight_b
    weights = [lanes_to_column(weight / total, rows) for weight in (weight_a, weight_b)]
    return *weights, top + jnp.log2(total)


def merge_kernel(level, last, keep_ref, sums_ref, got_ref, _, *outs):
    count, rows = keep_ref.shape[:2]
    column = jnp.concatenate([sums_ref[i] for i in range(count)], axis=0)
    got_sums = unpack_tail(got_ref[count * rows :], count * rows)
    mine, other, log_sums = merge_weights(column_to_lanes(column), got_sums, count * rows)
    merged = []
    for i in range(count):
        here = slice(i * rows, (i + 1) * rows)
        merged.append(keep_ref[i] * mine[here] + got_ref[here].astype(jnp.float32) * other[here])
    send = outs[0]
    if last:
        for i, out in enumerate(merged):
            send[i * rows : (i + 1) * rows] = out.astype(jnp.bfloat16)
        send[count * rows :] = pack_tail(log_sums, count * rows)
        return
    _, keep, wide = outs
    part = rows // 2
    bit = half_bit(level) == 1
    column = lanes_to_column(log_sums, count * rows)
    leaving = []
    for i, out in enumerate(merged):
        halves = [slice(0, part), slice(part, rows)]
        sums = column[i * rows : (i + 1) * rows]
        first, second = (out[half] for half in halves)
        send[i * part : (i + 1) * part] = jnp.where(bit, first, second).astype(jnp.bfloat16)
        keep[i] = jnp.where(bit, second, first)
        first, second = (sums[half] for half in halves)
        leaving.append(jnp.where(bit, first, second))
        wide[i] = jnp.broadcast_to(jnp.where(bit, second, first), (part, LANES))
    leaving = jnp.concatenate(leaving, axis=0)
    send[count * part :] = pack_tail(column_to_lanes(leaving), count * part)


def merge_parts(keep, sums, got, level, last, after):
    count, rows, size = keep.shape
    part = rows if last else rows // 2
    shapes = [jax.ShapeDtypeStruct(message_shape(count * part, size), jnp.bfloat16)]
    if not last:
        shapes.append(jax.ShapeDtypeStruct((count, part, size), jnp.float32))
        shapes.append(jax.ShapeDtypeStruct((count, part, LANES), jnp.float32))
    return pl.pallas_call(
        functools.partial(merge_kernel, level, last),
        in_specs=in_vmem(3),
        out_shape=tuple(shapes),
        compiler_params=pltpu.CompilerParams(vmem_limit_bytes=16 << 20),
        cost_estimate=SMALL,
    )(keep, sums, got, after)


def finish_kernel(mine_ref, got_ref, _, out_ref):
    count, rows = out_ref.shape[0], math.prod(out_ref.shape[1:-1])
    sums = [unpack_tail(ref[count * rows :], count * rows) for ref in (mine_ref, got_ref)]
    mine, other, _ = merge_weights(*sums, count * rows)
    for i in range(count):
        here = slice(i * rows, (i + 1) * rows)
        out = mine_ref[here].astype(jnp.float32) * mine[here]
        out = out + got_ref[here].astype(jnp.float32) * other[here]
        out_ref[i] = out.astype(jnp.bfloat16).reshape(out_ref.shape[1:])


def finish(mine, got, shape, after):
    return pl.pallas_call(
        finish_kernel,
        in_specs=in_vmem(2),
        out_shape=jax.ShapeDtypeStruct(shape, jnp.bfloat16),
        compiler_params=pltpu.CompilerParams(vmem_limit_bytes=16 << 20),
        cost_estimate=SMALL,
    )(mine, got, after)


def place_kernel(levels, plan, *refs):
    part_refs = refs[: len(plan)]
    out_ref, sems = refs[-2:]
    copies = []
    for (head, own), ref in zip(plan, part_refs):
        blocks = ref.shape[1]
        bit = half_bit(0)
        at = (bit if own else 1 - bit) * blocks
        for i in range(ref.shape[0]):
            there = out_ref.at[pl.ds(at, blocks), :, head + i]
            copies.append(pltpu.make_async_copy(ref.at[i], there, sems.at[len(copies)]))
    for copy in copies:
        copy.start()
    for copy in copies:
        copy.wait()


def place(out, parts, shape, levels, after):
    arrays = [array for array, _, _ in parts]
    plan = [(head, own) for _, head, own in parts]
    others = [after] if out is None else [after, out]
    return pl.pallas_call(
        functools.partial(place_kernel, levels, plan),
        in_specs=[pl.BlockSpec(memory_space=pltpu.VMEM)] * len(arrays)
        + [pl.BlockSpec(memory_space=pl.ANY), pl.BlockSpec(memory_space=pltpu.HBM)][: len(others)],
        out_specs=pl.BlockSpec(memory_space=pltpu.HBM),
        out_shape=pltpu.HBM(shape, jnp.bfloat16),
        input_output_aliases={} if out is None else {len(arrays) + 1: 0},
        scratch_shapes=[pltpu.SemaphoreType.DMA((sum(a.shape[0] for a in arrays),))],
        compiler_params=pltpu.CompilerParams(vmem_limit_bytes=16 << 20),
        cost_estimate=SMALL,
    )(*arrays, *others)


def on_device(shards, owners, queries, prompt_cache, suffix_cache, new_kv, ancestors, lengths):
    steps, per_owner, heads, group, size = queries.shape
    suffix_dev = suffix_cache.shape[2]
    factor = math.log2(math.e) / math.sqrt(size)
    levels = shards.bit_length() - 1
    if shards != 1 << levels or levels < 2 or steps % 2 or suffix_dev != steps:
        raise ValueError("unsupported sizes")

    def swap(value, bit):
        return lax.ppermute(value, "ctx", [(i, i ^ ((2 << bit) - 1)) for i in range(shards)])

    prompt_rows = prompt_cache.reshape(2, -1, size)
    mine, parents, extents, keys = build_message(
        suffix_cache.reshape(2, -1, size),
        new_kv.reshape(steps, 2, -1, size),
        ancestors,
        lengths,
        prompt_rows,
        heads,
        math.gcd(prompt_rows.shape[1] // 4, 1024 * heads),
    )
    row_list = [mine] + [
        lax.ppermute(mine, "dom", [(i, (i + hop) % owners) for i in range(owners)])
        for hop in range(1, owners)
    ]
    *prompt, bias = split_prompt(
        prompt_rows, keys, parents, extents, heads, owners, suffix_dev
    )
    prompt = prompt[:heads], prompt[heads:]
    last = [bias]

    def follow(results):
        last[0] = results[0] if isinstance(results, (tuple, list)) else results
        return results

    messages = {}
    blocks = steps * per_owner >> (levels - 1)

    def run_attend(group, kept, begun=()):
        return follow(
            attend(queries, prompt, bias, row_list, group, kept, factor, begun, last[0])
        )

    def run_merges(got, parts):
        for level in range(1, levels):
            send, *parts = follow(merge_parts(*parts, got, level, level == levels - 1, last[0]))
            got = swap(send, level)
        return send, got

    parts = []

    def run_finish(count, send, got):
        return follow(finish(send, got, (count, blocks, group, size), last[0]))

    def run_gather(head, done):
        count = done.shape[0]
        for level in range(levels - 2, 0, -1):
            other = swap(done, level)
            done = jnp.where(
                half_bit(level) == 1,
                jnp.concatenate([other, done], axis=1),
                jnp.concatenate([done, other], axis=1),
            )
        done = done.reshape(count, steps // 2, per_owner, group, size)
        parts.append((done, head, True))
        parts.append((swap(done, 0), head, False))

    first = max(heads // 2, 1)
    groups = [tuple(range(heads))[at : at + first] for at in range(0, heads, first)]
    begun = follow(begin(queries, prompt, groups[0], False, factor))
    arrived, kept = [], []
    for number, one in enumerate(groups):
        arrived.append(swap(run_attend(one, False, () if number else begun), 0))
        if not number:
            kept.append(run_attend(one, True))
    pairs = []
    for number, one in enumerate(groups):
        if number:
            kept.append(run_attend(one, True))
        pairs.append(run_merges(arrived[number], kept[number]))
    for one, pair in zip(groups, pairs):
        run_gather(one[0], run_finish(len(one), *pair))
    late = parts[-1:]
    early = [part for part in parts if not any(part is one for one in late)]
    out = place(None, early, queries.shape, levels, last[0]) if early else None
    return place(out, late, queries.shape, levels, last[0])


def solution(mesh):
    return jax.shard_map(
        functools.partial(on_device, mesh.shape["ctx"], mesh.shape["dom"]),
        mesh=mesh,
        in_specs=(
            P("groups", "dom", "tp", None, None),
            P("groups", "ctx", "tp", None),
            P("groups", "dom", "ctx", "tp", None),
            P("groups", None, "dom", "tp", None),
            P("groups", None),
            P("groups"),
        ),
        out_specs=P("groups", "dom", "tp", None, None),
        check_vma=False,
    )
```

```python
import functools
import math

import jax
import jax.numpy as jnp
from jax import lax
from jax.experimental import pallas as pl
from jax.experimental.pallas import tpu as pltpu
from jax.sharding import PartitionSpec as P

LANES = 128
HIDDEN = -1e30
NN = (((1,), (0,)), ((), ()))
NT = (((1,), (1,)), ((), ()))
SMALL = pl.CostEstimate(flops=0, bytes_accessed=4096, transcendentals=0)


def round_up(value, multiple):
    return -(-value // multiple) * multiple


def dot(a, b, dims):
    return lax.dot_general(a, b, dims, preferred_element_type=jnp.float32)


def eye_mask(rows):
    shape = (rows, LANES)
    return lax.broadcasted_iota(jnp.int32, shape, 0) == lax.broadcasted_iota(jnp.int32, shape, 1)


def column_to_lanes(column):
    rows = column.shape[0]
    block = min(rows, LANES)
    mask = eye_mask(block)
    return jnp.concatenate(
        [
            jnp.sum(jnp.where(mask, column[at : at + block], 0.0), axis=0, keepdims=True)
            for at in range(0, rows, block)
        ],
        axis=0,
    )


def lanes_to_column(lanes, rows):
    block = min(rows, LANES)
    mask = eye_mask(block)
    return jnp.concatenate(
        [
            jnp.sum(jnp.where(mask, lanes[i : i + 1], 0.0), axis=1, keepdims=True)
            for i in range(lanes.shape[0])
        ],
        axis=0,
    )


def tail_rows(rows):
    return round_up(3 * -(-rows // LANES), 16)


def message_shape(rows, size):
    return rows + tail_rows(rows), size


def pack_tail(lanes, rows):
    high = lanes.astype(jnp.bfloat16).astype(jnp.float32)
    middle = (lanes - high).astype(jnp.bfloat16).astype(jnp.float32)
    low = lanes - high - middle
    parts = jnp.concatenate([high, middle, low], axis=0)
    spare = tail_rows(rows) - parts.shape[0]
    return jnp.concatenate([parts, jnp.zeros((spare, LANES), jnp.float32)], axis=0).astype(
        jnp.bfloat16
    )


def unpack_tail(tail, rows):
    tail = tail.astype(jnp.float32)
    blocks = -(-rows // LANES)
    return tail[:blocks] + tail[blocks : 2 * blocks] + tail[2 * blocks : 3 * blocks]


def in_hbm(array):
    return pltpu.with_memory_space_constraint(array, pltpu.HBM)


def message_kernel(
    heads, suffix_ref, new_ref, ancestors_ref, lengths_ref, prompt_ref,
    out_ref, parents_ref, extents_ref, keys_ref, here, wide, sems,
):
    steps, each = new_ref.shape[0], new_ref.shape[2]
    total = here.shape[1]
    is_last = lax.axis_index("ctx") == lax.axis_size("ctx") - 1
    suffix_copy = pltpu.make_async_copy(suffix_ref, here, sems.at[0])
    token_copies = [
        pltpu.make_async_copy(
            new_ref.at[step], here.at[:, pl.ds(step * each, each)], sems.at[1 + step]
        )
        for step in range(steps)
    ]
    small = [
        pltpu.make_async_copy(ancestors_ref, parents_ref, sems.at[1 + steps]),
        pltpu.make_async_copy(lengths_ref, extents_ref, sems.at[2 + steps]),
        pltpu.make_async_copy(
            prompt_ref.at[0, pl.ds(0, keys_ref.shape[0])], keys_ref, sems.at[3 + steps]
        ),
    ]

    @pl.when(is_last)
    def _():
        for copy in token_copies + small:
            copy.start()
        for copy in token_copies:
            copy.wait()

    @pl.when(jnp.logical_not(is_last))
    def _():
        for copy in [suffix_copy] + small:
            copy.start()
        suffix_copy.wait()

    for kind in range(2):
        wide[kind] = here[kind].astype(jnp.float32)
        for head in range(heads):
            part = wide[kind, pl.ds(head, total // heads, stride=heads), :]
            out_ref[kind, head] = part.astype(out_ref.dtype)
    for copy in small:
        copy.wait()


def build_message(suffix, new, ancestors, lengths, prompt, heads, ahead):
    _, rows, size = suffix.shape
    lengths = lengths.reshape(1, -1)
    operands = (suffix, new, ancestors, lengths, prompt)
    return pl.pallas_call(
        functools.partial(message_kernel, heads),
        in_specs=[pl.BlockSpec(memory_space=pltpu.HBM)] * len(operands),
        out_shape=(
            jax.ShapeDtypeStruct((2, heads, rows // heads, size), suffix.dtype),
            jax.ShapeDtypeStruct(ancestors.shape, ancestors.dtype),
            jax.ShapeDtypeStruct(lengths.shape, lengths.dtype),
            jax.ShapeDtypeStruct((ahead, size), prompt.dtype),
        ),
        scratch_shapes=[
            pltpu.VMEM(suffix.shape, suffix.dtype),
            pltpu.VMEM(suffix.shape, jnp.float32),
            pltpu.SemaphoreType.DMA((4 + new.shape[0],)),
        ],
        compiler_params=pltpu.CompilerParams(vmem_limit_bytes=24 << 20),
        cost_estimate=SMALL,
    )(*[in_hbm(operand) for operand in operands])


def iota(shape, axis):
    return lax.broadcasted_iota(jnp.int32, shape, axis)


def lineage_bias(ancestors_ref, lengths_ref, states, owners, suffix_dev):
    steps, particles = ancestors_ref.shape
    per_owner = particles // owners
    each = per_owner * suffix_dev
    my_owner = lax.axis_index("dom")
    my_shard = lax.axis_index("ctx")
    is_last = my_shard == lax.axis_size("ctx") - 1
    square = (particles, particles)
    same = iota(square, 0) == iota(square, 1)

    def as_column(row):
        return jnp.sum(jnp.where(same, row, 0), axis=1, keepdims=True)

    products = {}
    for step in range(steps):
        parent = as_column(ancestors_ref[step : step + 1, :])
        products[step - 1, step] = (parent == iota(square, 1)).astype(jnp.bfloat16)
    for length in range(2, steps + 1):
        for step in range(length - 1, steps):
            after = step - length
            middle = (step + after + 1) // 2
            both = dot(products[middle, step], products[after, middle], NN)
            products[after, step] = both.astype(jnp.bfloat16)
    for step in range(steps):
        states[step, :, :particles] = products[-1, step].astype(jnp.float32)
        for token in range(steps):
            here = slice((1 + token) * particles, (2 + token) * particles)
            if token < step:
                states[step, :, here] = products[token, step].astype(jnp.float32)
            else:
                states[step, :, here] = same.astype(jnp.float32) * float(token == step)
    rows = pl.ds(pl.multiple_of(my_owner * per_owner, per_owner), per_owner)
    mine = jnp.concatenate([states[step, rows, :] for step in range(steps)], axis=0)
    mine = mine.astype(jnp.bfloat16)
    lengths = as_column(lengths_ref[...])
    shape = (particles, owners * each)
    column = iota(shape, 1)
    source = column // each
    first = lax.rem(my_owner + owners - source, owners) * per_owner
    inner = column - source * each
    position = my_shard * suffix_dev + lax.rem(inner, suffix_dev)
    by_particle = iota(shape, 0) == first + inner // suffix_dev
    by_token = iota(shape, 0) == first + lax.rem(inner, per_owner)
    seen = [by_particle & (position < lengths) & jnp.logical_not(is_last)]
    seen += [by_token & (inner // per_owner == token) & is_last for token in range(steps)]
    table = jnp.concatenate([s.astype(jnp.bfloat16) for s in seen], axis=0)
    return jnp.where(dot(mine, table, NN) > 0.5, 0.0, HIDDEN)


def split_kernel(
    heads, block, owners, suffix_dev,
    rows_ref, keys_ref, parents_ref, extents_ref, *refs,
):
    out_refs = refs[: 2 * heads]
    bias_ref, here, wide, states, sems = refs[2 * heads :]
    total = out_refs[0].shape[0]
    places = [(kind, at) for kind in range(2) for at in range(0, total, block)]
    ahead = keys_ref.shape[0] // (heads * block)
    copies = [
        pltpu.make_async_copy(
            rows_ref.at[kind, pl.ds(at * heads, block * heads)],
            here.at[kind, pl.ds(at * heads, block * heads)],
            sems.at[i],
        )
        for i, (kind, at) in enumerate(places)
    ]
    for copy in copies[ahead:]:
        copy.start()
    bias_ref[...] = lineage_bias(parents_ref, extents_ref, states, owners, suffix_dev)
    for i, (kind, at) in enumerate(places):
        there = slice(at * heads, (at + block) * heads)
        if i < ahead:
            wide[i % 2] = keys_ref[there].astype(jnp.float32)
        else:
            copies[i].wait()
            wide[i % 2] = here[kind, there].astype(jnp.float32)
        for head in range(heads):
            part = wide[i % 2, pl.ds(head, block, stride=heads), :]
            out_refs[kind * heads + head][at : at + block] = part.astype(rows_ref.dtype)


def split_prompt(rows, keys, parents, extents, heads, owners, suffix_dev):
    total = rows.shape[1] // heads
    block = math.gcd(total, 512)
    size = rows.shape[2]
    steps, particles = parents.shape
    return pl.pallas_call(
        functools.partial(split_kernel, heads, block, owners, suffix_dev),
        in_specs=[pl.BlockSpec(memory_space=pltpu.HBM)]
        + [pl.BlockSpec(memory_space=pltpu.VMEM)] * 3,
        out_shape=(
            *[jax.ShapeDtypeStruct((total, size), rows.dtype)] * (2 * heads),
            jax.ShapeDtypeStruct(
                (steps * particles // owners, particles * suffix_dev), jnp.float32
            ),
        ),
        scratch_shapes=[
            pltpu.VMEM(rows.shape, rows.dtype),
            pltpu.VMEM((2, block * heads, size), jnp.float32),
            pltpu.VMEM((steps, particles, (1 + steps) * particles), jnp.float32),
            pltpu.SemaphoreType.DMA((2 * total // block,)),
        ],
        compiler_params=pltpu.CompilerParams(vmem_limit_bytes=24 << 20),
        cost_estimate=SMALL,
    )(in_hbm(rows), keys, parents, extents)


def with_ones(values):
    return jnp.concatenate([values, jnp.ones_like(values)], axis=1)


def row_peak(scores):
    return jnp.max(scores, axis=1, keepdims=True)


def weigh(scores, factor, offset):
    return jnp.exp2(scores * factor - offset).astype(jnp.bfloat16)


def work_space(streams, rows, total, size):
    block = math.gcd(total, 512)
    return [
        pltpu.VMEM((3, rows, block), jnp.float32),
        pltpu.VMEM((streams, 2, rows, math.gcd(total, 2 * block)), jnp.bfloat16),
        pltpu.VMEM((streams * rows, 2 * size), jnp.float32),
    ]


def prompt_sum(streams, factor, scores, weights, sums):
    rows, total = streams[0][0].shape[0], streams[0][1].shape[0]
    block, wide = scores.shape[2], weights.shape[3]
    units = [(at, i) for at in range(0, total, block) for i in range(len(streams))]
    offsets = [None] * len(streams)

    def score(n):
        at, i = units[n]
        scores[n % 3] = dot(streams[i][0], streams[i][1][at : at + block], NT)

    def weight(n):
        at, i = units[n]
        if at == 0:
            top = row_peak(scores[n % 3])
            peak = streams[i][3]
            offsets[i] = (top if peak is None else jnp.maximum(top, peak)) * factor
        there = slice(at % wide, at % wide + block)
        weights[i, at // wide % 2, :, there] = weigh(scores[n % 3], factor, offsets[i])

    def gather(n):
        at, i = units[n]
        end = at + block
        if end % wide:
            return
        part = dot(weights[i, at // wide % 2], with_ones(streams[i][2][end - wide : end]), NN)
        here = slice(i * rows, (i + 1) * rows)
        sums[here] = part if end == wide else sums[here] + part

    score(0)
    score(1)
    for n in range(len(units)):
        if n + 2 < len(units):
            score(n + 2)
        weight(n)
        if n > 1:
            gather(n - 2)
    gather(len(units) - 2)
    gather(len(units) - 1)
    return offsets


def half_bit(level):
    shard = lax.axis_index("ctx")
    return lax.rem((shard >> level) + (shard >> (level + 1)), 2)


def first_step(q_ref, kept):
    bit = half_bit(0)
    return (bit if kept else 1 - bit) * (q_ref.shape[0] // 2)


def queries_of(q_ref, head, first, number):
    _, per_owner, _, group, size = q_ref.shape
    return q_ref[pl.ds(first, number), :, head].reshape(number * per_owner * group, size)


def prompt_kernel(heads, kept, factor, q_ref, *refs):
    k_refs, v_refs = refs[: len(heads)], refs[len(heads) : 2 * len(heads)]
    together_ref, offset_ref, scores, weights = refs[2 * len(heads) :]
    first, number = first_step(q_ref, kept), q_ref.shape[0] // 2
    streams = [
        (queries_of(q_ref, head, first, number), k_ref, v_ref, None)
        for head, k_ref, v_ref in zip(heads, k_refs, v_refs)
    ]
    offsets = prompt_sum(streams, factor, scores, weights, together_ref)
    offset = jnp.concatenate(offsets, axis=0)
    offset_ref[...] = jnp.broadcast_to(offset, offset_ref.shape)


def in_vmem(count, ordered=True):
    last = [pl.BlockSpec(memory_space=pl.ANY)] if ordered else []
    return [pl.BlockSpec(memory_space=pltpu.VMEM)] * count + last


def begin(queries, prompt, heads, kept, factor):
    steps, per_owner, _, group, size = queries.shape
    rows = steps * per_owner * group // 2
    keys, values = prompt
    space = work_space(len(heads), rows, keys[0].shape[0], size)
    return pl.pallas_call(
        functools.partial(prompt_kernel, heads, kept, factor),
        in_specs=in_vmem(1 + 2 * len(heads), False),
        out_shape=(
            jax.ShapeDtypeStruct((len(heads) * rows, 2 * size), jnp.float32),
            jax.ShapeDtypeStruct((len(heads) * rows, LANES), jnp.float32),
        ),
        scratch_shapes=space[:2],
        compiler_params=pltpu.CompilerParams(vmem_limit_bytes=24 << 20),
        cost_estimate=SMALL,
    )(queries, *[keys[head] for head in heads], *[values[head] for head in heads])


def attend_kernel(heads, kept, factor, owners, started, *refs):
    count = len(heads)
    q_ref, bias_ref = refs[:2]
    row_refs = refs[2 : 2 + owners]
    refs = refs[2 + owners :]
    k_refs, v_refs, refs = refs[:count], refs[count : 2 * count], refs[2 * count :]
    begun, refs = refs[: 2 * started], refs[2 * started + 1 :]
    if kept:
        out, log_sums, *work = refs
    else:
        send_ref, log_sums, *work = refs
    steps, per_owner, _, group, size = q_ref.shape
    columns = bias_ref.shape[1]
    number = steps // 2
    rows = number * per_owner * group
    start = first_step(q_ref, kept)

    def suffix_of(head, kind):
        return jnp.concatenate([ref[kind, head] for ref in row_refs], axis=0)

    def suffix_scores(q, head, first, number):
        at = pl.multiple_of(first * per_owner, per_owner)
        bias = bias_ref[pl.ds(at, number * per_owner), :]
        bias = jnp.broadcast_to(bias[:, None, :], (number * per_owner, group, columns))
        return dot(q, suffix_of(head, 0), NT) + bias.reshape(number * per_owner * group, columns)

    def store(i, at, together, offset):
        sums = together[:, size:]
        result = together[:, :size] / sums
        if kept:
            out[i, pl.ds(at, sums.shape[0]), :] = result
        else:
            there = pl.ds(pl.multiple_of(i * rows + at, LANES), sums.shape[0])
            send_ref[there, :] = result.astype(jnp.bfloat16)
        log_sums[i, pl.ds(at, sums.shape[0]), :] = offset + jnp.log2(sums)
        return sums

    queries = [queries_of(q_ref, head, start, number) for head in heads]
    extras = [suffix_scores(q, head, start, number) for q, head in zip(queries, heads)]
    if started:
        offsets = [begun[1][i * rows : (i + 1) * rows, :1] for i in range(count)]
        togethers = begun[0]
    else:
        streams = [(q, k, v, row_peak(e)) for q, k, v, e in zip(queries, k_refs, v_refs, extras)]
        offsets = prompt_sum(streams, factor, *work)
        togethers = work[-1]
    worst = []
    for i, head in enumerate(heads):
        weight = weigh(extras[i], factor, offsets[i])
        together = togethers[i * rows : (i + 1) * rows]
        together = together + dot(weight, with_ones(suffix_of(head, 1)), NN)
        worst.append(jnp.max(store(i, 0, together, offsets[i])))

    for i, head in enumerate(heads):

        @pl.when(jnp.logical_not(worst[i] < 2.0**100))
        def _():
            @pl.loop(0, number)
            def _(step):
                q = queries_of(q_ref, head, start + step, 1)
                extra = suffix_scores(q, head, start + step, 1)
                scores = dot(q, k_refs[i][...], NT)
                offset = jnp.maximum(row_peak(scores), row_peak(extra)) * factor
                weight = weigh(scores, factor, offset)
                together = dot(weight, with_ones(v_refs[i][...]), NN)
                weight = weigh(extra, factor, offset)
                together = together + dot(weight, with_ones(suffix_of(head, 1)), NN)
                here = per_owner * group
                store(i, pl.multiple_of(step * here, here), together, offset)

    if not kept:
        column = jnp.concatenate([log_sums[i] for i in range(count)], axis=0)
        send_ref[count * rows :] = pack_tail(column_to_lanes(column), count * rows)


def attend(queries, prompt, bias, row_list, heads, kept, factor, begun, after):
    steps, per_owner, _, group, size = queries.shape
    rows = steps * per_owner * group // 2
    count = len(heads)
    keys, values = prompt
    operands = (
        queries, bias, *row_list,
        *[keys[head] for head in heads], *[values[head] for head in heads], *begun,
    )
    parts = [((count, rows, size), jnp.float32), ((count, rows, LANES), jnp.float32)]
    send = jax.ShapeDtypeStruct(message_shape(count * rows, size), jnp.bfloat16)
    space = work_space(count, rows, keys[0].shape[0], size)
    return pl.pallas_call(
        functools.partial(
            attend_kernel, heads, kept, factor, len(row_list), len(begun) // 2
        ),
        in_specs=in_vmem(len(operands)),
        out_shape=tuple(jax.ShapeDtypeStruct(*part) for part in parts) if kept else send,
        scratch_shapes=[*([] if kept else [pltpu.VMEM(*parts[1])]), *space],
        compiler_params=pltpu.CompilerParams(vmem_limit_bytes=32 << 20),
        cost_estimate=SMALL,
    )(*operands, after)


def merge_weights(sums_a, sums_b, rows):
    top = jnp.maximum(sums_a, sums_b)
    weight_a = jnp.exp2(sums_a - top)
    weight_b = jnp.exp2(sums_b - top)
    total = weight_a + weight_b
    weights = [lanes_to_column(weight / total, rows) for weight in (weight_a, weight_b)]
    return *weights, top + jnp.log2(total)


def merge_kernel(level, last, keep_ref, sums_ref, got_ref, _, *outs):
    count, rows = keep_ref.shape[:2]
    column = jnp.concatenate([sums_ref[i] for i in range(count)], axis=0)
    got_sums = unpack_tail(got_ref[count * rows :], count * rows)
    mine, other, log_sums = merge_weights(column_to_lanes(column), got_sums, count * rows)
    merged = []
    for i in range(count):
        here = slice(i * rows, (i + 1) * rows)
        merged.append(keep_ref[i] * mine[here] + got_ref[here].astype(jnp.float32) * other[here])
    send = outs[0]
    if last:
        for i, out in enumerate(merged):
            send[i * rows : (i + 1) * rows] = out.astype(jnp.bfloat16)
        send[count * rows :] = pack_tail(log_sums, count * rows)
        return
    _, keep, wide = outs
    part = rows // 2
    bit = half_bit(level) == 1
    column = lanes_to_column(log_sums, count * rows)
    leaving = []
    for i, out in enumerate(merged):
        halves = [slice(0, part), slice(part, rows)]
        sums = column[i * rows : (i + 1) * rows]
        first, second = (out[half] for half in halves)
        send[i * part : (i + 1) * part] = jnp.where(bit, first, second).astype(jnp.bfloat16)
        keep[i] = jnp.where(bit, second, first)
        first, second = (sums[half] for half in halves)
        leaving.append(jnp.where(bit, first, second))
        wide[i] = jnp.broadcast_to(jnp.where(bit, second, first), (part, LANES))
    leaving = jnp.concatenate(leaving, axis=0)
    send[count * part :] = pack_tail(column_to_lanes(leaving), count * part)


def merge_parts(keep, sums, got, level, last, after):
    count, rows, size = keep.shape
    part = rows if last else rows // 2
    shapes = [jax.ShapeDtypeStruct(message_shape(count * part, size), jnp.bfloat16)]
    if not last:
        shapes.append(jax.ShapeDtypeStruct((count, part, size), jnp.float32))
        shapes.append(jax.ShapeDtypeStruct((count, part, LANES), jnp.float32))
    return pl.pallas_call(
        functools.partial(merge_kernel, level, last),
        in_specs=in_vmem(3),
        out_shape=tuple(shapes),
        compiler_params=pltpu.CompilerParams(vmem_limit_bytes=16 << 20),
        cost_estimate=SMALL,
    )(keep, sums, got, after)


def finish_kernel(mine_ref, got_ref, _, out_ref):
    count, rows = out_ref.shape[0], math.prod(out_ref.shape[1:-1])
    sums = [unpack_tail(ref[count * rows :], count * rows) for ref in (mine_ref, got_ref)]
    mine, other, _ = merge_weights(*sums, count * rows)
    for i in range(count):
        here = slice(i * rows, (i + 1) * rows)
        out = mine_ref[here].astype(jnp.float32) * mine[here]
        out = out + got_ref[here].astype(jnp.float32) * other[here]
        out_ref[i] = out.astype(jnp.bfloat16).reshape(out_ref.shape[1:])


def finish(mine, got, shape, after):
    return pl.pallas_call(
        finish_kernel,
        in_specs=in_vmem(2),
        out_shape=jax.ShapeDtypeStruct(shape, jnp.bfloat16),
        compiler_params=pltpu.CompilerParams(vmem_limit_bytes=16 << 20),
        cost_estimate=SMALL,
    )(mine, got, after)


def place_kernel(levels, plan, *refs):
    part_refs = refs[: len(plan)]
    out_ref, sems = refs[-2:]
    copies = []
    for (head, own), ref in zip(plan, part_refs):
        blocks = ref.shape[1]
        bit = half_bit(0)
        at = (bit if own else 1 - bit) * blocks
        for i in range(ref.shape[0]):
            there = out_ref.at[pl.ds(at, blocks), :, head + i]
            copies.append(pltpu.make_async_copy(ref.at[i], there, sems.at[len(copies)]))
    for copy in copies:
        copy.start()
    for copy in copies:
        copy.wait()


def place(out, parts, shape, levels, after):
    arrays = [array for array, _, _ in parts]
    plan = [(head, own) for _, head, own in parts]
    others = [after] if out is None else [after, out]
    return pl.pallas_call(
        functools.partial(place_kernel, levels, plan),
        in_specs=[pl.BlockSpec(memory_space=pltpu.VMEM)] * len(arrays)
        + [pl.BlockSpec(memory_space=pl.ANY), pl.BlockSpec(memory_space=pltpu.HBM)][: len(others)],
        out_specs=pl.BlockSpec(memory_space=pltpu.HBM),
        out_shape=pltpu.HBM(shape, jnp.bfloat16),
        input_output_aliases={} if out is None else {len(arrays) + 1: 0},
        scratch_shapes=[pltpu.SemaphoreType.DMA((sum(a.shape[0] for a in arrays),))],
        compiler_params=pltpu.CompilerParams(vmem_limit_bytes=16 << 20),
        cost_estimate=SMALL,
    )(*arrays, *others)


def on_device(shards, owners, queries, prompt_cache, suffix_cache, new_kv, ancestors, lengths):
    steps, per_owner, heads, group, size = queries.shape
    suffix_dev = suffix_cache.shape[2]
    factor = math.log2(math.e) / math.sqrt(size)
    levels = shards.bit_length() - 1
    if shards != 1 << levels or levels < 2 or steps % 2 or suffix_dev != steps:
        raise ValueError("unsupported sizes")

    def swap(value, bit):
        return lax.ppermute(value, "ctx", [(i, i ^ ((2 << bit) - 1)) for i in range(shards)])

    prompt_rows = prompt_cache.reshape(2, -1, size)
    mine, parents, extents, keys = build_message(
        suffix_cache.reshape(2, -1, size),
        new_kv.reshape(steps, 2, -1, size),
        ancestors,
        lengths,
        prompt_rows,
        heads,
        math.gcd(prompt_rows.shape[1] // 4, 1024 * heads),
    )
    row_list = [mine] + [
        lax.ppermute(mine, "dom", [(i, (i + hop) % owners) for i in range(owners)])
        for hop in range(1, owners)
    ]
    *prompt, bias = split_prompt(
        prompt_rows, keys, parents, extents, heads, owners, suffix_dev
    )
    prompt = prompt[:heads], prompt[heads:]
    last = [bias]

    def follow(results):
        last[0] = results[0] if isinstance(results, (tuple, list)) else results
        return results

    messages = {}
    blocks = steps * per_owner >> (levels - 1)

    def run_attend(group, kept, begun=()):
        return follow(
            attend(queries, prompt, bias, row_list, group, kept, factor, begun, last[0])
        )

    def run_merges(got, parts):
        for level in range(1, levels):
            send, *parts = follow(merge_parts(*parts, got, level, level == levels - 1, last[0]))
            got = swap(send, level)
        return send, got

    parts = []

    def run_finish(count, send, got):
        return follow(finish(send, got, (count, blocks, group, size), last[0]))

    def run_gather(head, done):
        count = done.shape[0]
        for level in range(levels - 2, 0, -1):
            other = swap(done, level)
            done = jnp.where(
                half_bit(level) == 1,
                jnp.concatenate([other, done], axis=1),
                jnp.concatenate([done, other], axis=1),
            )
        done = done.reshape(count, steps // 2, per_owner, group, size)
        parts.append((done, head, True))
        parts.append((swap(done, 0), head, False))

    first = max(heads // 2, 1)
    groups = [tuple(range(heads))[at : at + first] for at in range(0, heads, first)]
    begun = follow(begin(queries, prompt, groups[0], False, factor))
    arrived, kept = [], []
    for number, one in enumerate(groups):
        arrived.append(swap(run_attend(one, False, () if number else begun), 0))
        if not number:
            kept.append(run_attend(one, True))
    pairs = []
    for number, one in enumerate(groups):
        if number:
            kept.append(run_attend(one, True))
        pairs.append(run_merges(arrived[number], kept[number]))
    for one, pair in zip(groups, pairs):
        run_gather(one[0], run_finish(len(one), *pair))
    late = parts[-1:]
    early = [part for part in parts if not any(part is one for one in late)]
    out = place(None, early, queries.shape, levels, last[0]) if early else None
    return place(out, late, queries.shape, levels, last[0])


def solution(mesh):
    return jax.shard_map(
        functools.partial(on_device, mesh.shape["ctx"], mesh.shape["dom"]),
        mesh=mesh,
        in_specs=(
            P("groups", "dom", "tp", None, None),
            P("groups", "ctx", "tp", None),
            P("groups", "dom", "ctx", "tp", None),
            P("groups", None, "dom", "tp", None),
            P("groups", None),
            P("groups"),
        ),
        out_specs=P("groups", "dom", "tp", None, None),
        check_vma=False,
    )
```

```python
import functools
import math

import jax
import jax.numpy as jnp
from jax import lax
from jax.experimental import pallas as pl
from jax.experimental.pallas import tpu as pltpu
from jax.sharding import PartitionSpec as P

LANES = 128
HIDDEN = -1e30
NN = (((1,), (0,)), ((), ()))
NT = (((1,), (1,)), ((), ()))
SMALL = pl.CostEstimate(flops=0, bytes_accessed=4096, transcendentals=0)


def round_up(value, multiple):
    return -(-value // multiple) * multiple


def dot(a, b, dims):
    return lax.dot_general(a, b, dims, preferred_element_type=jnp.float32)


def eye_mask(rows):
    shape = (rows, LANES)
    return lax.broadcasted_iota(jnp.int32, shape, 0) == lax.broadcasted_iota(jnp.int32, shape, 1)


def column_to_lanes(column):
    rows = column.shape[0]
    block = min(rows, LANES)
    mask = eye_mask(block)
    return jnp.concatenate(
        [
            jnp.sum(jnp.where(mask, column[at : at + block], 0.0), axis=0, keepdims=True)
            for at in range(0, rows, block)
        ],
        axis=0,
    )


def lanes_to_column(lanes, rows):
    block = min(rows, LANES)
    mask = eye_mask(block)
    return jnp.concatenate(
        [
            jnp.sum(jnp.where(mask, lanes[i : i + 1], 0.0), axis=1, keepdims=True)
            for i in range(lanes.shape[0])
        ],
        axis=0,
    )


def tail_rows(rows):
    return round_up(3 * -(-rows // LANES), 16)


def message_shape(rows, size):
    return rows + tail_rows(rows), size


def pack_tail(lanes, rows):
    high = lanes.astype(jnp.bfloat16).astype(jnp.float32)
    middle = (lanes - high).astype(jnp.bfloat16).astype(jnp.float32)
    low = lanes - high - middle
    parts = jnp.concatenate([high, middle, low], axis=0)
    spare = tail_rows(rows) - parts.shape[0]
    return jnp.concatenate([parts, jnp.zeros((spare, LANES), jnp.float32)], axis=0).astype(
        jnp.bfloat16
    )


def unpack_tail(tail, rows):
    tail = tail.astype(jnp.float32)
    blocks = -(-rows // LANES)
    return tail[:blocks] + tail[blocks : 2 * blocks] + tail[2 * blocks : 3 * blocks]


def in_hbm(array):
    return pltpu.with_memory_space_constraint(array, pltpu.HBM)


def message_kernel(
    heads, suffix_ref, new_ref, ancestors_ref, lengths_ref, prompt_ref,
    out_ref, parents_ref, extents_ref, keys_ref, here, wide, sems,
):
    steps, each = new_ref.shape[0], new_ref.shape[2]
    total = here.shape[1]
    is_last = lax.axis_index("ctx") == lax.axis_size("ctx") - 1
    suffix_copy = pltpu.make_async_copy(suffix_ref, here, sems.at[0])
    token_copies = [
        pltpu.make_async_copy(
            new_ref.at[step], here.at[:, pl.ds(step * each, each)], sems.at[1 + step]
        )
        for step in range(steps)
    ]
    small = [
        pltpu.make_async_copy(ancestors_ref, parents_ref, sems.at[1 + steps]),
        pltpu.make_async_copy(lengths_ref, extents_ref, sems.at[2 + steps]),
        pltpu.make_async_copy(
            prompt_ref.at[0, pl.ds(0, keys_ref.shape[0])], keys_ref, sems.at[3 + steps]
        ),
    ]

    @pl.when(is_last)
    def _():
        for copy in token_copies + small:
            copy.start()
        for copy in token_copies:
            copy.wait()

    @pl.when(jnp.logical_not(is_last))
    def _():
        for copy in [suffix_copy] + small:
            copy.start()
        suffix_copy.wait()

    for kind in range(2):
        wide[kind] = here[kind].astype(jnp.float32)
        for head in range(heads):
            part = wide[kind, pl.ds(head, total // heads, stride=heads), :]
            out_ref[kind, head] = part.astype(out_ref.dtype)
    for copy in small:
        copy.wait()


def build_message(suffix, new, ancestors, lengths, prompt, heads, ahead):
    _, rows, size = suffix.shape
    lengths = lengths.reshape(1, -1)
    operands = (suffix, new, ancestors, lengths, prompt)
    return pl.pallas_call(
        functools.partial(message_kernel, heads),
        in_specs=[pl.BlockSpec(memory_space=pltpu.HBM)] * len(operands),
        out_shape=(
            jax.ShapeDtypeStruct((2, heads, rows // heads, size), suffix.dtype),
            jax.ShapeDtypeStruct(ancestors.shape, ancestors.dtype),
            jax.ShapeDtypeStruct(lengths.shape, lengths.dtype),
            jax.ShapeDtypeStruct((ahead, size), prompt.dtype),
        ),
        scratch_shapes=[
            pltpu.VMEM(suffix.shape, suffix.dtype),
            pltpu.VMEM(suffix.shape, jnp.float32),
            pltpu.SemaphoreType.DMA((4 + new.shape[0],)),
        ],
        compiler_params=pltpu.CompilerParams(vmem_limit_bytes=24 << 20),
        cost_estimate=SMALL,
    )(*[in_hbm(operand) for operand in operands])


def iota(shape, axis):
    return lax.broadcasted_iota(jnp.int32, shape, axis)


def lineage_bias(ancestors_ref, lengths_ref, states, owners, suffix_dev):
    steps, particles = ancestors_ref.shape
    per_owner = particles // owners
    each = per_owner * suffix_dev
    my_owner = lax.axis_index("dom")
    my_shard = lax.axis_index("ctx")
    is_last = my_shard == lax.axis_size("ctx") - 1
    square = (particles, particles)
    same = iota(square, 0) == iota(square, 1)

    def as_column(row):
        return jnp.sum(jnp.where(same, row, 0), axis=1, keepdims=True)

    products = {}
    for step in range(steps):
        parent = as_column(ancestors_ref[step : step + 1, :])
        products[step - 1, step] = (parent == iota(square, 1)).astype(jnp.bfloat16)
    for length in range(2, steps + 1):
        for step in range(length - 1, steps):
            after = step - length
            middle = (step + after + 1) // 2
            both = dot(products[middle, step], products[after, middle], NN)
            products[after, step] = both.astype(jnp.bfloat16)
    for step in range(steps):
        states[step, :, :particles] = products[-1, step].astype(jnp.float32)
        for token in range(steps):
            here = slice((1 + token) * particles, (2 + token) * particles)
            if token < step:
                states[step, :, here] = products[token, step].astype(jnp.float32)
            else:
                states[step, :, here] = same.astype(jnp.float32) * float(token == step)
    rows = pl.ds(pl.multiple_of(my_owner * per_owner, per_owner), per_owner)
    mine = jnp.concatenate([states[step, rows, :] for step in range(steps)], axis=0)
    mine = mine.astype(jnp.bfloat16)
    lengths = as_column(lengths_ref[...])
    shape = (particles, owners * each)
    column = iota(shape, 1)
    source = column // each
    first = lax.rem(my_owner + owners - source, owners) * per_owner
    inner = column - source * each
    position = my_shard * suffix_dev + lax.rem(inner, suffix_dev)
    by_particle = iota(shape, 0) == first + inner // suffix_dev
    by_token = iota(shape, 0) == first + lax.rem(inner, per_owner)
    seen = [by_particle & (position < lengths) & jnp.logical_not(is_last)]
    seen += [by_token & (inner // per_owner == token) & is_last for token in range(steps)]
    table = jnp.concatenate([s.astype(jnp.bfloat16) for s in seen], axis=0)
    return jnp.where(dot(mine, table, NN) > 0.5, 0.0, HIDDEN)


def split_kernel(
    heads, block, owners, suffix_dev,
    rows_ref, keys_ref, parents_ref, extents_ref, *refs,
):
    out_refs = refs[: 2 * heads]
    bias_ref, here, wide, states, sems = refs[2 * heads :]
    total = out_refs[0].shape[0]
    places = [(kind, at) for kind in range(2) for at in range(0, total, block)]
    ahead = keys_ref.shape[0] // (heads * block)
    copies = [
        pltpu.make_async_copy(
            rows_ref.at[kind, pl.ds(at * heads, block * heads)],
            here.at[kind, pl.ds(at * heads, block * heads)],
            sems.at[i],
        )
        for i, (kind, at) in enumerate(places)
    ]
    for copy in copies[ahead:]:
        copy.start()
    bias_ref[...] = lineage_bias(parents_ref, extents_ref, states, owners, suffix_dev)
    for i, (kind, at) in enumerate(places):
        there = slice(at * heads, (at + block) * heads)
        if i < ahead:
            wide[i % 2] = keys_ref[there].astype(jnp.float32)
        else:
            copies[i].wait()
            wide[i % 2] = here[kind, there].astype(jnp.float32)
        for head in range(heads):
            part = wide[i % 2, pl.ds(head, block, stride=heads), :]
            out_refs[kind * heads + head][at : at + block] = part.astype(rows_ref.dtype)


def split_prompt(rows, keys, parents, extents, heads, owners, suffix_dev):
    total = rows.shape[1] // heads
    block = math.gcd(total, 512)
    size = rows.shape[2]
    steps, particles = parents.shape
    return pl.pallas_call(
        functools.partial(split_kernel, heads, block, owners, suffix_dev),
        in_specs=[pl.BlockSpec(memory_space=pltpu.HBM)]
        + [pl.BlockSpec(memory_space=pltpu.VMEM)] * 3,
        out_shape=(
            *[jax.ShapeDtypeStruct((total, size), rows.dtype)] * (2 * heads),
            jax.ShapeDtypeStruct(
                (steps * particles // owners, particles * suffix_dev), jnp.float32
            ),
        ),
        scratch_shapes=[
            pltpu.VMEM(rows.shape, rows.dtype),
            pltpu.VMEM((2, block * heads, size), jnp.float32),
            pltpu.VMEM((steps, particles, (1 + steps) * particles), jnp.float32),
            pltpu.SemaphoreType.DMA((2 * total // block,)),
        ],
        compiler_params=pltpu.CompilerParams(vmem_limit_bytes=24 << 20),
        cost_estimate=SMALL,
    )(in_hbm(rows), keys, parents, extents)


def with_ones(values):
    return jnp.concatenate([values, jnp.ones_like(values)], axis=1)


def row_peak(scores):
    return jnp.max(scores, axis=1, keepdims=True)


def weigh(scores, factor, offset):
    return jnp.exp2(scores * factor - offset).astype(jnp.bfloat16)


def work_space(streams, rows, total, size):
    block = math.gcd(total, 512)
    return [
        pltpu.VMEM((3, rows, block), jnp.float32),
        pltpu.VMEM((streams, 2, rows, math.gcd(total, 2 * block)), jnp.bfloat16),
        pltpu.VMEM((streams * rows, 2 * size), jnp.float32),
    ]


def prompt_sum(streams, factor, scores, weights, sums):
    rows, total = streams[0][0].shape[0], streams[0][1].shape[0]
    block, wide = scores.shape[2], weights.shape[3]
    units = [(at, i) for at in range(0, total, block) for i in range(len(streams))]
    offsets = [None] * len(streams)

    def score(n):
        at, i = units[n]
        scores[n % 3] = dot(streams[i][0], streams[i][1][at : at + block], NT)

    def weight(n):
        at, i = units[n]
        if at == 0:
            top = row_peak(scores[n % 3])
            peak = streams[i][3]
            offsets[i] = (top if peak is None else jnp.maximum(top, peak)) * factor
        there = slice(at % wide, at % wide + block)
        weights[i, at // wide % 2, :, there] = weigh(scores[n % 3], factor, offsets[i])

    def gather(n):
        at, i = units[n]
        end = at + block
        if end % wide:
            return
        part = dot(weights[i, at // wide % 2], with_ones(streams[i][2][end - wide : end]), NN)
        here = slice(i * rows, (i + 1) * rows)
        sums[here] = part if end == wide else sums[here] + part

    score(0)
    score(1)
    for n in range(len(units)):
        if n + 2 < len(units):
            score(n + 2)
        weight(n)
        if n:
            gather(n - 1)
    gather(len(units) - 1)
    return offsets


def half_bit(level):
    shard = lax.axis_index("ctx")
    return lax.rem((shard >> level) + (shard >> (level + 1)), 2)


def first_step(q_ref, kept):
    bit = half_bit(0)
    return (bit if kept else 1 - bit) * (q_ref.shape[0] // 2)


def queries_of(q_ref, head, first, number):
    _, per_owner, _, group, size = q_ref.shape
    return q_ref[pl.ds(first, number), :, head].reshape(number * per_owner * group, size)


def prompt_kernel(heads, kept, factor, q_ref, *refs):
    k_refs, v_refs = refs[: len(heads)], refs[len(heads) : 2 * len(heads)]
    together_ref, offset_ref, scores, weights = refs[2 * len(heads) :]
    first, number = first_step(q_ref, kept), q_ref.shape[0] // 2
    streams = [
        (queries_of(q_ref, head, first, number), k_ref, v_ref, None)
        for head, k_ref, v_ref in zip(heads, k_refs, v_refs)
    ]
    offsets = prompt_sum(streams, factor, scores, weights, together_ref)
    offset = jnp.concatenate(offsets, axis=0)
    offset_ref[...] = jnp.broadcast_to(offset, offset_ref.shape)


def in_vmem(count, ordered=True):
    last = [pl.BlockSpec(memory_space=pl.ANY)] if ordered else []
    return [pl.BlockSpec(memory_space=pltpu.VMEM)] * count + last


def begin(queries, prompt, heads, kept, factor):
    steps, per_owner, _, group, size = queries.shape
    rows = steps * per_owner * group // 2
    keys, values = prompt
    space = work_space(len(heads), rows, keys[0].shape[0], size)
    return pl.pallas_call(
        functools.partial(prompt_kernel, heads, kept, factor),
        in_specs=in_vmem(1 + 2 * len(heads), False),
        out_shape=(
            jax.ShapeDtypeStruct((len(heads) * rows, 2 * size), jnp.float32),
            jax.ShapeDtypeStruct((len(heads) * rows, LANES), jnp.float32),
        ),
        scratch_shapes=space[:2],
        compiler_params=pltpu.CompilerParams(vmem_limit_bytes=24 << 20),
        cost_estimate=SMALL,
    )(queries, *[keys[head] for head in heads], *[values[head] for head in heads])


def attend_kernel(heads, kept, factor, owners, started, *refs):
    count = len(heads)
    q_ref, bias_ref = refs[:2]
    row_refs = refs[2 : 2 + owners]
    refs = refs[2 + owners :]
    k_refs, v_refs, refs = refs[:count], refs[count : 2 * count], refs[2 * count :]
    begun, refs = refs[: 2 * started], refs[2 * started + 1 :]
    if kept:
        out, log_sums, *work = refs
    else:
        send_ref, log_sums, *work = refs
    steps, per_owner, _, group, size = q_ref.shape
    columns = bias_ref.shape[1]
    number = steps // 2
    rows = number * per_owner * group
    start = first_step(q_ref, kept)

    def suffix_of(head, kind):
        return jnp.concatenate([ref[kind, head] for ref in row_refs], axis=0)

    def suffix_scores(q, head, first, number):
        at = pl.multiple_of(first * per_owner, per_owner)
        bias = bias_ref[pl.ds(at, number * per_owner), :]
        bias = jnp.broadcast_to(bias[:, None, :], (number * per_owner, group, columns))
        return dot(q, suffix_of(head, 0), NT) + bias.reshape(number * per_owner * group, columns)

    def store(i, at, together, offset):
        sums = together[:, size:]
        result = together[:, :size] / sums
        if kept:
            out[i, pl.ds(at, sums.shape[0]), :] = result
        else:
            there = pl.ds(pl.multiple_of(i * rows + at, LANES), sums.shape[0])
            send_ref[there, :] = result.astype(jnp.bfloat16)
        log_sums[i, pl.ds(at, sums.shape[0]), :] = offset + jnp.log2(sums)
        return sums

    queries = [queries_of(q_ref, head, start, number) for head in heads]
    extras = [suffix_scores(q, head, start, number) for q, head in zip(queries, heads)]
    if started:
        offsets = [begun[1][i * rows : (i + 1) * rows, :1] for i in range(count)]
        togethers = begun[0]
    else:
        streams = [(q, k, v, row_peak(e)) for q, k, v, e in zip(queries, k_refs, v_refs, extras)]
        offsets = prompt_sum(streams, factor, *work)
        togethers = work[-1]
    worst = []
    for i, head in enumerate(heads):
        weight = weigh(extras[i], factor, offsets[i])
        together = togethers[i * rows : (i + 1) * rows]
        together = together + dot(weight, with_ones(suffix_of(head, 1)), NN)
        worst.append(jnp.max(store(i, 0, together, offsets[i])))

    for i, head in enumerate(heads):

        @pl.when(jnp.logical_not(worst[i] < 2.0**100))
        def _():
            @pl.loop(0, number)
            def _(step):
                q = queries_of(q_ref, head, start + step, 1)
                extra = suffix_scores(q, head, start + step, 1)
                scores = dot(q, k_refs[i][...], NT)
                offset = jnp.maximum(row_peak(scores), row_peak(extra)) * factor
                weight = weigh(scores, factor, offset)
                together = dot(weight, with_ones(v_refs[i][...]), NN)
                weight = weigh(extra, factor, offset)
                together = together + dot(weight, with_ones(suffix_of(head, 1)), NN)
                here = per_owner * group
                store(i, pl.multiple_of(step * here, here), together, offset)

    if not kept:
        column = jnp.concatenate([log_sums[i] for i in range(count)], axis=0)
        send_ref[count * rows :] = pack_tail(column_to_lanes(column), count * rows)


def attend(queries, prompt, bias, row_list, heads, kept, factor, begun, after):
    steps, per_owner, _, group, size = queries.shape
    rows = steps * per_owner * group // 2
    count = len(heads)
    keys, values = prompt
    operands = (
        queries, bias, *row_list,
        *[keys[head] for head in heads], *[values[head] for head in heads], *begun,
    )
    parts = [((count, rows, size), jnp.float32), ((count, rows, LANES), jnp.float32)]
    send = jax.ShapeDtypeStruct(message_shape(count * rows, size), jnp.bfloat16)
    space = work_space(count, rows, keys[0].shape[0], size)
    return pl.pallas_call(
        functools.partial(
            attend_kernel, heads, kept, factor, len(row_list), len(begun) // 2
        ),
        in_specs=in_vmem(len(operands)),
        out_shape=tuple(jax.ShapeDtypeStruct(*part) for part in parts) if kept else send,
        scratch_shapes=[*([] if kept else [pltpu.VMEM(*parts[1])]), *space],
        compiler_params=pltpu.CompilerParams(vmem_limit_bytes=32 << 20),
        cost_estimate=SMALL,
    )(*operands, after)


def merge_weights(sums_a, sums_b, rows):
    top = jnp.maximum(sums_a, sums_b)
    weight_a = jnp.exp2(sums_a - top)
    weight_b = jnp.exp2(sums_b - top)
    total = weight_a + weight_b
    weights = [lanes_to_column(weight / total, rows) for weight in (weight_a, weight_b)]
    return *weights, top + jnp.log2(total)


def merge_kernel(level, last, keep_ref, sums_ref, got_ref, _, *outs):
    count, rows = keep_ref.shape[:2]
    column = jnp.concatenate([sums_ref[i] for i in range(count)], axis=0)
    got_sums = unpack_tail(got_ref[count * rows :], count * rows)
    mine, other, log_sums = merge_weights(column_to_lanes(column), got_sums, count * rows)
    merged = []
    for i in range(count):
        here = slice(i * rows, (i + 1) * rows)
        merged.append(keep_ref[i] * mine[here] + got_ref[here].astype(jnp.float32) * other[here])
    send = outs[0]
    if last:
        for i, out in enumerate(merged):
            send[i * rows : (i + 1) * rows] = out.astype(jnp.bfloat16)
        send[count * rows :] = pack_tail(log_sums, count * rows)
        return
    _, keep, wide = outs
    part = rows // 2
    bit = half_bit(level) == 1
    column = lanes_to_column(log_sums, count * rows)
    leaving = []
    for i, out in enumerate(merged):
        halves = [slice(0, part), slice(part, rows)]
        sums = column[i * rows : (i + 1) * rows]
        first, second = (out[half] for half in halves)
        send[i * part : (i + 1) * part] = jnp.where(bit, first, second).astype(jnp.bfloat16)
        keep[i] = jnp.where(bit, second, first)
        first, second = (sums[half] for half in halves)
        leaving.append(jnp.where(bit, first, second))
        wide[i] = jnp.broadcast_to(jnp.where(bit, second, first), (part, LANES))
    leaving = jnp.concatenate(leaving, axis=0)
    send[count * part :] = pack_tail(column_to_lanes(leaving), count * part)


def merge_parts(keep, sums, got, level, last, after):
    count, rows, size = keep.shape
    part = rows if last else rows // 2
    shapes = [jax.ShapeDtypeStruct(message_shape(count * part, size), jnp.bfloat16)]
    if not last:
        shapes.append(jax.ShapeDtypeStruct((count, part, size), jnp.float32))
        shapes.append(jax.ShapeDtypeStruct((count, part, LANES), jnp.float32))
    return pl.pallas_call(
        functools.partial(merge_kernel, level, last),
        in_specs=in_vmem(3),
        out_shape=tuple(shapes),
        compiler_params=pltpu.CompilerParams(vmem_limit_bytes=16 << 20),
        cost_estimate=SMALL,
    )(keep, sums, got, after)


def finish_kernel(mine_ref, got_ref, _, out_ref):
    count, rows = out_ref.shape[0], math.prod(out_ref.shape[1:-1])
    sums = [unpack_tail(ref[count * rows :], count * rows) for ref in (mine_ref, got_ref)]
    mine, other, _ = merge_weights(*sums, count * rows)
    for i in range(count):
        here = slice(i * rows, (i + 1) * rows)
        out = mine_ref[here].astype(jnp.float32) * mine[here]
        out = out + got_ref[here].astype(jnp.float32) * other[here]
        out_ref[i] = out.astype(jnp.bfloat16).reshape(out_ref.shape[1:])


def finish(mine, got, shape, after):
    return pl.pallas_call(
        finish_kernel,
        in_specs=in_vmem(2),
        out_shape=jax.ShapeDtypeStruct(shape, jnp.bfloat16),
        compiler_params=pltpu.CompilerParams(vmem_limit_bytes=16 << 20),
        cost_estimate=SMALL,
    )(mine, got, after)


def place_kernel(levels, plan, *refs):
    part_refs = refs[: len(plan)]
    out_ref, sems = refs[-2:]
    copies = []
    for (head, own), ref in zip(plan, part_refs):
        blocks = ref.shape[1]
        bit = half_bit(0)
        at = (bit if own else 1 - bit) * blocks
        for i in range(ref.shape[0]):
            there = out_ref.at[pl.ds(at, blocks), :, head + i]
            copies.append(pltpu.make_async_copy(ref.at[i], there, sems.at[len(copies)]))
    for copy in copies:
        copy.start()
    for copy in copies:
        copy.wait()


def place(out, parts, shape, levels, after):
    arrays = [array for array, _, _ in parts]
    plan = [(head, own) for _, head, own in parts]
    others = [after] if out is None else [after, out]
    return pl.pallas_call(
        functools.partial(place_kernel, levels, plan),
        in_specs=[pl.BlockSpec(memory_space=pltpu.VMEM)] * len(arrays)
        + [pl.BlockSpec(memory_space=pl.ANY), pl.BlockSpec(memory_space=pltpu.HBM)][: len(others)],
        out_specs=pl.BlockSpec(memory_space=pltpu.HBM),
        out_shape=pltpu.HBM(shape, jnp.bfloat16),
        input_output_aliases={} if out is None else {len(arrays) + 1: 0},
        scratch_shapes=[pltpu.SemaphoreType.DMA((sum(a.shape[0] for a in arrays),))],
        compiler_params=pltpu.CompilerParams(vmem_limit_bytes=16 << 20),
        cost_estimate=SMALL,
    )(*arrays, *others)


def on_device(shards, owners, queries, prompt_cache, suffix_cache, new_kv, ancestors, lengths):
    steps, per_owner, heads, group, size = queries.shape
    suffix_dev = suffix_cache.shape[2]
    factor = math.log2(math.e) / math.sqrt(size)
    levels = shards.bit_length() - 1
    if shards != 1 << levels or levels < 2 or steps % 2 or suffix_dev != steps:
        raise ValueError("unsupported sizes")

    def swap(value, bit):
        return lax.ppermute(value, "ctx", [(i, i ^ ((2 << bit) - 1)) for i in range(shards)])

    prompt_rows = prompt_cache.reshape(2, -1, size)
    mine, parents, extents, keys = build_message(
        suffix_cache.reshape(2, -1, size),
        new_kv.reshape(steps, 2, -1, size),
        ancestors,
        lengths,
        prompt_rows,
        heads,
        math.gcd(prompt_rows.shape[1] // 2, 1024 * heads),
    )
    row_list = [mine] + [
        lax.ppermute(mine, "dom", [(i, (i + hop) % owners) for i in range(owners)])
        for hop in range(1, owners)
    ]
    *prompt, bias = split_prompt(
        prompt_rows, keys, parents, extents, heads, owners, suffix_dev
    )
    prompt = prompt[:heads], prompt[heads:]
    last = [bias]

    def follow(results):
        last[0] = results[0] if isinstance(results, (tuple, list)) else results
        return results

    messages = {}
    blocks = steps * per_owner >> (levels - 1)

    def run_attend(group, kept, begun=()):
        return follow(
            attend(queries, prompt, bias, row_list, group, kept, factor, begun, last[0])
        )

    def run_merges(got, parts):
        for level in range(1, levels):
            send, *parts = follow(merge_parts(*parts, got, level, level == levels - 1, last[0]))
            got = swap(send, level)
        return send, got

    parts = []

    def run_finish(count, send, got):
        return follow(finish(send, got, (count, blocks, group, size), last[0]))

    def run_gather(head, done):
        count = done.shape[0]
        for level in range(levels - 2, 0, -1):
            other = swap(done, level)
            done = jnp.where(
                half_bit(level) == 1,
                jnp.concatenate([other, done], axis=1),
                jnp.concatenate([done, other], axis=1),
            )
        done = done.reshape(count, steps // 2, per_owner, group, size)
        parts.append((done, head, True))
        parts.append((swap(done, 0), head, False))

    first = max(heads // 2, 1)
    groups = [tuple(range(heads))[at : at + first] for at in range(0, heads, first)]
    begun = follow(begin(queries, prompt, groups[0], False, factor))
    arrived, kept = [], []
    for number, one in enumerate(groups):
        arrived.append(swap(run_attend(one, False, () if number else begun), 0))
        if not number:
            kept.append(run_attend(one, True))
    pairs = []
    for number, one in enumerate(groups):
        if number:
            kept.append(run_attend(one, True))
        pairs.append(run_merges(arrived[number], kept[number]))
    for one, pair in zip(groups, pairs):
        run_gather(one[0], run_finish(len(one), *pair))
    late = parts[-1:]
    early = [part for part in parts if not any(part is one for one in late)]
    out = place(None, early, queries.shape, levels, last[0]) if early else None
    return place(out, late, queries.shape, levels, last[0])


def solution(mesh):
    return jax.shard_map(
        functools.partial(on_device, mesh.shape["ctx"], mesh.shape["dom"]),
        mesh=mesh,
        in_specs=(
            P("groups", "dom", "tp", None, None),
            P("groups", "ctx", "tp", None),
            P("groups", "dom", "ctx", "tp", None),
            P("groups", None, "dom", "tp", None),
            P("groups", None),
            P("groups"),
        ),
        out_specs=P("groups", "dom", "tp", None, None),
        check_vma=False,
    )
```
